32 devices in a mesh: pipe: 2 (over x), dp: 16 (over z, y, core).
Axes of the slice: x: 2, y: 2, z: 4, core: 2. Of those that a mesh axis runs over, the one named last changes fastest.
Arguments:
- inputs: bfloat16 [2, 16384, 512], P('pipe', 'dp'), may hold values from -6 to 6
- src_len: int32 [32], P('dp'), may hold values from 128 to 512, as said below
- tgt_len: int32 [32], P('dp'), may hold values from 128 to 512, as said below
- cotangent: bfloat16 [16384, 512], P('dp'), may hold values from -6 to 6
- qkv_w: bfloat16 [2, 512, 1536], P('pipe'), may hold values from -0.375 to 0.375
- out_w: bfloat16 [2, 512, 512], P('pipe'), may hold values from -0.75 to 0.75
- in_w: bfloat16 [2, 512, 2048], P('pipe'), may hold values from -0.25 to 0.25
- in_b: bfloat16 [2, 2048], P('pipe'), may hold values from -3 to 3
- out2_w: bfloat16 [2, 2048, 512], P('pipe'), may hold values from -0.1875 to 0.1875
- out2_b: bfloat16 [2, 512], P('pipe'), may hold values from -3 to 3
- norm_gain: bfloat16 [2, 2, 512], P('pipe'), may hold values from 0.099609375 to 1.8984375
- norm_bias: bfloat16 [2, 2, 512], P('pipe'), may hold values from -2 to 2
- cross_qkv: bfloat16 [512, 1536], P('pipe'), may hold values from -0.375 to 0.375
- cross_out: bfloat16 [512, 512], P('pipe'), may hold values from -0.75 to 0.75
- slot_w: bfloat16 [1024, 512], P('pipe'), may hold values from -0.1875 to 0.1875
- cross_gain: bfloat16 [512], P('pipe'), may hold values from 0.099609375 to 1.8984375
- cross_bias: bfloat16 [512], P('pipe'), may hold values from -2 to 2
Outputs:
- block_out: bfloat16 [2, 16384, 512], P('pipe', 'dp')
- input_grad: float32 [2, 16384, 512], P('pipe', 'dp')
- grad_qkv_w: float32 [2, 512, 1536], P('pipe')
- grad_out_w: float32 [2, 512, 512], P('pipe')
- grad_in_w: float32 [2, 512, 2048], P('pipe')
- grad_in_b: float32 [2, 2048], P('pipe')
- grad_out2_w: float32 [2, 2048, 512], P('pipe')
- grad_out2_b: float32 [2, 512], P('pipe')
- grad_norm_gain: float32 [2, 2, 512], P('pipe')
- grad_norm_bias: float32 [2, 2, 512], P('pipe')
- grad_cross_qkv: float32 [512, 1536], P('pipe')
- grad_cross_out: float32 [512, 512], P('pipe')
- grad_slot_w: float32 [1024, 512], P('pipe')
- grad_cross_gain: float32 [512], P('pipe')
- grad_cross_bias: float32 [512], P('pipe')
The draws below stay inside these ranges and needn't reach their ends.
Inputs may be any that keep to these rules, and one draw needn't show every extreme that they name: `src_len`: some example has 512 valid source positions. `tgt_len`: some example has 512 valid target positions.
All inputs are finite; a program needn't handle non-finite values.
Results may differ from the reference program's by a relative error of at most 0.028.
The reference program's roundings to bfloat16 on the way count: a program that leaves them out, or rounds other values in their place, can miss the bound.
Values may be sent and summed in bfloat16 or wider, within the bound.
A program may use at most 256 MiB of HBM per device.

```python
import jax
import jax.numpy as jnp
from jax import lax

D = 512
HEADS = 8
FF = 2048
ROWS = 512
EXAMPLES = 32
TOKENS = 16384
N_PIPE = 2


def padded_lengths(key):
    draw_key, pick_key = jax.random.split(key)
    lengths = jax.random.randint(draw_key, (EXAMPLES,), ROWS // 4, ROWS + 1)
    chosen = jax.random.randint(pick_key, (), 0, EXAMPLES)
    return jnp.where(jnp.arange(EXAMPLES) == chosen, ROWS, lengths).astype(jnp.int32)


def draw_src_len(key, part):
    key = jax.random.fold_in(key, 11)
    return padded_lengths(key)


def draw_tgt_len(key, part):
    key = jax.random.fold_in(key, 12)
    return padded_lengths(key)


def steps_of(rng, extent, cuts, smallest, top_value):
    gain = 1.0
    for axis_at, parts in cuts:
        draws = jax.random.uniform(jax.random.fold_in(jax.random.fold_in(rng, 6), axis_at), (parts,), jnp.float32, smallest / len(cuts), top_value / len(cuts))
        gain = gain * jnp.repeat(jnp.exp(draws), extent[axis_at] // parts).reshape((-1,) + (1,) * (len(extent) - 1 - axis_at))
    return gain


def gaussian(own_key, extent, scale, reach, cuts=(), kind=jnp.bfloat16):
    gain = steps_of(own_key, extent, cuts, -0.22, 0.18) if cuts else 1.0
    array = jax.random.normal(own_key, extent, jnp.float32) * scale * gain
    return jnp.minimum(jnp.maximum(array, -reach), reach).astype(kind)


def setup_inputs(seed: int = 0) -> dict:
    splits = jax.random.split(jax.random.key(seed), 18)
    inputs = gaussian(splits[0], (N_PIPE, TOKENS, D), 1.0, 6.0, ((0, 2), (1, 16)))
    src_len = draw_src_len(jax.random.fold_in(splits[17], 71), 0)
    tgt_len = draw_tgt_len(jax.random.fold_in(splits[17], 71), 0)
    cotangent = gaussian(splits[3], (TOKENS, D), 1.0, 6.0, ((0, 16),))
    qkv_w = gaussian(splits[4], (N_PIPE, D, 3 * D), (D // 2) ** -0.5, 0.375, ((0, 2),))
    out_w = gaussian(splits[5], (N_PIPE, D, D), (D // 8) ** -0.5, 0.75, ((0, 2),))
    in_w = gaussian(splits[6], (N_PIPE, D, FF), D ** -0.5, 0.25, ((0, 2),))
    in_b = gaussian(splits[7], (N_PIPE, FF), 0.5, 3.0, ((0, 2),))
    out2_w = gaussian(splits[8], (N_PIPE, FF, D), (FF // 2) ** -0.5, 0.1875, ((0, 2),))
    out2_b = gaussian(splits[9], (N_PIPE, D), 0.5, 3.0, ((0, 2),))
    norm_gain = jnp.clip(1.0 + 0.18 * jax.random.normal(splits[10], (N_PIPE, 2, D), jnp.float32), 0.099609375, 1.8984375).astype(jnp.bfloat16)
    norm_bias = gaussian(splits[11], (N_PIPE, 2, D), 0.3, 2.0, ((0, 2),))
    cross_qkv = gaussian(splits[12], (D, 3 * D), (D // 2) ** -0.5, 0.375, ((0, 2),))
    cross_out = gaussian(splits[13], (D, D), (D // 8) ** -0.5, 0.75, ((0, 2),))
    slot_w = gaussian(splits[14], (2 * D, D), (2 * D) ** -0.5, 0.1875, ((0, 2),))
    cross_gain = jnp.clip(1.0 + 0.18 * jax.random.normal(splits[15], (D,), jnp.float32), 0.099609375, 1.8984375).astype(jnp.bfloat16)
    cross_bias = gaussian(splits[16], (D,), 0.3, 2.0, ((0, 2),))
    return {"inputs": inputs, "src_len": src_len, "tgt_len": tgt_len, "cotangent": cotangent, "qkv_w": qkv_w, "out_w": out_w, "in_w": in_w, "in_b": in_b, "out2_w": out2_w, "out2_b": out2_b, "norm_gain": norm_gain, "norm_bias": norm_bias, "cross_qkv": cross_qkv, "cross_out": cross_out, "slot_w": slot_w, "cross_gain": cross_gain, "cross_bias": cross_bias}


@jax.custom_vjp
def low(v):
    return lax.optimization_barrier(v.astype(jnp.bfloat16)).astype(jnp.float32)

@jax.custom_vjp
def low_back(v):
    return v

def low_keep(v):
    return (low(v), None)

def low_pass(kept, grad):
    return (grad,)

def back_keep(v):
    return (v, None)

def back_low(kept, grad):
    return (low(grad),)
low.defvjp(low_keep, low_pass)
low_back.defvjp(back_keep, back_low)

def multiply(left_side, right_side):
    return jnp.dot(left_side, right_side, precision=lax.Precision.HIGHEST)

def layer_norm(values, gain_row, bias_row):
    center = lax.optimization_barrier(jnp.mean(values, axis=-1, keepdims=True))
    shifted = values - center
    spread = lax.optimization_barrier(jnp.mean(shifted * shifted, axis=-1, keepdims=True))
    return shifted * lax.rsqrt(spread + 1e-05) * gain_row + bias_row

def attend(query_rows, key_rows, value_rows, keep_mask):
    count = query_rows.shape[0]
    head_size = query_rows.shape[1] // HEADS
    query_heads = query_rows.reshape(count, HEADS, head_size)
    key_heads = key_rows.reshape(count, HEADS, head_size)
    value_heads = value_rows.reshape(count, HEADS, head_size)
    scores = jnp.einsum('qhd,khd->hqk', query_heads, key_heads, precision=lax.Precision.HIGHEST) * head_size ** (-0.5)
    scores = low_back(scores)
    scores = jnp.where(keep_mask[None, None, :], scores, -1e+30)
    weights = low(jax.nn.softmax(scores, axis=-1))
    mixed_heads = jnp.einsum('hqk,khd->qhd', weights, value_heads, precision=lax.Precision.HIGHEST)
    return mixed_heads.reshape(query_rows.shape)

def self_block(rows_block, keep_mask, qkv_w, out_w, gain_row, bias_row):
    model_width = rows_block.shape[1]
    qkv = low(low_back(multiply(rows_block, qkv_w)))
    mixed_heads = low(low_back(attend(qkv[:, :model_width], qkv[:, model_width:2 * model_width], qkv[:, 2 * model_width:], keep_mask)))
    return layer_norm(rows_block + low_back(multiply(mixed_heads, out_w)), gain_row, bias_row)

def feed_forward(normed, in_w, in_b, out2_w, out2_b, gain_row, bias_row):
    pre_act = low_back(multiply(low(normed), in_w) + in_b)
    act_low = low(jax.nn.gelu(pre_act))
    return layer_norm(normed + low_back(multiply(act_low, out2_w) + out2_b), gain_row, bias_row)

def forward(params, source, target, src_keep, tgt_keep, slot_keep):
    qkv_w, out_w, in_w, in_b, out2_w, out2_b, norm_gain, norm_bias, cross_qkv, cross_out, slot_w, cross_gain, cross_bias = params
    model_width = source.shape[1]
    first_norm = self_block(source, src_keep, qkv_w[0], out_w[0], norm_gain[0, 0], norm_bias[0, 0])
    encoded = feed_forward(first_norm, in_w[0], in_b[0], out2_w[0], out2_b[0], norm_gain[0, 1], norm_bias[0, 1])
    memory = low(low_back(encoded * src_keep.astype(jnp.float32)[:, None]))
    target_norm = self_block(target, tgt_keep, qkv_w[1], out_w[1], norm_gain[1, 0], norm_bias[1, 0])
    target_low = low(target_norm)
    cross_query = low(low_back(multiply(target_low, cross_qkv[:, :model_width])))
    cross_pair = low(low_back(multiply(memory, cross_qkv[:, model_width:])))
    cross_mixed = low(low_back(attend(cross_query, cross_pair[:, :model_width], cross_pair[:, model_width:], src_keep)))
    middle = layer_norm(target_norm + low_back(multiply(cross_mixed, cross_out)), cross_gain, cross_bias)
    final_low = low(feed_forward(middle, in_w[1], in_b[1], out2_w[1], out2_b[1], norm_gain[1, 1], norm_bias[1, 1]))
    following = jnp.concatenate([final_low[1:], jnp.zeros_like(final_low[:1])], axis=0)
    slot_pairs = jnp.concatenate([final_low, following], axis=1)
    slot_out = multiply(slot_pairs, slot_w) * slot_keep[:, None]
    return (memory, slot_out)

def reference(inputs, src_len, tgt_len, cotangent, qkv_w, out_w, in_w, in_b, out2_w, out2_b, norm_gain, norm_bias, cross_qkv, cross_out, slot_w, cross_gain, cross_bias):
    params = tuple((weight.astype(jnp.float32) for weight in (qkv_w, out_w, in_w, in_b, out2_w, out2_b, norm_gain, norm_bias, cross_qkv, cross_out, slot_w, cross_gain, cross_bias)))
    sources = inputs[0].astype(jnp.float32).reshape(EXAMPLES, ROWS, D)
    targets = inputs[1].astype(jnp.float32).reshape(EXAMPLES, ROWS, D)
    grads_out = cotangent.astype(jnp.float32).reshape(EXAMPLES, ROWS, D)
    position = jnp.arange(ROWS, dtype=jnp.int32)

    def per_example(grad_total, example):
        source, target, grad_slot, source_count, target_count = example
        src_keep = position < source_count
        tgt_keep = position < target_count
        slot_keep = (position < target_count - 1).astype(jnp.float32)

        def run(weights_now, source_now, target_now):
            return forward(weights_now, source_now, target_now, src_keep, tgt_keep, slot_keep)
        (memory, slot_out), pull_back = jax.vjp(run, params, source, target)
        weight_grads, source_grad, target_grad = pull_back((jnp.zeros_like(memory), grad_slot))
        grad_total = jax.tree.map(jnp.add, grad_total, weight_grads)
        return (grad_total, (memory, slot_out, source_grad, target_grad))
    start = jax.tree.map(jnp.zeros_like, params)
    totals, (memory, slot_out, source_grad, target_grad) = lax.scan(per_example, start, (sources, targets, grads_out, src_len, tgt_len))
    block_out = jnp.stack([memory.reshape(TOKENS, D), slot_out.reshape(TOKENS, D)]).astype(jnp.bfloat16)
    input_grad = jnp.stack([source_grad.reshape(TOKENS, D), target_grad.reshape(TOKENS, D)])
    return (block_out, input_grad, totals[0], totals[1], totals[2], totals[3], totals[4], totals[5], totals[6], totals[7], totals[8], totals[9], totals[10], totals[11], totals[12])
```

```python
import functools

import jax
import jax.numpy as jnp
from jax import lax
from jax.experimental import pallas as pl
from jax.experimental.pallas import tpu as pltpu
from jax.sharding import PartitionSpec as P

HEADS = 8


def passed_along(block, axis, distance):
    devices = range(lax.axis_size(axis))
    route = [(i - distance, i) for i in devices if i - distance in devices]
    return lax.ppermute(block, axis, route)


def layer_norm(values, gain_row, bias_row):
    center = jnp.mean(values, axis=-1, keepdims=True)
    shifted = values - center
    spread = jnp.mean(shifted * shifted, axis=-1, keepdims=True)
    return shifted * lax.rsqrt(spread + 1e-05) * gain_row + bias_row


def norm_backward(values, gain_row, bias_row, grad_out):
    _, pull_back = jax.vjp(layer_norm, values, gain_row, bias_row)
    return pull_back(grad_out)


def row_product(left_side, right_side):
    return lax.dot_general(
        left_side, right_side, (((0,), (0,)), ((), ())), preferred_element_type=jnp.float32
    )


def back_product(left_side, right_side):
    return lax.dot_general(
        left_side, right_side, (((1,), (1,)), ((), ())), preferred_element_type=jnp.float32
    )


def split_heads(values):
    return values.reshape(values.shape[0], HEADS, values.shape[1] // HEADS)


def masked_scores(query_rows, key_rows, keep_mask):
    score_scale = (query_rows.shape[1] // HEADS) ** (-0.5)
    scores = (
        jnp.einsum(
            "qhd,khd->hqk",
            split_heads(query_rows),
            split_heads(key_rows),
            preferred_element_type=jnp.float32,
        )
        * score_scale
    )
    return jnp.where(keep_mask[None, None, :], scores, -1e30)


def attention_forward(query_rows, key_rows, value_rows, keep_mask):
    scores = masked_scores(query_rows, key_rows, keep_mask)
    row_top = jnp.max(scores, axis=-1, keepdims=True)
    exp_scores = jnp.exp(scores - row_top)
    row_total = jnp.sum(exp_scores, axis=-1, keepdims=True)
    weights = (exp_scores / row_total).astype(jnp.bfloat16)
    mixed_heads = jnp.einsum(
        "hqk,khd->qhd", weights, split_heads(value_rows), preferred_element_type=jnp.float32
    )
    return (mixed_heads.reshape(query_rows.shape), row_top + jnp.log(row_total))


def attention_backward(query_rows, key_rows, value_rows, keep_mask, logsum, grad_mixed):
    score_scale = (query_rows.shape[1] // HEADS) ** (-0.5)
    prob_rows = jnp.exp(masked_scores(query_rows, key_rows, keep_mask) - logsum)
    grad_heads = split_heads(grad_mixed)
    grad_probs = jnp.einsum(
        "qhd,khd->hqk", grad_heads, split_heads(value_rows), preferred_element_type=jnp.float32
    )
    grad_scores = (
        prob_rows * (grad_probs - jnp.sum(prob_rows * grad_probs, axis=-1, keepdims=True))
    ).astype(jnp.bfloat16)
    grad_query = (
        jnp.einsum(
            "hqk,khd->qhd", grad_scores, split_heads(key_rows), preferred_element_type=jnp.float32
        )
        * score_scale
    )
    grad_keys = (
        jnp.einsum(
            "hqk,qhd->khd", grad_scores, split_heads(query_rows), preferred_element_type=jnp.float32
        )
        * score_scale
    )
    grad_values = jnp.einsum(
        "hqk,qhd->khd",
        prob_rows.astype(jnp.bfloat16),
        grad_heads,
        preferred_element_type=jnp.float32,
    )
    return (
        grad_query.reshape(query_rows.shape),
        grad_keys.reshape(key_rows.shape),
        grad_values.reshape(value_rows.shape),
    )


def self_forward(rows_block, keep_mask, qkv_w, out_w):
    model_width = rows_block.shape[1]
    qkv = jnp.dot(rows_block, qkv_w, preferred_element_type=jnp.float32).astype(jnp.bfloat16)
    mixed_rows, logsum = attention_forward(
        qkv[:, :model_width],
        qkv[:, model_width : 2 * model_width],
        qkv[:, 2 * model_width :],
        keep_mask,
    )
    attn_low = mixed_rows.astype(jnp.bfloat16)
    residual = rows_block.astype(jnp.float32) + jnp.dot(
        attn_low, out_w, preferred_element_type=jnp.float32
    )
    return (residual, (qkv, logsum, attn_low))


def self_backward(rows_block, keep_mask, qkv_w, out_w, kept_values, grad_residual):
    qkv, logsum, attn_low = kept_values
    model_width = rows_block.shape[1]
    grad_branch = grad_residual.astype(jnp.bfloat16)
    grad_out_w = row_product(attn_low, grad_branch)
    grad_attn = back_product(grad_branch, out_w).astype(jnp.bfloat16)
    grad_query, grad_keys, grad_values = attention_backward(
        qkv[:, :model_width],
        qkv[:, model_width : 2 * model_width],
        qkv[:, 2 * model_width :],
        keep_mask,
        logsum,
        grad_attn,
    )
    grad_qkv_low = jnp.concatenate([grad_query, grad_keys, grad_values], axis=1).astype(
        jnp.bfloat16
    )
    grad_qkv_w = row_product(rows_block, grad_qkv_low)
    grad_rows = grad_residual + back_product(grad_qkv_low, qkv_w)
    return (grad_rows, grad_qkv_w, grad_out_w)


def ffn_forward(normed, in_w, in_b, out2_w, out2_b):
    normed_low = normed.astype(jnp.bfloat16)
    pre_act = jnp.dot(normed_low, in_w, preferred_element_type=jnp.float32) + in_b.astype(
        jnp.float32
    )
    act_low = jax.nn.gelu(pre_act).astype(jnp.bfloat16)
    residual_two = (
        normed
        + jnp.dot(act_low, out2_w, preferred_element_type=jnp.float32)
        + out2_b.astype(jnp.float32)
    )
    return (residual_two, (normed_low, pre_act, act_low))


def ffn_backward(grad_residual, in_w, out2_w, kept_values):
    normed_low, pre_act, act_low = kept_values
    grad_branch = grad_residual.astype(jnp.bfloat16)
    grad_out2_w = row_product(act_low, grad_branch)
    grad_out2_b = jnp.sum(grad_branch, axis=0, dtype=jnp.float32)
    grad_act = back_product(grad_branch, out2_w)
    _, pull_back = jax.vjp(jax.nn.gelu, pre_act)
    grad_pre = pull_back(grad_act)[0].astype(jnp.bfloat16)
    grad_in_b = jnp.sum(grad_pre, axis=0, dtype=jnp.float32)
    grad_in_w = row_product(normed_low, grad_pre)
    grad_normed = grad_residual + back_product(grad_pre, in_w)
    return (grad_normed, (grad_in_w, grad_in_b, grad_out2_w, grad_out2_b))


def encoder_forward(rows_block, keep_mask, weights):
    qkv_w, out_w, in_w, in_b, out2_w, out2_b, gain_rows, biases = weights
    gain_float = gain_rows.astype(jnp.float32)
    bias_float = biases.astype(jnp.float32)
    residual, attn_kept = self_forward(rows_block, keep_mask, qkv_w, out_w)
    first_norm = layer_norm(residual, gain_float[0], bias_float[0])
    residual_two, ffn_kept = ffn_forward(first_norm, in_w, in_b, out2_w, out2_b)
    final_norm = layer_norm(residual_two, gain_float[1], bias_float[1])
    memory = (final_norm * keep_mask.astype(jnp.float32)[:, None]).astype(jnp.bfloat16)
    return (memory, (attn_kept, residual, ffn_kept, residual_two))


def encoder_backward(rows_block, keep_mask, weights, kept_values, grad_memory):
    qkv_w, out_w, in_w, in_b, out2_w, out2_b, gain_rows, biases = weights
    gain_float = gain_rows.astype(jnp.float32)
    bias_float = biases.astype(jnp.float32)
    attn_kept, residual, ffn_kept, residual_two = kept_values
    grad_final = grad_memory.astype(jnp.float32) * keep_mask.astype(jnp.float32)[:, None]
    grad_two, grad_gain_one, grad_bias_one = norm_backward(
        residual_two, gain_float[1], bias_float[1], grad_final
    )
    grad_first, ffn_grads = ffn_backward(grad_two, in_w, out2_w, ffn_kept)
    grad_residual, grad_gain_zero, grad_bias_zero = norm_backward(
        residual, gain_float[0], bias_float[0], grad_first
    )
    grad_rows, grad_qkv_w, grad_out_w = self_backward(
        rows_block, keep_mask, qkv_w, out_w, attn_kept, grad_residual
    )
    shared = (
        (grad_qkv_w, grad_out_w)
        + ffn_grads
        + (jnp.stack([grad_gain_zero, grad_gain_one]), jnp.stack([grad_bias_zero, grad_bias_one]))
    )
    return (grad_rows, shared)


def decoder_block(rows_block, memory, src_keep, tgt_keep, slot_keep, grad_slot_in, weights, extras):
    qkv_w, out_w, in_w, in_b, out2_w, out2_b, gain_rows, biases = weights
    cross_qkv, cross_out, slot_w, cross_gain, cross_bias = extras
    model_width = rows_block.shape[1]
    gain_float = gain_rows.astype(jnp.float32)
    bias_float = biases.astype(jnp.float32)
    cross_gain_float = cross_gain.astype(jnp.float32)
    cross_bias_float = cross_bias.astype(jnp.float32)
    residual, attn_kept = self_forward(rows_block, tgt_keep, qkv_w, out_w)
    first_norm = layer_norm(residual, gain_float[0], bias_float[0])
    first_low = first_norm.astype(jnp.bfloat16)
    cross_query = jnp.dot(
        first_low, cross_qkv[:, :model_width], preferred_element_type=jnp.float32
    ).astype(jnp.bfloat16)
    cross_pair = jnp.dot(
        memory, cross_qkv[:, model_width:], preferred_element_type=jnp.float32
    ).astype(jnp.bfloat16)
    cross_mixed, cross_logsum = attention_forward(
        cross_query, cross_pair[:, :model_width], cross_pair[:, model_width:], src_keep
    )
    cross_low = cross_mixed.astype(jnp.bfloat16)
    cross_residual = first_norm + jnp.dot(cross_low, cross_out, preferred_element_type=jnp.float32)
    middle = layer_norm(cross_residual, cross_gain_float, cross_bias_float)
    residual_two, ffn_kept = ffn_forward(middle, in_w, in_b, out2_w, out2_b)
    final_low = layer_norm(residual_two, gain_float[1], bias_float[1]).astype(jnp.bfloat16)
    following = jnp.concatenate([final_low[1:], jnp.zeros_like(final_low[:1])], axis=0)
    slot_pairs = jnp.concatenate([final_low, following], axis=1)
    slot_mask = slot_keep.astype(jnp.float32)[:, None]
    slot_out = (jnp.dot(slot_pairs, slot_w, preferred_element_type=jnp.float32) * slot_mask).astype(
        jnp.bfloat16
    )
    grad_slot = (grad_slot_in.astype(jnp.float32) * slot_mask).astype(jnp.bfloat16)
    grad_slot_w = row_product(slot_pairs, grad_slot)
    grad_pairs = back_product(grad_slot, slot_w)
    grad_final = grad_pairs[:, :model_width] + jnp.concatenate(
        [jnp.zeros_like(grad_pairs[:1, model_width:]), grad_pairs[:-1, model_width:]], axis=0
    )
    grad_two, grad_gain_one, grad_bias_one = norm_backward(
        residual_two, gain_float[1], bias_float[1], grad_final
    )
    grad_middle, ffn_grads = ffn_backward(grad_two, in_w, out2_w, ffn_kept)
    grad_cross_residual, grad_cross_gain, grad_cross_bias = norm_backward(
        cross_residual, cross_gain_float, cross_bias_float, grad_middle
    )
    grad_cross_branch = grad_cross_residual.astype(jnp.bfloat16)
    grad_cross_out = row_product(cross_low, grad_cross_branch)
    grad_cross_low = back_product(grad_cross_branch, cross_out).astype(jnp.bfloat16)
    grad_query, grad_keys, grad_values = attention_backward(
        cross_query,
        cross_pair[:, :model_width],
        cross_pair[:, model_width:],
        src_keep,
        cross_logsum,
        grad_cross_low,
    )
    grad_query_low = grad_query.astype(jnp.bfloat16)
    grad_pair_low = jnp.concatenate([grad_keys, grad_values], axis=1).astype(jnp.bfloat16)
    grad_cross_qkv = jnp.concatenate(
        [row_product(first_low, grad_query_low), row_product(memory, grad_pair_low)], axis=1
    )
    grad_memory = back_product(grad_pair_low, cross_qkv[:, model_width:]).astype(jnp.bfloat16)
    grad_first = grad_cross_residual + back_product(grad_query_low, cross_qkv[:, :model_width])
    grad_residual, grad_gain_zero, grad_bias_zero = norm_backward(
        residual, gain_float[0], bias_float[0], grad_first
    )
    grad_rows, grad_qkv_w, grad_out_w = self_backward(
        rows_block, tgt_keep, qkv_w, out_w, attn_kept, grad_residual
    )
    shared = (
        (grad_qkv_w, grad_out_w)
        + ffn_grads
        + (jnp.stack([grad_gain_zero, grad_gain_one]), jnp.stack([grad_bias_zero, grad_bias_one]))
    )
    extra_grads = (grad_cross_qkv, grad_cross_out, grad_slot_w, grad_cross_gain, grad_cross_bias)
    return (slot_out, grad_rows, grad_memory, shared, extra_grads)


MESH = pl.DeviceIdType.MESH
PARTS = 2


def ring_place(chip, chips):
    half = chip // 2
    return jnp.where(chip % 2 == 0, half, chips - 1 - half)


def ring_chip(place, chips):
    return jnp.where(place < chips // 2, 2 * place, 2 * (chips - 1 - place) + 1)


def part_rows(chunk_rows):
    first = (chunk_rows // 2 + 15) // 16 * 16
    if first == chunk_rows:
        return ((0, chunk_rows),)
    return ((0, first), (first, chunk_rows - first))


def ring_kernel(
    devices, mine, small, total, small_total, sibling, arrived, small_sent, small_arrived,
    sib_send, sib_recv, ring_send, ring_recv, gather_send, gather_recv, share_send, share_recv,
    small_send, small_recv,
):
    pipe = lax.axis_index("pipe")
    me = lax.axis_index("dp")
    chips = devices // 2
    core = me % 2
    place = ring_place(me // 2, chips)
    right = ring_chip((place + 1) % chips, chips) * 2 + core
    left = ring_chip((place + chips - 1) % chips, chips) * 2 + core
    other = me + 1 - 2 * core
    chunk_rows = mine.shape[3]
    parts = part_rows(chunk_rows)
    levels = devices.bit_length() - 1

    def paired(bit):
        return me + bit - 2 * bit * ((me // bit) % 2)

    barrier = pltpu.get_barrier_semaphore()
    greeted = [right, left] + [paired(1 << level) for level in range(levels)]
    for friend in greeted:
        pl.semaphore_signal(barrier, inc=1, device_id=(pipe, friend), device_id_type=MESH)
    pl.semaphore_wait(barrier, len(greeted))

    def chunk_at(way, step):
        if way == 0:
            return (place - step + 2 * chips) % chips
        return (place + step + chips) % chips

    def to_other(way, step):
        chunk = chunk_at(way, step)
        return pltpu.make_async_remote_copy(
            src_ref=mine.at[1 - core, way, chunk],
            dst_ref=sibling.at[way, chunk],
            send_sem=sib_send.at[way, step],
            recv_sem=sib_recv.at[way, step],
            device_id=(pipe, other),
            device_id_type=MESH,
        )

    def ring_copy(way, step, part):
        begin, rows = parts[part]
        spot = pl.ds(begin, rows)
        return pltpu.make_async_remote_copy(
            src_ref=arrived.at[way, step, spot],
            dst_ref=arrived.at[way, step + 1, spot],
            send_sem=ring_send.at[way, step, part],
            recv_sem=ring_recv.at[way, step, part],
            device_id=(pipe, (right, left)[way]),
            device_id_type=MESH,
        )

    def gather_copy(way, step, part):
        begin, rows = parts[part]
        spot = pl.ds(begin, rows)
        chunk = chunk_at(way, step - 1)
        return pltpu.make_async_remote_copy(
            src_ref=total.at[core, way, chunk, spot],
            dst_ref=total.at[core, way, chunk, spot],
            send_sem=gather_send.at[way, step, part],
            recv_sem=gather_recv.at[way, step, part],
            device_id=(pipe, (right, left)[way]),
            device_id_type=MESH,
        )

    def share_copy(way, step, part):
        begin, rows = parts[part]
        spot = pl.ds(begin, rows)
        chunk = chunk_at(way, step - 1)
        return pltpu.make_async_remote_copy(
            src_ref=total.at[core, way, chunk, spot],
            dst_ref=total.at[core, way, chunk, spot],
            send_sem=share_send.at[way, step, part],
            recv_sem=share_recv.at[way, step, part],
            device_id=(pipe, other),
            device_id_type=MESH,
        )

    def small_copy(level, bit):
        return pltpu.make_async_remote_copy(
            src_ref=small_sent.at[level],
            dst_ref=small_arrived.at[level],
            send_sem=small_send.at[level],
            recv_sem=small_recv.at[level],
            device_id=(pipe, paired(bit)),
            device_id_type=MESH,
        )

    def start_sibling(step, carry):
        for way in range(2):
            to_other(way, step).start()
        return carry

    lax.fori_loop(0, chips, start_sibling, 0)
    small_sent[0] = small[...]
    small_copy(0, 1).start()

    for way in range(2):
        to_other(way, 0).wait_recv()
        for part, (begin, rows) in enumerate(parts):
            spot = pl.ds(begin, rows)
            arrived[way, 0, spot] = (
                mine[core, way, place, spot].astype(jnp.float32)
                + sibling[way, place, spot].astype(jnp.float32)
            ).astype(jnp.bfloat16)
            ring_copy(way, 0, part).start()

    def merge_small(level, bit):
        small_copy(level, bit).wait_recv()
        merged = small_sent[level] + small_arrived[level]

        @pl.when(level + 1 < levels)
        def _():
            small_sent[level + 1] = merged
            small_copy(level + 1, 2 * bit).start()

        @pl.when(level + 1 == levels)
        def _():
            small_total[...] = merged

    def own_sum(way, step, part):
        begin, rows = parts[part]
        spot = pl.ds(begin, rows)
        chunk = chunk_at(way, step + 1)
        return (
            arrived[way, step + 1, spot].astype(jnp.float32)
            + mine[core, way, chunk, spot].astype(jnp.float32)
            + sibling[way, chunk, spot].astype(jnp.float32)
        ).astype(jnp.bfloat16)

    def ring_step(step, bit):
        @pl.when(step < levels)
        def _():
            merge_small(step, bit)

        for way in range(2):
            to_other(way, step + 1).wait_recv()
        for part, (begin, rows) in enumerate(parts):
            for way in range(2):
                ring_copy(way, step, part).wait_recv()
                arrived[way, step + 1, pl.ds(begin, rows)] = own_sum(way, step, part)
                ring_copy(way, step + 1, part).start()
        return 2 * bit

    lax.fori_loop(0, chips - 2, ring_step, 1)

    last = chips - 2
    for way in range(2):
        to_other(way, last + 1).wait_recv()
    for part, (begin, rows) in enumerate(parts):
        for way in range(2):
            ring_copy(way, last, part).wait_recv()
            total[core, way, chunk_at(way, last + 1), pl.ds(begin, rows)] = own_sum(
                way, last, part
            )
            gather_copy(way, 0, part).start()
            share_copy(way, 0, part).start()

    def gather_step(step, carry):
        for part in range(len(parts)):
            for way in range(2):
                gather_copy(way, step, part).wait_recv()
                gather_copy(way, step + 1, part).start()
                share_copy(way, step + 1, part).start()
        return carry

    lax.fori_loop(0, chips - 2, gather_step, 0)
    for part in range(len(parts)):
        for way in range(2):
            gather_copy(way, last, part).wait_recv()
            share_copy(way, last + 1, part).start()

    def finish_share(step, carry):
        for way in range(2):
            to_other(way, step).wait_send()
            for part in range(len(parts)):
                share_copy(way, step, part).wait()
        return carry

    lax.fori_loop(0, chips, finish_share, 0)

    def finish_ring(step, carry):
        for way in range(2):
            for part in range(len(parts)):
                ring_copy(way, step, part).wait_send()
                gather_copy(way, step, part).wait_send()
        return carry

    lax.fori_loop(0, chips - 1, finish_ring, 0)
    for level in range(levels):
        small_copy(level, 1 << level).wait_send()


def ring_layout(rows, devices):
    chips = devices // 2
    chunk_rows = -(-rows // (4 * chips * 16)) * 16
    return chips, chunk_rows


def ring_sum(packed, small, devices):
    rows, width = packed.shape
    chips, chunk_rows = ring_layout(rows, devices)
    padded = 4 * chips * chunk_rows
    if padded != rows:
        packed = jnp.pad(packed, ((0, padded - rows), (0, 0)))
    levels = devices.bit_length() - 1
    pieces = len(part_rows(chunk_rows))
    dma = pltpu.SemaphoreType.DMA
    vmem = pl.BlockSpec(memory_space=pltpu.VMEM)
    total, small_total = pl.pallas_call(
        functools.partial(ring_kernel, devices),
        out_shape=(
            jax.ShapeDtypeStruct((2, 2, chips, chunk_rows, width), jnp.bfloat16),
            jax.ShapeDtypeStruct(small.shape, jnp.float32),
        ),
        in_specs=[vmem, vmem],
        out_specs=(vmem, vmem),
        scratch_shapes=[
            pltpu.VMEM((2, chips, chunk_rows, width), jnp.bfloat16),
            pltpu.VMEM((2, chips, chunk_rows, width), jnp.bfloat16),
            pltpu.VMEM((levels,) + small.shape, jnp.float32),
            pltpu.VMEM((levels,) + small.shape, jnp.float32),
            dma((2, chips)),
            dma((2, chips)),
            dma((2, chips, pieces)),
            dma((2, chips, pieces)),
            dma((2, chips, pieces)),
            dma((2, chips, pieces)),
            dma((2, chips, pieces)),
            dma((2, chips, pieces)),
            dma((levels,)),
            dma((levels,)),
        ],
        compiler_params=pltpu.CompilerParams(
            collective_id=0, has_side_effects=True, vmem_limit_bytes=48 * 2**20
        ),
        name="ring_sum",
    )(packed.reshape(2, 2, chips, chunk_rows, width), small)
    return total.reshape(padded, width)[:rows], small_total


def add_trees(left_side, right_side):
    if left_side is None:
        return right_side
    return jax.tree.map(jnp.add, left_side, right_side)


def on_section(active, section_work, operand):

    def skipped(operand_now):
        return jax.tree.map(jnp.zeros_like, section_work(operand_now))

    return lax.cond(active, section_work, skipped, operand)


def local(
    inputs,
    src_len,
    tgt_len,
    cotangent,
    qkv_w,
    out_w,
    in_w,
    in_b,
    out2_w,
    out2_b,
    norm_gain,
    norm_bias,
    cross_qkv,
    cross_out,
    slot_w,
    cross_gain,
    cross_bias,
):
    section_index = lax.axis_index("pipe")
    weights = (
        qkv_w[0],
        out_w[0],
        in_w[0],
        in_b[0],
        out2_w[0],
        out2_b[0],
        norm_gain[0],
        norm_bias[0],
    )
    extras = (
        lax.all_gather(cross_qkv, "pipe", axis=0, tiled=True),
        lax.all_gather(cross_out, "pipe", axis=0, tiled=True),
        lax.all_gather(slot_w, "pipe", axis=0, tiled=True),
        lax.all_gather(cross_gain, "pipe", axis=0, tiled=True),
        lax.all_gather(cross_bias, "pipe", axis=0, tiled=True),
    )
    rows_all = inputs[0]
    blocks = src_len.shape[0]
    length = rows_all.shape[0] // blocks
    position = jnp.arange(length, dtype=jnp.int32)
    memory_list = []
    slot_list = []
    target_list = []
    source_list = []
    returned = []
    kept_list = []
    decoder_shared = None
    extra_full = None
    encoder_shared = None
    for turn_index in range(blocks + 1):
        if turn_index < blocks:
            lower = turn_index * length
            upper = lower + length
            src_keep = position < src_len[turn_index]
            tgt_keep = position < tgt_len[turn_index]
            slot_keep = position < tgt_len[turn_index] - 1

            def encode_block(rows_now, keep_now=src_keep):
                return encoder_forward(rows_now, keep_now, weights)

            memory_block, kept_block = on_section(
                section_index == 0, encode_block, rows_all[lower:upper]
            )
            kept_list.append(kept_block)
            memory_list.append(memory_block)
            memory_in = passed_along(memory_block, "pipe", 1)

            def decode_block(
                memory_now,
                lower_now=lower,
                upper_now=upper,
                src_now=src_keep,
                tgt_now=tgt_keep,
                slot_now=slot_keep,
            ):
                return decoder_block(
                    rows_all[lower_now:upper_now],
                    memory_now,
                    src_now,
                    tgt_now,
                    slot_now,
                    cotangent[lower_now:upper_now],
                    weights,
                    extras,
                )

            slot_out, grad_rows, grad_memory, shared, extra_grads = on_section(
                section_index == 1, decode_block, memory_in
            )
            slot_list.append(slot_out)
            target_list.append(grad_rows)
            decoder_shared = add_trees(decoder_shared, shared)
            extra_full = add_trees(extra_full, extra_grads)
            returned.append(passed_along(grad_memory, "pipe", -1))
        if turn_index >= 1:
            back_index = turn_index - 1
            back_lower = back_index * length
            back_keep = position < src_len[back_index]

            def encode_back_block(
                grad_now, lower_now=back_lower, keep_now=back_keep, kept_now=kept_list[back_index]
            ):
                return encoder_backward(
                    rows_all[lower_now : lower_now + length], keep_now, weights, kept_now, grad_now
                )

            grad_rows, shared = on_section(
                section_index == 0, encode_back_block, returned[back_index]
            )
            source_list.append(grad_rows)
            encoder_shared = add_trees(encoder_shared, shared)
    memory_all = jnp.concatenate(memory_list, axis=0)
    slot_all = jnp.concatenate(slot_list, axis=0)
    target_grad = jnp.concatenate(target_list, axis=0)
    source_grad = jnp.concatenate(source_list, axis=0)
    shared_local = jax.tree.map(jnp.add, decoder_shared, encoder_shared)
    low = jnp.bfloat16
    width = rows_all.shape[1]
    extra_low = [part.astype(low) for part in extra_full[:3]]
    extra_small = jnp.stack([extra_full[3], extra_full[4]])

    def own_half(values, axis=0):
        half = values.shape[axis] // 2
        sent = lax.slice_in_dim(values, 0, half, axis=axis)
        kept = lax.slice_in_dim(values, half, 2 * half, axis=axis)
        came = lax.ppermute(sent, "pipe", [(1, 0)])
        return jnp.where(section_index == 0, came, kept)

    blocks_low = []
    grad_list = [shared_local[0], shared_local[1], shared_local[2], shared_local[4]]
    for grad in [part.astype(low) for part in grad_list] + [own_half(part) for part in extra_low]:
        for column in range(grad.shape[1] // width):
            blocks_low.append(grad[:, column * width : (column + 1) * width])
    packed = jnp.concatenate(blocks_low, axis=0)
    small_rows = [
        shared_local[3].reshape(-1, width),
        shared_local[5].reshape(-1, width),
        shared_local[6],
        shared_local[7],
        own_half(extra_small.astype(low), axis=1).astype(jnp.float32).reshape(1, width),
    ]
    small = jnp.concatenate(small_rows, axis=0)
    small = jnp.pad(small, ((0, -small.shape[0] % 8), (0, 0)))
    total, small_total = ring_sum(packed, small, lax.axis_size("dp"))

    grads_out = []
    begin = 0
    for rows, columns in [grad.shape for grad in grad_list] + [
        (part.shape[0] // 2, part.shape[1]) for part in extra_low
    ]:
        pieces = []
        for _ in range(columns // width):
            pieces.append(total[begin : begin + rows])
            begin += rows
        grads_out.append(jnp.concatenate(pieces, axis=1).astype(jnp.float32))
    hidden_rows = shared_local[3].shape[0] // width
    small_out = [
        small_total[:hidden_rows].reshape(-1),
        small_total[hidden_rows],
        small_total[hidden_rows + 1 : hidden_rows + 3],
        small_total[hidden_rows + 3 : hidden_rows + 5],
        small_total[hidden_rows + 5, : width // 2],
        small_total[hidden_rows + 5, width // 2 :],
    ]
    block_out = jnp.where(section_index == 0, memory_all, slot_all)[None]
    input_grad = (target_grad + source_grad)[None]
    return (
        block_out,
        input_grad,
        grads_out[0][None],
        grads_out[1][None],
        grads_out[2][None],
        small_out[0][None],
        grads_out[3][None],
        small_out[1][None],
        small_out[2][None],
        small_out[3][None],
        grads_out[4],
        grads_out[5],
        grads_out[6],
        small_out[4],
        small_out[5],
    )


def solution(mesh):
    in_specs = (
        P("pipe", "dp", None),
        P("dp"),
        P("dp"),
        P("dp", None),
        P("pipe", None, None),
        P("pipe", None, None),
        P("pipe", None, None),
        P("pipe", None),
        P("pipe", None, None),
        P("pipe", None),
        P("pipe", None, None),
        P("pipe", None, None),
        P("pipe", None),
        P("pipe", None),
        P("pipe", None),
        P("pipe"),
        P("pipe"),
    )
    out_specs = (
        P("pipe", "dp", None),
        P("pipe", "dp", None),
        P("pipe", None, None),
        P("pipe", None, None),
        P("pipe", None, None),
        P("pipe", None),
        P("pipe", None, None),
        P("pipe", None),
        P("pipe", None, None),
        P("pipe", None, None),
        P("pipe", None),
        P("pipe", None),
        P("pipe", None),
        P("pipe"),
        P("pipe"),
    )
    return jax.shard_map(local, mesh=mesh, in_specs=in_specs, out_specs=out_specs, check_vma=False)
```

```python
import functools

import jax
import jax.numpy as jnp
from jax import lax
from jax.experimental import pallas as pl
from jax.experimental.pallas import tpu as pltpu
from jax.sharding import PartitionSpec as P

HEADS = 8
LOW = jnp.bfloat16
WIDE = jnp.float32
HEAD_SIZE = 64
PAIR = 2 * HEAD_SIZE
GELU_SCALE = 0.7978845608
GELU_CUBE = 0.044715
MASKED = -1e30
VMEM_LIMIT = 56 * 2**20


def product(left, right, left_dim=1, right_dim=0):
    return lax.dot_general(
        left, right, (((left_dim,), (right_dim,)), ((), ())), preferred_element_type=WIDE
    )


class Copies:
    def __init__(self, semaphores):
        self.semaphores = semaphores
        self.count = 0

    def start(self, source, target):
        copy = pltpu.make_async_copy(source, target, self.semaphores.at[self.count])
        self.count += 1
        copy.start()
        return copy


def pair_columns(pair):
    return pl.ds(pl.multiple_of(pair * PAIR, PAIR), PAIR)


def lanes(rows):
    return lax.broadcasted_iota(jnp.int32, (rows, PAIR), 1)


def split_three(column):
    high = column.astype(LOW).astype(WIDE)
    rest = column - high
    middle = rest.astype(LOW).astype(WIDE)
    return high, middle, rest - middle


def key_side(keys, head, bias, lane):
    base = HEAD_SIZE * (1 - head)
    own = lane // HEAD_SIZE == head
    extra = jnp.where(lane == base, bias, jnp.where((lane > base) & (lane < base + 4), 1.0, 0.0))
    return jnp.where(own, keys, extra).astype(LOW)


def attend(query_ref, key_ref, value_ref, count, mixed_ref, logsum_ref, tile=256):
    rows = query_ref.shape[0]
    lane = lanes(rows)
    row = lax.broadcasted_iota(jnp.int32, (rows, PAIR), 0)
    bias = jnp.where(row < count, 0.0, MASKED)
    logsum_ref[...] = jnp.zeros_like(logsum_ref)

    def pair_step(pair, carry):
        columns = pair_columns(pair)
        queries = query_ref[:, columns].astype(WIDE) * HEAD_SIZE**-0.5
        keys = key_ref[:, columns].astype(WIDE)
        values = value_ref[:, columns].astype(WIDE)
        sides = []
        for head in range(2):
            base = HEAD_SIZE * (1 - head)
            own = lane // HEAD_SIZE == head
            one = jnp.where(lane == base, 1.0, 0.0)
            sides.append(
                (
                    jnp.where(own, queries, one).astype(LOW),
                    key_side(keys, head, bias, lane),
                    jnp.where(own, values, one).astype(LOW),
                )
            )
        for begin in range(0, rows, tile):
            mixed = []
            logsum = logsum_ref[begin : begin + tile]
            for head in range(2):
                base = HEAD_SIZE * (1 - head)
                query_side, keys_side, value_side = sides[head]
                scores = product(query_side[begin : begin + tile], keys_side, 1, 1)
                top = jnp.max(scores, axis=1, keepdims=True)
                weights = jnp.exp(scores - top).astype(LOW)
                summed = product(weights, value_side)
                total = summed[:, base : base + 1]
                mixed.append(summed * (1.0 / total))
                logsum = jnp.where(
                    lane[:tile] == 2 * pair + head, top + jnp.log(total), logsum
                )
            mixed_ref[begin : begin + tile, columns] = jnp.where(
                lane[:tile] < HEAD_SIZE, mixed[0], mixed[1]
            ).astype(LOW)
            logsum_ref[begin : begin + tile] = logsum
        return carry

    lax.fori_loop(0, HEADS // 2, pair_step, 0)


def attend_back(
    query_ref, key_ref, value_ref, count, mixed_ref, logsum_ref, grad_ref,
    query_grad_ref, key_grad_ref, value_grad_ref, tile=256,
):
    rows = query_ref.shape[0]
    lane = lanes(rows)
    row = lax.broadcasted_iota(jnp.int32, (rows, PAIR), 0)
    bias = jnp.where(row < count, 0.0, MASKED)

    def pair_step(pair, carry):
        columns = pair_columns(pair)
        queries = query_ref[:, columns].astype(WIDE) * HEAD_SIZE**-0.5
        keys = key_ref[:, columns].astype(WIDE)
        values = value_ref[:, columns].astype(WIDE)
        grads = grad_ref[:, columns].astype(WIDE)
        along = grads * mixed_ref[:, columns].astype(WIDE)
        logsums = logsum_ref[...]
        query_sum = []
        key_parts = []
        value_parts = []
        for head in range(2):
            base = HEAD_SIZE * (1 - head)
            own = lane // HEAD_SIZE == head
            column = jnp.sum(
                jnp.where(lane == 2 * pair + head, logsums, 0.0), axis=1, keepdims=True
            )
            inner = jnp.sum(jnp.where(own, along, 0.0), axis=1, keepdims=True)
            query_side = jnp.where(own, queries, jnp.where(lane == base, 1.0, 0.0))
            grad_side = jnp.where(own, grads, 0.0)
            for place, part in enumerate(split_three(column)):
                query_side = jnp.where(lane == base + 1 + place, -part, query_side)
            for place, part in enumerate(split_three(inner)):
                grad_side = jnp.where(lane == base + 1 + place, -part, grad_side)
            query_side = query_side.astype(LOW)
            grad_side = grad_side.astype(LOW)
            keys_side = key_side(keys, head, bias, lane)
            value_side = key_side(values, head, 0.0, lane)
            query_total = None
            for begin in range(0, rows, tile):
                spot = slice(begin, begin + tile)
                probs = jnp.exp(product(keys_side[spot], query_side, 1, 1))
                slopes = (probs * product(value_side[spot], grad_side, 1, 1)).astype(LOW)
                value_part = product(probs.astype(LOW), grad_side)
                key_part = product(slopes, query_side)
                query_part = product(slopes, keys_side[spot], 0, 0)
                query_total = query_part if query_total is None else query_total + query_part
                key_parts.append(key_part)
                value_parts.append(value_part)
            query_sum.append(query_total)
        query_grad_ref[:, columns] = (
            jnp.where(lane < HEAD_SIZE, query_sum[0], query_sum[1]) * HEAD_SIZE**-0.5
        ).astype(LOW)
        pieces = rows // tile
        for piece in range(pieces):
            spot = slice(piece * tile, (piece + 1) * tile)
            first = lane[:tile] < HEAD_SIZE
            key_grad_ref[spot, columns] = jnp.where(
                first, key_parts[piece], key_parts[pieces + piece]
            ).astype(LOW)
            value_grad_ref[spot, columns] = jnp.where(
                first, value_parts[piece], value_parts[pieces + piece]
            ).astype(LOW)
        return carry

    lax.fori_loop(0, HEADS // 2, pair_step, 0)


def normed(values):
    shifted = values - jnp.mean(values, axis=1, keepdims=True)
    scale = lax.rsqrt(jnp.mean(shifted * shifted, axis=1, keepdims=True) + 1e-05)
    return shifted * scale, scale


def norm(values, gain, bias):
    return normed(values)[0] * gain + bias


def norm_back(values, gain, grad):
    unit, scale = normed(values)
    inner = grad * gain
    back = scale * (
        inner
        - jnp.mean(inner, axis=1, keepdims=True)
        - unit * jnp.mean(inner * unit, axis=1, keepdims=True)
    )
    return back, column_sum(grad * unit), column_sum(grad)


def column_sum(values):
    return jnp.sum(values, axis=0, keepdims=True)


def row_tiles(rows, tile, body):
    def step(index, carry):
        body(pl.ds(pl.multiple_of(index * tile, tile), tile))
        return carry

    lax.fori_loop(0, rows // tile, step, 0)


def gelu_pair(value):
    square = value * value
    curve = jnp.tanh(GELU_SCALE * (value + GELU_CUBE * value * square))
    half = 0.5 * (1.0 + curve)
    slope = half + (0.5 * GELU_SCALE) * value * (1.0 - curve * curve) * (
        1.0 + 3.0 * GELU_CUBE * square
    )
    return value * half, slope


SMALL_ROWS = 16
ROW_TILE = 128
HALF_TILE = 256


def columns_of(index, width):
    return pl.ds(pl.multiple_of(index * width, width), width)


def project(left_ref, right_ref, target_ref, width):
    def step(index, carry):
        columns = columns_of(index, width)
        target_ref[:, columns] = product(left_ref[...], right_ref[:, columns]).astype(LOW)
        return carry

    lax.fori_loop(0, target_ref.shape[1] // width, step, 0)


def wide_row(ref, row):
    return ref[0, row : row + 1, :].astype(WIDE)


def feed_forward(low_ref, wide_ref, in_w, in_b, out2_w, out2_b, act_ref, slope_ref, residual_ref):
    rows, width = low_ref.shape

    def hidden_step(index, carry):
        columns = columns_of(index, width)
        bias = in_b[:, columns].astype(WIDE)
        for begin in range(0, rows, HALF_TILE):
            spot = slice(begin, begin + HALF_TILE)
            act, slope = gelu_pair(product(low_ref[spot], in_w[:, columns]) + bias)
            act_ref[spot, columns] = act.astype(LOW)
            slope_ref[spot, columns] = slope.astype(LOW)
        return carry

    lax.fori_loop(0, act_ref.shape[1] // width, hidden_step, 0)
    bias_out = out2_b[...].astype(WIDE)

    def out_step(spot):
        residual_ref[spot] = wide_ref[spot] + product(act_ref[spot], out2_w[...]) + bias_out

    row_tiles(rows, HALF_TILE, out_step)


def feed_back(residual_grad, grad_low, slope_ref, in_w, out2_w, hidden_grad, bias_rows, out_ref):
    rows, width = grad_low.shape

    def hidden_step(index, carry):
        columns = columns_of(index, width)
        total = jnp.zeros((1, width), WIDE)
        for begin in range(0, rows, HALF_TILE):
            spot = slice(begin, begin + HALF_TILE)
            grads = product(grad_low[spot], out2_w[columns, :], 1, 1)
            grads = (grads * slope_ref[spot, columns].astype(WIDE)).astype(LOW)
            hidden_grad[spot, columns] = grads
            total = total + column_sum(grads.astype(WIDE))
        bias_rows[pl.ds(index, 1), :] = total
        return carry

    lax.fori_loop(0, hidden_grad.shape[1] // width, hidden_step, 0)

    def out_step(spot):
        out_ref[spot] = residual_grad[spot] + product(hidden_grad[spot], in_w[...], 1, 1)

    row_tiles(rows, HALF_TILE, out_step)


def norm_back_rows(values_ref, gain, grad_ref, wide_ref, low_ref, gain_row, bias_row):
    rows, width = values_ref.shape
    gain_row[...] = jnp.zeros((1, width), WIDE)
    bias_row[...] = jnp.zeros((1, width), WIDE)

    def step(spot):
        back, gain_part, bias_part = norm_back(values_ref[spot], gain, grad_ref[spot])
        wide_ref[spot] = back
        low_ref[spot] = back.astype(LOW)
        gain_row[...] += gain_part
        bias_row[...] += bias_part

    row_tiles(rows, ROW_TILE, step)


def self_kernel(
    example, src_len, tgt_len, in_b, out2_b, gains, biases, inputs, qkv_w, out_w, in_w, out2_w,
    qkv_out, logsum_out, mixed_out, residual_out, low_out, act_out, slope_out, second_out,
    memory_out, x_s, qkv_w_s, out_w_s, in_w_s, out2_w_s, qkv_s, logsum_s, mixed_s, residual_s,
    wide_s, low_s, act_s, slope_s, second_s, memory_s, semaphores,
):
    section = lax.axis_index("pipe")
    rows, width = x_s.shape
    copies = Copies(semaphores)
    x_copy = copies.start(inputs.at[0, pl.ds(example * rows, rows)], x_s)
    qkv_copy = copies.start(qkv_w.at[0], qkv_w_s)
    out_copy = copies.start(out_w.at[0], out_w_s)
    encoder = section == 0
    ffn_copies = [
        pltpu.make_async_copy(in_w.at[0], in_w_s, semaphores.at[14]),
        pltpu.make_async_copy(out2_w.at[0], out2_w_s, semaphores.at[15]),
    ]

    @pl.when(encoder)
    def _():
        for copy in ffn_copies:
            copy.start()

    x_copy.wait()
    qkv_copy.wait()
    project(x_s, qkv_w_s, qkv_s, width)
    out_copies = [copies.start(qkv_s, qkv_out)]
    count = jnp.where(encoder, src_len[example], tgt_len[example])
    attend(
        qkv_s.at[:, :width],
        qkv_s.at[:, width : 2 * width],
        qkv_s.at[:, 2 * width :],
        count,
        mixed_s,
        logsum_s,
    )
    out_copies.append(copies.start(mixed_s, mixed_out))
    out_copies.append(copies.start(logsum_s, logsum_out))
    out_copy.wait()

    def residual_step(spot):
        residual_s[spot] = x_s[spot].astype(WIDE) + product(mixed_s[spot], out_w_s[...])

    row_tiles(rows, HALF_TILE, residual_step)
    out_copies.append(copies.start(residual_s, residual_out))

    @pl.when(encoder)
    def _():
        gain, bias = wide_row(gains, 0), wide_row(biases, 0)

        def norm_step(spot):
            value = norm(residual_s[spot], gain, bias)
            wide_s[spot] = value
            low_s[spot] = value.astype(LOW)

        row_tiles(rows, ROW_TILE, norm_step)
        more = Copies(semaphores)
        more.count = 8
        kept = [more.start(low_s, low_out)]
        for copy in ffn_copies:
            copy.wait()
        feed_forward(
            low_s, wide_s, in_w_s, in_b, out2_w_s, out2_b, act_s, slope_s, second_s
        )
        kept.append(more.start(act_s, act_out))
        kept.append(more.start(slope_s, slope_out))
        kept.append(more.start(second_s, second_out))
        gain_last, bias_last = wide_row(gains, 1), wide_row(biases, 1)

        def memory_step(index, carry):
            spot = pl.ds(pl.multiple_of(index * ROW_TILE, ROW_TILE), ROW_TILE)
            row = lax.broadcasted_iota(jnp.int32, (ROW_TILE, width), 0) + index * ROW_TILE
            value = norm(second_s[spot], gain_last, bias_last)
            memory_s[spot] = jnp.where(row < count, value, 0.0).astype(LOW)
            return carry

        lax.fori_loop(0, rows // ROW_TILE, memory_step, 0)
        kept.append(more.start(memory_s, memory_out))
        for copy in kept:
            copy.wait()

    for copy in out_copies:
        copy.wait()


def cross_kernel(
    example, src_len, tgt_len, in_b, out2_b, gains, biases, cross_gains, residual_in, memory_in,
    cotangent, in_w, out2_w, qkv_own, qkv_near, qkv_far, out_own, out_near, out_far, slot_own,
    slot_near, slot_far, low_in, act_in, small_out, low_out, act_out, slot_out, final_out,
    grad_out, hidden_out, first_out, mixed_out, branch_out, query_out, pair_out, memory_out,
    rest_out, residual_s, memory_s, grad_s, in_w_s, out2_w_s, qkv_w_s, out_w_s, slot_w_s, wide_s,
    first_s, query_s, pair_s, mixed_s, logsum_s, cross_s, low_s, act_s, slope_s, second_s,
    final_s, earlier_s, slot_s, wide_grad_s, grad_low_s, hidden_s, back_s, rest_s, branch_s,
    cross_grad_s, query_grad_s, pair_grad_s, memory_grad_s, semaphores,
):
    section = lax.axis_index("pipe")
    core = lax.axis_index("dp") % 2
    rows, width = residual_s.shape
    small_out[...] = jnp.zeros_like(small_out)

    @pl.when(section == 1)
    def _():
        copies = Copies(semaphores)
        begin = pl.ds(example * rows, rows)
        first_copy = copies.start(residual_in, residual_s)

        def gathered(own, near, far, target):
            half = own.shape[0]
            part = half // 2
            near_at = pl.ds(pl.multiple_of(core * part, part), part)
            far_at = pl.ds(pl.multiple_of((1 - core) * part, part), part)
            return [
                copies.start(near, target.at[near_at]),
                copies.start(far, target.at[far_at]),
                copies.start(own, target.at[pl.ds(half, half)]),
            ]

        qkv_copies = gathered(qkv_own, qkv_near, qkv_far, qkv_w_s)
        memory_copy = copies.start(memory_in, memory_s)
        out_copies = gathered(out_own, out_near, out_far, out_w_s)
        ffn_copies = [copies.start(in_w.at[0], in_w_s), copies.start(out2_w.at[0], out2_w_s)]
        grad_copy = copies.start(cotangent.at[begin], grad_s)
        slot_copies = gathered(slot_own, slot_near, slot_far, slot_w_s)
        kept = []
        first_copy.wait()
        gain, bias = wide_row(gains, 0), wide_row(biases, 0)

        def norm_step(spot):
            value = norm(residual_s[spot], gain, bias)
            wide_s[spot] = value
            first_s[spot] = value.astype(LOW)

        row_tiles(rows, ROW_TILE, norm_step)
        kept.append(copies.start(first_s, first_out))
        for copy in qkv_copies:
            copy.wait()
        query_s[...] = product(first_s[...], qkv_w_s[:, :width]).astype(LOW)
        memory_copy.wait()
        project(memory_s, qkv_w_s.at[:, width:], pair_s, width)
        key_ref, value_ref = pair_s.at[:, :width], pair_s.at[:, width:]
        count = src_len[example]
        attend(query_s, key_ref, value_ref, count, mixed_s, logsum_s)
        kept.append(copies.start(mixed_s, mixed_out))
        for copy in out_copies:
            copy.wait()
        cross_gain = cross_gains[0:1, :].astype(WIDE)
        cross_bias = cross_gains[1:2, :].astype(WIDE)

        def cross_step(spot):
            value = wide_s[spot] + product(mixed_s[spot], out_w_s[...])
            cross_s[spot] = value
            value = norm(value, cross_gain, cross_bias)
            wide_s[spot] = value
            low_s[spot] = value.astype(LOW)

        row_tiles(rows, HALF_TILE, cross_step)
        kept.append(copies.start(low_s, low_out))
        for copy in ffn_copies:
            copy.wait()
        feed_forward(
            low_s, wide_s, in_w_s, in_b, out2_w_s, out2_b, act_s, slope_s, second_s
        )
        kept.append(copies.start(act_s, act_out))
        gain_last, bias_last = wide_row(gains, 1), wide_row(biases, 1)

        def final_step(spot):
            final_s[spot] = norm(second_s[spot], gain_last, bias_last).astype(LOW)

        row_tiles(rows, ROW_TILE, final_step)
        kept.append(copies.start(final_s, final_out))
        grad_copy.wait()
        for copy in slot_copies:
            copy.wait()
        row = lax.broadcasted_iota(jnp.int32, (rows, width), 0)
        slots = tgt_len[example] - 1
        slot_grad = jnp.where(row < slots, grad_s[...].astype(WIDE), 0.0)
        grad_s[...] = slot_grad.astype(LOW)
        earlier = jnp.where(row == 0, 0.0, pltpu.roll(slot_grad, 1, 0))
        earlier_s[...] = earlier.astype(LOW)
        wide_grad_s[...] = product(final_s[...], slot_w_s[width:, :])
        value = product(final_s[...], slot_w_s[:width, :]) + pltpu.roll(
            wide_grad_s[...], rows - 1, 0
        )
        slot_s[...] = jnp.where(row < slots, value, 0.0).astype(LOW)
        kept.append(copies.start(slot_s, slot_out))
        wide_grad_s[...] = product(grad_s[...], slot_w_s[:width, :], 1, 1) + product(
            earlier_s[...], slot_w_s[width:, :], 1, 1
        )
        norm_back_rows(
            second_s, gain_last, wide_grad_s, second_s, grad_low_s,
            small_out.at[6:7, :], small_out.at[8:9, :],
        )
        kept.append(copies.start(grad_low_s, grad_out))
        small_out[4:5, :] = column_sum(grad_low_s[...].astype(WIDE))
        feed_back(
            second_s, grad_low_s, slope_s, in_w_s, out2_w_s, hidden_s, small_out.at[0:4, :],
            back_s,
        )
        kept.append(copies.start(hidden_s, hidden_out))
        norm_back_rows(
            cross_s, cross_gain, back_s, rest_s, branch_s,
            small_out.at[9:10, :], small_out.at[10:11, :],
        )
        kept.append(copies.start(rest_s, rest_out))
        kept.append(copies.start(branch_s, branch_out))
        cross_grad_s[...] = product(branch_s[...], out_w_s[...], 1, 1).astype(LOW)
        attend_back(
            query_s, key_ref, value_ref, count, mixed_s, logsum_s, cross_grad_s,
            query_grad_s, pair_grad_s.at[:, :width], pair_grad_s.at[:, width:],
        )
        kept.append(copies.start(query_grad_s, query_out))
        kept.append(copies.start(pair_grad_s, pair_out))
        memory_grad_s[...] = product(pair_grad_s[...], qkv_w_s[:, width:], 1, 1).astype(LOW)
        kept.append(copies.start(memory_grad_s, memory_out))
        for copy in kept:
            copy.wait()


def back_kernel(
    example, src_len, tgt_len, gains, inputs_unused, qkv_w, out_w, in_w, out2_w, query_near,
    query_far, query_own, memory_grad, second_in, slope_in, query_grad, rest_in, residual_in,
    qkv_in, logsum_in, mixed_in, grad_in, hidden_in, order_in, small_out, grad_out, hidden_out,
    branch_out, qkv_grad_out, rows_out, qkv_w_s, out_w_s, in_w_s, out2_w_s, query_w_s,
    memory_s, second_s, slope_s, wide_s, grad_low_s, hidden_s, back_s, query_grad_s, residual_s,
    qkv_s, logsum_s, mixed_s, rest_s, branch_s, attn_grad_s, qkv_grad_s, semaphores,
):
    section = lax.axis_index("pipe")
    core = lax.axis_index("dp") % 2
    rows, width = residual_s.shape
    small_out[...] = jnp.zeros_like(small_out)
    gain_first, gain_last = wide_row(gains, 0), wide_row(gains, 1)
    copies = Copies(semaphores)
    copies.count = 16
    residual_copy = copies.start(residual_in, residual_s)
    out_copy = copies.start(out_w.at[0], out_w_s)
    qkv_copies = [
        copies.start(qkv_in, qkv_s),
        copies.start(logsum_in, logsum_s),
        copies.start(mixed_in, mixed_s),
    ]
    qkv_w_copy = copies.start(qkv_w.at[0], qkv_w_s)

    @pl.when(section == 0)
    def _():
        more = Copies(semaphores)
        fetched = [
            more.start(memory_grad, memory_s),
            more.start(second_in, second_s),
            more.start(slope_in, slope_s),
            more.start(out2_w.at[0], out2_w_s),
            more.start(in_w.at[0], in_w_s),
        ]
        fetched[0].wait()
        fetched[1].wait()
        row = lax.broadcasted_iota(jnp.int32, (rows, width), 0)
        wide_s[...] = jnp.where(
            row < src_len[example], memory_s[...].astype(WIDE), 0.0
        )
        norm_back_rows(
            second_s, gain_last, wide_s, second_s, grad_low_s,
            small_out.at[6:7, :], small_out.at[8:9, :],
        )
        kept = [more.start(grad_low_s, grad_out)]
        small_out[4:5, :] = column_sum(grad_low_s[...].astype(WIDE))
        for copy in fetched[2:]:
            copy.wait()
        feed_back(
            second_s, grad_low_s, slope_s, in_w_s, out2_w_s, hidden_s, small_out.at[0:4, :],
            back_s,
        )
        kept.append(more.start(hidden_s, hidden_out))
        for copy in kept:
            copy.wait()

    @pl.when(section == 1)
    def _():
        more = Copies(semaphores)
        part = query_near.shape[0]
        near_at = pl.ds(pl.multiple_of(core * part, part), part)
        far_at = pl.ds(pl.multiple_of((1 - core) * part, part), part)
        fetched = [
            more.start(query_grad, query_grad_s),
            more.start(query_near.at[:, :width], query_w_s.at[near_at]),
            more.start(query_far.at[:, :width], query_w_s.at[far_at]),
            more.start(query_own.at[:, :width], query_w_s.at[pl.ds(2 * part, 2 * part)]),
            more.start(rest_in, rest_s),
        ]
        for copy in fetched:
            copy.wait()

        def first_step(spot):
            back_s[spot] = rest_s[spot] + product(query_grad_s[spot], query_w_s[...], 1, 1)

        row_tiles(rows, HALF_TILE, first_step)

    residual_copy.wait()
    norm_back_rows(
        residual_s, gain_first, back_s, rest_s, branch_s,
        small_out.at[5:6, :], small_out.at[7:8, :],
    )
    kept = [copies.start(branch_s, branch_out)]
    out_copy.wait()
    attn_grad_s[...] = product(branch_s[...], out_w_s[...], 1, 1).astype(LOW)
    for copy in qkv_copies:
        copy.wait()
    count = jnp.where(section == 0, src_len[example], tgt_len[example])
    attend_back(
        qkv_s.at[:, :width],
        qkv_s.at[:, width : 2 * width],
        qkv_s.at[:, 2 * width :],
        count,
        mixed_s,
        logsum_s,
        attn_grad_s,
        qkv_grad_s.at[:, :width],
        qkv_grad_s.at[:, width : 2 * width],
        qkv_grad_s.at[:, 2 * width :],
    )
    kept.append(copies.start(qkv_grad_s, qkv_grad_out))
    qkv_w_copy.wait()

    def rows_step(spot):
        back_s[spot] = rest_s[spot] + product(qkv_grad_s[spot], qkv_w_s[...], 1, 1)

    row_tiles(rows, HALF_TILE, rows_step)
    kept.append(copies.start(back_s, rows_out))
    for copy in kept:
        copy.wait()


MESH = pl.DeviceIdType.MESH
PARTS = 2


def ring_place(chip, chips):
    half = chip // 2
    return jnp.where(chip % 2 == 0, half, chips - 1 - half)


def ring_chip(place, chips):
    return jnp.where(place < chips // 2, 2 * place, 2 * (chips - 1 - place) + 1)


def part_rows(chunk_rows):
    first = (chunk_rows // 2 + 15) // 16 * 16
    if first == chunk_rows:
        return ((0, chunk_rows),)
    return ((0, first), (first, chunk_rows - first))


def ring_kernel(
    devices, chips, chunk_rows, packed, own_extra, came_extra, small, total, small_total, mine,
    sibling, arrived, small_sent, small_arrived, load_sem,
    sib_send, sib_recv, ring_send, ring_recv, gather_send, gather_recv, share_send, share_recv,
    small_send, small_recv,
):
    pipe = lax.axis_index("pipe")
    me = lax.axis_index("dp")
    core = me % 2
    place = ring_place(me // 2, chips)
    right = ring_chip((place + 1) % chips, chips) * 2 + core
    left = ring_chip((place + chips - 1) % chips, chips) * 2 + core
    other = me + 1 - 2 * core
    section_rows, extra_rows = packed.shape[0], own_extra.shape[0]
    used_rows = section_rows + extra_rows
    section_load = pltpu.make_async_copy(
        packed, mine.at[pl.ds(0, section_rows)], load_sem.at[0]
    )
    extra_spot = mine.at[pl.ds(section_rows, extra_rows)]
    section_load.start()

    @pl.when(pipe == 0)
    def _():
        load = pltpu.make_async_copy(came_extra, extra_spot, load_sem.at[1])
        load.start()
        load.wait()

    @pl.when(pipe != 0)
    def _():
        load = pltpu.make_async_copy(own_extra, extra_spot, load_sem.at[2])
        load.start()
        load.wait()

    if mine.shape[0] > used_rows:
        mine[used_rows:] = jnp.zeros_like(mine[used_rows:])
    section_load.wait()

    def mine_at(core_at, way, chunk, begin=0, rows=chunk_rows):
        start = ((core_at * 2 + way) * chips + chunk) * chunk_rows + begin
        return pl.ds(pl.multiple_of(start, 16), rows)

    parts = part_rows(chunk_rows)
    levels = devices.bit_length() - 1

    def paired(bit):
        return me + bit - 2 * bit * ((me // bit) % 2)

    barrier = pltpu.get_barrier_semaphore()
    greeted = [right, left] + [paired(1 << level) for level in range(levels)]
    for friend in greeted:
        pl.semaphore_signal(barrier, inc=1, device_id=(pipe, friend), device_id_type=MESH)
    pl.semaphore_wait(barrier, len(greeted))

    def chunk_at(way, step):
        if way == 0:
            return (place - step + 2 * chips) % chips
        return (place + step + chips) % chips

    def to_other(way, step):
        chunk = chunk_at(way, step)
        return pltpu.make_async_remote_copy(
            src_ref=mine.at[mine_at(1 - core, way, chunk)],
            dst_ref=sibling.at[way, chunk],
            send_sem=sib_send.at[way, step],
            recv_sem=sib_recv.at[way, step],
            device_id=(pipe, other),
            device_id_type=MESH,
        )

    def ring_copy(way, step, part):
        begin, rows = parts[part]
        spot = pl.ds(begin, rows)
        return pltpu.make_async_remote_copy(
            src_ref=arrived.at[way, step, spot],
            dst_ref=arrived.at[way, step + 1, spot],
            send_sem=ring_send.at[way, step, part],
            recv_sem=ring_recv.at[way, step, part],
            device_id=(pipe, (right, left)[way]),
            device_id_type=MESH,
        )

    def gather_copy(way, step, part):
        begin, rows = parts[part]
        spot = pl.ds(begin, rows)
        chunk = chunk_at(way, step - 1)
        return pltpu.make_async_remote_copy(
            src_ref=total.at[core, way, chunk, spot],
            dst_ref=total.at[core, way, chunk, spot],
            send_sem=gather_send.at[way, step, part],
            recv_sem=gather_recv.at[way, step, part],
            device_id=(pipe, (right, left)[way]),
            device_id_type=MESH,
        )

    def share_copy(way, step, part):
        begin, rows = parts[part]
        spot = pl.ds(begin, rows)
        chunk = chunk_at(way, step - 1)
        return pltpu.make_async_remote_copy(
            src_ref=total.at[core, way, chunk, spot],
            dst_ref=total.at[core, way, chunk, spot],
            send_sem=share_send.at[way, step, part],
            recv_sem=share_recv.at[way, step, part],
            device_id=(pipe, other),
            device_id_type=MESH,
        )

    def small_copy(level, bit):
        return pltpu.make_async_remote_copy(
            src_ref=small_sent.at[level],
            dst_ref=small_arrived.at[level],
            send_sem=small_send.at[level],
            recv_sem=small_recv.at[level],
            device_id=(pipe, paired(bit)),
            device_id_type=MESH,
        )

    def start_sibling(step, carry):
        for way in range(2):
            to_other(way, step).start()
        return carry

    lax.fori_loop(0, chips, start_sibling, 0)
    small_sent[0] = small[...]
    small_copy(0, 1).start()

    for way in range(2):
        to_other(way, 0).wait_recv()
        for part, (begin, rows) in enumerate(parts):
            spot = pl.ds(begin, rows)
            arrived[way, 0, spot] = (
                mine[mine_at(core, way, place, begin, rows)].astype(jnp.float32)
                + sibling[way, place, spot].astype(jnp.float32)
            ).astype(jnp.bfloat16)
            ring_copy(way, 0, part).start()

    def merge_small(level, bit):
        small_copy(level, bit).wait_recv()
        merged = small_sent[level] + small_arrived[level]

        @pl.when(level + 1 < levels)
        def _():
            small_sent[level + 1] = merged
            small_copy(level + 1, 2 * bit).start()

        @pl.when(level + 1 == levels)
        def _():
            small_total[...] = merged

    def own_sum(way, step, part):
        begin, rows = parts[part]
        spot = pl.ds(begin, rows)
        chunk = chunk_at(way, step + 1)
        return (
            arrived[way, step + 1, spot].astype(jnp.float32)
            + mine[mine_at(core, way, chunk, begin, rows)].astype(jnp.float32)
            + sibling[way, chunk, spot].astype(jnp.float32)
        ).astype(jnp.bfloat16)

    def ring_step(step, bit):
        @pl.when(step < levels)
        def _():
            merge_small(step, bit)

        for way in range(2):
            to_other(way, step + 1).wait_recv()
        for part, (begin, rows) in enumerate(parts):
            for way in range(2):
                ring_copy(way, step, part).wait_recv()
                arrived[way, step + 1, pl.ds(begin, rows)] = own_sum(way, step, part)
                ring_copy(way, step + 1, part).start()
        return 2 * bit

    lax.fori_loop(0, chips - 2, ring_step, 1)

    last = chips - 2
    for way in range(2):
        to_other(way, last + 1).wait_recv()
    for part, (begin, rows) in enumerate(parts):
        for way in range(2):
            ring_copy(way, last, part).wait_recv()
            total[core, way, chunk_at(way, last + 1), pl.ds(begin, rows)] = own_sum(
                way, last, part
            )
            gather_copy(way, 0, part).start()
            share_copy(way, 0, part).start()

    def gather_step(step, carry):
        for part in range(len(parts)):
            for way in range(2):
                gather_copy(way, step, part).wait_recv()
                gather_copy(way, step + 1, part).start()
                share_copy(way, step + 1, part).start()
        return carry

    lax.fori_loop(0, chips - 2, gather_step, 0)
    for part in range(len(parts)):
        for way in range(2):
            gather_copy(way, last, part).wait_recv()
            share_copy(way, last + 1, part).start()

    def finish_share(step, carry):
        for way in range(2):
            to_other(way, step).wait_send()
            for part in range(len(parts)):
                share_copy(way, step, part).wait()
        return carry

    lax.fori_loop(0, chips, finish_share, 0)

    def finish_ring(step, carry):
        for way in range(2):
            for part in range(len(parts)):
                ring_copy(way, step, part).wait_send()
                gather_copy(way, step, part).wait_send()
        return carry

    lax.fori_loop(0, chips - 1, finish_ring, 0)
    for level in range(levels):
        small_copy(level, 1 << level).wait_send()


def ring_layout(rows, devices):
    chips = devices // 2
    chunk_rows = -(-rows // (4 * chips * 16)) * 16
    return chips, chunk_rows


def ring_sum(packed, own_extra, came_extra, small, devices):
    width = packed.shape[1]
    rows = packed.shape[0] + own_extra.shape[0]
    chips, chunk_rows = ring_layout(rows, devices)
    padded = 4 * chips * chunk_rows
    levels = devices.bit_length() - 1
    pieces = len(part_rows(chunk_rows))
    dma = pltpu.SemaphoreType.DMA
    vmem = pl.BlockSpec(memory_space=pltpu.VMEM)
    outer = pl.BlockSpec(memory_space=pl.ANY)
    total, small_total = pl.pallas_call(
        functools.partial(ring_kernel, devices, chips, chunk_rows),
        out_shape=(
            jax.ShapeDtypeStruct((2, 2, chips, chunk_rows, width), LOW),
            jax.ShapeDtypeStruct(small.shape, WIDE),
        ),
        in_specs=[outer, outer, outer, vmem],
        out_specs=(vmem, vmem),
        scratch_shapes=[
            pltpu.VMEM((padded, width), LOW),
            pltpu.VMEM((2, chips, chunk_rows, width), LOW),
            pltpu.VMEM((2, chips, chunk_rows, width), LOW),
            pltpu.VMEM((levels,) + small.shape, WIDE),
            pltpu.VMEM((levels,) + small.shape, WIDE),
            dma((3,)),
            dma((2, chips)),
            dma((2, chips)),
            dma((2, chips, pieces)),
            dma((2, chips, pieces)),
            dma((2, chips, pieces)),
            dma((2, chips, pieces)),
            dma((2, chips, pieces)),
            dma((2, chips, pieces)),
            dma((levels,)),
            dma((levels,)),
        ],
        compiler_params=pltpu.CompilerParams(
            collective_id=0, has_side_effects=True, vmem_limit_bytes=48 * 2**20
        ),
        name="ring_sum",
    )(packed, own_extra, came_extra, small)
    return total.reshape(padded, width)[:rows], small_total


def cross_weight_kernel(
    tgt_len, first_a, first_b, query_a, query_b, memory_a, memory_b, pair_a, pair_b, mixed_a,
    mixed_b, branch_a, branch_b, final_a, final_b, cotangent, own_out, sent_out, first_s, query_s,
    memory_s, pair_s, mixed_s, branch_s, final_s, grad_s, earlier_s, own_s, sent_s, semaphores,
):
    section = lax.axis_index("pipe")

    @pl.when(section == 1)
    def _():
        copies = Copies(semaphores)

        def both(first, second, target):
            rows = first.shape[0]
            return [
                copies.start(first, target.at[pl.ds(0, rows)]),
                copies.start(second, target.at[pl.ds(rows, rows)]),
            ]

        grad_copy = copies.start(cotangent, grad_s)
        final_copies = both(final_a, final_b, final_s)
        mixed_copies = both(mixed_a, mixed_b, mixed_s) + both(branch_a, branch_b, branch_s)
        pair_copies = both(memory_a, memory_b, memory_s) + both(pair_a, pair_b, pair_s)
        query_copies = both(first_a, first_b, first_s) + both(query_a, query_b, query_s)
        total, width = grad_s.shape
        rows = total // 2
        half = width // 2
        grad_copy.wait()
        row = lax.broadcasted_iota(jnp.int32, (rows, width), 0)
        for example in range(2):
            spot = slice(example * rows, (example + 1) * rows)
            slot_grad = jnp.where(
                row < tgt_len[example] - 1, grad_s[spot].astype(WIDE), 0.0
            )
            grad_s[spot] = slot_grad.astype(LOW)
            earlier = jnp.where(row == 0, 0.0, pltpu.roll(slot_grad, 1, 0))
            earlier_s[spot] = earlier.astype(LOW)
        for copy in final_copies:
            copy.wait()
        sent_s[4 * half :] = product(final_s[...], grad_s[...], 0, 0).astype(LOW)
        own_s[4 * half :] = product(final_s[...], earlier_s[...], 0, 0).astype(LOW)

        def keep(place, value):
            spot = slice(place * half, (place + 1) * half)
            sent_s[spot] = value[:half].astype(LOW)
            own_s[spot] = value[half:].astype(LOW)

        for copy in mixed_copies:
            copy.wait()
        keep(3, product(mixed_s[...], branch_s[...], 0, 0))
        for copy in pair_copies:
            copy.wait()
        keep(1, product(memory_s[...], pair_s[:, :width], 0, 0))
        keep(2, product(memory_s[...], pair_s[:, width:], 0, 0))
        for copy in query_copies:
            copy.wait()
        keep(0, product(first_s[...], query_s[...], 0, 0))
        kept = [copies.start(own_s, own_out), copies.start(sent_s, sent_out)]
        for copy in kept:
            copy.wait()


def weight_kernel(
    low_a, low_b, hidden_a, hidden_b, act_a, act_b, grad_a, grad_b, mixed_a, mixed_b, branch_a,
    branch_b, qkv_grad_a, qkv_grad_b, inputs, packed_out, low_s, hidden_s, act_s, grad_s, mixed_s,
    branch_s, x_s, qkv_grad_s, packed_s, semaphores,
):
    copies = Copies(semaphores)
    width = low_s.shape[1]

    def both(first, second, target):
        rows = first.shape[0]
        return [
            copies.start(first, target.at[pl.ds(0, rows)]),
            copies.start(second, target.at[pl.ds(rows, rows)]),
        ]

    low_copies = both(low_a, low_b, low_s) + both(hidden_a, hidden_b, hidden_s)
    act_copies = both(grad_a, grad_b, grad_s) + both(act_a, act_b, act_s)
    mixed_copies = both(mixed_a, mixed_b, mixed_s) + both(branch_a, branch_b, branch_s)
    qkv_copies = [copies.start(inputs.at[0], x_s)] + both(qkv_grad_a, qkv_grad_b, qkv_grad_s)
    base = copies.count

    def block_copy(index):
        spot = columns_of(index, width)
        return pltpu.make_async_copy(
            packed_s.at[spot], packed_out.at[spot], semaphores.at[base + index]
        )

    def blocks(begin, count, block):
        def step(index, carry):
            packed_s[columns_of(begin + index, width), :] = block(index).astype(LOW)
            block_copy(begin + index).start()
            return carry

        lax.fori_loop(0, count, step, 0)

    for copy in low_copies:
        copy.wait()
    hidden_blocks = hidden_s.shape[1] // width
    blocks(
        4, hidden_blocks,
        lambda index: product(low_s[...], hidden_s[:, columns_of(index, width)], 0, 0),
    )
    for copy in act_copies:
        copy.wait()
    blocks(
        4 + hidden_blocks, hidden_blocks,
        lambda index: product(act_s[:, columns_of(index, width)], grad_s[...], 0, 0),
    )
    for copy in mixed_copies:
        copy.wait()
    blocks(3, 1, lambda index: product(mixed_s[...], branch_s[...], 0, 0))
    for copy in qkv_copies:
        copy.wait()
    blocks(0, 3, lambda index: product(x_s[...], qkv_grad_s[:, columns_of(index, width)], 0, 0))

    def finish(index, carry):
        block_copy(index).wait()
        return carry

    lax.fori_loop(0, packed_s.shape[0] // width, finish, 0)


ANY = pl.BlockSpec(memory_space=pl.ANY)
INNER = pl.BlockSpec(memory_space=pltpu.VMEM)
SCALAR = pl.BlockSpec(memory_space=pltpu.SMEM)


def local_call(body, name, scalars, inner, outer, outputs, scratch, flops, aliases=None, count=32):
    shapes = [jax.ShapeDtypeStruct(shape, kind) for shape, kind, _ in outputs]
    inputs = list(scalars) + list(inner) + list(outer)
    specs = [SCALAR] * len(scalars) + [INNER] * len(inner) + [ANY] * len(outer)
    moved = sum(value.size * value.dtype.itemsize for value in inputs)
    return pl.pallas_call(
        body,
        out_shape=shapes,
        in_specs=specs,
        out_specs=[INNER if kept else ANY for _, _, kept in outputs],
        scratch_shapes=[pltpu.VMEM(shape, kind) for shape, kind in scratch]
        + [pltpu.SemaphoreType.DMA((count,))],
        input_output_aliases=aliases or {},
        compiler_params=pltpu.CompilerParams(vmem_limit_bytes=VMEM_LIMIT),
        cost_estimate=pl.CostEstimate(flops=flops, bytes_accessed=moved, transcendentals=0),
        name=name,
    )(*inputs)


def local(
    inputs, src_len, tgt_len, cotangent, qkv_w, out_w, in_w, in_b, out2_w, out2_b, norm_gain,
    norm_bias, cross_qkv, cross_out, slot_w, cross_gain, cross_bias,
):
    section = lax.axis_index("pipe")
    core = lax.axis_index("dp") % 2
    devices = lax.axis_size("dp")
    blocks = src_len.shape[0]
    total_rows, width = inputs.shape[1:]
    rows = total_rows // blocks
    hidden = in_w.shape[2]
    square, wide3, deep = (rows, width), (rows, 3 * width), (rows, hidden)
    weight_square = (width, width)

    def near_far(values):
        part = values.shape[0] // 2
        piece = lax.dynamic_slice_in_dim(values, core * part, part, axis=0)
        near = lax.ppermute(piece, "pipe", [(0, 1)])
        far = lax.ppermute(near, "dp", [(place, place ^ 1) for place in range(devices)])
        return near, far

    qkv_near, qkv_far = near_far(cross_qkv)
    out_near, out_far = near_far(cross_out)
    slot_near, slot_far = near_far(slot_w)
    own_gains = jnp.stack([cross_gain, cross_bias])
    came_gains = lax.ppermute(own_gains, "pipe", [(0, 1)])
    cross_gains = jnp.concatenate([came_gains, own_gains], axis=1)

    started = []
    block_out = None
    for example in range(blocks):
        first_shape = (square, LOW)
        scratch = [
            first_shape, ((width, 3 * width), LOW), (weight_square, LOW), ((width, hidden), LOW),
            ((hidden, width), LOW), (wide3, LOW), ((rows, PAIR), WIDE), first_shape,
            (square, WIDE), (square, WIDE), first_shape, (deep, LOW), (deep, LOW), (square, WIDE),
            first_shape,
        ]
        outputs = [
            (wide3, LOW, False), ((rows, PAIR), WIDE, False), (square, LOW, False),
            (square, WIDE, False), (square, LOW, False), (deep, LOW, False), (deep, LOW, False),
            (square, WIDE, False), (square, LOW, False),
        ]
        started.append(
            local_call(
                functools.partial(self_kernel, example), f"self_rows_{example}",
                [src_len, tgt_len], [in_b, out2_b, norm_gain, norm_bias],
                [inputs, qkv_w, out_w, in_w, out2_w], outputs, scratch, 6 * 10**9,
            )
        )
    sent_memory = [lax.ppermute(values[8], "pipe", [(0, 1)]) for values in started]

    crossed = []
    for example in range(blocks):
        values = started[example]
        scratch = [
            (square, WIDE), (square, LOW), (square, LOW), ((width, hidden), LOW),
            ((hidden, width), LOW), ((width, 3 * width), LOW), (weight_square, LOW),
            ((2 * width, width), LOW), (square, WIDE), (square, LOW), (square, LOW),
            ((rows, 2 * width), LOW), (square, LOW), ((rows, PAIR), WIDE), (square, WIDE),
            (square, LOW), (deep, LOW), (deep, LOW), (square, WIDE), (square, LOW), (square, LOW),
            (square, LOW), (square, WIDE), (square, LOW), (deep, LOW), (square, WIDE),
            (square, WIDE), (square, LOW), (square, LOW), (square, LOW), ((rows, 2 * width), LOW),
            (square, LOW),
        ]
        outputs = [
            ((SMALL_ROWS, width), WIDE, True), (square, LOW, False), (deep, LOW, False),
            (square, LOW, False), (square, LOW, False), (square, LOW, False), (deep, LOW, False),
            (square, LOW, False), (square, LOW, False), (square, LOW, False), (square, LOW, False),
            ((rows, 2 * width), LOW, False), (square, LOW, False), (square, WIDE, False),
        ]
        outer = [
            values[3], sent_memory[example], cotangent, in_w, out2_w, cross_qkv, qkv_near, qkv_far,
            cross_out, out_near, out_far, slot_w, slot_near, slot_far, values[4], values[5],
        ]
        inner = [in_b, out2_b, norm_gain, norm_bias, cross_gains]
        shift = 2 + len(inner)
        crossed.append(
            local_call(
                functools.partial(cross_kernel, example), f"cross_rows_{example}",
                [src_len, tgt_len], inner, outer, outputs, scratch, 20 * 10**9,
                aliases={shift + 14: 1, shift + 15: 2}, count=48,
            )
        )
    back_memory = [lax.ppermute(values[12], "pipe", [(1, 0)]) for values in crossed]

    def pairs_of(group, place):
        return [values[place] for values in group]

    extra_rows = 3 * width
    own_extra, sent_extra = local_call(
        cross_weight_kernel, "cross_weights", [tgt_len], [],
        pairs_of(crossed, 7) + pairs_of(crossed, 10) + sent_memory + pairs_of(crossed, 11)
        + pairs_of(crossed, 8) + pairs_of(crossed, 9) + pairs_of(crossed, 4) + [cotangent],
        [((extra_rows, width), LOW, False), ((extra_rows, width), LOW, False)],
        [
            ((total_rows, width), LOW), ((total_rows, width), LOW), ((total_rows, width), LOW),
            ((total_rows, 2 * width), LOW), ((total_rows, width), LOW), ((total_rows, width), LOW),
            ((total_rows, width), LOW), ((total_rows, width), LOW), ((total_rows, width), LOW),
            ((extra_rows, width), LOW), ((extra_rows, width), LOW),
        ],
        5 * 10**9,
    )
    came_extra = lax.ppermute(sent_extra, "pipe", [(1, 0)])

    backs = []
    order = own_extra
    for example in range(blocks):
        values, after = started[example], crossed[example]
        scratch = [
            ((width, 3 * width), LOW), (weight_square, LOW), ((width, hidden), LOW),
            ((hidden, width), LOW), (weight_square, LOW), (square, LOW), (square, WIDE),
            (deep, LOW), (square, WIDE), (square, LOW), (deep, LOW), (square, WIDE), (square, LOW),
            (square, WIDE), (wide3, LOW), ((rows, PAIR), WIDE), (square, LOW), (square, WIDE),
            (square, LOW), (square, LOW), (wide3, LOW),
        ]
        outputs = [
            ((SMALL_ROWS, width), WIDE, True), (square, LOW, False), (deep, LOW, False),
            (square, LOW, False), (wide3, LOW, False), (square, WIDE, False),
        ]
        outer = [
            inputs, qkv_w, out_w, in_w, out2_w, qkv_near, qkv_far, cross_qkv,
            back_memory[example], values[7], values[6], after[10], after[13], values[3], values[0],
            values[1], values[2], after[5], after[6], order,
        ]
        backs.append(
            local_call(
                functools.partial(back_kernel, example), f"back_rows_{example}",
                [src_len, tgt_len], [norm_gain], outer, outputs, scratch, 14 * 10**9,
                aliases={3 + 17: 1, 3 + 18: 2}, count=48,
            )
        )
        order = backs[-1][3]

    section_rows = 3 * width + width + 2 * hidden
    (packed,) = local_call(
        weight_kernel, "section_weights", [], [],
        pairs_of(crossed, 1) + pairs_of(backs, 2) + pairs_of(crossed, 2) + pairs_of(backs, 1)
        + pairs_of(started, 2) + pairs_of(backs, 3) + pairs_of(backs, 4) + [inputs],
        [((section_rows, width), LOW, False)],
        [
            ((total_rows, width), LOW), ((total_rows, hidden), LOW), ((total_rows, hidden), LOW),
            ((total_rows, width), LOW), ((total_rows, width), LOW), ((total_rows, width), LOW),
            ((total_rows, width), LOW), ((total_rows, 3 * width), LOW),
            ((section_rows, width), LOW),
        ],
        7 * 10**9,
    )

    small = crossed[0][0] + crossed[1][0] + backs[0][0] + backs[1][0]
    half = width // 2
    came_small = lax.ppermute(crossed[0][0][9:11, :half] + crossed[1][0][9:11, :half], "pipe", [(1, 0)])
    small_cross = jnp.where(section == 0, came_small, small[9:11, half:])
    small = jnp.concatenate([small[:9], small_cross.reshape(1, width), small[10:]], axis=0)
    total, small_total = ring_sum(packed, own_extra, came_extra, small, devices)

    sizes = [(width, 3), (width, 1), (width, hidden // width), (hidden, 1), (half, 3), (half, 1), (width, 1)]
    grads = []
    begin = 0
    for size, pieces in sizes:
        parts = []
        for _ in range(pieces):
            parts.append(total[begin : begin + size])
            begin += size
        grads.append(jnp.concatenate(parts, axis=1).astype(WIDE))
    memory_rows = jnp.concatenate(pairs_of(started, 8), axis=0)
    slot_rows = jnp.concatenate(pairs_of(crossed, 3), axis=0)
    block_out = jnp.where(section == 0, memory_rows, slot_rows)[None]
    input_grad = jnp.concatenate(pairs_of(backs, 5), axis=0)[None]
    return (
        block_out,
        input_grad,
        grads[0][None],
        grads[1][None],
        grads[2][None],
        small_total[0:4].reshape(1, hidden),
        grads[3][None],
        small_total[4:5],
        small_total[5:7][None],
        small_total[7:9][None],
        grads[4],
        grads[5],
        grads[6],
        small_total[9, :half],
        small_total[9, half:],
    )


def solution(mesh):
    in_specs = (
        P("pipe", "dp", None),
        P("dp"),
        P("dp"),
        P("dp", None),
        P("pipe", None, None),
        P("pipe", None, None),
        P("pipe", None, None),
        P("pipe", None),
        P("pipe", None, None),
        P("pipe", None),
        P("pipe", None, None),
        P("pipe", None, None),
        P("pipe", None),
        P("pipe", None),
        P("pipe", None),
        P("pipe"),
        P("pipe"),
    )
    out_specs = (
        P("pipe", "dp", None),
        P("pipe", "dp", None),
        P("pipe", None, None),
        P("pipe", None, None),
        P("pipe", None, None),
        P("pipe", None),
        P("pipe", None, None),
        P("pipe", None),
        P("pipe", None, None),
        P("pipe", None, None),
        P("pipe", None),
        P("pipe", None),
        P("pipe", None),
        P("pipe"),
        P("pipe"),
    )
    return jax.shard_map(local, mesh=mesh, in_specs=in_specs, out_specs=out_specs, check_vma=False)
```

```python
import functools

import jax
import jax.numpy as jnp
from jax import lax
from jax.experimental import pallas as pl
from jax.experimental.pallas import tpu as pltpu
from jax.sharding import PartitionSpec as P

HEADS = 8
LOW = jnp.bfloat16
WIDE = jnp.float32
HEAD_SIZE = 64
PAIR = 2 * HEAD_SIZE
GELU_SCALE = 0.7978845608
GELU_CUBE = 0.044715
MASKED = -1e30
VMEM_LIMIT = 56 * 2**20


def product(left, right, left_dim=1, right_dim=0):
    return lax.dot_general(
        left, right, (((left_dim,), (right_dim,)), ((), ())), preferred_element_type=WIDE
    )


class Copies:
    def __init__(self, semaphores):
        self.semaphores = semaphores
        self.count = 0

    def start(self, source, target):
        copy = pltpu.make_async_copy(source, target, self.semaphores.at[self.count])
        self.count += 1
        copy.start()
        return copy


def pair_columns(pair):
    return pl.ds(pl.multiple_of(pair * PAIR, PAIR), PAIR)


def lanes(rows):
    return lax.broadcasted_iota(jnp.int32, (rows, PAIR), 1)


def split_three(column):
    high = column.astype(LOW).astype(WIDE)
    rest = column - high
    middle = rest.astype(LOW).astype(WIDE)
    return high, middle, rest - middle


def key_side(keys, head, bias, lane):
    base = HEAD_SIZE * (1 - head)
    own = lane // HEAD_SIZE == head
    extra = jnp.where(lane == base, bias, jnp.where((lane > base) & (lane < base + 4), 1.0, 0.0))
    return jnp.where(own, keys, extra).astype(LOW)


def attend(query_ref, key_ref, value_ref, count, mixed_ref, logsum_ref, tile=512):
    rows = query_ref.shape[0]
    lane = lanes(rows)
    row = lax.broadcasted_iota(jnp.int32, (rows, PAIR), 0)
    bias = jnp.where(row < count, 0.0, MASKED)
    logsum_ref[...] = jnp.zeros_like(logsum_ref)

    def pair_step(pair, carry):
        columns = pair_columns(pair)
        queries = query_ref[:, columns].astype(WIDE) * HEAD_SIZE**-0.5
        keys = key_ref[:, columns].astype(WIDE)
        values = value_ref[:, columns].astype(WIDE)
        sides = []
        for head in range(2):
            base = HEAD_SIZE * (1 - head)
            own = lane // HEAD_SIZE == head
            one = jnp.where(lane == base, 1.0, 0.0)
            sides.append(
                (
                    jnp.where(own, queries, one).astype(LOW),
                    key_side(keys, head, bias, lane),
                    jnp.where(own, values, one).astype(LOW),
                )
            )
        for begin in range(0, rows, tile):
            mixed = []
            logsum = logsum_ref[begin : begin + tile]
            for head in range(2):
                base = HEAD_SIZE * (1 - head)
                query_side, keys_side, value_side = sides[head]
                scores = product(query_side[begin : begin + tile], keys_side, 1, 1)
                top = jnp.max(scores, axis=1, keepdims=True)
                weights = jnp.exp(scores - top).astype(LOW)
                summed = product(weights, value_side)
                total = summed[:, base : base + 1]
                mixed.append(summed * (1.0 / total))
                logsum = jnp.where(
                    lane[:tile] == 2 * pair + head, top + jnp.log(total), logsum
                )
            mixed_ref[begin : begin + tile, columns] = jnp.where(
                lane[:tile] < HEAD_SIZE, mixed[0], mixed[1]
            ).astype(LOW)
            logsum_ref[begin : begin + tile] = logsum
        return carry

    lax.fori_loop(0, HEADS // 2, pair_step, 0)


def attend_back(
    query_ref, key_ref, value_ref, count, mixed_ref, logsum_ref, grad_ref,
    query_grad_ref, key_grad_ref, value_grad_ref, tile=512, after=None,
):
    rows = query_ref.shape[0]
    lane = lanes(rows)
    row = lax.broadcasted_iota(jnp.int32, (rows, PAIR), 0)
    bias = jnp.where(row < count, 0.0, MASKED)

    def pair_step(pair, carry):
        columns = pair_columns(pair)
        queries = query_ref[:, columns].astype(WIDE) * HEAD_SIZE**-0.5
        keys = key_ref[:, columns].astype(WIDE)
        values = value_ref[:, columns].astype(WIDE)
        grads = grad_ref[:, columns].astype(WIDE)
        along = grads * mixed_ref[:, columns].astype(WIDE)
        logsums = logsum_ref[...]
        query_sum = []
        key_parts = []
        value_parts = []
        for head in range(2):
            base = HEAD_SIZE * (1 - head)
            own = lane // HEAD_SIZE == head
            column = jnp.sum(
                jnp.where(lane == 2 * pair + head, logsums, 0.0), axis=1, keepdims=True
            )
            inner = jnp.sum(jnp.where(own, along, 0.0), axis=1, keepdims=True)
            query_side = jnp.where(own, queries, jnp.where(lane == base, 1.0, 0.0))
            grad_side = jnp.where(own, grads, 0.0)
            for place, part in enumerate(split_three(column)):
                query_side = jnp.where(lane == base + 1 + place, -part, query_side)
            for place, part in enumerate(split_three(inner)):
                grad_side = jnp.where(lane == base + 1 + place, -part, grad_side)
            query_side = query_side.astype(LOW)
            grad_side = grad_side.astype(LOW)
            keys_side = key_side(keys, head, bias, lane)
            value_side = key_side(values, head, 0.0, lane)
            query_total = None
            for begin in range(0, rows, tile):
                spot = slice(begin, begin + tile)
                probs = jnp.exp(product(keys_side[spot], query_side, 1, 1))
                slopes = (probs * product(value_side[spot], grad_side, 1, 1)).astype(LOW)
                value_part = product(probs.astype(LOW), grad_side)
                key_part = product(slopes, query_side)
                query_part = product(slopes, keys_side[spot], 0, 0)
                query_total = query_part if query_total is None else query_total + query_part
                key_parts.append(key_part)
                value_parts.append(value_part)
            query_sum.append(query_total)
        query_grad_ref[:, columns] = (
            jnp.where(lane < HEAD_SIZE, query_sum[0], query_sum[1]) * HEAD_SIZE**-0.5
        ).astype(LOW)
        pieces = rows // tile
        for piece in range(pieces):
            spot = slice(piece * tile, (piece + 1) * tile)
            first = lane[:tile] < HEAD_SIZE
            key_grad_ref[spot, columns] = jnp.where(
                first, key_parts[piece], key_parts[pieces + piece]
            ).astype(LOW)
            value_grad_ref[spot, columns] = jnp.where(
                first, value_parts[piece], value_parts[pieces + piece]
            ).astype(LOW)
        if after is not None:
            after(pair)
        return carry

    lax.fori_loop(0, HEADS // 2, pair_step, 0)


def normed(values):
    shifted = values - jnp.mean(values, axis=1, keepdims=True)
    scale = lax.rsqrt(jnp.mean(shifted * shifted, axis=1, keepdims=True) + 1e-05)
    return shifted * scale, scale


def norm(values, gain, bias):
    return normed(values)[0] * gain + bias


def norm_back(values, gain, grad):
    unit, scale = normed(values)
    inner = grad * gain
    back = scale * (
        inner
        - jnp.mean(inner, axis=1, keepdims=True)
        - unit * jnp.mean(inner * unit, axis=1, keepdims=True)
    )
    return back, column_sum(grad * unit), column_sum(grad)


def column_sum(values):
    return jnp.sum(values, axis=0, keepdims=True)


def row_tiles(rows, tile, body):
    def step(index, carry):
        body(pl.ds(pl.multiple_of(index * tile, tile), tile))
        return carry

    lax.fori_loop(0, rows // tile, step, 0)


def gelu_pair(value):
    square = value * value
    half = 0.5 * jnp.tanh(value * (GELU_SCALE + (GELU_SCALE * GELU_CUBE) * square)) + 0.5
    act = value * half
    slope = half + act * (1.0 - half) * (
        2.0 * GELU_SCALE + (6.0 * GELU_SCALE * GELU_CUBE) * square
    )
    return act, slope


SMALL_ROWS = 16
ROW_TILE = 128
HALF_TILE = 256


def columns_of(index, width):
    return pl.ds(pl.multiple_of(index * width, width), width)


def project(left_ref, right_ref, target_ref, width):
    def step(index, carry):
        columns = columns_of(index, width)
        target_ref[:, columns] = product(left_ref[...], right_ref[:, columns]).astype(LOW)
        return carry

    lax.fori_loop(0, target_ref.shape[1] // width, step, 0)


def wide_row(ref, row):
    return ref[0, row : row + 1, :].astype(WIDE)


def feed_forward(low_ref, wide_ref, in_w, in_b, out2_w, out2_b, act_ref, slope_ref, residual_ref):
    rows, width = low_ref.shape

    def hidden_step(index, carry):
        columns = columns_of(index, width)
        bias = in_b[:, columns].astype(WIDE)
        for begin in range(0, rows, HALF_TILE):
            spot = slice(begin, begin + HALF_TILE)
            act, slope = gelu_pair(product(low_ref[spot], in_w[:, columns]) + bias)
            act_ref[spot, columns] = act.astype(LOW)
            slope_ref[spot, columns] = slope.astype(LOW)
        return carry

    lax.fori_loop(0, act_ref.shape[1] // width, hidden_step, 0)
    bias_out = out2_b[...].astype(WIDE)

    def out_step(spot):
        residual_ref[spot] = wide_ref[spot] + product(act_ref[spot], out2_w[...]) + bias_out

    row_tiles(rows, HALF_TILE, out_step)


def feed_back(residual_grad, grad_low, slope_ref, in_w, out2_w, hidden_grad, bias_rows, out_ref):
    rows, width = grad_low.shape

    def hidden_step(index, carry):
        columns = columns_of(index, width)
        total = jnp.zeros((1, width), WIDE)
        for begin in range(0, rows, HALF_TILE):
            spot = slice(begin, begin + HALF_TILE)
            grads = product(grad_low[spot], out2_w[columns, :], 1, 1)
            grads = (grads * slope_ref[spot, columns].astype(WIDE)).astype(LOW)
            hidden_grad[spot, columns] = grads
            total = total + column_sum(grads.astype(WIDE))
        bias_rows[pl.ds(index, 1), :] = total
        return carry

    lax.fori_loop(0, hidden_grad.shape[1] // width, hidden_step, 0)

    def out_step(spot):
        out_ref[spot] = residual_grad[spot] + product(hidden_grad[spot], in_w[...], 1, 1)

    row_tiles(rows, HALF_TILE, out_step)


def norm_back_rows(values_ref, gain, grad_ref, wide_ref, low_ref, gain_row, bias_row):
    rows, width = values_ref.shape
    gain_row[...] = jnp.zeros((1, width), WIDE)
    bias_row[...] = jnp.zeros((1, width), WIDE)

    def step(spot):
        back, gain_part, bias_part = norm_back(values_ref[spot], gain, grad_ref[spot])
        wide_ref[spot] = back
        low_ref[spot] = back.astype(LOW)
        gain_row[...] += gain_part
        bias_row[...] += bias_part

    row_tiles(rows, ROW_TILE, step)


def self_kernel(
    example, src_len, tgt_len, in_b, out2_b, gains, biases, inputs, qkv_w, out_w, in_w, out2_w,
    *refs,
):
    (
        qkv_out, logsum_out, mixed_out, residual_out, low_out, act_out, slope_out, second_out,
        memory_out, block_out, x_s, qkv_w_s, out_w_s, in_w_s, out2_w_s, qkv_s, logsum_s, mixed_s,
        residual_s, wide_s, low_s, act_s, slope_s, second_s, memory_s, semaphores,
    ) = refs[1:] if example else refs
    section = lax.axis_index("pipe")
    rows, width = x_s.shape
    copies = Copies(semaphores)
    x_copy = copies.start(inputs.at[0, pl.ds(example * rows, rows)], x_s)
    qkv_copy = copies.start(qkv_w.at[0], qkv_w_s)
    out_copy = copies.start(out_w.at[0], out_w_s)
    encoder = section == 0
    ffn_copies = [
        pltpu.make_async_copy(in_w.at[0], in_w_s, semaphores.at[14]),
        pltpu.make_async_copy(out2_w.at[0], out2_w_s, semaphores.at[15]),
    ]

    @pl.when(encoder)
    def _():
        for copy in ffn_copies:
            copy.start()

    x_copy.wait()
    qkv_copy.wait()
    project(x_s, qkv_w_s, qkv_s, width)
    out_copies = [copies.start(qkv_s, qkv_out)]
    count = jnp.where(encoder, src_len[example], tgt_len[example])
    attend(
        qkv_s.at[:, :width],
        qkv_s.at[:, width : 2 * width],
        qkv_s.at[:, 2 * width :],
        count,
        mixed_s,
        logsum_s,
    )
    out_copies.append(copies.start(mixed_s, mixed_out))
    out_copies.append(copies.start(logsum_s, logsum_out))
    out_copy.wait()

    def residual_step(spot):
        residual_s[spot] = x_s[spot].astype(WIDE) + product(mixed_s[spot], out_w_s[...])

    row_tiles(rows, HALF_TILE, residual_step)
    out_copies.append(copies.start(residual_s, residual_out))

    @pl.when(encoder)
    def _():
        gain, bias = wide_row(gains, 0), wide_row(biases, 0)

        def norm_step(spot):
            value = norm(residual_s[spot], gain, bias)
            wide_s[spot] = value
            low_s[spot] = value.astype(LOW)

        row_tiles(rows, ROW_TILE, norm_step)
        more = Copies(semaphores)
        more.count = 8
        kept = [more.start(low_s, low_out)]
        for copy in ffn_copies:
            copy.wait()
        feed_forward(
            low_s, wide_s, in_w_s, in_b, out2_w_s, out2_b, act_s, slope_s, second_s
        )
        kept.append(more.start(act_s, act_out))
        kept.append(more.start(slope_s, slope_out))
        kept.append(more.start(second_s, second_out))
        gain_last, bias_last = wide_row(gains, 1), wide_row(biases, 1)

        def memory_step(index, carry):
            spot = pl.ds(pl.multiple_of(index * ROW_TILE, ROW_TILE), ROW_TILE)
            row = lax.broadcasted_iota(jnp.int32, (ROW_TILE, width), 0) + index * ROW_TILE
            value = norm(second_s[spot], gain_last, bias_last)
            memory_s[spot] = jnp.where(row < count, value, 0.0).astype(LOW)
            return carry

        lax.fori_loop(0, rows // ROW_TILE, memory_step, 0)
        kept.append(more.start(memory_s, memory_out))
        block_rows = pl.ds(example * rows, rows)
        block_copy = pltpu.make_async_copy(
            memory_s, block_out.at[0, block_rows], semaphores.at[16]
        )
        block_copy.start()
        kept.append(block_copy)
        for copy in kept:
            copy.wait()

    for copy in out_copies:
        copy.wait()


def cross_kernel(
    example, src_len, tgt_len, in_b, out2_b, gains, biases, own_gains, residual_in, memory_in,
    cotangent, in_w, out2_w, qkv_own, out_own, slot_own, near, far, low_in, act_in, block_in,
    small_out, low_out, act_out, block_out, final_out,
    grad_out, hidden_out, first_out, mixed_out, branch_out, query_out, pair_out, memory_out,
    rest_out, residual_s, memory_s, grad_s, in_w_s, out2_w_s, qkv_w_s, out_w_s, slot_w_s, wide_s,
    first_s, query_s, pair_s, mixed_s, logsum_s, cross_s, low_s, act_s, slope_s, second_s,
    final_s, earlier_s, slot_s, wide_grad_s, grad_low_s, hidden_s, back_s, rest_s, branch_s,
    cross_grad_s, query_grad_s, pair_grad_s, memory_grad_s, gains_s, semaphores,
):
    section = lax.axis_index("pipe")
    core = lax.axis_index("dp") % 2
    rows, width = residual_s.shape
    part = qkv_own.shape[0] // 2
    small_out[...] = jnp.zeros_like(small_out)

    @pl.when(section == 1)
    def _():
        copies = Copies(semaphores)
        begin = pl.ds(example * rows, rows)
        first_copy = copies.start(residual_in, residual_s)

        def gathered(own, begin, rows, target, columns=None):
            half = 2 * rows
            fetched = []
            for source, place in ((near, core), (far, 1 - core)):
                spot = pl.ds(pl.multiple_of(place * rows, rows), rows)
                spot = target.at[spot] if columns is None else target.at[spot, columns]
                fetched.append(copies.start(source.at[pl.ds(begin, rows)], spot))
            if own is not None:
                fetched.append(copies.start(own, target.at[pl.ds(half, half)]))
            return fetched

        qkv_copies = []
        for index in range(3):
            qkv_copies += gathered(
                None if index else qkv_own, index * part, part, qkv_w_s,
                pl.ds(index * width, width),
            )
        memory_copy = copies.start(memory_in, memory_s)
        out_copies = gathered(out_own, 3 * part, part, out_w_s)
        out_copies.append(copies.start(near.at[pl.ds(6 * part, SMALL_ROWS)], gains_s))
        ffn_copies = [copies.start(in_w.at[0], in_w_s), copies.start(out2_w.at[0], out2_w_s)]
        grad_copy = copies.start(cotangent.at[begin], grad_s)
        slot_copies = gathered(slot_own, 4 * part, 2 * part, slot_w_s)
        kept = []
        first_copy.wait()
        gain, bias = wide_row(gains, 0), wide_row(biases, 0)

        def norm_step(spot):
            value = norm(residual_s[spot], gain, bias)
            wide_s[spot] = value
            first_s[spot] = value.astype(LOW)

        row_tiles(rows, ROW_TILE, norm_step)
        kept.append(copies.start(first_s, first_out))
        for copy in qkv_copies:
            copy.wait()
        query_s[...] = product(first_s[...], qkv_w_s[:, :width]).astype(LOW)
        memory_copy.wait()
        project(memory_s, qkv_w_s.at[:, width:], pair_s, width)
        key_ref, value_ref = pair_s.at[:, :width], pair_s.at[:, width:]
        count = src_len[example]
        attend(query_s, key_ref, value_ref, count, mixed_s, logsum_s)
        kept.append(copies.start(mixed_s, mixed_out))
        for copy in out_copies:
            copy.wait()
        came_row, own_row = gains_s[0:1, :].astype(WIDE), own_gains[0:1, :].astype(WIDE)
        half = width // 2
        cross_gain = jnp.concatenate([came_row[:, :half], own_row[:, :half]], axis=1)
        cross_bias = jnp.concatenate([came_row[:, half:], own_row[:, half:]], axis=1)

        def cross_step(spot):
            value = wide_s[spot] + product(mixed_s[spot], out_w_s[...])
            cross_s[spot] = value
            value = norm(value, cross_gain, cross_bias)
            wide_s[spot] = value
            low_s[spot] = value.astype(LOW)

        row_tiles(rows, HALF_TILE, cross_step)
        kept.append(copies.start(low_s, low_out))
        for copy in ffn_copies:
            copy.wait()
        feed_forward(
            low_s, wide_s, in_w_s, in_b, out2_w_s, out2_b, act_s, slope_s, second_s
        )
        kept.append(copies.start(act_s, act_out))
        gain_last, bias_last = wide_row(gains, 1), wide_row(biases, 1)

        def final_step(spot):
            final_s[spot] = norm(second_s[spot], gain_last, bias_last).astype(LOW)

        row_tiles(rows, ROW_TILE, final_step)
        kept.append(copies.start(final_s, final_out))
        grad_copy.wait()
        for copy in slot_copies:
            copy.wait()
        row = lax.broadcasted_iota(jnp.int32, (rows, width), 0)
        slots = tgt_len[example] - 1
        slot_grad = jnp.where(row < slots, grad_s[...].astype(WIDE), 0.0)
        grad_s[...] = slot_grad.astype(LOW)
        earlier = jnp.where(row == 0, 0.0, pltpu.roll(slot_grad, 1, 0))
        earlier_s[...] = earlier.astype(LOW)
        wide_grad_s[...] = product(final_s[...], slot_w_s[width:, :])
        value = product(final_s[...], slot_w_s[:width, :]) + pltpu.roll(
            wide_grad_s[...], rows - 1, 0
        )
        slot_s[...] = jnp.where(row < slots, value, 0.0).astype(LOW)
        kept.append(copies.start(slot_s, block_out.at[0, begin]))
        wide_grad_s[...] = product(grad_s[...], slot_w_s[:width, :], 1, 1) + product(
            earlier_s[...], slot_w_s[width:, :], 1, 1
        )
        norm_back_rows(
            second_s, gain_last, wide_grad_s, second_s, grad_low_s,
            small_out.at[6:7, :], small_out.at[8:9, :],
        )
        kept.append(copies.start(grad_low_s, grad_out))
        small_out[4:5, :] = column_sum(grad_low_s[...].astype(WIDE))
        feed_back(
            second_s, grad_low_s, slope_s, in_w_s, out2_w_s, hidden_s, small_out.at[0:4, :],
            back_s,
        )
        kept.append(copies.start(hidden_s, hidden_out))
        norm_back_rows(
            cross_s, cross_gain, back_s, rest_s, branch_s,
            small_out.at[9:10, :], small_out.at[10:11, :],
        )
        kept.append(copies.start(rest_s, rest_out))
        kept.append(copies.start(branch_s, branch_out))
        cross_grad_s[...] = product(branch_s[...], out_w_s[...], 1, 1).astype(LOW)
        attend_back(
            query_s, key_ref, value_ref, count, mixed_s, logsum_s, cross_grad_s,
            query_grad_s, pair_grad_s.at[:, :width], pair_grad_s.at[:, width:],
        )
        kept.append(copies.start(query_grad_s, query_out))
        kept.append(copies.start(pair_grad_s, pair_out))
        memory_grad_s[...] = product(pair_grad_s[...], qkv_w_s[:, width:], 1, 1).astype(LOW)
        kept.append(copies.start(memory_grad_s, memory_out))
        for copy in kept:
            copy.wait()


def back_kernel(
    example, src_len, tgt_len, gains, qkv_w, out_w, in_w, out2_w, near, far, query_own,
    memory_grad, second_in, slope_in, query_grad, rest_in, residual_in,
    qkv_in, logsum_in, mixed_in, grad_in, hidden_in, order_in, small_out, grad_out, hidden_out,
    branch_out, qkv_grad_out, rows_out, qkv_w_s, out_w_s, in_w_s, out2_w_s, query_w_s,
    memory_s, second_s, slope_s, wide_s, grad_low_s, hidden_s, back_s, query_grad_s, residual_s,
    qkv_s, logsum_s, mixed_s, rest_s, branch_s, attn_grad_s, qkv_grad_s, semaphores,
):
    section = lax.axis_index("pipe")
    core = lax.axis_index("dp") % 2
    rows, width = residual_s.shape
    small_out[...] = jnp.zeros_like(small_out)
    gain_first, gain_last = wide_row(gains, 0), wide_row(gains, 1)
    copies = Copies(semaphores)
    copies.count = 16
    residual_copy = copies.start(residual_in, residual_s)
    out_copy = copies.start(out_w.at[0], out_w_s)
    qkv_copies = [
        copies.start(qkv_in, qkv_s),
        copies.start(logsum_in, logsum_s),
        copies.start(mixed_in, mixed_s),
    ]
    qkv_w_copy = copies.start(qkv_w.at[0], qkv_w_s)

    @pl.when(section == 0)
    def _():
        more = Copies(semaphores)
        fetched = [
            more.start(memory_grad, memory_s),
            more.start(second_in, second_s),
            more.start(slope_in, slope_s),
            more.start(out2_w.at[0], out2_w_s),
            more.start(in_w.at[0], in_w_s),
        ]
        fetched[0].wait()
        fetched[1].wait()
        row = lax.broadcasted_iota(jnp.int32, (rows, width), 0)
        wide_s[...] = jnp.where(
            row < src_len[example], memory_s[...].astype(WIDE), 0.0
        )
        norm_back_rows(
            second_s, gain_last, wide_s, second_s, grad_low_s,
            small_out.at[6:7, :], small_out.at[8:9, :],
        )
        kept = [more.start(grad_low_s, grad_out)]
        small_out[4:5, :] = column_sum(grad_low_s[...].astype(WIDE))
        for copy in fetched[2:]:
            copy.wait()
        feed_back(
            second_s, grad_low_s, slope_s, in_w_s, out2_w_s, hidden_s, small_out.at[0:4, :],
            back_s,
        )
        kept.append(more.start(hidden_s, hidden_out))
        for copy in kept:
            copy.wait()

    @pl.when(section == 1)
    def _():
        more = Copies(semaphores)
        part = query_own.shape[0] // 2
        near_at = pl.ds(pl.multiple_of(core * part, part), part)
        far_at = pl.ds(pl.multiple_of((1 - core) * part, part), part)
        fetched = [
            more.start(query_grad, query_grad_s),
            more.start(near.at[pl.ds(0, part)], query_w_s.at[near_at]),
            more.start(far.at[pl.ds(0, part)], query_w_s.at[far_at]),
            more.start(query_own.at[:, :width], query_w_s.at[pl.ds(2 * part, 2 * part)]),
            more.start(rest_in, rest_s),
        ]
        for copy in fetched:
            copy.wait()

        def first_step(spot):
            back_s[spot] = rest_s[spot] + product(query_grad_s[spot], query_w_s[...], 1, 1)

        row_tiles(rows, HALF_TILE, first_step)

    residual_copy.wait()
    norm_back_rows(
        residual_s, gain_first, back_s, rest_s, branch_s,
        small_out.at[5:6, :], small_out.at[7:8, :],
    )
    kept = [copies.start(branch_s, branch_out)]
    out_copy.wait()
    attn_grad_s[...] = product(branch_s[...], out_w_s[...], 1, 1).astype(LOW)
    for copy in qkv_copies:
        copy.wait()
    count = jnp.where(section == 0, src_len[example], tgt_len[example])
    attend_back(
        qkv_s.at[:, :width],
        qkv_s.at[:, width : 2 * width],
        qkv_s.at[:, 2 * width :],
        count,
        mixed_s,
        logsum_s,
        attn_grad_s,
        qkv_grad_s.at[:, :width],
        qkv_grad_s.at[:, width : 2 * width],
        qkv_grad_s.at[:, 2 * width :],
    )
    kept.append(copies.start(qkv_grad_s, qkv_grad_out))
    qkv_w_copy.wait()

    def rows_step(spot):
        back_s[spot] = rest_s[spot] + product(qkv_grad_s[spot], qkv_w_s[...], 1, 1)

    row_tiles(rows, HALF_TILE, rows_step)
    kept.append(copies.start(back_s, rows_out.at[0, pl.ds(example * rows, rows)]))
    for copy in kept:
        copy.wait()


MESH = pl.DeviceIdType.MESH


def ring_place(chip, chips):
    half = chip // 2
    return jnp.where(chip % 2 == 0, half, chips - 1 - half)


def ring_chip(place, chips):
    return jnp.where(place < chips // 2, 2 * place, 2 * (chips - 1 - place) + 1)


def part_rows(chunk_rows):
    first = (chunk_rows // 2 + 15) // 16 * 16
    if first == chunk_rows or chunk_rows <= 64:
        return ((0, chunk_rows),)
    return ((0, first), (first, chunk_rows - first))


def ring_layout(rows, devices):
    chips = devices // 2
    ways = 2 if rows >= 64 * chips else 1
    return ways, chips, -(-rows // (2 * ways * chips * 16)) * 16


def ring_rows(rows, devices):
    ways, chips, chunk_rows = ring_layout(rows, devices)
    return 2 * ways * chips * chunk_rows


class Links:
    def __init__(self, devices):
        self.pipe = lax.axis_index("pipe")
        self.me = lax.axis_index("dp")
        self.chips = devices // 2
        self.levels = devices.bit_length() - 1
        self.core = self.me % 2
        self.place = ring_place(self.me // 2, self.chips)
        self.sides = tuple(
            ring_chip((self.place + step) % self.chips, self.chips) * 2 + self.core
            for step in (1, self.chips - 1)
        )
        self.other = self.paired(1)
        self.across = (1 - self.pipe, self.me)

    def paired(self, bit):
        return self.me + bit - 2 * bit * ((self.me // bit) % 2)

    def greet(self):
        barrier = pltpu.get_barrier_semaphore()
        greeted = list(self.sides) + [self.paired(1 << level) for level in range(self.levels)]
        for friend in greeted:
            pl.semaphore_signal(
                barrier, inc=1, device_id=(self.pipe, friend), device_id_type=MESH
            )
        pl.semaphore_signal(barrier, inc=1, device_id=self.across, device_id_type=MESH)
        pl.semaphore_wait(barrier, len(greeted) + 1)

    def copy(self, source, target, send, recv, friend):
        return pltpu.make_async_remote_copy(
            src_ref=source,
            dst_ref=target,
            send_sem=send,
            recv_sem=recv,
            device_id=friend if isinstance(friend, tuple) else (self.pipe, friend),
            device_id_type=MESH,
        )


class Ring:
    def __init__(self, links, layout, total, refs):
        self.links = links
        ways, self.chips, self.chunk_rows = layout
        self.ways = range(ways)
        self.parts = part_rows(self.chunk_rows)
        self.total = total
        (
            self.mine, self.sibling, self.arrived, self.pair_send, self.pair_recv, self.ring_send,
            self.ring_recv, self.gather_send, self.gather_recv, self.share_send, self.share_recv,
        ) = refs

    def chunk_at(self, way, step):
        if way == 0:
            return (self.links.place - step + 2 * self.chips) % self.chips
        return (self.links.place + step + self.chips) % self.chips

    def start_row(self, core, way, chunk, part):
        begin = 0 if part is None else self.parts[part][0]
        return ((core * len(self.ways) + way) * self.chips + chunk) * self.chunk_rows + begin

    def mine_at(self, core, way, chunk, part=None):
        rows = self.chunk_rows if part is None else self.parts[part][1]
        return pl.ds(pl.multiple_of(self.start_row(core, way, chunk, part), 16), rows)

    def total_at(self, way, step, part):
        start = self.start_row(self.links.core, way, self.chunk_at(way, step), part)
        rows = self.parts[part][1]
        if len(self.total.shape) == 2:
            return self.total.at[pl.ds(pl.multiple_of(start, 16), rows)]
        size = self.total.shape[1]
        return self.total.at[start // size, pl.ds(pl.multiple_of(start % size, 16), rows)]

    def pair_copy(self, way, step, mine=None, sibling=None, send=None, recv=None):
        chunk = self.chunk_at(way, step)
        return self.links.copy(
            (self.mine if mine is None else mine).at[
                self.mine_at(1 - self.links.core, way, chunk)
            ],
            (self.sibling if sibling is None else sibling).at[way, chunk],
            (self.pair_send if send is None else send).at[way, step],
            (self.pair_recv if recv is None else recv).at[way, step],
            self.links.other,
        )

    def ring_copy(self, way, step, part):
        spot = pl.ds(*self.parts[part])
        return self.links.copy(
            self.arrived.at[way, step, spot],
            self.arrived.at[way, step + 1, spot],
            self.ring_send.at[way, step, part],
            self.ring_recv.at[way, step, part],
            self.links.sides[way],
        )

    def gather_copy(self, way, step, part):
        spot = self.total_at(way, step - 1, part)
        return self.links.copy(
            spot,
            spot,
            self.gather_send.at[way, step, part],
            self.gather_recv.at[way, step, part],
            self.links.sides[way],
        )

    def share_copy(self, way, step, part):
        spot = self.total_at(way, step - 1, part)
        return self.links.copy(
            spot,
            spot,
            self.share_send.at[way, step, part],
            self.share_recv.at[way, step, part],
            self.links.other,
        )

    def pairs_start(self):
        def start(step, carry):
            for way in self.ways:
                self.pair_copy(way, step).start()
            return carry

        lax.fori_loop(0, self.chips, start, 0)

    def pair_ready(self, way, step):
        self.pair_copy(way, step).wait_recv()

    def pairs_end(self):
        def end(step, carry):
            for way in self.ways:
                self.pair_copy(way, step).wait_send()
            return carry

        lax.fori_loop(0, self.chips, end, 0)

    def begin(self):
        self.pairs_start()
        for way in self.ways:
            self.pair_ready(way, 0)
            for part in range(len(self.parts)):
                spot = pl.ds(*self.parts[part])
                chunk = self.links.place
                own = self.mine[self.mine_at(self.links.core, way, chunk, part)]
                pair = self.sibling[way, chunk, spot]
                self.arrived[way, 0, spot] = (own.astype(WIDE) + pair.astype(WIDE)).astype(LOW)
                self.ring_copy(way, 0, part).start()

    def merged(self, way, step, part):
        spot = pl.ds(*self.parts[part])
        chunk = self.chunk_at(way, step + 1)
        self.ring_copy(way, step, part).wait_recv()
        own = self.mine[self.mine_at(self.links.core, way, chunk, part)]
        return (
            self.arrived[way, step + 1, spot].astype(WIDE)
            + own.astype(WIDE)
            + self.sibling[way, chunk, spot].astype(WIDE)
        ).astype(LOW)

    def reduce(self, step):
        for way in self.ways:
            self.pair_ready(way, step + 1)
        for part in range(len(self.parts)):
            spot = pl.ds(*self.parts[part])
            for way in self.ways:
                self.arrived[way, step + 1, spot] = self.merged(way, step, part)
                self.ring_copy(way, step + 1, part).start()

    def settle(self):
        last = self.chips - 2
        for way in self.ways:
            self.pair_ready(way, last + 1)
        for part in range(len(self.parts)):
            for way in self.ways:
                self.total_at(way, -1, part)[...] = self.merged(way, last, part)
                self.gather_copy(way, 0, part).start()
                self.share_copy(way, 0, part).start()

    def gather(self, step):
        for part in range(len(self.parts)):
            for way in self.ways:
                self.gather_copy(way, step, part).wait_recv()
                self.gather_copy(way, step + 1, part).start()
                self.share_copy(way, step + 1, part).start()

    def gather_last(self):
        last = self.chips - 2
        for part in range(len(self.parts)):
            for way in self.ways:
                self.gather_copy(way, last, part).wait_recv()
                self.share_copy(way, last + 1, part).start()

    def finish(self):
        self.pairs_end()

        def shares(step, carry):
            for way in self.ways:
                for part in range(len(self.parts)):
                    self.share_copy(way, step, part).wait()
            return carry

        lax.fori_loop(0, self.chips, shares, 0)

        def sends(step, carry):
            for way in self.ways:
                for part in range(len(self.parts)):
                    self.ring_copy(way, step, part).wait_send()
                    self.gather_copy(way, step, part).wait_send()
            return carry

        lax.fori_loop(0, self.chips - 1, sends, 0)


class CrossRing(Ring):
    def __init__(self, links, layout, total, refs, foreign_refs):
        super().__init__(links, layout, total, refs)
        self.foreign, self.foreign_sibling = foreign_refs[:2]
        self.foreign_send, self.foreign_recv, self.cross_send, self.cross_recv = foreign_refs[2:]

    def foreign_pair(self, way, step):
        return self.pair_copy(
            way, step, self.foreign, self.foreign_sibling, self.foreign_send, self.foreign_recv
        )

    def cross_copy(self, way, step):
        spot = self.mine_at(self.links.core, way, self.chunk_at(way, step))
        return self.links.copy(
            self.foreign.at[spot],
            self.mine.at[spot],
            self.cross_send.at[way, step],
            self.cross_recv.at[way, step],
            self.links.across,
        )

    def each(self, body):
        def step_all(step, carry):
            for way in self.ways:
                body(way, step)
            return carry

        lax.fori_loop(0, self.chips, step_all, 0)

    def foreign_start(self):
        self.each(lambda way, step: self.foreign_pair(way, step).start())

    def foreign_pass(self):
        def hand_over(way, step):
            chunk = self.chunk_at(way, step)
            spot = self.mine_at(self.links.core, way, chunk)
            self.foreign_pair(way, step).wait_recv()
            self.foreign[spot] = (
                self.foreign[spot].astype(WIDE) + self.foreign_sibling[way, chunk].astype(WIDE)
            ).astype(LOW)
            self.cross_copy(way, step).start()

        self.each(hand_over)

    def pairs_start(self):
        pl.when(self.links.pipe == 1)(super().pairs_start)

        @pl.when(self.links.pipe == 0)
        def _():
            self.sibling[...] = jnp.zeros_like(self.sibling)

    def pair_ready(self, way, step):
        @pl.when(self.links.pipe == 1)
        def _():
            self.pair_copy(way, step).wait_recv()

        @pl.when(self.links.pipe == 0)
        def _():
            self.cross_copy(way, step).wait_recv()

    def pairs_end(self):
        @pl.when(self.links.pipe == 1)
        def _():
            self.each(lambda way, step: self.pair_copy(way, step).wait_send())
            self.each(lambda way, step: self.foreign_pair(way, step).wait_send())
            self.each(lambda way, step: self.cross_copy(way, step).wait_send())


def ring_scratch(rows, width, devices):
    ways, chips, chunk_rows = ring_layout(rows, devices)
    pieces = len(part_rows(chunk_rows))
    dma = pltpu.SemaphoreType.DMA
    return [
        pltpu.VMEM((2 * ways * chips * chunk_rows, width), LOW),
        pltpu.VMEM((ways, chips, chunk_rows, width), LOW),
        pltpu.VMEM((ways, chips, chunk_rows, width), LOW),
        dma((ways, chips)),
        dma((ways, chips)),
    ] + [dma((ways, chips, pieces)) for _ in range(6)]


def foreign_scratch(rows, width, devices):
    ways, chips, chunk_rows = ring_layout(rows, devices)
    dma = pltpu.SemaphoreType.DMA
    return [
        pltpu.VMEM((2 * ways * chips * chunk_rows, width), LOW),
        pltpu.VMEM((ways, chips, chunk_rows, width), LOW),
    ] + [dma((ways, chips)) for _ in range(4)]


def last_kernel(
    devices, example, src_len, tgt_len, gains, small_a, small_b, small_c, inputs, qkv_w,
    out_w, in_w, out2_w, near, far, query_own, memory_grad, second_in, slope_in, query_grad,
    rest_in, residual_in, qkv_in, logsum_in, mixed_a, mixed_b, low_a, low_b, act_a, act_b, grad_a,
    grad_b, hidden_a, hidden_b, branch_a, qkv_grad_a, own_extra, sent_extra, first_total,
    second_total, cross_total, small_total, rows_out, qkv_w_s, out_w_s, in_w_s, out2_w_s, low_s, hidden_s, act_s,
    grad_s, mixed_s, branch_s, x_s, qkv_grad_s, memory_s, second_s, slope_s, back_s, query_w_s, residual_s, qkv_s, logsum_s, rest_s, attn_grad_s, small_s, small_arrived,
    cross_total_s, small_send, small_recv, small_cross_sem, semaphores, *ring_refs,
):
    links = Links(devices)
    section, core = links.pipe, links.core
    rows, width = residual_s.shape
    half = width // 2
    hidden = hidden_s.shape[1]
    hidden_blocks = hidden // width
    extra_rows = own_extra.shape[0]
    sizes = (2 * hidden, 4 * width, extra_rows)
    layouts = [ring_layout(size, devices) for size in sizes]
    early = Ring(links, layouts[0], act_s, ring_refs[:11])
    late = Ring(links, layouts[1], out2_w_s, ring_refs[11:22])
    cross = CrossRing(links, layouts[2], cross_total_s, ring_refs[22:33], ring_refs[33:])
    front, rear = pl.ds(0, rows), pl.ds(rows, rows)
    gain_first, gain_last = wide_row(gains, 0), wide_row(gains, 1)
    small_s[0] = small_a[...] + small_b[...] + small_c[...]
    partial = small_arrived.at[0]
    partial[...] = jnp.zeros_like(small_a)

    encoder = section == 0
    copies = Copies(semaphores)

    def declared(source, target):
        copy = pltpu.make_async_copy(source, target, semaphores.at[copies.count])
        copies.count += 1
        return copy

    def start(*group):
        for copy in group:
            copy.start()

    def wait(*group):
        for copy in group:
            copy.wait()

    hidden_front = [declared(low_a, low_s.at[front]), declared(low_b, low_s.at[rear]),
                    declared(hidden_a, hidden_s.at[front])]
    act_front = [declared(grad_a, grad_s.at[front])]
    for index in range(hidden_blocks):
        columns = pl.ds(index * width, width)
        act_front.append(declared(act_a.at[:, columns], act_s.at[index, front]))
        act_front.append(declared(act_b.at[:, columns], act_s.at[index, rear]))
    hidden_rear = declared(hidden_b, hidden_s.at[rear])
    grad_rear = declared(grad_b, grad_s.at[rear])
    back_inputs = [declared(memory_grad, memory_s), declared(second_in, second_s),
                   declared(slope_in, slope_s), declared(out2_w.at[0], out2_w_s),
                   declared(in_w.at[0], in_w_s)]
    part = query_own.shape[0] // 2
    near_at = pl.ds(pl.multiple_of(core * part, part), part)
    far_at = pl.ds(pl.multiple_of((1 - core) * part, part), part)
    query_inputs = [
        declared(query_grad, memory_s),
        declared(near.at[pl.ds(0, part)], query_w_s.at[near_at]),
        declared(far.at[pl.ds(0, part)], query_w_s.at[far_at]),
        declared(query_own.at[:, :width], query_w_s.at[pl.ds(2 * part, 2 * part)]),
        declared(rest_in, second_s),
    ]
    residual_copy = declared(residual_in, residual_s)
    out_w_copy = declared(out_w.at[0], out_w_s)
    attn_inputs = [declared(qkv_in, qkv_s), declared(logsum_in, logsum_s),
                   declared(mixed_b, mixed_s.at[rear])]
    qkv_w_copy = declared(qkv_w.at[0], qkv_w_s)
    weight_inputs = [declared(mixed_a, mixed_s.at[front]), declared(branch_a, branch_s.at[front]),
                     declared(qkv_grad_a, qkv_grad_s.at[front]), declared(inputs.at[0], x_s)]
    extra_loads = [declared(own_extra, cross.mine.at[pl.ds(0, extra_rows)]),
                   declared(sent_extra, cross.foreign.at[pl.ds(0, extra_rows)])]
    if cross.mine.shape[0] > extra_rows:
        cross.mine[extra_rows:] = jnp.zeros_like(cross.mine[extra_rows:])
        cross.foreign[extra_rows:] = jnp.zeros_like(cross.foreign[extra_rows:])
    rows_copy = declared(back_s, rows_out)

    @pl.when(encoder)
    def _():
        start(*back_inputs, *hidden_front, *act_front, residual_copy, out_w_copy, *attn_inputs,
              qkv_w_copy, *weight_inputs)
        wait(*back_inputs[:2])
        row = lax.broadcasted_iota(jnp.int32, (rows, width), 0)
        rest_s[...] = jnp.where(row < src_len[example], memory_s[...].astype(WIDE), 0.0)
        norm_back_rows(
            second_s, gain_last, rest_s, second_s, grad_s.at[rear],
            partial.at[6:7, :], partial.at[8:9, :],
        )
        partial[4:5, :] = column_sum(grad_s[rear].astype(WIDE))
        wait(*back_inputs[2:])
        feed_back(
            second_s, grad_s.at[rear], slope_s, in_w_s, out2_w_s, hidden_s.at[rear],
            partial.at[0:4, :], back_s,
        )

    @pl.when(section == 1)
    def _():
        start(*hidden_front, hidden_rear, *act_front, grad_rear, *extra_loads, *query_inputs,
              residual_copy, out_w_copy, *attn_inputs, qkv_w_copy, *weight_inputs)
        wait(hidden_rear, grad_rear)

    links.greet()

    def blocks(target, begin, count, block):
        def step(index, carry):
            target[columns_of(begin + index, width), :] = block(index).astype(LOW)
            return carry

        lax.fori_loop(0, count, step, 0)

    wait(*hidden_front)
    blocks(
        early.mine, 0, hidden_blocks,
        lambda index: product(low_s[...], hidden_s[:, columns_of(index, width)], 0, 0),
    )
    wait(*act_front)
    blocks(
        early.mine, hidden_blocks, hidden_blocks,
        lambda index: product(act_s[index], grad_s[...], 0, 0),
    )
    early.begin()

    @pl.when(section == 1)
    def _():
        wait(*extra_loads)
        cross.foreign_start()
        wait(*query_inputs)

        def first_step(spot):
            back_s[spot] = second_s[spot] + product(memory_s[spot], query_w_s[...], 1, 1)

        row_tiles(rows, HALF_TILE, first_step)
        cross.foreign_pass()

    wait(residual_copy)
    norm_back_rows(
        residual_s, gain_first, back_s, rest_s, branch_s.at[rear],
        partial.at[5:6, :], partial.at[7:8, :],
    )
    wait(out_w_copy)
    attn_grad_s[...] = product(branch_s[rear], out_w_s[...], 1, 1).astype(LOW)
    wait(*attn_inputs)
    count = jnp.where(encoder, src_len[example], tgt_len[example])
    chips, levels = links.chips, links.levels
    pairs = HEADS // 2

    attend_back(
        qkv_s.at[:, :width],
        qkv_s.at[:, width : 2 * width],
        qkv_s.at[:, 2 * width :],
        count,
        mixed_s.at[rear],
        logsum_s,
        attn_grad_s,
        qkv_grad_s.at[rear, pl.ds(0, width)],
        qkv_grad_s.at[rear, pl.ds(width, width)],
        qkv_grad_s.at[rear, pl.ds(2 * width, width)],
        after=early.reduce,
    )
    wait(qkv_w_copy)

    def rows_step(spot):
        back_s[spot] = rest_s[spot] + product(
            qkv_grad_s[pl.ds(rows + spot.start, spot.size)], qkv_w_s[...], 1, 1
        )

    row_tiles(rows, HALF_TILE, rows_step)
    rows_copy.start()
    early.reduce(pairs)
    wait(*weight_inputs)
    blocks(
        late.mine, 0, 3,
        lambda index: product(x_s[...], qkv_grad_s[:, columns_of(index, width)], 0, 0),
    )
    blocks(late.mine, 3, 1, lambda index: product(mixed_s[...], branch_s[...], 0, 0))

    if late.mine.shape[0] > 4 * width:
        late.mine[4 * width :] = jnp.zeros_like(late.mine[4 * width :])
    late.begin()
    cross.begin()

    small_s[0] = small_s[0] + partial[...]
    small_cross = links.copy(
        small_s.at[1], small_arrived.at[1], small_cross_sem.at[0], small_cross_sem.at[1],
        links.across,
    )

    @pl.when(section == 1)
    def _():
        small_s[1, 0:1, :] = jnp.concatenate(
            [small_s[0, 9:10, :half], small_s[0, 10:11, :half]], axis=1
        )
        small_cross.start()
        small_s[0, 9:10, :] = jnp.concatenate(
            [small_s[0, 9:10, half:], small_s[0, 10:11, half:]], axis=1
        )
        small_cross.wait_send()

    @pl.when(encoder)
    def _():
        small_cross.wait_recv()
        small_s[0, 9:10, :] = small_arrived[1, 0:1, :]

    def small_copy(level, bit):
        return links.copy(
            small_s.at[level],
            small_arrived.at[level + 2],
            small_send.at[level],
            small_recv.at[level],
            links.paired(bit),
        )

    small_copy(0, 1).start()

    def early_step(step, carry):
        early.reduce(step)
        return carry

    lax.fori_loop(pairs + 1, chips - 2, early_step, 0)
    early.settle()

    def merge_small(level, bit):
        small_copy(level, bit).wait_recv()
        merged = small_s[level] + small_arrived[level + 2]

        @pl.when(level + 1 < levels)
        def _():
            small_s[level + 1] = merged
            small_copy(level + 1, 2 * bit).start()

        @pl.when(level + 1 == levels)
        def _():
            small_total[...] = merged

    def both_step(step, bit):
        late.reduce(step)
        cross.reduce(step)
        early.gather(step)

        @pl.when(step < levels)
        def _():
            merge_small(step, bit)

        return 2 * bit

    lax.fori_loop(0, chips - 2, both_step, 1)
    late.settle()
    cross.settle()
    early.gather_last()

    def late_step(step, carry):
        late.gather(step)
        cross.gather(step)
        return carry

    lax.fori_loop(0, chips - 2, late_step, 0)
    late.gather_last()
    cross.gather_last()
    early.finish()
    kept = [pltpu.make_async_copy(
        act_s.at[index], first_total.at[pl.ds(index * 2 * rows, 2 * rows)], semaphores.at[index]
    ) for index in range(hidden_blocks)]
    late.finish()
    kept.append(pltpu.make_async_copy(
        out2_w_s.at[pl.ds(0, second_total.shape[0])], second_total, semaphores.at[hidden_blocks]
    ))
    cross.finish()
    kept.append(pltpu.make_async_copy(
        cross_total_s, cross_total, semaphores.at[hidden_blocks + 1]
    ))
    start(*kept)
    wait(*kept)
    for level in range(levels):
        small_copy(level, 1 << level).wait_send()
    rows_copy.wait()


def result_kernel(
    small_total, first_total, second_total, cross_total, rows_in, rows_buffer, rows_out, qkv_out, out_out,
    in_out, out2_out, cross_qkv_out, cross_out_out, slot_out, in_b_out, out2_b_out, gain_out,
    bias_out, cross_gain_out, cross_bias_out, first_s, second_s, rows_s, wide_s, semaphores,
):
    width = first_s.shape[1]
    half = width // 2
    for index in range(in_b_out.shape[1] // width):
        in_b_out[:, index * width : (index + 1) * width] = small_total[index : index + 1, :]
    out2_b_out[...] = small_total[4:5, :]
    gain_out[0] = small_total[5:7, :]
    bias_out[0] = small_total[7:9, :]
    cross_gain_out[...] = small_total[9:10, :half]
    cross_bias_out[...] = small_total[9:10, half:]
    rows = rows_in.shape[0]
    copies = Copies(semaphores)
    rows_copy = copies.start(rows_in, rows_s)
    kept = []
    loads = {width: [], half: []}
    second_rows = 4 * width
    for index in range(first_s.shape[0] // width):
        spot = pl.ds(index * width, width)
        loads[width].append(copies.start(first_total.at[spot], first_s.at[spot]))
    for index in range(second_s.shape[0] // half):
        begin = index * half
        if begin < second_rows:
            source = second_total.at[pl.ds(begin, half)]
        else:
            source = cross_total.at[pl.ds(begin - second_rows, half)]
        loads[half].append(copies.start(source, second_s.at[pl.ds(begin, half)]))
    targets = []
    for index in range(first_s.shape[0] // width):
        hidden_blocks = in_out.shape[2] // width
        if index < hidden_blocks:
            target = in_out.at[0, :, pl.ds(index * width, width)]
        else:
            target = out2_out.at[0, pl.ds((index - hidden_blocks) * width, width)]
        targets.append((loads[width][index : index + 1], first_s, index * width, width, target))
    for index in range(4):
        if index < 3:
            target = qkv_out.at[0, :, pl.ds(index * width, width)]
        else:
            target = out_out.at[0]
        targets.append(
            (loads[half][2 * index : 2 * index + 2], second_s, index * width, width, target)
        )
    for index in range(4):
        if index < 3:
            target = cross_qkv_out.at[:, pl.ds(index * width, width)]
        else:
            target = cross_out_out
        targets.append(
            (loads[half][8 + index : 9 + index], second_s, 4 * width + index * half, half, target)
        )
    targets.append((loads[half][12:14], second_s, 6 * width, width, slot_out))
    place = 0
    for waits, stage, begin, size, target in targets:
        for copy in waits:
            copy.wait()
        wide_s[place : place + size] = stage[begin : begin + size].astype(WIDE)
        kept.append(copies.start(wide_s.at[pl.ds(place, size)], target))
        place += size
    rows_copy.wait()
    kept.append(copies.start(rows_s, rows_out.at[0, pl.ds(rows, rows)]))
    for copy in kept:
        copy.wait()


def cross_weight_kernel(
    tgt_len, first_a, first_b, query_a, query_b, memory_a, memory_b, pair_a, pair_b, mixed_a,
    mixed_b, branch_a, branch_b, final_a, final_b, cotangent, own_out, sent_out, first_s, query_s,
    memory_s, pair_s, mixed_s, branch_s, final_s, grad_s, earlier_s, own_s, sent_s, semaphores,
):
    section = lax.axis_index("pipe")

    @pl.when(section == 1)
    def _():
        copies = Copies(semaphores)

        def both(first, second, target):
            rows = first.shape[0]
            return [
                copies.start(first, target.at[pl.ds(0, rows)]),
                copies.start(second, target.at[pl.ds(rows, rows)]),
            ]

        grad_copy = copies.start(cotangent, grad_s)
        final_copies = both(final_a, final_b, final_s)
        mixed_copies = both(mixed_a, mixed_b, mixed_s) + both(branch_a, branch_b, branch_s)
        pair_copies = both(memory_a, memory_b, memory_s) + both(pair_a, pair_b, pair_s)
        query_copies = both(first_a, first_b, first_s) + both(query_a, query_b, query_s)
        total, width = grad_s.shape
        rows = total // 2
        half = width // 2
        grad_copy.wait()
        row = lax.broadcasted_iota(jnp.int32, (rows, width), 0)
        for example in range(2):
            spot = slice(example * rows, (example + 1) * rows)
            slot_grad = jnp.where(
                row < tgt_len[example] - 1, grad_s[spot].astype(WIDE), 0.0
            )
            grad_s[spot] = slot_grad.astype(LOW)
            earlier = jnp.where(row == 0, 0.0, pltpu.roll(slot_grad, 1, 0))
            earlier_s[spot] = earlier.astype(LOW)
        for copy in final_copies:
            copy.wait()
        sent_s[4 * half :] = product(final_s[...], grad_s[...], 0, 0).astype(LOW)
        own_s[4 * half :] = product(final_s[...], earlier_s[...], 0, 0).astype(LOW)

        def keep(place, value):
            spot = slice(place * half, (place + 1) * half)
            sent_s[spot] = value[:half].astype(LOW)
            own_s[spot] = value[half:].astype(LOW)

        for copy in mixed_copies:
            copy.wait()
        keep(3, product(mixed_s[...], branch_s[...], 0, 0))
        for copy in pair_copies:
            copy.wait()
        keep(1, product(memory_s[...], pair_s[:, :width], 0, 0))
        keep(2, product(memory_s[...], pair_s[:, width:], 0, 0))
        for copy in query_copies:
            copy.wait()
        keep(0, product(first_s[...], query_s[...], 0, 0))
        kept = [copies.start(own_s, own_out), copies.start(sent_s, sent_out)]
        for copy in kept:
            copy.wait()


ANY = pl.BlockSpec(memory_space=pl.ANY)
INNER = pl.BlockSpec(memory_space=pltpu.VMEM)
SCALAR = pl.BlockSpec(memory_space=pltpu.SMEM)


def local_call(
    body, name, scalars, inner, outer, outputs, scratch, flops, aliases=None, count=32,
    semaphores=(), **compiler,
):
    shapes = [jax.ShapeDtypeStruct(shape, kind) for shape, kind, _ in outputs]
    inputs = list(scalars) + list(inner) + list(outer)
    specs = [SCALAR] * len(scalars) + [INNER] * len(inner) + [ANY] * len(outer)
    moved = sum(value.size * value.dtype.itemsize for value in inputs)
    return pl.pallas_call(
        body,
        out_shape=shapes,
        in_specs=specs,
        out_specs=[INNER if kept else ANY for _, _, kept in outputs],
        scratch_shapes=[pltpu.VMEM(shape, kind) for shape, kind in scratch]
        + list(semaphores or [pltpu.SemaphoreType.DMA((count,))]),
        input_output_aliases=aliases or {},
        compiler_params=pltpu.CompilerParams(vmem_limit_bytes=VMEM_LIMIT, **compiler),
        cost_estimate=pl.CostEstimate(flops=flops, bytes_accessed=moved, transcendentals=0),
        name=name,
    )(*inputs)


def local(
    inputs, src_len, tgt_len, cotangent, qkv_w, out_w, in_w, in_b, out2_w, out2_b, norm_gain,
    norm_bias, cross_qkv, cross_out, slot_w, cross_gain, cross_bias,
):
    core = lax.axis_index("dp") % 2
    devices = lax.axis_size("dp")
    blocks = src_len.shape[0]
    total_rows, width = inputs.shape[1:]
    rows = total_rows // blocks
    half = width // 2
    hidden = in_w.shape[2]
    square, wide3, deep = (rows, width), (rows, 3 * width), (rows, hidden)
    weight_square, logsum = (width, width), (rows, PAIR)
    tall, tall3, tall_deep = (total_rows, width), (total_rows, 3 * width), (total_rows, hidden)

    part = half // 2
    own_gains = jnp.concatenate([cross_gain, cross_bias]).reshape(1, width)
    pieces = [
        lax.dynamic_slice(cross_qkv, (core * part, column * width), (part, width))
        for column in range(3)
    ]
    pieces.append(lax.dynamic_slice_in_dim(cross_out, core * part, part, axis=0))
    pieces.append(lax.dynamic_slice_in_dim(slot_w, 2 * core * part, 2 * part, axis=0))
    pieces.append(jnp.pad(own_gains, ((0, SMALL_ROWS - 1), (0, 0))))
    near = lax.ppermute(jnp.concatenate(pieces, axis=0), "pipe", [(0, 1)])
    started = []
    for example in range(blocks):
        scratch = [
            (square, LOW), ((width, 3 * width), LOW), (weight_square, LOW), ((width, hidden), LOW),
            ((hidden, width), LOW), (wide3, LOW), (logsum, WIDE), (square, LOW),
            (square, WIDE), (square, WIDE), (square, LOW), (deep, LOW), (deep, LOW), (square, WIDE),
            (square, LOW),
        ]
        outputs = [
            (wide3, LOW, False), (logsum, WIDE, False), (square, LOW, False),
            (square, WIDE, False), (square, LOW, False), (deep, LOW, False), (deep, LOW, False),
            (square, WIDE, False), (square, LOW, False), ((1,) + tall, LOW, False),
        ]
        outer = [inputs, qkv_w, out_w, in_w, out2_w]
        if example:
            outer.append(started[-1][9])
        started.append(
            local_call(
                functools.partial(self_kernel, example), f"self_rows_{example}",
                [src_len, tgt_len], [in_b, out2_b, norm_gain, norm_bias], outer, outputs, scratch,
                6 * 10**9, aliases={11: 9} if example else None,
            )
        )
    near, _ = lax.optimization_barrier((near, started[0][8]))
    far = lax.ppermute(near, "dp", [(place, place ^ 1) for place in range(devices)])
    sent_memory = [lax.ppermute(values[8], "pipe", [(0, 1)]) for values in started]

    crossed = []
    block_out = started[-1][9]
    for example in range(blocks):
        values = started[example]
        scratch = [
            (square, WIDE), (square, LOW), (square, LOW), ((width, hidden), LOW),
            ((hidden, width), LOW), ((width, 3 * width), LOW), (weight_square, LOW),
            ((2 * width, width), LOW), (square, WIDE), (square, LOW), (square, LOW),
            ((rows, 2 * width), LOW), (square, LOW), (logsum, WIDE), (square, WIDE),
            (square, LOW), (deep, LOW), (deep, LOW), (square, WIDE), (square, LOW), (square, LOW),
            (square, LOW), (square, WIDE), (square, LOW), (deep, LOW), (square, WIDE),
            (square, WIDE), (square, LOW), (square, LOW), (square, LOW), ((rows, 2 * width), LOW),
            (square, LOW), ((SMALL_ROWS, width), LOW),
        ]
        outputs = [
            ((SMALL_ROWS, width), WIDE, True), (square, LOW, False), (deep, LOW, False),
            ((1,) + tall, LOW, False), (square, LOW, False), (square, LOW, False),
            (deep, LOW, False), (square, LOW, False), (square, LOW, False), (square, LOW, False),
            (square, LOW, False), ((rows, 2 * width), LOW, False), (square, LOW, False),
            (square, WIDE, False),
        ]
        outer = [
            values[3], sent_memory[example], cotangent, in_w, out2_w, cross_qkv, cross_out, slot_w,
            near, far, values[4], values[5], block_out,
        ]
        inner = [in_b, out2_b, norm_gain, norm_bias, own_gains]
        shift = 2 + len(inner)
        crossed.append(
            local_call(
                functools.partial(cross_kernel, example), f"cross_rows_{example}",
                [src_len, tgt_len], inner, outer, outputs, scratch, 20 * 10**9,
                aliases={shift + 10: 1, shift + 11: 2, shift + 12: 3}, count=48,
            )
        )
        block_out = crossed[-1][3]
    back_memory = [lax.ppermute(values[12], "pipe", [(1, 0)]) for values in crossed]

    def pairs_of(group, place):
        return [values[place] for values in group]

    extra_rows = 3 * width
    own_extra, sent_extra = local_call(
        cross_weight_kernel, "cross_weights", [tgt_len], [],
        pairs_of(crossed, 7) + pairs_of(crossed, 10) + sent_memory + pairs_of(crossed, 11)
        + pairs_of(crossed, 8) + pairs_of(crossed, 9) + pairs_of(crossed, 4) + [cotangent],
        [((extra_rows, width), LOW, False), ((extra_rows, width), LOW, False)],
        [
            (tall, LOW), (tall, LOW), (tall, LOW), ((total_rows, 2 * width), LOW), (tall, LOW),
            (tall, LOW), (tall, LOW), (tall, LOW), (tall, LOW), ((extra_rows, width), LOW),
            ((extra_rows, width), LOW),
        ],
        5 * 10**9,
    )
    values, after = started[0], crossed[0]
    scratch = [
        ((width, 3 * width), LOW), (weight_square, LOW), ((width, hidden), LOW),
        ((hidden, width), LOW), (weight_square, LOW), (square, LOW), (square, WIDE),
        (deep, LOW), (square, WIDE), (square, LOW), (deep, LOW), (square, WIDE), (square, LOW),
        (square, WIDE), (wide3, LOW), (logsum, WIDE), (square, LOW), (square, WIDE),
        (square, LOW), (square, LOW), (wide3, LOW),
    ]
    outputs = [
        ((SMALL_ROWS, width), WIDE, True), (square, LOW, False), (deep, LOW, False),
        (square, LOW, False), (wide3, LOW, False), ((1,) + tall, WIDE, False),
    ]
    outer = [
        qkv_w, out_w, in_w, out2_w, near, far, cross_qkv, back_memory[0], values[7], values[6],
        after[10], after[13], values[3], values[0], values[1], values[2], after[5], after[6],
        own_extra,
    ]
    back = local_call(
        functools.partial(back_kernel, 0), "back_rows_0", [src_len, tgt_len], [norm_gain], outer,
        outputs, scratch, 14 * 10**9, aliases={3 + 16: 1, 3 + 17: 2}, count=48,
    )

    values, after = started[1], crossed[1]
    sizes = (2 * hidden, 4 * width, extra_rows)
    padded = [ring_rows(size, devices) for size in sizes]
    levels = devices.bit_length() - 1
    small_shape = (SMALL_ROWS, width)
    dma = pltpu.SemaphoreType.DMA
    rings = [part for size in sizes for part in ring_scratch(size, width, devices)]
    rings += foreign_scratch(extra_rows, width, devices)
    first_total, second_total, cross_total, small_total, last_rows = local_call(
        functools.partial(last_kernel, devices, 1), "last_rows", [src_len, tgt_len],
        [norm_gain, crossed[0][0], crossed[1][0], back[0]],
        [
            inputs, qkv_w, out_w, in_w, out2_w, near, far, cross_qkv, back_memory[1], values[7],
            values[6], after[10], after[13], values[3], values[0], values[1], started[0][2],
            values[2], crossed[0][1], after[1], crossed[0][2], after[2], back[1], after[5],
            back[2], after[6], back[3], back[4], own_extra, sent_extra,
        ],
        [
            ((padded[0], width), LOW, False),
            ((padded[1], width), LOW, False),
            ((padded[2], width), LOW, False),
            (small_shape, WIDE, True),
            (square, WIDE, False),
        ],
        [
            ((width, 3 * width), LOW), (weight_square, LOW), ((width, hidden), LOW),
            ((hidden, width), LOW), (tall, LOW), (tall_deep, LOW),
            ((hidden // width,) + tall, LOW), (tall, LOW), (tall, LOW), (tall, LOW), (tall, LOW),
            (tall3, LOW), (square, LOW), (square, WIDE), (deep, LOW), (square, WIDE),
            (weight_square, LOW), (square, WIDE), (wide3, LOW), (logsum, WIDE), (square, WIDE),
            (square, LOW), ((levels,) + small_shape, WIDE), ((levels + 2,) + small_shape, WIDE),
            ((padded[2], width), LOW),
        ],
        20 * 10**9,
        semaphores=[dma((levels,)), dma((levels,)), dma((2,)), dma((64,))] + rings,
        collective_id=0, has_side_effects=True,
    )

    results = local_call(
        result_kernel, "results", [], [small_total],
        [
            first_total, second_total, cross_total, last_rows, back[5],
        ],
        [
            ((1,) + tall, WIDE, False), ((1, width, 3 * width), WIDE, False),
            ((1,) + weight_square, WIDE, False), ((1, width, hidden), WIDE, False),
            ((1, hidden, width), WIDE, False), ((half, 3 * width), WIDE, False),
            ((half, width), WIDE, False), ((width, width), WIDE, False),
            ((1, hidden), WIDE, True), ((1, width), WIDE, True), ((1, 2, width), WIDE, True),
            ((1, 2, width), WIDE, True), ((1, half), WIDE, True), ((1, half), WIDE, True),
        ],
        [
            ((sizes[0], width), LOW), ((sizes[1] + sizes[2], width), LOW), (square, WIDE),
            ((sum(sizes), width), WIDE),
        ],
        10**9, aliases={5: 0}, count=64,
    )
    return (
        block_out, results[0], results[1], results[2], results[3], results[8], results[4],
        results[9], results[10], results[11], results[5], results[6], results[7],
        results[12].reshape(half), results[13].reshape(half),
    )


def solution(mesh):
    in_specs = (
        P("pipe", "dp", None),
        P("dp"),
        P("dp"),
        P("dp", None),
        P("pipe", None, None),
        P("pipe", None, None),
        P("pipe", None, None),
        P("pipe", None),
        P("pipe", None, None),
        P("pipe", None),
        P("pipe", None, None),
        P("pipe", None, None),
        P("pipe", None),
        P("pipe", None),
        P("pipe", None),
        P("pipe"),
        P("pipe"),
    )
    out_specs = (
        P("pipe", "dp", None),
        P("pipe", "dp", None),
        P("pipe", None, None),
        P("pipe", None, None),
        P("pipe", None, None),
        P("pipe", None),
        P("pipe", None, None),
        P("pipe", None),
        P("pipe", None, None),
        P("pipe", None, None),
        P("pipe", None),
        P("pipe", None),
        P("pipe", None),
        P("pipe"),
        P("pipe"),
    )
    return jax.shard_map(local, mesh=mesh, in_specs=in_specs, out_specs=out_specs, check_vma=False)
```

```python
import functools

import jax
import jax.numpy as jnp
from jax import lax
from jax.experimental import pallas as pl
from jax.experimental.pallas import tpu as pltpu
from jax.sharding import PartitionSpec as P

HEADS = 8
LOW = jnp.bfloat16
WIDE = jnp.float32
HEAD_SIZE = 64
PAIR = 2 * HEAD_SIZE
GELU_SCALE = 0.7978845608
GELU_CUBE = 0.044715
MASKED = -1e30
VMEM_LIMIT = 56 * 2**20


def product(left, right, left_dim=1, right_dim=0):
    return lax.dot_general(
        left, right, (((left_dim,), (right_dim,)), ((), ())), preferred_element_type=WIDE
    )


class Copies:
    def __init__(self, semaphores):
        self.semaphores = semaphores
        self.count = 0

    def start(self, source, target):
        copy = pltpu.make_async_copy(source, target, self.semaphores.at[self.count])
        self.count += 1
        copy.start()
        return copy


def pair_columns(pair):
    return pl.ds(pl.multiple_of(pair * PAIR, PAIR), PAIR)


def lanes(rows):
    return lax.broadcasted_iota(jnp.int32, (rows, PAIR), 1)


def split_three(column):
    high = column.astype(LOW).astype(WIDE)
    rest = column - high
    middle = rest.astype(LOW).astype(WIDE)
    return high, middle, rest - middle


def key_side(keys, head, bias, lane):
    base = HEAD_SIZE * (1 - head)
    own = lane // HEAD_SIZE == head
    extra = jnp.where(lane == base, bias, jnp.where((lane > base) & (lane < base + 4), 1.0, 0.0))
    return jnp.where(own, keys, extra).astype(LOW)


def attend(query_ref, key_ref, value_ref, count, mixed_ref, logsum_ref, tile=512):
    rows = query_ref.shape[0]
    lane = lanes(rows)
    row = lax.broadcasted_iota(jnp.int32, (rows, PAIR), 0)
    bias = jnp.where(row < count, 0.0, MASKED)
    logsum_ref[...] = jnp.zeros_like(logsum_ref)

    def pair_step(pair, carry):
        columns = pair_columns(pair)
        queries = query_ref[:, columns].astype(WIDE) * HEAD_SIZE**-0.5
        keys = key_ref[:, columns].astype(WIDE)
        values = value_ref[:, columns].astype(WIDE)
        sides = []
        for head in range(2):
            base = HEAD_SIZE * (1 - head)
            own = lane // HEAD_SIZE == head
            one = jnp.where(lane == base, 1.0, 0.0)
            sides.append(
                (
                    jnp.where(own, queries, one).astype(LOW),
                    key_side(keys, head, bias, lane),
                    jnp.where(own, values, one).astype(LOW),
                )
            )
        for begin in range(0, rows, tile):
            mixed = []
            logsum = logsum_ref[begin : begin + tile]
            for head in range(2):
                base = HEAD_SIZE * (1 - head)
                query_side, keys_side, value_side = sides[head]
                scores = product(query_side[begin : begin + tile], keys_side, 1, 1)
                top = jnp.max(scores, axis=1, keepdims=True)
                weights = jnp.exp(scores - top).astype(LOW)
                summed = product(weights, value_side)
                total = summed[:, base : base + 1]
                mixed.append(summed * (1.0 / total))
                logsum = jnp.where(
                    lane[:tile] == 2 * pair + head, top + jnp.log(total), logsum
                )
            mixed_ref[begin : begin + tile, columns] = jnp.where(
                lane[:tile] < HEAD_SIZE, mixed[0], mixed[1]
            ).astype(LOW)
            logsum_ref[begin : begin + tile] = logsum
        return carry

    lax.fori_loop(0, HEADS // 2, pair_step, 0)


def attend_back(
    query_ref, key_ref, value_ref, count, mixed_ref, logsum_ref, grad_ref,
    query_grad_ref, key_grad_ref, value_grad_ref, tile=512, after=None,
):
    rows = query_ref.shape[0]
    lane = lanes(rows)
    row = lax.broadcasted_iota(jnp.int32, (rows, PAIR), 0)
    bias = jnp.where(row < count, 0.0, MASKED)

    def pair_step(pair, carry):
        columns = pair_columns(pair)
        queries = query_ref[:, columns].astype(WIDE) * HEAD_SIZE**-0.5
        keys = key_ref[:, columns].astype(WIDE)
        values = value_ref[:, columns].astype(WIDE)
        grads = grad_ref[:, columns].astype(WIDE)
        along = grads * mixed_ref[:, columns].astype(WIDE)
        logsums = logsum_ref[...]
        query_sum = []
        key_parts = []
        value_parts = []
        for head in range(2):
            base = HEAD_SIZE * (1 - head)
            own = lane // HEAD_SIZE == head
            column = jnp.sum(
                jnp.where(lane == 2 * pair + head, logsums, 0.0), axis=1, keepdims=True
            )
            inner = jnp.sum(jnp.where(own, along, 0.0), axis=1, keepdims=True)
            query_side = jnp.where(own, queries, jnp.where(lane == base, 1.0, 0.0))
            grad_side = jnp.where(own, grads, 0.0)
            for place, part in enumerate(split_three(column)):
                query_side = jnp.where(lane == base + 1 + place, -part, query_side)
            for place, part in enumerate(split_three(inner)):
                grad_side = jnp.where(lane == base + 1 + place, -part, grad_side)
            query_side = query_side.astype(LOW)
            grad_side = grad_side.astype(LOW)
            keys_side = key_side(keys, head, bias, lane)
            value_side = key_side(values, head, 0.0, lane)
            query_total = None
            for begin in range(0, rows, tile):
                spot = slice(begin, begin + tile)
                probs = jnp.exp(product(keys_side[spot], query_side, 1, 1))
                slopes = (probs * product(value_side[spot], grad_side, 1, 1)).astype(LOW)
                value_part = product(probs.astype(LOW), grad_side)
                key_part = product(slopes, query_side)
                query_part = product(slopes, keys_side[spot], 0, 0)
                query_total = query_part if query_total is None else query_total + query_part
                key_parts.append(key_part)
                value_parts.append(value_part)
            query_sum.append(query_total)
        query_grad_ref[:, columns] = (
            jnp.where(lane < HEAD_SIZE, query_sum[0], query_sum[1]) * HEAD_SIZE**-0.5
        ).astype(LOW)
        pieces = rows // tile
        for piece in range(pieces):
            spot = slice(piece * tile, (piece + 1) * tile)
            first = lane[:tile] < HEAD_SIZE
            key_grad_ref[spot, columns] = jnp.where(
                first, key_parts[piece], key_parts[pieces + piece]
            ).astype(LOW)
            value_grad_ref[spot, columns] = jnp.where(
                first, value_parts[piece], value_parts[pieces + piece]
            ).astype(LOW)
        if after is not None:
            after(pair)
        return carry

    lax.fori_loop(0, HEADS // 2, pair_step, 0)


def normed(values):
    shifted = values - jnp.mean(values, axis=1, keepdims=True)
    scale = lax.rsqrt(jnp.mean(shifted * shifted, axis=1, keepdims=True) + 1e-05)
    return shifted * scale, scale


def norm(values, gain, bias):
    return normed(values)[0] * gain + bias


def norm_back(values, gain, grad):
    unit, scale = normed(values)
    inner = grad * gain
    back = scale * (
        inner
        - jnp.mean(inner, axis=1, keepdims=True)
        - unit * jnp.mean(inner * unit, axis=1, keepdims=True)
    )
    return back, column_sum(grad * unit), column_sum(grad)


def column_sum(values):
    return jnp.sum(values, axis=0, keepdims=True)


def row_tiles(rows, tile, body):
    def step(index, carry):
        body(pl.ds(pl.multiple_of(index * tile, tile), tile))
        return carry

    lax.fori_loop(0, rows // tile, step, 0)


def gelu_pair(value):
    square = value * value
    half = 0.5 * jnp.tanh(value * (GELU_SCALE + (GELU_SCALE * GELU_CUBE) * square)) + 0.5
    act = value * half
    slope = half + act * (1.0 - half) * (
        2.0 * GELU_SCALE + (6.0 * GELU_SCALE * GELU_CUBE) * square
    )
    return act, slope


SMALL_ROWS = 16
ROW_TILE = 128
HALF_TILE = 256


def columns_of(index, width):
    return pl.ds(pl.multiple_of(index * width, width), width)


def project(left_ref, right_ref, target_ref, width):
    def step(index, carry):
        columns = columns_of(index, width)
        target_ref[:, columns] = product(left_ref[...], right_ref[:, columns]).astype(LOW)
        return carry

    lax.fori_loop(0, target_ref.shape[1] // width, step, 0)


def wide_row(ref, row):
    return ref[0, row : row + 1, :].astype(WIDE)


def feed_forward(low_ref, wide_ref, in_w, in_b, out2_w, out2_b, act_ref, slope_ref, residual_ref):
    rows, width = low_ref.shape

    def hidden_step(index, carry):
        columns = columns_of(index, width)
        bias = in_b[:, columns].astype(WIDE)
        for begin in range(0, rows, HALF_TILE):
            spot = slice(begin, begin + HALF_TILE)
            act, slope = gelu_pair(product(low_ref[spot], in_w[:, columns]) + bias)
            act_ref[spot, columns] = act.astype(LOW)
            slope_ref[spot, columns] = slope.astype(LOW)
        return carry

    lax.fori_loop(0, act_ref.shape[1] // width, hidden_step, 0)
    bias_out = out2_b[...].astype(WIDE)

    def out_step(spot):
        residual_ref[spot] = wide_ref[spot] + product(act_ref[spot], out2_w[...]) + bias_out

    row_tiles(rows, HALF_TILE, out_step)


def feed_back(residual_grad, grad_low, slope_ref, in_w, out2_w, hidden_grad, bias_rows, out_ref):
    rows, width = grad_low.shape

    def hidden_step(index, carry):
        columns = columns_of(index, width)
        total = jnp.zeros((1, width), WIDE)
        for begin in range(0, rows, HALF_TILE):
            spot = slice(begin, begin + HALF_TILE)
            grads = product(grad_low[spot], out2_w[columns, :], 1, 1)
            grads = (grads * slope_ref[spot, columns].astype(WIDE)).astype(LOW)
            hidden_grad[spot, columns] = grads
            total = total + column_sum(grads.astype(WIDE))
        bias_rows[pl.ds(index, 1), :] = total
        return carry

    lax.fori_loop(0, hidden_grad.shape[1] // width, hidden_step, 0)

    def out_step(spot):
        out_ref[spot] = residual_grad[spot] + product(hidden_grad[spot], in_w[...], 1, 1)

    row_tiles(rows, HALF_TILE, out_step)


def norm_back_rows(values_ref, gain, grad_ref, wide_ref, low_ref, gain_row, bias_row):
    rows, width = values_ref.shape
    gain_row[...] = jnp.zeros((1, width), WIDE)
    bias_row[...] = jnp.zeros((1, width), WIDE)

    def step(spot):
        back, gain_part, bias_part = norm_back(values_ref[spot], gain, grad_ref[spot])
        wide_ref[spot] = back
        low_ref[spot] = back.astype(LOW)
        gain_row[...] += gain_part
        bias_row[...] += bias_part

    row_tiles(rows, ROW_TILE, step)


def self_kernel(
    example, src_len, tgt_len, in_b, out2_b, gains, biases, inputs, qkv_w, out_w, in_w, out2_w,
    *refs,
):
    (
        qkv_out, logsum_out, mixed_out, residual_out, low_out, act_out, slope_out, second_out,
        memory_out, block_out, x_s, qkv_w_s, out_w_s, in_w_s, out2_w_s, qkv_s, logsum_s, mixed_s,
        residual_s, wide_s, low_s, act_s, slope_s, second_s, memory_s, semaphores,
    ) = refs[1:] if example else refs
    section = lax.axis_index("pipe")
    rows, width = x_s.shape
    copies = Copies(semaphores)
    x_copy = copies.start(inputs.at[0, pl.ds(example * rows, rows)], x_s)
    qkv_copy = copies.start(qkv_w.at[0], qkv_w_s)
    out_copy = copies.start(out_w.at[0], out_w_s)
    encoder = section == 0
    ffn_copies = [
        pltpu.make_async_copy(in_w.at[0], in_w_s, semaphores.at[14]),
        pltpu.make_async_copy(out2_w.at[0], out2_w_s, semaphores.at[15]),
    ]

    @pl.when(encoder)
    def _():
        for copy in ffn_copies:
            copy.start()

    x_copy.wait()
    qkv_copy.wait()
    project(x_s, qkv_w_s, qkv_s, width)
    out_copies = [copies.start(qkv_s, qkv_out)]
    count = jnp.where(encoder, src_len[example], tgt_len[example])
    attend(
        qkv_s.at[:, :width],
        qkv_s.at[:, width : 2 * width],
        qkv_s.at[:, 2 * width :],
        count,
        mixed_s,
        logsum_s,
    )
    out_copies.append(copies.start(mixed_s, mixed_out))
    out_copies.append(copies.start(logsum_s, logsum_out))
    out_copy.wait()

    def residual_step(spot):
        residual_s[spot] = x_s[spot].astype(WIDE) + product(mixed_s[spot], out_w_s[...])

    row_tiles(rows, HALF_TILE, residual_step)
    out_copies.append(copies.start(residual_s, residual_out))

    @pl.when(encoder)
    def _():
        gain, bias = wide_row(gains, 0), wide_row(biases, 0)

        def norm_step(spot):
            value = norm(residual_s[spot], gain, bias)
            wide_s[spot] = value
            low_s[spot] = value.astype(LOW)

        row_tiles(rows, ROW_TILE, norm_step)
        more = Copies(semaphores)
        more.count = 8
        kept = [more.start(low_s, low_out)]
        for copy in ffn_copies:
            copy.wait()
        feed_forward(
            low_s, wide_s, in_w_s, in_b, out2_w_s, out2_b, act_s, slope_s, second_s
        )
        kept.append(more.start(act_s, act_out))
        kept.append(more.start(slope_s, slope_out))
        kept.append(more.start(second_s, second_out))
        gain_last, bias_last = wide_row(gains, 1), wide_row(biases, 1)

        def memory_step(index, carry):
            spot = pl.ds(pl.multiple_of(index * ROW_TILE, ROW_TILE), ROW_TILE)
            row = lax.broadcasted_iota(jnp.int32, (ROW_TILE, width), 0) + index * ROW_TILE
            value = norm(second_s[spot], gain_last, bias_last)
            memory_s[spot] = jnp.where(row < count, value, 0.0).astype(LOW)
            return carry

        lax.fori_loop(0, rows // ROW_TILE, memory_step, 0)
        kept.append(more.start(memory_s, memory_out))
        block_rows = pl.ds(example * rows, rows)
        block_copy = pltpu.make_async_copy(
            memory_s, block_out.at[0, block_rows], semaphores.at[16]
        )
        block_copy.start()
        kept.append(block_copy)
        for copy in kept:
            copy.wait()

    for copy in out_copies:
        copy.wait()


def cross_kernel(
    example, src_len, tgt_len, in_b, out2_b, gains, biases, own_gains, residual_in, memory_in,
    cotangent, in_w, out2_w, qkv_own, out_own, slot_own, near, far, low_in, act_in, block_in,
    small_out, low_out, act_out, block_out, final_out,
    grad_out, hidden_out, first_out, mixed_out, branch_out, query_out, pair_out, memory_out,
    rest_out, residual_s, memory_s, grad_s, in_w_s, out2_w_s, qkv_w_s, out_w_s, slot_w_s, wide_s,
    first_s, query_s, pair_s, mixed_s, logsum_s, cross_s, low_s, act_s, slope_s, second_s,
    final_s, earlier_s, slot_s, wide_grad_s, grad_low_s, hidden_s, back_s, rest_s, branch_s,
    cross_grad_s, query_grad_s, pair_grad_s, memory_grad_s, gains_s, semaphores,
):
    section = lax.axis_index("pipe")
    core = lax.axis_index("dp") % 2
    rows, width = residual_s.shape
    part = qkv_own.shape[0] // 2
    small_out[...] = jnp.zeros_like(small_out)

    @pl.when(section == 1)
    def _():
        copies = Copies(semaphores)
        begin = pl.ds(example * rows, rows)
        first_copy = copies.start(residual_in, residual_s)

        def gathered(own, begin, rows, target, columns=None):
            half = 2 * rows
            fetched = []
            for source, place in ((near, core), (far, 1 - core)):
                spot = pl.ds(pl.multiple_of(place * rows, rows), rows)
                spot = target.at[spot] if columns is None else target.at[spot, columns]
                fetched.append(copies.start(source.at[pl.ds(begin, rows)], spot))
            if own is not None:
                fetched.append(copies.start(own, target.at[pl.ds(half, half)]))
            return fetched

        qkv_copies = []
        for index in range(3):
            qkv_copies += gathered(
                None if index else qkv_own, index * part, part, qkv_w_s,
                pl.ds(index * width, width),
            )
        memory_copy = copies.start(memory_in, memory_s)
        out_copies = gathered(out_own, 3 * part, part, out_w_s)
        out_copies.append(copies.start(near.at[pl.ds(6 * part, SMALL_ROWS)], gains_s))
        ffn_copies = [copies.start(in_w.at[0], in_w_s), copies.start(out2_w.at[0], out2_w_s)]
        grad_copy = copies.start(cotangent.at[begin], grad_s)
        slot_copies = gathered(slot_own, 4 * part, 2 * part, slot_w_s)
        kept = []
        first_copy.wait()
        gain, bias = wide_row(gains, 0), wide_row(biases, 0)

        def norm_step(spot):
            value = norm(residual_s[spot], gain, bias)
            wide_s[spot] = value
            first_s[spot] = value.astype(LOW)

        row_tiles(rows, ROW_TILE, norm_step)
        kept.append(copies.start(first_s, first_out))
        for copy in qkv_copies:
            copy.wait()
        query_s[...] = product(first_s[...], qkv_w_s[:, :width]).astype(LOW)
        memory_copy.wait()
        project(memory_s, qkv_w_s.at[:, width:], pair_s, width)
        key_ref, value_ref = pair_s.at[:, :width], pair_s.at[:, width:]
        count = src_len[example]
        attend(query_s, key_ref, value_ref, count, mixed_s, logsum_s)
        kept.append(copies.start(mixed_s, mixed_out))
        for copy in out_copies:
            copy.wait()
        came_row, own_row = gains_s[0:1, :].astype(WIDE), own_gains[0:1, :].astype(WIDE)
        half = width // 2
        cross_gain = jnp.concatenate([came_row[:, :half], own_row[:, :half]], axis=1)
        cross_bias = jnp.concatenate([came_row[:, half:], own_row[:, half:]], axis=1)

        def cross_step(spot):
            value = wide_s[spot] + product(mixed_s[spot], out_w_s[...])
            cross_s[spot] = value
            value = norm(value, cross_gain, cross_bias)
            wide_s[spot] = value
            low_s[spot] = value.astype(LOW)

        row_tiles(rows, HALF_TILE, cross_step)
        kept.append(copies.start(low_s, low_out))
        for copy in ffn_copies:
            copy.wait()
        feed_forward(
            low_s, wide_s, in_w_s, in_b, out2_w_s, out2_b, act_s, slope_s, second_s
        )
        kept.append(copies.start(act_s, act_out))
        gain_last, bias_last = wide_row(gains, 1), wide_row(biases, 1)

        def final_step(spot):
            final_s[spot] = norm(second_s[spot], gain_last, bias_last).astype(LOW)

        row_tiles(rows, ROW_TILE, final_step)
        kept.append(copies.start(final_s, final_out))
        grad_copy.wait()
        for copy in slot_copies:
            copy.wait()
        row = lax.broadcasted_iota(jnp.int32, (rows, width), 0)
        slots = tgt_len[example] - 1
        slot_grad = jnp.where(row < slots, grad_s[...].astype(WIDE), 0.0)
        grad_s[...] = slot_grad.astype(LOW)
        earlier = jnp.where(row == 0, 0.0, pltpu.roll(slot_grad, 1, 0))
        earlier_s[...] = earlier.astype(LOW)
        wide_grad_s[...] = product(final_s[...], slot_w_s[width:, :])
        value = product(final_s[...], slot_w_s[:width, :]) + pltpu.roll(
            wide_grad_s[...], rows - 1, 0
        )
        slot_s[...] = jnp.where(row < slots, value, 0.0).astype(LOW)
        kept.append(copies.start(slot_s, block_out.at[0, begin]))
        wide_grad_s[...] = product(grad_s[...], slot_w_s[:width, :], 1, 1) + product(
            earlier_s[...], slot_w_s[width:, :], 1, 1
        )
        norm_back_rows(
            second_s, gain_last, wide_grad_s, second_s, grad_low_s,
            small_out.at[6:7, :], small_out.at[8:9, :],
        )
        kept.append(copies.start(grad_low_s, grad_out))
        small_out[4:5, :] = column_sum(grad_low_s[...].astype(WIDE))
        feed_back(
            second_s, grad_low_s, slope_s, in_w_s, out2_w_s, hidden_s, small_out.at[0:4, :],
            back_s,
        )
        kept.append(copies.start(hidden_s, hidden_out))
        norm_back_rows(
            cross_s, cross_gain, back_s, rest_s, branch_s,
            small_out.at[9:10, :], small_out.at[10:11, :],
        )
        kept.append(copies.start(rest_s, rest_out))
        kept.append(copies.start(branch_s, branch_out))
        cross_grad_s[...] = product(branch_s[...], out_w_s[...], 1, 1).astype(LOW)
        attend_back(
            query_s, key_ref, value_ref, count, mixed_s, logsum_s, cross_grad_s,
            query_grad_s, pair_grad_s.at[:, :width], pair_grad_s.at[:, width:],
        )
        kept.append(copies.start(query_grad_s, query_out))
        kept.append(copies.start(pair_grad_s, pair_out))
        memory_grad_s[...] = product(pair_grad_s[...], qkv_w_s[:, width:], 1, 1).astype(LOW)
        kept.append(copies.start(memory_grad_s, memory_out))
        for copy in kept:
            copy.wait()


def back_kernel(
    example, src_len, gains, qkv_w, out_w, in_w, out2_w, memory_grad, second_in, slope_in,
    residual_in, qkv_in, logsum_in, mixed_in, grad_in, hidden_in, order_in, small_out, grad_out,
    hidden_out, branch_out, qkv_grad_out, rows_out, qkv_w_s, out_w_s, in_w_s, out2_w_s, memory_s,
    second_s, slope_s, wide_s, grad_low_s, hidden_s, back_s, residual_s, qkv_s, logsum_s, mixed_s,
    rest_s, branch_s, attn_grad_s, qkv_grad_s, semaphores,
):
    rows, width = residual_s.shape
    small_out[...] = jnp.zeros_like(small_out)

    @pl.when(lax.axis_index("pipe") == 0)
    def _():
        gain_first, gain_last = wide_row(gains, 0), wide_row(gains, 1)
        copies = Copies(semaphores)
        fetched = [
            copies.start(memory_grad, memory_s),
            copies.start(second_in, second_s),
            copies.start(slope_in, slope_s),
            copies.start(out2_w.at[0], out2_w_s),
            copies.start(in_w.at[0], in_w_s),
        ]
        residual_copy = copies.start(residual_in, residual_s)
        out_copy = copies.start(out_w.at[0], out_w_s)
        qkv_copies = [
            copies.start(qkv_in, qkv_s),
            copies.start(logsum_in, logsum_s),
            copies.start(mixed_in, mixed_s),
        ]
        qkv_w_copy = copies.start(qkv_w.at[0], qkv_w_s)
        fetched[0].wait()
        fetched[1].wait()
        row = lax.broadcasted_iota(jnp.int32, (rows, width), 0)
        wide_s[...] = jnp.where(
            row < src_len[example], memory_s[...].astype(WIDE), 0.0
        )
        norm_back_rows(
            second_s, gain_last, wide_s, second_s, grad_low_s,
            small_out.at[6:7, :], small_out.at[8:9, :],
        )
        kept = [copies.start(grad_low_s, grad_out)]
        small_out[4:5, :] = column_sum(grad_low_s[...].astype(WIDE))
        for copy in fetched[2:]:
            copy.wait()
        feed_back(
            second_s, grad_low_s, slope_s, in_w_s, out2_w_s, hidden_s, small_out.at[0:4, :],
            back_s,
        )
        kept.append(copies.start(hidden_s, hidden_out))
        residual_copy.wait()
        norm_back_rows(
            residual_s, gain_first, back_s, rest_s, branch_s,
            small_out.at[5:6, :], small_out.at[7:8, :],
        )
        kept.append(copies.start(branch_s, branch_out))
        out_copy.wait()
        attn_grad_s[...] = product(branch_s[...], out_w_s[...], 1, 1).astype(LOW)
        for copy in qkv_copies:
            copy.wait()
        attend_back(
            qkv_s.at[:, :width],
            qkv_s.at[:, width : 2 * width],
            qkv_s.at[:, 2 * width :],
            src_len[example],
            mixed_s,
            logsum_s,
            attn_grad_s,
            qkv_grad_s.at[:, :width],
            qkv_grad_s.at[:, width : 2 * width],
            qkv_grad_s.at[:, 2 * width :],
        )
        kept.append(copies.start(qkv_grad_s, qkv_grad_out))
        qkv_w_copy.wait()

        def rows_step(spot):
            back_s[spot] = rest_s[spot] + product(qkv_grad_s[spot], qkv_w_s[...], 1, 1)

        row_tiles(rows, HALF_TILE, rows_step)
        kept.append(copies.start(back_s, rows_out.at[0, pl.ds(example * rows, rows)]))
        for copy in kept:
            copy.wait()


MESH = pl.DeviceIdType.MESH


def ring_place(chip, chips):
    half = chip // 2
    return jnp.where(chip % 2 == 0, half, chips - 1 - half)


def ring_chip(place, chips):
    return jnp.where(place < chips // 2, 2 * place, 2 * (chips - 1 - place) + 1)


def part_rows(chunk_rows):
    count = 4 if chunk_rows >= 96 else 2 if chunk_rows == 64 else 1
    tiles = chunk_rows // 16
    parts = []
    begin = 0
    for index in range(count):
        rows = 16 * (tiles // count + (index < tiles % count))
        parts.append((begin, rows))
        begin += rows
    return tuple(parts)


def ring_layout(rows, devices):
    chips = devices // 2
    ways = 2 if rows >= 64 * chips else 1
    return ways, chips, -(-rows // (2 * ways * chips * 16)) * 16


def ring_rows(rows, devices):
    ways, chips, chunk_rows = ring_layout(rows, devices)
    return 2 * ways * chips * chunk_rows


class Links:
    def __init__(self, devices):
        self.pipe = lax.axis_index("pipe")
        self.me = lax.axis_index("dp")
        self.chips = devices // 2
        self.levels = devices.bit_length() - 1
        self.core = self.me % 2
        self.place = ring_place(self.me // 2, self.chips)
        self.sides = tuple(
            ring_chip((self.place + step) % self.chips, self.chips) * 2 + self.core
            for step in (1, self.chips - 1)
        )
        self.other = self.paired(1)
        self.across = (1 - self.pipe, self.me)

    def paired(self, bit):
        return self.me + bit - 2 * bit * ((self.me // bit) % 2)

    def greet(self):
        barrier = pltpu.get_barrier_semaphore()
        greeted = list(self.sides) + [self.paired(1 << level) for level in range(self.levels)]
        for friend in greeted:
            pl.semaphore_signal(
                barrier, inc=1, device_id=(self.pipe, friend), device_id_type=MESH
            )
        pl.semaphore_signal(barrier, inc=1, device_id=self.across, device_id_type=MESH)

    def greeted(self):
        pl.semaphore_wait(pltpu.get_barrier_semaphore(), self.levels + 3)

    def copy(self, source, target, send, recv, friend):
        return pltpu.make_async_remote_copy(
            src_ref=source,
            dst_ref=target,
            send_sem=send,
            recv_sem=recv,
            device_id=friend if isinstance(friend, tuple) else (self.pipe, friend),
            device_id_type=MESH,
        )


class Ring:
    def __init__(self, links, layout, total, refs):
        self.links = links
        ways, self.chips, self.chunk_rows = layout
        self.ways = range(ways)
        self.parts = part_rows(self.chunk_rows)
        self.all_parts = range(len(self.parts))
        self.total = total
        (
            self.mine, self.sibling, self.arrived, self.pair_send, self.pair_recv, self.ring_send,
            self.ring_recv, self.gather_send, self.gather_recv, self.share_send, self.share_recv,
        ) = refs

    def chunk_at(self, way, step):
        if way == 0:
            return lax.rem(self.links.place - step + 2 * self.chips, self.chips)
        return lax.rem(self.links.place + step + self.chips, self.chips)

    def start_row(self, core, way, chunk, part):
        begin = 0 if part is None else self.parts[part][0]
        return ((core * len(self.ways) + way) * self.chips + chunk) * self.chunk_rows + begin

    def mine_at(self, core, way, chunk, part=None):
        rows = self.chunk_rows if part is None else self.parts[part][1]
        return pl.ds(pl.multiple_of(self.start_row(core, way, chunk, part), 16), rows)

    def total_at(self, way, step, part):
        start = self.start_row(self.links.core, way, self.chunk_at(way, step), part)
        rows = self.parts[part][1]
        if len(self.total.shape) == 2:
            return self.total.at[pl.ds(pl.multiple_of(start, 16), rows)]
        size = self.total.shape[1]
        return self.total.at[
            lax.div(start, size), pl.ds(pl.multiple_of(lax.rem(start, size), 16), rows)
        ]

    def pair_copy(self, way, step, mine=None, sibling=None, send=None, recv=None):
        chunk = self.chunk_at(way, step)
        return self.links.copy(
            (self.mine if mine is None else mine).at[
                self.mine_at(1 - self.links.core, way, chunk)
            ],
            (self.sibling if sibling is None else sibling).at[way, chunk],
            (self.pair_send if send is None else send).at[way, step],
            (self.pair_recv if recv is None else recv).at[way, step],
            self.links.other,
        )

    def ring_copy(self, way, step, part):
        spot = pl.ds(*self.parts[part])
        return self.links.copy(
            self.arrived.at[way, step, spot],
            self.arrived.at[way, step + 1, spot],
            self.ring_send.at[way, step, part],
            self.ring_recv.at[way, step, part],
            self.links.sides[way],
        )

    def gather_copy(self, way, step, part):
        spot = self.total_at(way, step - 1, part)
        return self.links.copy(
            spot,
            spot,
            self.gather_send.at[way, step, part],
            self.gather_recv.at[way, step, part],
            self.links.sides[way],
        )

    def share_copy(self, way, step, part):
        spot = self.total_at(way, step - 1, part)
        return self.links.copy(
            spot,
            spot,
            self.share_send.at[way, step, part],
            self.share_recv.at[way, step, part],
            self.links.other,
        )

    def pairs_start(self):
        def start(step, carry):
            for way in self.ways:
                self.pair_copy(way, step).start()
            return carry

        lax.fori_loop(0, self.chips, start, 0)

    def pair_ready(self, way, step):
        self.pair_copy(way, step).wait_recv()

    def pairs_end(self):
        def end(step, carry):
            for way in self.ways:
                self.pair_copy(way, step).wait_send()
            return carry

        lax.fori_loop(0, self.chips, end, 0)

    def begin(self):
        self.pairs_start()
        for way in self.ways:
            self.pair_ready(way, 0)
            for part in range(len(self.parts)):
                spot = pl.ds(*self.parts[part])
                chunk = self.links.place
                own = self.mine[self.mine_at(self.links.core, way, chunk, part)]
                pair = self.sibling[way, chunk, spot]
                self.arrived[way, 0, spot] = (own.astype(WIDE) + pair.astype(WIDE)).astype(LOW)
                self.ring_copy(way, 0, part).start()

    def merged(self, way, step, part):
        spot = pl.ds(*self.parts[part])
        chunk = self.chunk_at(way, step + 1)
        self.ring_copy(way, step, part).wait_recv()
        own = self.mine[self.mine_at(self.links.core, way, chunk, part)]
        return (
            self.arrived[way, step + 1, spot].astype(WIDE)
            + own.astype(WIDE)
            + self.sibling[way, chunk, spot].astype(WIDE)
        ).astype(LOW)

    def reduce(self, step):
        for way in self.ways:
            self.pair_ready(way, step + 1)
        for part in range(len(self.parts)):
            spot = pl.ds(*self.parts[part])
            for way in self.ways:
                self.arrived[way, step + 1, spot] = self.merged(way, step, part)
                self.ring_copy(way, step + 1, part).start()

    def settle(self, parts=None):
        last = self.chips - 2
        for way in self.ways:
            self.pair_ready(way, last + 1)
        for part in self.all_parts:
            for way in self.ways:
                self.total_at(way, -1, part)[...] = self.merged(way, last, part)
                if parts is None or part in parts:
                    self.gather_copy(way, 0, part).start()
                    self.share_copy(way, 0, part).start()

    def gather_begin(self, parts):
        for part in parts:
            for way in self.ways:
                self.gather_copy(way, 0, part).start()
                self.share_copy(way, 0, part).start()

    def gather(self, step, parts=None):
        for part in self.all_parts if parts is None else parts:
            for way in self.ways:
                self.gather_copy(way, step, part).wait_recv()
                self.gather_copy(way, step + 1, part).start()
                self.share_copy(way, step + 1, part).start()

    def gather_last(self, parts=None):
        last = self.chips - 2
        for part in self.all_parts if parts is None else parts:
            for way in self.ways:
                self.gather_copy(way, last, part).wait_recv()
                self.share_copy(way, last + 1, part).start()

    def finish(self):
        self.pairs_end()

        def shares(step, carry):
            for way in self.ways:
                for part in range(len(self.parts)):
                    self.share_copy(way, step, part).wait()
            return carry

        lax.fori_loop(0, self.chips, shares, 0)

        def sends(step, carry):
            for way in self.ways:
                for part in range(len(self.parts)):
                    self.ring_copy(way, step, part).wait_send()
                    self.gather_copy(way, step, part).wait_send()
            return carry

        lax.fori_loop(0, self.chips - 1, sends, 0)


class CrossRing(Ring):
    def __init__(self, links, layout, total, refs, foreign_refs):
        super().__init__(links, layout, total, refs)
        self.foreign, self.foreign_sibling = foreign_refs[:2]
        self.foreign_send, self.foreign_recv, self.cross_send, self.cross_recv = foreign_refs[2:]

    def foreign_pair(self, way, step):
        return self.pair_copy(
            way, step, self.foreign, self.foreign_sibling, self.foreign_send, self.foreign_recv
        )

    def cross_copy(self, way, step):
        spot = self.mine_at(self.links.core, way, self.chunk_at(way, step))
        return self.links.copy(
            self.foreign.at[spot],
            self.mine.at[spot],
            self.cross_send.at[way, step],
            self.cross_recv.at[way, step],
            self.links.across,
        )

    def each(self, body):
        def step_all(step, carry):
            for way in self.ways:
                body(way, step)
            return carry

        lax.fori_loop(0, self.chips, step_all, 0)

    def foreign_start(self):
        self.each(lambda way, step: self.foreign_pair(way, step).start())

    def foreign_pass(self):
        def hand_over(way, step):
            chunk = self.chunk_at(way, step)
            spot = self.mine_at(self.links.core, way, chunk)
            self.foreign_pair(way, step).wait_recv()
            self.foreign[spot] = (
                self.foreign[spot].astype(WIDE) + self.foreign_sibling[way, chunk].astype(WIDE)
            ).astype(LOW)
            self.cross_copy(way, step).start()

        self.each(hand_over)

    def pairs_start(self):
        pl.when(self.links.pipe == 1)(super().pairs_start)

        @pl.when(self.links.pipe == 0)
        def _():
            self.sibling[...] = jnp.zeros_like(self.sibling)

    def pair_ready(self, way, step):
        @pl.when(self.links.pipe == 1)
        def _():
            self.pair_copy(way, step).wait_recv()

        @pl.when(self.links.pipe == 0)
        def _():
            self.cross_copy(way, step).wait_recv()

    def pairs_end(self):
        @pl.when(self.links.pipe == 1)
        def _():
            self.each(lambda way, step: self.pair_copy(way, step).wait_send())
            self.each(lambda way, step: self.foreign_pair(way, step).wait_send())
            self.each(lambda way, step: self.cross_copy(way, step).wait_send())


def ring_scratch(rows, width, devices):
    ways, chips, chunk_rows = ring_layout(rows, devices)
    pieces = len(part_rows(chunk_rows))
    dma = pltpu.SemaphoreType.DMA
    return [
        pltpu.VMEM((2 * ways * chips * chunk_rows, width), LOW),
        pltpu.VMEM((ways, chips, chunk_rows, width), LOW),
        pltpu.VMEM((ways, chips, chunk_rows, width), LOW),
        dma((ways, chips)),
        dma((ways, chips)),
    ] + [dma((ways, chips, pieces)) for _ in range(6)]


def foreign_scratch(rows, width, devices):
    ways, chips, chunk_rows = ring_layout(rows, devices)
    dma = pltpu.SemaphoreType.DMA
    return [
        pltpu.VMEM((2 * ways * chips * chunk_rows, width), LOW),
        pltpu.VMEM((ways, chips, chunk_rows, width), LOW),
    ] + [dma((ways, chips)) for _ in range(4)]


def last_kernel(
    devices, src_len, tgt_len, gains, small_a, small_b, small_c, inputs, qkv_w,
    out_w, in_w, out2_w, near, far, query_own, memory_grad, second_in, slope_in, query_grad_a,
    query_grad_b, rest_a, rest_b, residual_a, residual_b, qkv_a, qkv_b, logsum_a, logsum_b, mixed_a, mixed_b, low_a, low_b, act_a, act_b, grad_a,
    grad_b, hidden_a, hidden_b, branch_a, qkv_grad_a, own_extra, sent_extra, first_total,
    second_total, cross_total, small_total, rows_out, qkv_w_s, out_w_s, in_w_s, out2_w_s, low_s, hidden_s, act_s,
    grad_s, mixed_s, branch_s, x_s, qkv_grad_s, memory_s, second_s, slope_s, back_s, query_w_s, residual_s, qkv_s, logsum_s, rest_s, attn_grad_s, small_s, small_arrived,
    cross_total_s, small_send, small_recv, small_cross_sem, semaphores, *ring_refs,
):
    links = Links(devices)
    links.greet()
    chips, levels = links.chips, links.levels
    section, core = links.pipe, links.core
    rows, width = residual_s.shape
    half = width // 2
    hidden = hidden_s.shape[1]
    hidden_blocks = hidden // width
    extra_rows = own_extra.shape[0]
    sizes = (2 * hidden, 4 * width, extra_rows)
    layouts = [ring_layout(size, devices) for size in sizes]
    early = Ring(links, layouts[0], act_s, ring_refs[:11])
    late = Ring(links, layouts[1], out2_w_s, ring_refs[11:22])
    cross = CrossRing(links, layouts[2], cross_total_s, ring_refs[22:33], ring_refs[33:])
    front, rear = pl.ds(0, rows), pl.ds(rows, rows)
    gain_first, gain_last = wide_row(gains, 0), wide_row(gains, 1)
    small_s[0] = small_a[...] + small_b[...] + small_c[...]
    partial = small_arrived.at[0]
    partial[...] = jnp.zeros_like(small_a)

    encoder = section == 0
    copies = Copies(semaphores)

    def declared(source, target):
        copy = pltpu.make_async_copy(source, target, semaphores.at[copies.count])
        copies.count += 1
        return copy

    def start(*group):
        for copy in group:
            copy.start()

    def wait(*group):
        for copy in group:
            copy.wait()

    hidden_front = [declared(low_a, low_s.at[front]), declared(low_b, low_s.at[rear]),
                    declared(hidden_a, hidden_s.at[front])]
    act_front = [declared(grad_a, grad_s.at[front])]
    for index in range(hidden_blocks):
        columns = pl.ds(index * width, width)
        act_front.append(declared(act_a.at[:, columns], act_s.at[index, front]))
        act_front.append(declared(act_b.at[:, columns], act_s.at[index, rear]))
    hidden_rear = declared(hidden_b, hidden_s.at[rear])
    grad_rear = declared(grad_b, grad_s.at[rear])
    back_inputs = [declared(memory_grad, memory_s), declared(second_in, second_s),
                   declared(slope_in, slope_s), declared(out2_w.at[0], out2_w_s),
                   declared(in_w.at[0], in_w_s)]
    part = query_own.shape[0] // 2
    near_at = pl.ds(pl.multiple_of(core * part, part), part)
    far_at = pl.ds(pl.multiple_of((1 - core) * part, part), part)
    query_weights = [
        declared(near.at[pl.ds(0, part)], query_w_s.at[near_at]),
        declared(far.at[pl.ds(0, part)], query_w_s.at[far_at]),
        declared(query_own.at[:, :width], query_w_s.at[pl.ds(2 * part, 2 * part)]),
    ]
    out_w_copy = declared(out_w.at[0], out_w_s)
    qkv_w_copy = declared(qkv_w.at[0], qkv_w_s)
    mixed_copies = [declared(mixed_a, mixed_s.at[front]), declared(mixed_b, mixed_s.at[rear])]
    saved = []
    base = copies.count
    for parts in ((residual_a, query_grad_a, rest_a, qkv_a, logsum_a),
                  (residual_b, query_grad_b, rest_b, qkv_b, logsum_b)):
        copies.count = base
        targets = (residual_s, memory_s, second_s, qkv_s, logsum_s)
        saved.append([declared(source, target) for source, target in zip(parts, targets)])
    encoder_inputs = [declared(branch_a, branch_s.at[front]),
                      declared(qkv_grad_a, qkv_grad_s.at[front])]
    inputs_copy = declared(inputs.at[0], x_s)
    extra_loads = [declared(own_extra, cross.mine.at[pl.ds(0, extra_rows)]),
                   declared(sent_extra, cross.foreign.at[pl.ds(0, extra_rows)])]
    if cross.mine.shape[0] > extra_rows:
        cross.mine[extra_rows:] = jnp.zeros_like(cross.mine[extra_rows:])
        cross.foreign[extra_rows:] = jnp.zeros_like(cross.foreign[extra_rows:])

    def rows_copy(example):
        spot = pl.ds(pl.multiple_of(example * rows, rows), rows)
        return pltpu.make_async_copy(rest_s, rows_out.at[spot], semaphores.at[copies.count])

    @pl.when(encoder)
    def _():
        start(*back_inputs, *hidden_front, *act_front, out_w_copy, qkv_w_copy, *mixed_copies,
              *encoder_inputs, inputs_copy)
        wait(*back_inputs[:2])
        row = lax.broadcasted_iota(jnp.int32, (rows, width), 0)
        rest_s[...] = jnp.where(row < src_len[1], memory_s[...].astype(WIDE), 0.0)
        norm_back_rows(
            second_s, gain_last, rest_s, second_s, grad_s.at[rear],
            partial.at[6:7, :], partial.at[8:9, :],
        )
        partial[4:5, :] = column_sum(grad_s[rear].astype(WIDE))
        wait(*back_inputs[2:])
        feed_back(
            second_s, grad_s.at[rear], slope_s, in_w_s, out2_w_s, hidden_s.at[rear],
            partial.at[0:4, :], back_s,
        )
        start(saved[1][0], *saved[1][3:])

    @pl.when(section == 1)
    def _():
        start(*hidden_front, hidden_rear, *act_front, grad_rear, *saved[0], *query_weights,
              out_w_copy, qkv_w_copy, *mixed_copies, *extra_loads, inputs_copy)
        wait(hidden_rear, grad_rear)

    def blocks(target, begin, count, block):
        def step(index, carry):
            target[columns_of(begin + index, width), :] = block(index).astype(LOW)
            return carry

        lax.fori_loop(0, count, step, 0)

    wait(*hidden_front)
    blocks(
        early.mine, 0, hidden_blocks,
        lambda index: product(low_s[...], hidden_s[:, columns_of(index, width)], 0, 0),
    )
    wait(*act_front)
    blocks(
        early.mine, hidden_blocks, hidden_blocks,
        lambda index: product(act_s[index], grad_s[...], 0, 0),
    )
    links.greeted()
    small_cross = links.copy(
        small_s.at[levels], small_arrived.at[1], small_cross_sem.at[0], small_cross_sem.at[1],
        links.across,
    )

    @pl.when(section == 1)
    def _():
        small_s[levels, 0:1, :] = jnp.concatenate(
            [small_s[0, 9:10, :half], small_s[0, 10:11, :half]], axis=1
        )
        small_cross.start()
        wait(*extra_loads)
        cross.foreign_start()

    early.begin()

    @pl.when(section == 1)
    def _():
        cross.foreign_pass()

    cross.begin()
    per_example = 4
    begin_at = jnp.where(encoder, 1, 0)
    ahead, behind = early.all_parts[::2], early.all_parts[1::2]

    @pl.when(section == 1)
    def _():
        wait(*query_weights)

    wait(out_w_copy, qkv_w_copy, *mixed_copies)

    def advance(turn):
        @pl.when(turn < chips - 2)
        def _():
            early.reduce(turn)
            cross.reduce(turn)

        @pl.when(turn == chips - 2)
        def _():
            early.settle(ahead)
            cross.settle()

        @pl.when((turn > chips - 2) & (turn < 2 * chips - 3))
        def _():
            early.gather(turn - (chips - 1), ahead)
            cross.gather(turn - (chips - 1))

        @pl.when(turn == 2 * chips - 3)
        def _():
            early.gather_last(ahead)
            cross.gather_last()

    def back_step(example, carry):
        spot = pl.ds(pl.multiple_of(example * rows, rows), rows)
        turn = (example - begin_at) * per_example

        @pl.when(section == 1)
        def _():
            wait(*saved[0][:3])

            def first_step(tile):
                back_s[tile] = second_s[tile] + product(memory_s[tile], query_w_s[...], 1, 1)

            row_tiles(rows, HALF_TILE, first_step)

        @pl.when(encoder)
        def _():
            wait(saved[0][0])

        @pl.when((section == 1) & (example == 1))
        def _():
            rows_copy(0).wait()

        low_branch = branch_s.at[spot]
        norm_back_rows(
            residual_s, gain_first, back_s, rest_s, low_branch,
            partial.at[12:13, :], partial.at[13:14, :],
        )
        partial[5:6, :] += partial[12:13, :]
        partial[7:8, :] += partial[13:14, :]
        attn_grad_s[...] = product(low_branch[...], out_w_s[...], 1, 1).astype(LOW)
        wait(*saved[0][3:])
        advance(turn)
        count = jnp.where(encoder, src_len[example], tgt_len[example])
        attend_back(
            qkv_s.at[:, :width],
            qkv_s.at[:, width : 2 * width],
            qkv_s.at[:, 2 * width :],
            count,
            mixed_s.at[spot],
            logsum_s,
            attn_grad_s,
            qkv_grad_s.at[spot, pl.ds(0, width)],
            qkv_grad_s.at[spot, pl.ds(width, width)],
            qkv_grad_s.at[spot, pl.ds(2 * width, width)],
            after=lambda pair: pl.when(lax.rem(pair, 2) == 1)(
                lambda: advance(turn + 1 + lax.div(pair, 2))
            ),
        )

        @pl.when(example == 0)
        def _():
            start(*saved[1])

        def rows_step(index, inner):
            tile = pl.ds(pl.multiple_of(index * HALF_TILE, HALF_TILE), HALF_TILE)
            begin = pl.multiple_of(example * rows + index * HALF_TILE, HALF_TILE)
            rest_s[tile] += product(qkv_grad_s[pl.ds(begin, HALF_TILE)], qkv_w_s[...], 1, 1)
            return inner

        lax.fori_loop(0, rows // HALF_TILE, rows_step, 0)
        rows_copy(example).start()
        advance(turn + 3)
        return carry

    lax.fori_loop(begin_at, 2, back_step, 0)
    wait(inputs_copy)

    @pl.when(encoder)
    def _():
        wait(*encoder_inputs)

    blocks(
        late.mine, 0, 3,
        lambda index: product(x_s[...], qkv_grad_s[:, columns_of(index, width)], 0, 0),
    )
    done = (2 - begin_at) * per_example
    advance(done)
    blocks(late.mine, 3, 1, lambda index: product(mixed_s[...], branch_s[...], 0, 0))

    if late.mine.shape[0] > 4 * width:
        late.mine[4 * width :] = jnp.zeros_like(late.mine[4 * width :])
    late.begin()
    advance(done + 1)
    done = done + 2

    small_s[0] = small_s[0] + partial[...]
    @pl.when(section == 1)
    def _():
        small_s[0, 9:10, :] = jnp.concatenate(
            [small_s[0, 9:10, half:], small_s[0, 10:11, half:]], axis=1
        )
        small_cross.wait_send()

    @pl.when(encoder)
    def _():
        small_cross.wait_recv()
        small_s[0, 9:10, :] = small_arrived[1, 0:1, :]

    def small_copy(level, bit):
        return links.copy(
            small_s.at[level],
            small_arrived.at[level + 2],
            small_send.at[level],
            small_recv.at[level],
            links.paired(bit),
        )

    small_copy(0, 1).start()

    def early_step(turn, carry):
        advance(turn)
        return carry

    lax.fori_loop(done, chips - 1, early_step, 0)
    done = jnp.maximum(done, chips - 1)

    def merge_small(level, bit):
        small_copy(level, bit).wait_recv()
        merged = small_s[level] + small_arrived[level + 2]

        @pl.when(level + 1 < levels)
        def _():
            small_s[level + 1] = merged
            small_copy(level + 1, 2 * bit).start()

        @pl.when(level + 1 == levels)
        def _():
            small_total[...] = merged

    def both_step(step, bit):
        late.reduce(step)
        advance(done + step)

        @pl.when(step < levels)
        def _():
            merge_small(step, bit)

        return 2 * bit

    lax.fori_loop(0, chips - 2, both_step, 1)
    late.settle()
    lax.fori_loop(done + chips - 2, 2 * chips - 2, early_step, 0)
    early.gather_begin(behind)
    cross.finish()
    def late_step(step, carry):
        late.gather(step)
        early.gather(step, behind)
        return carry

    lax.fori_loop(0, chips - 2, late_step, 0)
    late.gather_last()
    early.gather_last(behind)
    late.finish()
    kept = [
        pltpu.make_async_copy(
            out2_w_s.at[pl.ds(0, second_total.shape[0])], second_total, semaphores.at[0]
        ),
        pltpu.make_async_copy(cross_total_s, cross_total, semaphores.at[1]),
    ]
    for index in range(hidden_blocks):
        kept.append(
            pltpu.make_async_copy(
                act_s.at[index], first_total.at[pl.ds(index * 2 * rows, 2 * rows)],
                semaphores.at[2 + index],
            )
        )
    start(*kept[:2])
    early.finish()
    start(*kept[2:])
    wait(*kept)
    for level in range(levels):
        small_copy(level, 1 << level).wait_send()
    rows_copy(1).wait()


def result_kernel(
    small_total, first_total, second_total, cross_total, rows_in, rows_buffer, rows_out, qkv_out, out_out,
    in_out, out2_out, cross_qkv_out, cross_out_out, slot_out, in_b_out, out2_b_out, gain_out,
    bias_out, cross_gain_out, cross_bias_out, first_s, second_s, rows_s, wide_s, semaphores,
):
    width = first_s.shape[1]
    half = width // 2
    for index in range(in_b_out.shape[1] // width):
        in_b_out[:, index * width : (index + 1) * width] = small_total[index : index + 1, :]
    out2_b_out[...] = small_total[4:5, :]
    gain_out[0] = small_total[5:7, :]
    bias_out[0] = small_total[7:9, :]
    cross_gain_out[...] = small_total[9:10, :half]
    cross_bias_out[...] = small_total[9:10, half:]
    copies = Copies(semaphores)
    rows_copy = copies.start(rows_in, rows_s)
    rows = rows_in.shape[0] // 2
    kept = []
    loads = {width: [], half: []}
    second_rows = 4 * width
    for index in range(first_s.shape[0] // width):
        spot = pl.ds(index * width, width)
        loads[width].append(copies.start(first_total.at[spot], first_s.at[spot]))
    for index in range(second_s.shape[0] // half):
        begin = index * half
        if begin < second_rows:
            source = second_total.at[pl.ds(begin, half)]
        else:
            source = cross_total.at[pl.ds(begin - second_rows, half)]
        loads[half].append(copies.start(source, second_s.at[pl.ds(begin, half)]))
    targets = []
    for index in range(first_s.shape[0] // width):
        hidden_blocks = in_out.shape[2] // width
        if index < hidden_blocks:
            target = in_out.at[0, :, pl.ds(index * width, width)]
        else:
            target = out2_out.at[0, pl.ds((index - hidden_blocks) * width, width)]
        targets.append((loads[width][index : index + 1], first_s, index * width, width, target))
    for index in range(4):
        if index < 3:
            target = qkv_out.at[0, :, pl.ds(index * width, width)]
        else:
            target = out_out.at[0]
        targets.append(
            (loads[half][2 * index : 2 * index + 2], second_s, index * width, width, target)
        )
    for index in range(4):
        if index < 3:
            target = cross_qkv_out.at[:, pl.ds(index * width, width)]
        else:
            target = cross_out_out
        targets.append(
            (loads[half][8 + index : 9 + index], second_s, 4 * width + index * half, half, target)
        )
    targets.append((loads[half][12:14], second_s, 6 * width, width, slot_out))
    place = 0
    for waits, stage, begin, size, target in targets:
        for copy in waits:
            copy.wait()
        wide_s[place : place + size] = stage[begin : begin + size].astype(WIDE)
        kept.append(copies.start(wide_s.at[pl.ds(place, size)], target))
        place += size
    rows_copy.wait()
    kept.append(
        copies.start(rows_s.at[pl.ds(rows, rows)], rows_out.at[0, pl.ds(rows, rows)])
    )

    @pl.when(lax.axis_index("pipe") == 1)
    def _():
        front = pl.ds(0, rows)
        more = Copies(semaphores)
        more.count = copies.count
        more.start(rows_s.at[front], rows_out.at[0, front]).wait()

    for copy in kept:
        copy.wait()


def cross_weight_kernel(
    tgt_len, first_a, first_b, query_a, query_b, memory_a, memory_b, pair_a, pair_b, mixed_a,
    mixed_b, branch_a, branch_b, final_a, final_b, cotangent, own_out, sent_out, first_s, query_s,
    memory_s, pair_s, mixed_s, branch_s, final_s, grad_s, earlier_s, own_s, sent_s, semaphores,
):
    section = lax.axis_index("pipe")

    @pl.when(section == 1)
    def _():
        copies = Copies(semaphores)

        def both(first, second, target):
            rows = first.shape[0]
            return [
                copies.start(first, target.at[pl.ds(0, rows)]),
                copies.start(second, target.at[pl.ds(rows, rows)]),
            ]

        grad_copy = copies.start(cotangent, grad_s)
        final_copies = both(final_a, final_b, final_s)
        mixed_copies = both(mixed_a, mixed_b, mixed_s) + both(branch_a, branch_b, branch_s)
        pair_copies = both(memory_a, memory_b, memory_s) + both(pair_a, pair_b, pair_s)
        query_copies = both(first_a, first_b, first_s) + both(query_a, query_b, query_s)
        total, width = grad_s.shape
        rows = total // 2
        half = width // 2
        grad_copy.wait()
        row = lax.broadcasted_iota(jnp.int32, (rows, width), 0)
        for example in range(2):
            spot = slice(example * rows, (example + 1) * rows)
            slot_grad = jnp.where(
                row < tgt_len[example] - 1, grad_s[spot].astype(WIDE), 0.0
            )
            grad_s[spot] = slot_grad.astype(LOW)
            earlier = jnp.where(row == 0, 0.0, pltpu.roll(slot_grad, 1, 0))
            earlier_s[spot] = earlier.astype(LOW)
        for copy in final_copies:
            copy.wait()
        sent_s[4 * half :] = product(final_s[...], grad_s[...], 0, 0).astype(LOW)
        own_s[4 * half :] = product(final_s[...], earlier_s[...], 0, 0).astype(LOW)

        def keep(place, value):
            spot = slice(place * half, (place + 1) * half)
            sent_s[spot] = value[:half].astype(LOW)
            own_s[spot] = value[half:].astype(LOW)

        for copy in mixed_copies:
            copy.wait()
        keep(3, product(mixed_s[...], branch_s[...], 0, 0))
        for copy in pair_copies:
            copy.wait()
        keep(1, product(memory_s[...], pair_s[:, :width], 0, 0))
        keep(2, product(memory_s[...], pair_s[:, width:], 0, 0))
        for copy in query_copies:
            copy.wait()
        keep(0, product(first_s[...], query_s[...], 0, 0))
        kept = [copies.start(own_s, own_out), copies.start(sent_s, sent_out)]
        for copy in kept:
            copy.wait()


ANY = pl.BlockSpec(memory_space=pl.ANY)
INNER = pl.BlockSpec(memory_space=pltpu.VMEM)
SCALAR = pl.BlockSpec(memory_space=pltpu.SMEM)


def local_call(
    body, name, scalars, inner, outer, outputs, scratch, flops, aliases=None, count=32,
    semaphores=(), **compiler,
):
    shapes = [jax.ShapeDtypeStruct(shape, kind) for shape, kind, _ in outputs]
    inputs = list(scalars) + list(inner) + list(outer)
    specs = [SCALAR] * len(scalars) + [INNER] * len(inner) + [ANY] * len(outer)
    moved = sum(value.size * value.dtype.itemsize for value in inputs)
    return pl.pallas_call(
        body,
        out_shape=shapes,
        in_specs=specs,
        out_specs=[INNER if kept else ANY for _, _, kept in outputs],
        scratch_shapes=[pltpu.VMEM(shape, kind) for shape, kind in scratch]
        + list(semaphores or [pltpu.SemaphoreType.DMA((count,))]),
        input_output_aliases=aliases or {},
        compiler_params=pltpu.CompilerParams(vmem_limit_bytes=VMEM_LIMIT, **compiler),
        cost_estimate=pl.CostEstimate(flops=flops, bytes_accessed=moved, transcendentals=0),
        name=name,
    )(*inputs)


def local(
    inputs, src_len, tgt_len, cotangent, qkv_w, out_w, in_w, in_b, out2_w, out2_b, norm_gain,
    norm_bias, cross_qkv, cross_out, slot_w, cross_gain, cross_bias,
):
    core = lax.axis_index("dp") % 2
    devices = lax.axis_size("dp")
    blocks = src_len.shape[0]
    total_rows, width = inputs.shape[1:]
    rows = total_rows // blocks
    half = width // 2
    hidden = in_w.shape[2]
    square, wide3, deep = (rows, width), (rows, 3 * width), (rows, hidden)
    weight_square, logsum = (width, width), (rows, PAIR)
    tall, tall3, tall_deep = (total_rows, width), (total_rows, 3 * width), (total_rows, hidden)

    part = half // 2
    own_gains = jnp.concatenate([cross_gain, cross_bias]).reshape(1, width)
    pieces = [
        lax.dynamic_slice(cross_qkv, (core * part, column * width), (part, width))
        for column in range(3)
    ]
    pieces.append(lax.dynamic_slice_in_dim(cross_out, core * part, part, axis=0))
    pieces.append(lax.dynamic_slice_in_dim(slot_w, 2 * core * part, 2 * part, axis=0))
    pieces.append(jnp.pad(own_gains, ((0, SMALL_ROWS - 1), (0, 0))))
    near = lax.ppermute(jnp.concatenate(pieces, axis=0), "pipe", [(0, 1)])
    started = []
    for example in range(blocks):
        scratch = [
            (square, LOW), ((width, 3 * width), LOW), (weight_square, LOW), ((width, hidden), LOW),
            ((hidden, width), LOW), (wide3, LOW), (logsum, WIDE), (square, LOW),
            (square, WIDE), (square, WIDE), (square, LOW), (deep, LOW), (deep, LOW), (square, WIDE),
            (square, LOW),
        ]
        outputs = [
            (wide3, LOW, False), (logsum, WIDE, False), (square, LOW, False),
            (square, WIDE, False), (square, LOW, False), (deep, LOW, False), (deep, LOW, False),
            (square, WIDE, False), (square, LOW, False), ((1,) + tall, LOW, False),
        ]
        outer = [inputs, qkv_w, out_w, in_w, out2_w]
        if example:
            outer.append(started[-1][9])
        started.append(
            local_call(
                functools.partial(self_kernel, example), f"self_rows_{example}",
                [src_len, tgt_len], [in_b, out2_b, norm_gain, norm_bias], outer, outputs, scratch,
                6 * 10**9, aliases={11: 9} if example else None,
            )
        )
    near, _ = lax.optimization_barrier((near, started[0][8]))
    far = lax.ppermute(near, "dp", [(place, place ^ 1) for place in range(devices)])
    sent_memory = [lax.ppermute(values[8], "pipe", [(0, 1)]) for values in started]

    crossed = []
    block_out = started[-1][9]
    for example in range(blocks):
        values = started[example]
        scratch = [
            (square, WIDE), (square, LOW), (square, LOW), ((width, hidden), LOW),
            ((hidden, width), LOW), ((width, 3 * width), LOW), (weight_square, LOW),
            ((2 * width, width), LOW), (square, WIDE), (square, LOW), (square, LOW),
            ((rows, 2 * width), LOW), (square, LOW), (logsum, WIDE), (square, WIDE),
            (square, LOW), (deep, LOW), (deep, LOW), (square, WIDE), (square, LOW), (square, LOW),
            (square, LOW), (square, WIDE), (square, LOW), (deep, LOW), (square, WIDE),
            (square, WIDE), (square, LOW), (square, LOW), (square, LOW), ((rows, 2 * width), LOW),
            (square, LOW), ((SMALL_ROWS, width), LOW),
        ]
        outputs = [
            ((SMALL_ROWS, width), WIDE, True), (square, LOW, False), (deep, LOW, False),
            ((1,) + tall, LOW, False), (square, LOW, False), (square, LOW, False),
            (deep, LOW, False), (square, LOW, False), (square, LOW, False), (square, LOW, False),
            (square, LOW, False), ((rows, 2 * width), LOW, False), (square, LOW, False),
            (square, WIDE, False),
        ]
        outer = [
            values[3], sent_memory[example], cotangent, in_w, out2_w, cross_qkv, cross_out, slot_w,
            near, far, values[4], values[5], block_out,
        ]
        inner = [in_b, out2_b, norm_gain, norm_bias, own_gains]
        shift = 2 + len(inner)
        crossed.append(
            local_call(
                functools.partial(cross_kernel, example), f"cross_rows_{example}",
                [src_len, tgt_len], inner, outer, outputs, scratch, 20 * 10**9,
                aliases={shift + 10: 1, shift + 11: 2, shift + 12: 3}, count=48,
            )
        )
        block_out = crossed[-1][3]
    back_memory = [lax.ppermute(values[12], "pipe", [(1, 0)]) for values in crossed]

    def pairs_of(group, place):
        return [values[place] for values in group]

    extra_rows = 3 * width
    own_extra, sent_extra = local_call(
        cross_weight_kernel, "cross_weights", [tgt_len], [],
        pairs_of(crossed, 7) + pairs_of(crossed, 10) + sent_memory + pairs_of(crossed, 11)
        + pairs_of(crossed, 8) + pairs_of(crossed, 9) + pairs_of(crossed, 4) + [cotangent],
        [((extra_rows, width), LOW, False), ((extra_rows, width), LOW, False)],
        [
            (tall, LOW), (tall, LOW), (tall, LOW), ((total_rows, 2 * width), LOW), (tall, LOW),
            (tall, LOW), (tall, LOW), (tall, LOW), (tall, LOW), ((extra_rows, width), LOW),
            ((extra_rows, width), LOW),
        ],
        5 * 10**9,
    )
    values, after = started[0], crossed[0]
    scratch = [
        ((width, 3 * width), LOW), (weight_square, LOW), ((width, hidden), LOW),
        ((hidden, width), LOW), (square, LOW), (square, WIDE), (deep, LOW), (square, WIDE),
        (square, LOW), (deep, LOW), (square, WIDE), (square, WIDE), (wide3, LOW), (logsum, WIDE),
        (square, LOW), (square, WIDE), (square, LOW), (square, LOW), (wide3, LOW),
    ]
    outputs = [
        ((SMALL_ROWS, width), WIDE, True), (square, LOW, False), (deep, LOW, False),
        (square, LOW, False), (wide3, LOW, False), ((1,) + tall, WIDE, False),
    ]
    outer = [
        qkv_w, out_w, in_w, out2_w, back_memory[0], values[7], values[6], values[3], values[0],
        values[1], values[2], after[5], after[6], own_extra,
    ]
    back = local_call(
        functools.partial(back_kernel, 0), "back_rows_0", [src_len], [norm_gain], outer,
        outputs, scratch, 14 * 10**9, aliases={2 + 11: 1, 2 + 12: 2},
    )

    values, after = started[1], crossed[1]
    sizes = (2 * hidden, 4 * width, extra_rows)
    padded = [ring_rows(size, devices) for size in sizes]
    levels = devices.bit_length() - 1
    small_shape = (SMALL_ROWS, width)
    dma = pltpu.SemaphoreType.DMA
    rings = [part for size in sizes for part in ring_scratch(size, width, devices)]
    rings += foreign_scratch(extra_rows, width, devices)
    first_total, second_total, cross_total, small_total, last_rows = local_call(
        functools.partial(last_kernel, devices), "last_rows", [src_len, tgt_len],
        [norm_gain, crossed[0][0], crossed[1][0], back[0]],
        [
            inputs, qkv_w, out_w, in_w, out2_w, near, far, cross_qkv, back_memory[1], values[7],
            values[6], crossed[0][10], after[10], crossed[0][13], after[13], started[0][3],
            values[3], started[0][0], values[0], started[0][1], values[1], started[0][2],
            values[2], crossed[0][1], after[1], crossed[0][2], after[2], back[1], after[5],
            back[2], after[6], back[3], back[4], own_extra, sent_extra,
        ],
        [
            ((padded[0], width), LOW, False),
            ((padded[1], width), LOW, False),
            ((padded[2], width), LOW, False),
            (small_shape, WIDE, True),
            (tall, WIDE, False),
        ],
        [
            ((width, 3 * width), LOW), (weight_square, LOW), ((width, hidden), LOW),
            ((hidden, width), LOW), (tall, LOW), (tall_deep, LOW),
            ((hidden // width,) + tall, LOW), (tall, LOW), (tall, LOW), (tall, LOW), (tall, LOW),
            (tall3, LOW), (square, LOW), (square, WIDE), (deep, LOW), (square, WIDE),
            (weight_square, LOW), (square, WIDE), (wide3, LOW), (logsum, WIDE), (square, WIDE),
            (square, LOW), ((levels + 1,) + small_shape, WIDE), ((levels + 2,) + small_shape, WIDE),
            ((padded[2], width), LOW),
        ],
        20 * 10**9,
        semaphores=[dma((levels,)), dma((levels,)), dma((2,)), dma((64,))] + rings,
        collective_id=0, has_side_effects=True,
    )

    results = local_call(
        result_kernel, "results", [], [small_total],
        [
            first_total, second_total, cross_total, last_rows, back[5],
        ],
        [
            ((1,) + tall, WIDE, False), ((1, width, 3 * width), WIDE, False),
            ((1,) + weight_square, WIDE, False), ((1, width, hidden), WIDE, False),
            ((1, hidden, width), WIDE, False), ((half, 3 * width), WIDE, False),
            ((half, width), WIDE, False), ((width, width), WIDE, False),
            ((1, hidden), WIDE, True), ((1, width), WIDE, True), ((1, 2, width), WIDE, True),
            ((1, 2, width), WIDE, True), ((1, half), WIDE, True), ((1, half), WIDE, True),
        ],
        [
            ((sizes[0], width), LOW), ((sizes[1] + sizes[2], width), LOW), (tall, WIDE),
            ((sum(sizes), width), WIDE),
        ],
        10**9, aliases={5: 0}, count=64,
    )
    return (
        block_out, results[0], results[1], results[2], results[3], results[8], results[4],
        results[9], results[10], results[11], results[5], results[6], results[7],
        results[12].reshape(half), results[13].reshape(half),
    )


def solution(mesh):
    in_specs = (
        P("pipe", "dp", None),
        P("dp"),
        P("dp"),
        P("dp", None),
        P("pipe", None, None),
        P("pipe", None, None),
        P("pipe", None, None),
        P("pipe", None),
        P("pipe", None, None),
        P("pipe", None),
        P("pipe", None, None),
        P("pipe", None, None),
        P("pipe", None),
        P("pipe", None),
        P("pipe", None),
        P("pipe"),
        P("pipe"),
    )
    out_specs = (
        P("pipe", "dp", None),
        P("pipe", "dp", None),
        P("pipe", None, None),
        P("pipe", None, None),
        P("pipe", None, None),
        P("pipe", None),
        P("pipe", None, None),
        P("pipe", None),
        P("pipe", None, None),
        P("pipe", None, None),
        P("pipe", None),
        P("pipe", None),
        P("pipe", None),
        P("pipe"),
        P("pipe"),
    )
    return jax.shard_map(local, mesh=mesh, in_specs=in_specs, out_specs=out_specs, check_vma=False)
```

```python
import functools

import jax
import jax.numpy as jnp
from jax import lax
from jax.experimental import pallas as pl
from jax.experimental.pallas import tpu as pltpu
from jax.sharding import PartitionSpec as P

HEADS = 8
LOW = jnp.bfloat16
WIDE = jnp.float32
HEAD_SIZE = 64
PAIR = 2 * HEAD_SIZE
GELU_SCALE = 0.7978845608
GELU_CUBE = 0.044715
MASKED = -1e30
VMEM_LIMIT = 60 * 2**20


def product(left, right, left_dim=1, right_dim=0):
    return lax.dot_general(
        left, right, (((left_dim,), (right_dim,)), ((), ())), preferred_element_type=WIDE
    )


class Copies:
    def __init__(self, semaphores):
        self.semaphores = semaphores
        self.count = 0

    def start(self, source, target):
        copy = pltpu.make_async_copy(source, target, self.semaphores.at[self.count])
        self.count += 1
        copy.start()
        return copy


def pair_columns(pair):
    return pl.ds(pl.multiple_of(pair * PAIR, PAIR), PAIR)


def lanes(rows):
    return lax.broadcasted_iota(jnp.int32, (rows, PAIR), 1)


def split_three(column):
    high = column.astype(LOW).astype(WIDE)
    rest = column - high
    middle = rest.astype(LOW).astype(WIDE)
    return high, middle, rest - middle


def key_side(keys, head, bias, lane):
    base = HEAD_SIZE * (1 - head)
    own = lane // HEAD_SIZE == head
    extra = jnp.where(lane == base, bias, jnp.where((lane > base) & (lane < base + 4), 1.0, 0.0))
    return jnp.where(own, keys, extra).astype(LOW)


def attend(query_ref, key_ref, value_ref, count, mixed_ref, logsum_ref, tile=512):
    rows = query_ref.shape[0]
    lane = lanes(rows)
    row = lax.broadcasted_iota(jnp.int32, (rows, PAIR), 0)
    bias = jnp.where(row < count, 0.0, MASKED)
    logsum_ref[...] = jnp.zeros_like(logsum_ref)

    def pair_step(pair, carry):
        columns = pair_columns(pair)
        queries = query_ref[:, columns].astype(WIDE) * HEAD_SIZE**-0.5
        keys = key_ref[:, columns].astype(WIDE)
        values = value_ref[:, columns].astype(WIDE)
        sides = []
        for head in range(2):
            base = HEAD_SIZE * (1 - head)
            own = lane // HEAD_SIZE == head
            one = jnp.where(lane == base, 1.0, 0.0)
            sides.append(
                (
                    jnp.where(own, queries, one).astype(LOW),
                    key_side(keys, head, bias, lane),
                    jnp.where(own, values, one).astype(LOW),
                )
            )
        for begin in range(0, rows, tile):
            mixed = []
            logsum = logsum_ref[begin : begin + tile]
            for head in range(2):
                base = HEAD_SIZE * (1 - head)
                query_side, keys_side, value_side = sides[head]
                scores = product(query_side[begin : begin + tile], keys_side, 1, 1)
                top = jnp.max(scores, axis=1, keepdims=True)
                weights = jnp.exp(scores - top).astype(LOW)
                summed = product(weights, value_side)
                total = summed[:, base : base + 1]
                mixed.append(summed * (1.0 / total))
                logsum = jnp.where(
                    lane[:tile] == 2 * pair + head, top + jnp.log(total), logsum
                )
            mixed_ref[begin : begin + tile, columns] = jnp.where(
                lane[:tile] < HEAD_SIZE, mixed[0], mixed[1]
            ).astype(LOW)
            logsum_ref[begin : begin + tile] = logsum
        return carry

    lax.fori_loop(0, HEADS // 2, pair_step, 0, unroll=2)


def attend_back(
    query_ref, key_ref, value_ref, count, mixed_ref, logsum_ref, grad_ref,
    query_grad_ref, key_grad_ref, value_grad_ref, tile=512, after=None,
):
    rows = query_ref.shape[0]
    lane = lanes(rows)
    row = lax.broadcasted_iota(jnp.int32, (rows, PAIR), 0)
    bias = jnp.where(row < count, 0.0, MASKED)

    def pair_step(pair):
        columns = pair_columns(pair)
        queries = query_ref[:, columns].astype(WIDE) * HEAD_SIZE**-0.5
        keys = key_ref[:, columns].astype(WIDE)
        values = value_ref[:, columns].astype(WIDE)
        grads = grad_ref[:, columns].astype(WIDE)
        along = grads * mixed_ref[:, columns].astype(WIDE)
        logsums = logsum_ref[...]
        query_sum = []
        key_parts = []
        value_parts = []
        for head in range(2):
            base = HEAD_SIZE * (1 - head)
            own = lane // HEAD_SIZE == head
            column = jnp.sum(
                jnp.where(lane == 2 * pair + head, logsums, 0.0), axis=1, keepdims=True
            )
            inner = jnp.sum(jnp.where(own, along, 0.0), axis=1, keepdims=True)
            query_side = jnp.where(own, queries, jnp.where(lane == base, 1.0, 0.0))
            grad_side = jnp.where(own, grads, 0.0)
            for place, part in enumerate(split_three(column)):
                query_side = jnp.where(lane == base + 1 + place, -part, query_side)
            for place, part in enumerate(split_three(inner)):
                grad_side = jnp.where(lane == base + 1 + place, -part, grad_side)
            query_side = query_side.astype(LOW)
            grad_side = grad_side.astype(LOW)
            keys_side = key_side(keys, head, bias, lane)
            value_side = key_side(values, head, 0.0, lane)
            query_total = None
            for begin in range(0, rows, tile):
                spot = slice(begin, begin + tile)
                probs = jnp.exp(product(keys_side[spot], query_side, 1, 1))
                slopes = (probs * product(value_side[spot], grad_side, 1, 1)).astype(LOW)
                value_part = product(probs.astype(LOW), grad_side)
                key_part = product(slopes, query_side)
                query_part = product(slopes, keys_side[spot], 0, 0)
                query_total = query_part if query_total is None else query_total + query_part
                key_parts.append(key_part)
                value_parts.append(value_part)
            query_sum.append(query_total)
        query_grad_ref[:, columns] = (
            jnp.where(lane < HEAD_SIZE, query_sum[0], query_sum[1]) * HEAD_SIZE**-0.5
        ).astype(LOW)
        pieces = rows // tile
        for piece in range(pieces):
            spot = slice(piece * tile, (piece + 1) * tile)
            first = lane[:tile] < HEAD_SIZE
            key_grad_ref[spot, columns] = jnp.where(
                first, key_parts[piece], key_parts[pieces + piece]
            ).astype(LOW)
            value_grad_ref[spot, columns] = jnp.where(
                first, value_parts[piece], value_parts[pieces + piece]
            ).astype(LOW)

    def pairs_step(step, carry):
        for place in range(2):
            pair_step(2 * step + place)
        if after is not None:
            after(step)
        return carry

    lax.fori_loop(0, HEADS // 4, pairs_step, 0, unroll=2 if after is None else 1)


def normed(values):
    shifted = values - jnp.mean(values, axis=1, keepdims=True)
    scale = lax.rsqrt(jnp.mean(shifted * shifted, axis=1, keepdims=True) + 1e-05)
    return shifted * scale, scale


def norm(values, gain, bias):
    return normed(values)[0] * gain + bias


def norm_back(values, gain, grad):
    unit, scale = normed(values)
    inner = grad * gain
    back = scale * (
        inner
        - jnp.mean(inner, axis=1, keepdims=True)
        - unit * jnp.mean(inner * unit, axis=1, keepdims=True)
    )
    return back, column_sum(grad * unit), column_sum(grad)


def column_sum(values):
    return jnp.sum(values, axis=0, keepdims=True)


def row_tiles(rows, tile, body):
    def step(index, carry):
        body(pl.ds(pl.multiple_of(index * tile, tile), tile))
        return carry

    lax.fori_loop(0, rows // tile, step, 0)


def gelu_pair(value):
    square = value * value
    half = 0.5 * jnp.tanh(value * (GELU_SCALE + (GELU_SCALE * GELU_CUBE) * square)) + 0.5
    act = value * half
    slope = half + act * (1.0 - half) * (
        2.0 * GELU_SCALE + (6.0 * GELU_SCALE * GELU_CUBE) * square
    )
    return act, slope


SMALL_ROWS = 16
ROW_TILE = 128
HALF_TILE = 256


def columns_of(index, width):
    return pl.ds(pl.multiple_of(index * width, width), width)


def project(left_ref, right_ref, target_ref, width):
    def step(index, carry):
        columns = columns_of(index, width)
        target_ref[:, columns] = product(left_ref[...], right_ref[:, columns]).astype(LOW)
        return carry

    lax.fori_loop(0, target_ref.shape[1] // width, step, 0)


def wide_row(ref, row):
    return ref[0, row : row + 1, :].astype(WIDE)


def feed_forward(low_ref, wide_ref, in_w, in_b, out2_w, out2_b, act_ref, slope_ref, residual_ref):
    rows, width = low_ref.shape

    for index in range(act_ref.shape[1] // width):
        columns = pl.ds(index * width, width)
        bias = in_b[:, columns].astype(WIDE)
        for begin in range(0, rows, HALF_TILE):
            spot = slice(begin, begin + HALF_TILE)
            act, slope = gelu_pair(product(low_ref[spot], in_w[:, columns]) + bias)
            act_ref[spot, columns] = act.astype(LOW)
            slope_ref[spot, columns] = slope.astype(LOW)
    bias_out = out2_b[...].astype(WIDE)
    for begin in range(0, rows, HALF_TILE):
        spot = slice(begin, begin + HALF_TILE)
        residual_ref[spot] = wide_ref[spot] + product(act_ref[spot], out2_w[...]) + bias_out


def feed_back(residual_grad, grad_low, slope_ref, in_w, out2_w, hidden_grad, bias_rows, out_ref):
    rows, width = grad_low.shape

    for index in range(hidden_grad.shape[1] // width):
        columns = pl.ds(index * width, width)
        total = jnp.zeros((1, width), WIDE)
        for begin in range(0, rows, HALF_TILE):
            spot = slice(begin, begin + HALF_TILE)
            grads = product(grad_low[spot], out2_w[columns, :], 1, 1)
            grads = (grads * slope_ref[spot, columns].astype(WIDE)).astype(LOW)
            hidden_grad[spot, columns] = grads
            total = total + column_sum(grads.astype(WIDE))
        bias_rows[index : index + 1, :] = total
    for begin in range(0, rows, HALF_TILE):
        spot = slice(begin, begin + HALF_TILE)
        out_ref[spot] = residual_grad[spot] + product(hidden_grad[spot], in_w[...], 1, 1)


def norm_back_rows(values_ref, gain, grad_ref, wide_ref, low_ref, gain_row, bias_row):
    back, gain_part, bias_part = norm_back(values_ref[...], gain, grad_ref[...])
    wide_ref[...] = back
    low_ref[...] = back.astype(LOW)
    gain_row[...] = gain_part
    bias_row[...] = bias_part


MESH = pl.DeviceIdType.MESH


def ring_place(chip, chips):
    half = chip // 2
    return jnp.where(chip % 2 == 0, half, chips - 1 - half)


def ring_chip(place, chips):
    return jnp.where(place < chips // 2, 2 * place, 2 * (chips - 1 - place) + 1)


def part_rows(chunk_rows):
    count = 4 if chunk_rows >= 96 else 2 if chunk_rows == 64 else 1
    tiles = chunk_rows // 16
    parts = []
    begin = 0
    for index in range(count):
        rows = 16 * (tiles // count + (index < tiles % count))
        parts.append((begin, rows))
        begin += rows
    return tuple(parts)


def ring_layout(rows, devices):
    chips = devices // 2
    ways = 2 if rows >= 64 * chips else 1
    return ways, chips, -(-rows // (2 * ways * chips * 16)) * 16


def ring_rows(rows, devices):
    ways, chips, chunk_rows = ring_layout(rows, devices)
    return 2 * ways * chips * chunk_rows


class Links:
    def __init__(self, devices):
        self.pipe = lax.axis_index("pipe")
        self.me = lax.axis_index("dp")
        self.chips = devices // 2
        self.levels = devices.bit_length() - 1
        self.core = self.me % 2
        self.place = ring_place(self.me // 2, self.chips)
        self.sides = tuple(
            ring_chip((self.place + step) % self.chips, self.chips) * 2 + self.core
            for step in (1, self.chips - 1)
        )
        self.other = self.paired(1)
        self.across = (1 - self.pipe, self.me)

    def paired(self, bit):
        return self.me + bit - 2 * bit * ((self.me // bit) % 2)

    def greet(self):
        barrier = pltpu.get_barrier_semaphore()
        greeted = list(self.sides) + [self.paired(1 << level) for level in range(self.levels)]
        for friend in greeted:
            pl.semaphore_signal(
                barrier, inc=1, device_id=(self.pipe, friend), device_id_type=MESH
            )
        pl.semaphore_signal(barrier, inc=1, device_id=self.across, device_id_type=MESH)

    def greeted(self):
        pl.semaphore_wait(pltpu.get_barrier_semaphore(), self.levels + 3)

    def copy(self, source, target, send, recv, friend):
        return pltpu.make_async_remote_copy(
            src_ref=source,
            dst_ref=target,
            send_sem=send,
            recv_sem=recv,
            device_id=friend if isinstance(friend, tuple) else (self.pipe, friend),
            device_id_type=MESH,
        )


class Ring:
    def __init__(self, links, layout, total, refs):
        self.links = links
        ways, self.chips, self.chunk_rows = layout
        self.ways = range(ways)
        self.parts = part_rows(self.chunk_rows)
        self.all_parts = range(len(self.parts))
        self.total = total
        (
            self.mine, self.sibling, self.arrived, self.pair_send, self.pair_recv, self.ring_send,
            self.ring_recv, self.gather_send, self.gather_recv, self.share_send, self.share_recv,
        ) = refs

    def chunk_at(self, way, step):
        if way == 0:
            return lax.rem(self.links.place - step + 2 * self.chips, self.chips)
        return lax.rem(self.links.place + step + self.chips, self.chips)

    def start_row(self, core, way, chunk, part):
        begin = 0 if part is None else self.parts[part][0]
        return ((core * len(self.ways) + way) * self.chips + chunk) * self.chunk_rows + begin

    def mine_at(self, core, way, chunk, part=None):
        rows = self.chunk_rows if part is None else self.parts[part][1]
        return pl.ds(pl.multiple_of(self.start_row(core, way, chunk, part), 16), rows)

    def total_at(self, way, step, part):
        start = self.start_row(self.links.core, way, self.chunk_at(way, step), part)
        rows = self.parts[part][1]
        if len(self.total.shape) == 2:
            return self.total.at[pl.ds(pl.multiple_of(start, 16), rows)]
        size = self.total.shape[1]
        return self.total.at[
            lax.div(start, size), pl.ds(pl.multiple_of(lax.rem(start, size), 16), rows)
        ]

    def pair_copy(self, way, step, mine=None, sibling=None, send=None, recv=None):
        chunk = self.chunk_at(way, step)
        return self.links.copy(
            (self.mine if mine is None else mine).at[
                self.mine_at(1 - self.links.core, way, chunk)
            ],
            (self.sibling if sibling is None else sibling).at[way, chunk],
            (self.pair_send if send is None else send).at[way, step],
            (self.pair_recv if recv is None else recv).at[way, step],
            self.links.other,
        )

    def ring_copy(self, way, step, part):
        spot = pl.ds(*self.parts[part])
        return self.links.copy(
            self.arrived.at[way, step, spot],
            self.arrived.at[way, step + 1, spot],
            self.ring_send.at[way, step, part],
            self.ring_recv.at[way, step, part],
            self.links.sides[way],
        )

    def gather_copy(self, way, step, part):
        spot = self.total_at(way, step - 1, part)
        return self.links.copy(
            spot,
            spot,
            self.gather_send.at[way, step, part],
            self.gather_recv.at[way, step, part],
            self.links.sides[way],
        )

    def share_copy(self, way, step, part):
        spot = self.total_at(way, step - 1, part)
        return self.links.copy(
            spot,
            spot,
            self.share_send.at[way, step, part],
            self.share_recv.at[way, step, part],
            self.links.other,
        )

    def pairs_start(self):
        def start(step, carry):
            for way in self.ways:
                self.pair_copy(way, step).start()
            return carry

        lax.fori_loop(0, self.chips, start, 0)

    def pair_ready(self, way, step):
        self.pair_copy(way, step).wait_recv()

    def pairs_end(self):
        def end(step, carry):
            for way in self.ways:
                self.pair_copy(way, step).wait_send()
            return carry

        lax.fori_loop(0, self.chips, end, 0)

    def begin(self):
        self.pairs_start()
        for way in self.ways:
            self.pair_ready(way, 0)
            for part in range(len(self.parts)):
                spot = pl.ds(*self.parts[part])
                chunk = self.links.place
                own = self.mine[self.mine_at(self.links.core, way, chunk, part)]
                pair = self.sibling[way, chunk, spot]
                self.arrived[way, 0, spot] = (own.astype(WIDE) + pair.astype(WIDE)).astype(LOW)
                self.ring_copy(way, 0, part).start()

    def merged(self, way, step, part):
        spot = pl.ds(*self.parts[part])
        chunk = self.chunk_at(way, step + 1)
        self.ring_copy(way, step, part).wait_recv()
        own = self.mine[self.mine_at(self.links.core, way, chunk, part)]
        return (
            self.arrived[way, step + 1, spot].astype(WIDE)
            + own.astype(WIDE)
            + self.sibling[way, chunk, spot].astype(WIDE)
        ).astype(LOW)

    def reduce(self, step):
        for way in self.ways:
            self.pair_ready(way, step + 1)
        for part in range(len(self.parts)):
            spot = pl.ds(*self.parts[part])
            for way in self.ways:
                self.arrived[way, step + 1, spot] = self.merged(way, step, part)
                self.ring_copy(way, step + 1, part).start()

    def settle(self, parts=None):
        last = self.chips - 2
        for way in self.ways:
            self.pair_ready(way, last + 1)
        for part in self.all_parts:
            for way in self.ways:
                self.total_at(way, -1, part)[...] = self.merged(way, last, part)
                if parts is None or part in parts:
                    self.gather_copy(way, 0, part).start()
                    self.share_copy(way, 0, part).start()

    def gather_begin(self, parts):
        for part in parts:
            for way in self.ways:
                self.gather_copy(way, 0, part).start()
                self.share_copy(way, 0, part).start()

    def gather(self, step, parts=None):
        for part in self.all_parts if parts is None else parts:
            for way in self.ways:
                self.gather_copy(way, step, part).wait_recv()
                self.gather_copy(way, step + 1, part).start()
                self.share_copy(way, step + 1, part).start()

    def gather_last(self, parts=None):
        last = self.chips - 2
        for part in self.all_parts if parts is None else parts:
            for way in self.ways:
                self.gather_copy(way, last, part).wait_recv()
                self.share_copy(way, last + 1, part).start()

    def finish(self):
        self.pairs_end()

        def shares(step, carry):
            for way in self.ways:
                for part in range(len(self.parts)):
                    self.share_copy(way, step, part).wait()
            return carry

        lax.fori_loop(0, self.chips, shares, 0)

        def sends(step, carry):
            for way in self.ways:
                for part in range(len(self.parts)):
                    self.ring_copy(way, step, part).wait_send()
                    self.gather_copy(way, step, part).wait_send()
            return carry

        lax.fori_loop(0, self.chips - 1, sends, 0)


class CrossRing(Ring):
    def __init__(self, links, layout, total, refs, foreign_refs):
        super().__init__(links, layout, total, refs)
        self.foreign, self.foreign_sibling = foreign_refs[:2]
        self.foreign_send, self.foreign_recv, self.cross_send, self.cross_recv = foreign_refs[2:]

    def foreign_pair(self, way, step):
        return self.pair_copy(
            way, step, self.foreign, self.foreign_sibling, self.foreign_send, self.foreign_recv
        )

    def cross_copy(self, way, step):
        spot = self.mine_at(self.links.core, way, self.chunk_at(way, step))
        return self.links.copy(
            self.foreign.at[spot],
            self.mine.at[spot],
            self.cross_send.at[way, step],
            self.cross_recv.at[way, step],
            self.links.across,
        )

    def each(self, body):
        def step_all(step, carry):
            for way in self.ways:
                body(way, step)
            return carry

        lax.fori_loop(0, self.chips, step_all, 0)

    def foreign_start(self):
        self.each(lambda way, step: self.foreign_pair(way, step).start())

    def foreign_pass(self):
        def hand_over(way, step):
            chunk = self.chunk_at(way, step)
            spot = self.mine_at(self.links.core, way, chunk)
            self.foreign_pair(way, step).wait_recv()
            self.foreign[spot] = (
                self.foreign[spot].astype(WIDE) + self.foreign_sibling[way, chunk].astype(WIDE)
            ).astype(LOW)
            self.cross_copy(way, step).start()

        self.each(hand_over)

    def pairs_start(self):
        pl.when(self.links.pipe == 1)(super().pairs_start)

        @pl.when(self.links.pipe == 0)
        def _():
            self.sibling[...] = jnp.zeros_like(self.sibling)

    def pair_ready(self, way, step):
        @pl.when(self.links.pipe == 1)
        def _():
            self.pair_copy(way, step).wait_recv()

        @pl.when(self.links.pipe == 0)
        def _():
            self.cross_copy(way, step).wait_recv()

    def pairs_end(self):
        @pl.when(self.links.pipe == 1)
        def _():
            self.each(lambda way, step: self.pair_copy(way, step).wait_send())
            self.each(lambda way, step: self.foreign_pair(way, step).wait_send())
            self.each(lambda way, step: self.cross_copy(way, step).wait_send())


def ring_scratch(rows, width, devices):
    ways, chips, chunk_rows = ring_layout(rows, devices)
    pieces = len(part_rows(chunk_rows))
    dma = pltpu.SemaphoreType.DMA
    return [
        pltpu.VMEM((2 * ways * chips * chunk_rows, width), LOW),
        pltpu.VMEM((ways, chips, chunk_rows, width), LOW),
        pltpu.VMEM((ways, chips, chunk_rows, width), LOW),
        dma((ways, chips)),
        dma((ways, chips)),
    ] + [dma((ways, chips, pieces)) for _ in range(6)]


def foreign_scratch(rows, width, devices):
    ways, chips, chunk_rows = ring_layout(rows, devices)
    dma = pltpu.SemaphoreType.DMA
    return [
        pltpu.VMEM((2 * ways * chips * chunk_rows, width), LOW),
        pltpu.VMEM((ways, chips, chunk_rows, width), LOW),
    ] + [dma((ways, chips)) for _ in range(4)]


def flat_row(ref):
    return ref[...].astype(WIDE).reshape(1, ref.shape[0])


class Outs:
    def __init__(self, semaphores, table):
        self.semaphores = semaphores
        self.table = table
        self.order = {name: place for place, name in enumerate(table)}

    def copy(self, name, example):
        source, target = self.table[name](example)
        return pltpu.make_async_copy(
            source, target, self.semaphores.at[example, self.order[name]]
        )

    def start(self, name, example):
        self.copy(name, example).start()

    def free(self, name, example):
        @pl.when(example == 1)
        def _():
            self.copy(name, 0).wait()

    def wait(self, names, examples):
        for name in names:
            for example in examples:
                self.copy(name, example).wait()


def main_kernel(
    src_len, tgt_len, in_b, out2_b, gains, biases, cross_gain, cross_bias, inputs, cotangent,
    qkv_w, out_w, in_w, out2_w, cross_qkv, cross_out, slot_w, small_out, block_out, qkv_out,
    logsum_out, mixed_out, residual_out, low_out, act_out, slope_out, second_out, grad_out,
    hidden_out, branch_out, qkv_grad_out, rows_out, query_out, rest_out, memory_out, query_w_out,
    own_out, sent_out, x_s, qkv_w_s, out_w_s, in_w_s, out2_w_s, cross_w_s, cross_out_s, slot_w_s,
    gains_s, qkv_s, logsum_s, mixed_s, residual_s, wide_s, low_s, act_s, slope_s, second_s,
    memory_s, first_s, query_s, pair_s, cross_mixed_s, cross_logsum_s, cross_s, final_s, grad_s,
    earlier_s, slot_s, wide_grad_s, grad_low_s, hidden_s, back_s, rest_s, branch_s, attn_grad_s,
    query_grad_s, pair_grad_s, memory_grad_s, qkv_grad_s, part_s, load_sem, out_sem, memory_send,
    memory_recv, return_send, return_recv, weight_send, weight_recv, near_send, near_recv,
):
    section = lax.axis_index("pipe")
    me = lax.axis_index("dp")
    core = lax.rem(me, 2)
    across, other = (1 - section, me), (section, me + 1 - 2 * core)
    encoder, decoder = section == 0, section == 1
    total_rows, width = x_s.shape
    rows = total_rows // 2
    half = width // 2
    part = half // 2
    barrier = pltpu.get_barrier_semaphore()
    for friend in (across, other):
        pl.semaphore_signal(barrier, inc=1, device_id=friend, device_id_type=MESH)

    copies = Copies(load_sem)
    x_copy = copies.start(inputs.at[0], x_s)
    qkv_w_copy = copies.start(qkv_w.at[0], qkv_w_s)
    out_w_copy = copies.start(out_w.at[0], out_w_s)
    in_w_copy = copies.start(in_w.at[0], in_w_s)
    out2_w_copy = copies.start(out2_w.at[0], out2_w_s)
    decoder_loads = [
        pltpu.make_async_copy(source, target, load_sem.at[copies.count + place])
        for place, (source, target) in enumerate(
            (
                (cotangent, grad_s),
                (cross_qkv, cross_w_s.at[pl.ds(half, half)]),
                (cross_out, cross_out_s.at[pl.ds(half, half)]),
                (slot_w, slot_w_s.at[pl.ds(width, width)]),
            )
        )
    ]

    def remote(source, target, send, recv, friend):
        return pltpu.make_async_remote_copy(
            src_ref=source, dst_ref=target, send_sem=send, recv_sem=recv, device_id=friend,
            device_id_type=MESH,
        )

    def piece(rows_each):
        return pl.ds(pl.multiple_of(core * rows_each, rows_each), rows_each)

    weight_pieces = (
        (cross_qkv, cross_w_s, piece(part)),
        (cross_out, cross_out_s, piece(part)),
        (slot_w, slot_w_s, piece(2 * part)),
    )
    gains_copy = remote(gains_s, gains_s, weight_send.at[3], weight_recv.at[3], across)
    weight_copies = [
        remote(source.at[spot], target.at[spot], weight_send.at[place], weight_recv.at[place], across)
        for place, (source, target, spot) in enumerate(weight_pieces)
    ]
    near_copies = [
        remote(target.at[spot], target.at[spot], near_send.at[place], near_recv.at[place], other)
        for place, (_, target, spot) in enumerate(weight_pieces)
    ]

    def memory_copy(example, tile):
        begin = pl.multiple_of(example * rows + tile * ROW_TILE, ROW_TILE)
        block = memory_s.at[pl.ds(begin, ROW_TILE)]
        return remote(
            block, block, memory_send.at[example, tile], memory_recv.at[example, tile], across
        )

    def return_copy(example, tile):
        spot = pl.ds(pl.multiple_of(tile * HALF_TILE, HALF_TILE), HALF_TILE)
        block = memory_grad_s.at[example, spot]
        return remote(
            block, block, return_send.at[example, tile], return_recv.at[example, tile], across
        )

    def rows_of(example):
        return pl.ds(pl.multiple_of(example * rows, rows), rows)

    outs = Outs(
        out_sem,
        {
            "qkv": lambda e: (qkv_s.at[e], qkv_out.at[e]),
            "logsum": lambda e: (logsum_s.at[e], logsum_out.at[e]),
            "mixed": lambda e: (mixed_s.at[e], mixed_out.at[e]),
            "residual": lambda e: (residual_s.at[e], residual_out.at[e]),
            "low": lambda e: (low_s, low_out.at[e]),
            "act": lambda e: (act_s, act_out.at[e]),
            "slope": lambda e: (slope_s.at[e], slope_out),
            "second": lambda e: (second_s.at[e], second_out),
            "memory": lambda e: (memory_s.at[rows_of(e)], block_out.at[0, rows_of(e)]),
            "slot": lambda e: (slot_s, block_out.at[0, rows_of(e)]),
            "grad": lambda e: (grad_low_s, grad_out.at[e]),
            "hidden": lambda e: (hidden_s, hidden_out.at[e]),
            "rest": lambda e: (rest_s, rest_out.at[e]),
            "query": lambda e: (query_grad_s.at[rows_of(e)], query_out.at[e]),
            "branch": lambda e: (branch_s.at[rows_of(e)], branch_out),
            "qkv_grad": lambda e: (qkv_grad_s, qkv_grad_out),
            "rows": lambda e: (back_s, rows_out.at[0, rows_of(e)]),
            "return": lambda e: (memory_grad_s.at[e], memory_out),
            "query_w": lambda e: (cross_w_s.at[:, pl.ds(0, width)], query_w_out),
        },
    )
    small_out[...] = jnp.zeros_like(small_out)
    gain_first, bias_first = wide_row(gains, 0), wide_row(biases, 0)
    gain_last, bias_last = wide_row(gains, 1), wide_row(biases, 1)
    pl.semaphore_wait(barrier, 2)

    @pl.when(encoder)
    def _():
        row = jnp.concatenate([flat_row(cross_gain), flat_row(cross_bias)], axis=1)
        gains_s[...] = jnp.broadcast_to(row, gains_s.shape).astype(LOW)
        gains_copy.start()
        for copy in weight_copies:
            copy.start()

    @pl.when(decoder)
    def _():
        for copy in decoder_loads:
            copy.start()

    x_copy.wait()
    qkv_w_copy.wait()

    def self_step(example, carry):
        x_rows = x_s.at[rows_of(example)]
        qkv_rows = qkv_s.at[example]
        project(x_rows, qkv_w_s, qkv_rows, width)
        outs.start("qkv", example)
        count = jnp.where(encoder, src_len[example], tgt_len[example])
        attend(
            qkv_s.at[example, :, pl.ds(0, width)],
            qkv_s.at[example, :, pl.ds(width, width)],
            qkv_s.at[example, :, pl.ds(2 * width, width)],
            count,
            mixed_s.at[example],
            logsum_s.at[example],
        )
        outs.start("mixed", example)
        outs.start("logsum", example)

        @pl.when(example == 0)
        def _():
            out_w_copy.wait()

        def residual_step(spot):
            residual_s[example, spot] = x_rows[spot].astype(WIDE) + product(
                mixed_s[example, spot], out_w_s[...]
            )

        row_tiles(rows, HALF_TILE, residual_step)
        outs.start("residual", example)

        @pl.when(example == 0)
        def _():
            in_w_copy.wait()
            out2_w_copy.wait()

        @pl.when(encoder)
        def _():
            outs.free("low", example)

            value = norm(residual_s[example], gain_first, bias_first)
            wide_s[...] = value
            low_s[...] = value.astype(LOW)
            outs.start("low", example)
            outs.free("act", example)
            feed_forward(
                low_s, wide_s, in_w_s, in_b, out2_w_s, out2_b, act_s, slope_s.at[example],
                second_s.at[example],
            )
            outs.start("act", example)

            def memory_step(tile, inner):
                spot = pl.ds(pl.multiple_of(tile * ROW_TILE, ROW_TILE), ROW_TILE)
                row = lax.broadcasted_iota(jnp.int32, (ROW_TILE, width), 0) + tile * ROW_TILE
                value = norm(second_s[example, spot], gain_last, bias_last)
                begin = pl.multiple_of(example * rows + tile * ROW_TILE, ROW_TILE)
                memory_s[pl.ds(begin, ROW_TILE)] = jnp.where(row < count, value, 0.0).astype(LOW)
                memory_copy(example, tile).start()
                return inner

            lax.fori_loop(0, rows // ROW_TILE, memory_step, 0)
            outs.start("memory", example)

            @pl.when(example == 1)
            def _():
                outs.start("slope", 1)
                outs.start("second", 1)

        return carry

    lax.fori_loop(0, 2, self_step, 0)

    @pl.when(encoder)
    def _():
        for tile in range(rows // HALF_TILE):
            return_copy(0, tile).wait_recv()
        row = lax.broadcasted_iota(jnp.int32, (rows, width), 0)
        wide_grad_s[...] = jnp.where(row < src_len[0], memory_grad_s[0].astype(WIDE), 0.0)
        norm_back_rows(
            second_s.at[0], gain_last, wide_grad_s, wide_s, grad_low_s,
            small_out.at[6:7, :], small_out.at[8:9, :],
        )
        outs.start("grad", 0)
        small_out[4:5, :] = column_sum(grad_low_s[...].astype(WIDE))
        feed_back(
            wide_s, grad_low_s, slope_s.at[0], in_w_s, out2_w_s, hidden_s, small_out.at[0:4, :],
            wide_grad_s,
        )
        outs.start("hidden", 0)
        norm_back_rows(
            residual_s.at[0], gain_first, wide_grad_s, rest_s, branch_s.at[pl.ds(0, rows)],
            small_out.at[5:6, :], small_out.at[7:8, :],
        )
        outs.start("branch", 0)
        attn_grad_s[...] = product(branch_s[:rows], out_w_s[...], 1, 1).astype(LOW)
        attend_back(
            qkv_s.at[0, :, pl.ds(0, width)],
            qkv_s.at[0, :, pl.ds(width, width)],
            qkv_s.at[0, :, pl.ds(2 * width, width)],
            src_len[0],
            mixed_s.at[0],
            logsum_s.at[0],
            attn_grad_s,
            qkv_grad_s.at[:, pl.ds(0, width)],
            qkv_grad_s.at[:, pl.ds(width, width)],
            qkv_grad_s.at[:, pl.ds(2 * width, width)],
        )
        outs.start("qkv_grad", 0)

        def rows_step(spot):
            back_s[spot] = rest_s[spot] + product(qkv_grad_s[spot], qkv_w_s[...], 1, 1)

        row_tiles(rows, HALF_TILE, rows_step)
        outs.start("rows", 0)
        gains_copy.wait_send()
        for copy in weight_copies:
            copy.wait_send()

        def sent_step(tile, inner):
            for example in range(2):
                memory_copy(example, tile).wait_send()
            return inner

        lax.fori_loop(0, rows // ROW_TILE, sent_step, 0)
        outs.wait(("low", "act", "slope", "second"), (1,))
        outs.wait(("memory",), (0, 1))
        outs.wait(("grad", "hidden", "branch", "qkv_grad", "rows"), (0,))
        for tile in range(rows // HALF_TILE):
            return_copy(1, tile).wait_recv()
        outs.start("return", 1)
        outs.wait(("return",), (1,))

    @pl.when(decoder)
    def _():
        for copy in decoder_loads:
            copy.wait()
        for example in range(2):
            spot = slice(example * rows, (example + 1) * rows)
            row = lax.broadcasted_iota(jnp.int32, (rows, width), 0)
            slot_grad = jnp.where(
                row < tgt_len[example] - 1, grad_s[spot].astype(WIDE), 0.0
            )
            grad_s[spot] = slot_grad.astype(LOW)
            earlier = jnp.where(row == 0, 0.0, pltpu.roll(slot_grad, 1, 0))
            earlier_s[spot] = earlier.astype(LOW)
        for place in range(3):
            weight_copies[place].wait_recv()
            near_copies[place].start()
        gains_copy.wait_recv()
        for copy in near_copies:
            copy.wait_recv()
        outs.start("query_w", 0)
        came_row = gains_s[0:1, :].astype(WIDE)
        gain_cross = jnp.concatenate([came_row[:, :half], flat_row(cross_gain)], axis=1)
        bias_cross = jnp.concatenate([came_row[:, half:], flat_row(cross_bias)], axis=1)

        def cross_step(example, carry):
            spot_rows = rows_of(example)
            first = first_s.at[spot_rows]
            final = final_s.at[spot_rows]
            slot_grad, earlier = grad_s.at[spot_rows], earlier_s.at[spot_rows]
            mixed, branch = cross_mixed_s.at[spot_rows], branch_s.at[spot_rows]
            query_grad, pair_grad = query_grad_s.at[spot_rows], pair_grad_s.at[spot_rows]
            second = second_s.at[0]
            slope = slope_s.at[0]

            value = norm(residual_s[example], gain_first, bias_first)
            wide_s[...] = value
            first[...] = value.astype(LOW)
            query_s[...] = product(first[...], cross_w_s[:, :width]).astype(LOW)

            def arrive(tile, inner):
                memory_copy(example, tile).wait_recv()
                return inner

            lax.fori_loop(0, rows // ROW_TILE, arrive, 0)
            project(memory_s.at[spot_rows], cross_w_s.at[:, width:], pair_s, width)
            key_ref, value_ref = pair_s.at[:, :width], pair_s.at[:, width:]
            count = src_len[example]
            attend(query_s, key_ref, value_ref, count, mixed, cross_logsum_s)
            outs.free("low", example)

            for begin in range(0, rows, HALF_TILE):
                spot = slice(begin, begin + HALF_TILE)
                value = wide_s[spot] + product(mixed[spot], cross_out_s[...])
                cross_s[spot] = value
                value = norm(value, gain_cross, bias_cross)
                wide_s[spot] = value
                low_s[spot] = value.astype(LOW)
            outs.start("low", example)
            outs.free("act", example)
            feed_forward(
                low_s, wide_s, in_w_s, in_b, out2_w_s, out2_b, act_s, slope, second
            )
            outs.start("act", example)

            final[...] = norm(second[...], gain_last, bias_last).astype(LOW)
            wide_grad_s[...] = product(slot_grad[...], slot_w_s[:width, :], 1, 1) + product(
                earlier[...], slot_w_s[width:, :], 1, 1
            )
            outs.free("grad", example)
            part_s[...] = jnp.zeros_like(part_s)
            norm_back_rows(
                second, gain_last, wide_grad_s, second, grad_low_s,
                part_s.at[6:7, :], part_s.at[8:9, :],
            )
            outs.start("grad", example)
            part_s[4:5, :] = column_sum(grad_low_s[...].astype(WIDE))
            outs.free("hidden", example)
            feed_back(
                second, grad_low_s, slope, in_w_s, out2_w_s, hidden_s, part_s.at[0:4, :], back_s
            )
            outs.start("hidden", example)
            outs.free("rest", example)
            norm_back_rows(
                cross_s, gain_cross, back_s, rest_s, branch, part_s.at[9:10, :],
                part_s.at[10:11, :],
            )
            outs.start("rest", example)
            small_out[...] += part_s[...]
            attn_grad_s[...] = product(branch[...], cross_out_s[...], 1, 1).astype(LOW)
            attend_back(
                query_s, key_ref, value_ref, count, mixed, cross_logsum_s, attn_grad_s,
                query_grad, pair_grad.at[:, pl.ds(0, width)], pair_grad.at[:, pl.ds(width, width)],
            )
            for tile in range(rows // HALF_TILE):
                spot = pl.ds(tile * HALF_TILE, HALF_TILE)
                memory_grad_s[example, spot] = product(
                    pair_grad[spot], cross_w_s[:, width:], 1, 1
                ).astype(LOW)
                return_copy(example, tile).start()
            outs.start("query", example)
            outs.free("slot", example)
            wide_grad_s[...] = product(final[...], slot_w_s[width:, :])
            value = product(final[...], slot_w_s[:width, :]) + pltpu.roll(
                wide_grad_s[...], rows - 1, 0
            )
            row = lax.broadcasted_iota(jnp.int32, (rows, width), 0)
            slot_s[...] = jnp.where(row < tgt_len[example] - 1, value, 0.0).astype(LOW)
            outs.start("slot", example)
            return carry

        lax.fori_loop(0, 2, cross_step, 0)
        outs.wait(("qkv",), (0, 1))

        def keep(place, value):
            block, begin = place // 2, (place % 2) * half
            columns = pl.ds(block * width, width)
            qkv_s[1, pl.ds(begin, half), columns] = value[:half].astype(LOW)
            qkv_s[0, pl.ds(begin, half), columns] = value[half:].astype(LOW)

        last_columns = pl.ds(2 * width, width)
        qkv_s[1, :, last_columns] = product(final_s[...], grad_s[...], 0, 0).astype(LOW)
        qkv_s[0, :, last_columns] = product(final_s[...], earlier_s[...], 0, 0).astype(LOW)
        keep(3, product(cross_mixed_s[...], branch_s[...], 0, 0))
        keep(1, product(memory_s[...], pair_grad_s[:, :width], 0, 0))
        keep(2, product(memory_s[...], pair_grad_s[:, width:], 0, 0))
        keep(0, product(first_s[...], query_grad_s[...], 0, 0))
        kept = []
        for target, slot in ((own_out, 0), (sent_out, 1)):
            for block in range(3):
                kept.append(
                    pltpu.make_async_copy(
                        qkv_s.at[slot, :, pl.ds(block * width, width)],
                        target.at[pl.ds(block * width, width)],
                        load_sem.at[3 * slot + block],
                    )
                )
        for copy in kept:
            copy.start()
        for copy in near_copies:
            copy.wait_send()

        def returned(tile, inner):
            for example in range(2):
                return_copy(example, tile).wait_send()
            return inner

        lax.fori_loop(0, rows // HALF_TILE, returned, 0)
        outs.wait(("low", "act", "grad", "hidden", "rest", "slot"), (1,))
        outs.wait(("query",), (0, 1))
        outs.wait(("query_w",), (0,))
        for copy in kept:
            copy.wait()

    @pl.when(encoder)
    def _():
        outs.wait(("qkv",), (0, 1))

    outs.wait(("mixed", "logsum", "residual"), (0, 1))


def last_kernel(
    devices, src_len, tgt_len, gains, small_in, inputs, qkv_w, out_w, in_w, out2_w, query_w,
    memory_grad, second_in, slope_in, query_grad, rest_in, residual_in, qkv_in, logsum_in, mixed_in,
    low_in, act_in, grad_in, hidden_in, branch_a, qkv_grad_a, own_extra, sent_extra, first_total,
    second_total, cross_total, small_total, rows_out, qkv_w_s, out_w_s, in_w_s, out2_w_s, low_s,
    hidden_s, act_s, grad_s, mixed_s, branch_s, x_s, qkv_grad_s, memory_s, second_s, slope_s,
    back_s, query_w_s, residual_s, qkv_s, logsum_s, rest_s, attn_grad_s, small_s, small_arrived,
    cross_total_s, small_send, small_recv, small_cross_sem, semaphores, *ring_refs,
):
    mixed_a, mixed_b = mixed_in.at[0], mixed_in.at[1]
    low_a, low_b = low_in.at[0], low_in.at[1]
    act_a, act_b = act_in.at[0], act_in.at[1]
    grad_a, grad_b = grad_in.at[0], grad_in.at[1]
    hidden_a, hidden_b = hidden_in.at[0], hidden_in.at[1]
    links = Links(devices)
    links.greet()
    chips, levels = links.chips, links.levels
    section = links.pipe
    rows, width = residual_s.shape
    half = width // 2
    hidden = hidden_s.shape[1]
    hidden_blocks = hidden // width
    extra_rows = own_extra.shape[0]
    sizes = (2 * hidden, 4 * width, extra_rows)
    layouts = [ring_layout(size, devices) for size in sizes]
    early = Ring(links, layouts[0], act_s, ring_refs[:11])
    late = Ring(links, layouts[1], out2_w_s, ring_refs[11:22])
    cross = CrossRing(links, layouts[2], cross_total_s, ring_refs[22:33], ring_refs[33:])
    front, rear = pl.ds(0, rows), pl.ds(rows, rows)
    gain_first, gain_last = wide_row(gains, 0), wide_row(gains, 1)
    small_s[0] = small_in[...]
    partial = small_arrived.at[0]
    partial[...] = jnp.zeros_like(small_in)

    encoder = section == 0
    copies = Copies(semaphores)

    def declared(source, target):
        copy = pltpu.make_async_copy(source, target, semaphores.at[copies.count])
        copies.count += 1
        return copy

    def start(*group):
        for copy in group:
            copy.start()

    def wait(*group):
        for copy in group:
            copy.wait()

    hidden_front = [declared(low_a, low_s.at[front]), declared(low_b, low_s.at[rear]),
                    declared(hidden_a, hidden_s.at[front])]
    act_front = [declared(grad_a, grad_s.at[front])]
    for index in range(hidden_blocks):
        columns = pl.ds(index * width, width)
        act_front.append(declared(act_a.at[:, columns], act_s.at[index, front]))
        act_front.append(declared(act_b.at[:, columns], act_s.at[index, rear]))
    hidden_rear = declared(hidden_b, hidden_s.at[rear])
    grad_rear = declared(grad_b, grad_s.at[rear])
    back_inputs = [declared(memory_grad, memory_s), declared(second_in, second_s),
                   declared(slope_in, slope_s), declared(out2_w.at[0], out2_w_s),
                   declared(in_w.at[0], in_w_s)]
    query_weights = [declared(query_w, query_w_s)]
    out_w_copy = declared(out_w.at[0], out_w_s)
    qkv_w_copy = declared(qkv_w.at[0], qkv_w_s)
    mixed_copies = [declared(mixed_a, mixed_s.at[front]), declared(mixed_b, mixed_s.at[rear])]
    saved = []
    base = copies.count
    for example in range(2):
        copies.count = base
        parts = [
            ref.at[example] for ref in (residual_in, query_grad, rest_in, qkv_in, logsum_in)
        ]
        targets = (residual_s, memory_s, second_s, qkv_s, logsum_s)
        saved.append([declared(source, target) for source, target in zip(parts, targets)])
    encoder_inputs = [declared(branch_a, branch_s.at[front]),
                      declared(qkv_grad_a, qkv_grad_s.at[front])]
    inputs_copy = declared(inputs.at[0], x_s)
    extra_loads = [declared(own_extra, cross.mine.at[pl.ds(0, extra_rows)]),
                   declared(sent_extra, cross.foreign.at[pl.ds(0, extra_rows)])]
    if cross.mine.shape[0] > extra_rows:
        cross.mine[extra_rows:] = jnp.zeros_like(cross.mine[extra_rows:])
        cross.foreign[extra_rows:] = jnp.zeros_like(cross.foreign[extra_rows:])

    def rows_copy(example):
        spot = pl.ds(pl.multiple_of(example * rows, rows), rows)
        return pltpu.make_async_copy(rest_s, rows_out.at[spot], semaphores.at[copies.count])

    @pl.when(encoder)
    def _():
        start(*back_inputs, *hidden_front, *act_front, out_w_copy, qkv_w_copy, *mixed_copies,
              *encoder_inputs, inputs_copy)
        wait(*back_inputs[:2])
        row = lax.broadcasted_iota(jnp.int32, (rows, width), 0)
        rest_s[...] = jnp.where(row < src_len[1], memory_s[...].astype(WIDE), 0.0)
        norm_back_rows(
            second_s, gain_last, rest_s, second_s, grad_s.at[rear],
            partial.at[6:7, :], partial.at[8:9, :],
        )
        partial[4:5, :] = column_sum(grad_s[rear].astype(WIDE))
        wait(*back_inputs[2:])
        feed_back(
            second_s, grad_s.at[rear], slope_s, in_w_s, out2_w_s, hidden_s.at[rear],
            partial.at[0:4, :], back_s,
        )
        start(saved[1][0], *saved[1][3:])

    @pl.when(section == 1)
    def _():
        start(*hidden_front, hidden_rear, *act_front, grad_rear, *saved[0], *query_weights,
              out_w_copy, qkv_w_copy, *mixed_copies, *extra_loads, inputs_copy)
        wait(hidden_rear, grad_rear)

    def blocks(target, begin, count, block):
        def step(index, carry):
            target[columns_of(begin + index, width), :] = block(index).astype(LOW)
            return carry

        lax.fori_loop(0, count, step, 0)

    wait(*hidden_front)
    blocks(
        early.mine, 0, hidden_blocks,
        lambda index: product(low_s[...], hidden_s[:, columns_of(index, width)], 0, 0),
    )
    wait(*act_front)
    blocks(
        early.mine, hidden_blocks, hidden_blocks,
        lambda index: product(act_s[index], grad_s[...], 0, 0),
    )
    links.greeted()
    small_cross = links.copy(
        small_s.at[levels], small_arrived.at[1], small_cross_sem.at[0], small_cross_sem.at[1],
        links.across,
    )

    @pl.when(section == 1)
    def _():
        small_s[levels, 0:1, :] = jnp.concatenate(
            [small_s[0, 9:10, :half], small_s[0, 10:11, :half]], axis=1
        )
        small_cross.start()
        wait(*extra_loads)
        cross.foreign_start()

    early.begin()

    @pl.when(section == 1)
    def _():
        cross.foreign_pass()

    cross.begin()
    per_example = 3
    begin_at = jnp.where(encoder, 1, 0)
    ahead = early.all_parts

    @pl.when(section == 1)
    def _():
        wait(*query_weights)

    wait(out_w_copy, qkv_w_copy, *mixed_copies)

    def advance(turn):
        @pl.when(turn < chips - 2)
        def _():
            early.reduce(turn)
            cross.reduce(turn)

        @pl.when(turn == chips - 2)
        def _():
            early.settle(ahead)
            cross.settle()

        @pl.when((turn > chips - 2) & (turn < 2 * chips - 3))
        def _():
            early.gather(turn - (chips - 1), ahead)
            cross.gather(turn - (chips - 1))

        @pl.when(turn == 2 * chips - 3)
        def _():
            early.gather_last(ahead)
            cross.gather_last()

    def back_step(example, carry):
        spot = pl.ds(pl.multiple_of(example * rows, rows), rows)
        turn = (example - begin_at) * per_example

        @pl.when(section == 1)
        def _():
            wait(*saved[0][:3])

            def first_step(tile):
                back_s[tile] = second_s[tile] + product(memory_s[tile], query_w_s[...], 1, 1)

            row_tiles(rows, HALF_TILE, first_step)

        @pl.when(encoder)
        def _():
            wait(saved[0][0])

        @pl.when((section == 1) & (example == 1))
        def _():
            rows_copy(0).wait()

        low_branch = branch_s.at[spot]
        norm_back_rows(
            residual_s, gain_first, back_s, rest_s, low_branch,
            partial.at[12:13, :], partial.at[13:14, :],
        )
        partial[5:6, :] += partial[12:13, :]
        partial[7:8, :] += partial[13:14, :]
        attn_grad_s[...] = product(low_branch[...], out_w_s[...], 1, 1).astype(LOW)
        wait(*saved[0][3:])
        advance(turn)
        count = jnp.where(encoder, src_len[example], tgt_len[example])
        attend_back(
            qkv_s.at[:, :width],
            qkv_s.at[:, width : 2 * width],
            qkv_s.at[:, 2 * width :],
            count,
            mixed_s.at[spot],
            logsum_s,
            attn_grad_s,
            qkv_grad_s.at[spot, pl.ds(0, width)],
            qkv_grad_s.at[spot, pl.ds(width, width)],
            qkv_grad_s.at[spot, pl.ds(2 * width, width)],
            after=lambda step: advance(turn + 1 + step),
        )

        @pl.when(example == 0)
        def _():
            start(*saved[1])

        def rows_step(index, inner):
            tile = pl.ds(pl.multiple_of(index * HALF_TILE, HALF_TILE), HALF_TILE)
            begin = pl.multiple_of(example * rows + index * HALF_TILE, HALF_TILE)
            rest_s[tile] += product(qkv_grad_s[pl.ds(begin, HALF_TILE)], qkv_w_s[...], 1, 1)
            return inner

        lax.fori_loop(0, rows // HALF_TILE, rows_step, 0)
        rows_copy(example).start()
        return carry

    lax.fori_loop(begin_at, 2, back_step, 0)
    wait(inputs_copy)

    @pl.when(encoder)
    def _():
        wait(*encoder_inputs)

    blocks(
        late.mine, 0, 3,
        lambda index: product(x_s[...], qkv_grad_s[:, columns_of(index, width)], 0, 0),
    )
    done = (2 - begin_at) * per_example
    advance(done)
    blocks(late.mine, 3, 1, lambda index: product(mixed_s[...], branch_s[...], 0, 0))

    if late.mine.shape[0] > 4 * width:
        late.mine[4 * width :] = jnp.zeros_like(late.mine[4 * width :])
    late.begin()
    advance(done + 1)
    done = done + 2

    small_s[0] = small_s[0] + partial[...]
    @pl.when(section == 1)
    def _():
        small_s[0, 9:10, :] = jnp.concatenate(
            [small_s[0, 9:10, half:], small_s[0, 10:11, half:]], axis=1
        )
        small_cross.wait_send()

    @pl.when(encoder)
    def _():
        small_cross.wait_recv()
        small_s[0, 9:10, :] = small_arrived[1, 0:1, :]

    def small_copy(level, bit):
        return links.copy(
            small_s.at[level],
            small_arrived.at[level + 2],
            small_send.at[level],
            small_recv.at[level],
            links.paired(bit),
        )

    small_copy(0, 1).start()

    def early_step(turn, carry):
        advance(turn)
        return carry


    def merge_small(level, bit):
        small_copy(level, bit).wait_recv()
        merged = small_s[level] + small_arrived[level + 2]

        @pl.when(level + 1 < levels)
        def _():
            small_s[level + 1] = merged
            small_copy(level + 1, 2 * bit).start()

        @pl.when(level + 1 == levels)
        def _():
            small_total[...] = merged

    def both_step(step, bit):
        late.reduce(step)
        advance(done + step)

        @pl.when(step < levels)
        def _():
            merge_small(step, bit)

        return 2 * bit

    lax.fori_loop(0, chips - 2, both_step, 1)
    late.settle()
    advance(done + chips - 2)

    def late_step(step, carry):
        late.gather(step)
        advance(done + chips - 1 + step)
        return carry

    lax.fori_loop(0, chips - 2, late_step, 0)
    lax.fori_loop(done + 2 * chips - 3, 2 * chips - 2, early_step, 0)
    late.gather_last()
    late.finish()
    cross.finish()
    kept = [
        pltpu.make_async_copy(
            out2_w_s.at[pl.ds(0, second_total.shape[0])], second_total, semaphores.at[0]
        ),
        pltpu.make_async_copy(cross_total_s, cross_total, semaphores.at[1]),
    ]
    for index in range(hidden_blocks):
        kept.append(
            pltpu.make_async_copy(
                act_s.at[index], first_total.at[pl.ds(index * 2 * rows, 2 * rows)],
                semaphores.at[2 + index],
            )
        )
    start(*kept[:2])
    early.finish()
    start(*kept[2:])
    wait(*kept)
    for level in range(levels):
        small_copy(level, 1 << level).wait_send()
    rows_copy(1).wait()


def result_kernel(
    small_total, first_total, second_total, cross_total, rows_in, block_in,
    rows_buffer, block_out, rows_out, qkv_out, out_out,
    in_out, out2_out, cross_qkv_out, cross_out_out, slot_out, in_b_out, out2_b_out, gain_out,
    bias_out, cross_gain_out, cross_bias_out, first_s, second_s, rows_s, block_s,
    wide_s, semaphores,
):
    width = first_s.shape[1]
    half = width // 2
    for index in range(in_b_out.shape[1] // width):
        in_b_out[:, index * width : (index + 1) * width] = small_total[index : index + 1, :]
    out2_b_out[...] = small_total[4:5, :]
    gain_out[0] = small_total[5:7, :]
    bias_out[0] = small_total[7:9, :]
    cross_gain_out[...] = small_total[9:10, :half]
    cross_bias_out[...] = small_total[9:10, half:]
    copies = Copies(semaphores)
    rows = rows_in.shape[0] // 2
    front, rear = pl.ds(0, rows), pl.ds(rows, rows)
    rows_copy = copies.start(rows_in.at[rear], rows_s.at[rear])
    front_sem = semaphores.at[copies.count]
    copies.count += 1
    from_last = pltpu.make_async_copy(rows_in.at[front], rows_s.at[front], front_sem)
    from_main = pltpu.make_async_copy(rows_buffer.at[0, front], rows_s.at[front], front_sem)
    pl.when(lax.axis_index("pipe") == 1)(from_last.start)
    pl.when(lax.axis_index("pipe") == 0)(from_main.start)
    block_copy = copies.start(block_in.at[0], block_s)
    rows = rows_in.shape[0] // 2
    kept = []
    loads = {width: [], half: []}
    second_rows = 4 * width
    for index in range(first_s.shape[0] // width):
        spot = pl.ds(index * width, width)
        loads[width].append(copies.start(first_total.at[spot], first_s.at[spot]))
    for index in range(second_s.shape[0] // half):
        begin = index * half
        if begin < second_rows:
            source = second_total.at[pl.ds(begin, half)]
        else:
            source = cross_total.at[pl.ds(begin - second_rows, half)]
        loads[half].append(copies.start(source, second_s.at[pl.ds(begin, half)]))
    targets = []
    for index in range(first_s.shape[0] // width):
        hidden_blocks = in_out.shape[2] // width
        if index < hidden_blocks:
            target = in_out.at[0, :, pl.ds(index * width, width)]
        else:
            target = out2_out.at[0, pl.ds((index - hidden_blocks) * width, width)]
        targets.append((loads[width][index : index + 1], first_s, index * width, width, target))
    for index in range(4):
        if index < 3:
            target = qkv_out.at[0, :, pl.ds(index * width, width)]
        else:
            target = out_out.at[0]
        targets.append(
            (loads[half][2 * index : 2 * index + 2], second_s, index * width, width, target)
        )
    for index in range(4):
        if index < 3:
            target = cross_qkv_out.at[:, pl.ds(index * width, width)]
        else:
            target = cross_out_out
        targets.append(
            (loads[half][8 + index : 9 + index], second_s, 4 * width + index * half, half, target)
        )
    targets.append((loads[half][12:14], second_s, 6 * width, width, slot_out))
    place = 0
    for waits, stage, begin, size, target in targets:
        for copy in waits:
            copy.wait()
        wide_s[place : place + size] = stage[begin : begin + size].astype(WIDE)
        kept.append(copies.start(wide_s.at[pl.ds(place, size)], target))
        place += size
    block_copy.wait()
    kept.append(copies.start(block_s, block_out.at[0]))
    rows_copy.wait()
    from_last.wait()
    kept.append(copies.start(rows_s, rows_out.at[0]))
    for copy in kept:
        copy.wait()


ANY = pl.BlockSpec(memory_space=pl.ANY)
INNER = pl.BlockSpec(memory_space=pltpu.VMEM)
SCALAR = pl.BlockSpec(memory_space=pltpu.SMEM)


def local_call(
    body, name, scalars, inner, outer, outputs, scratch, flops, aliases=None, count=32,
    semaphores=(), **compiler,
):
    shapes = [jax.ShapeDtypeStruct(shape, kind) for shape, kind, _ in outputs]
    inputs = list(scalars) + list(inner) + list(outer)
    specs = [SCALAR] * len(scalars) + [INNER] * len(inner) + [ANY] * len(outer)
    moved = sum(value.size * value.dtype.itemsize for value in inputs)
    return pl.pallas_call(
        body,
        out_shape=shapes,
        in_specs=specs,
        out_specs=[INNER if kept else ANY for _, _, kept in outputs],
        scratch_shapes=[pltpu.VMEM(shape, kind) for shape, kind in scratch]
        + list(semaphores or [pltpu.SemaphoreType.DMA((count,))]),
        input_output_aliases=aliases or {},
        compiler_params=pltpu.CompilerParams(vmem_limit_bytes=VMEM_LIMIT, **compiler),
        cost_estimate=pl.CostEstimate(flops=flops, bytes_accessed=moved, transcendentals=0),
        name=name,
    )(*inputs)


def local(
    inputs, src_len, tgt_len, cotangent, qkv_w, out_w, in_w, in_b, out2_w, out2_b, norm_gain,
    norm_bias, cross_qkv, cross_out, slot_w, cross_gain, cross_bias,
):
    devices = lax.axis_size("dp")
    blocks = src_len.shape[0]
    total_rows, width = inputs.shape[1:]
    rows = total_rows // blocks
    half = width // 2
    hidden = in_w.shape[2]
    square, wide3, deep = (rows, width), (rows, 3 * width), (rows, hidden)
    weight_square, logsum = (width, width), (rows, PAIR)
    tall, tall3, tall_deep = (total_rows, width), (total_rows, 3 * width), (total_rows, hidden)
    extra_rows = 3 * width
    small_shape = (SMALL_ROWS, width)
    dma = pltpu.SemaphoreType.DMA
    tiles, halves = rows // ROW_TILE, rows // HALF_TILE

    (
        small, block_out, qkv, logsums, mixed, residual, low, act, slope, second, grad, hidden_grad,
        branch, qkv_grad, source_rows, query_grad, rest, memory_grad, query_w, own_extra,
        sent_extra,
    ) = local_call(
        main_kernel, "main_rows", [src_len, tgt_len],
        [
            in_b, out2_b, norm_gain, norm_bias, cross_gain, cross_bias,
        ],
        [inputs, cotangent, qkv_w, out_w, in_w, out2_w, cross_qkv, cross_out, slot_w],
        [
            (small_shape, WIDE, True), ((1,) + tall, LOW, False), ((2,) + wide3, LOW, False),
            ((2,) + logsum, WIDE, False), ((2,) + square, LOW, False), ((2,) + square, WIDE, False),
            ((2,) + square, LOW, False), ((2,) + deep, LOW, False), (deep, LOW, False),
            (square, WIDE, False), ((2,) + square, LOW, False), ((2,) + deep, LOW, False),
            (square, LOW, False), (wide3, LOW, False), ((1,) + tall, WIDE, False),
            ((2,) + square, LOW, False), ((2,) + square, WIDE, False), (square, LOW, False),
            (weight_square, LOW, False), ((extra_rows, width), LOW, False),
            ((extra_rows, width), LOW, False),
        ],
        [
            (tall, LOW), ((width, 3 * width), LOW), (weight_square, LOW), ((width, hidden), LOW),
            ((hidden, width), LOW), ((width, 3 * width), LOW), (weight_square, LOW),
            ((2 * width, width), LOW), (small_shape, LOW), ((2,) + wide3, LOW),
            ((2,) + logsum, WIDE), ((2,) + square, LOW), ((2,) + square, WIDE), (square, WIDE),
            (square, LOW), (deep, LOW), ((2,) + deep, LOW), ((2,) + square, WIDE), (tall, LOW),
            (tall, LOW), (square, LOW), ((rows, 2 * width), LOW), (tall, LOW), (logsum, WIDE),
            (square, WIDE), (tall, LOW), (tall, LOW), (tall, LOW), (square, LOW), (square, WIDE),
            (square, LOW), (deep, LOW), (square, WIDE), (square, WIDE), (tall, LOW), (square, LOW),
            (tall, LOW), ((total_rows, 2 * width), LOW), ((2,) + square, LOW), (wide3, LOW),
            (small_shape, WIDE),
        ],
        70 * 10**9,
        semaphores=[
            dma((16,)), dma((2, 24)), dma((2, tiles)), dma((2, tiles)), dma((2, halves)),
            dma((2, halves)), dma((4,)), dma((4,)), dma((3,)), dma((3,)),
        ],
        collective_id=1, has_side_effects=True,
    )

    sizes = (2 * hidden, 4 * width, extra_rows)
    padded = [ring_rows(size, devices) for size in sizes]
    levels = devices.bit_length() - 1
    rings = [part for size in sizes for part in ring_scratch(size, width, devices)]
    rings += foreign_scratch(extra_rows, width, devices)
    first_total, second_total, cross_total, small_total, last_rows = local_call(
        functools.partial(last_kernel, devices), "last_rows", [src_len, tgt_len],
        [norm_gain, small],
        [
            inputs, qkv_w, out_w, in_w, out2_w, query_w, memory_grad, second, slope, query_grad,
            rest, residual, qkv, logsums, mixed, low, act, grad, hidden_grad, branch, qkv_grad,
            own_extra, sent_extra,
        ],
        [
            ((padded[0], width), LOW, False),
            ((padded[1], width), LOW, False),
            ((padded[2], width), LOW, False),
            (small_shape, WIDE, True),
            (tall, WIDE, False),
        ],
        [
            ((width, 3 * width), LOW), (weight_square, LOW), ((width, hidden), LOW),
            ((hidden, width), LOW), (tall, LOW), (tall_deep, LOW),
            ((hidden // width,) + tall, LOW), (tall, LOW), (tall, LOW), (tall, LOW), (tall, LOW),
            (tall3, LOW), (square, LOW), (square, WIDE), (deep, LOW), (square, WIDE),
            (weight_square, LOW), (square, WIDE), (wide3, LOW), (logsum, WIDE), (square, WIDE),
            (square, LOW), ((levels + 1,) + small_shape, WIDE), ((levels + 2,) + small_shape, WIDE),
            ((padded[2], width), LOW),
        ],
        20 * 10**9,
        semaphores=[dma((levels,)), dma((levels,)), dma((2,)), dma((64,))] + rings,
        collective_id=0, has_side_effects=True,
    )

    results = local_call(
        result_kernel, "results", [], [small_total],
        [first_total, second_total, cross_total, last_rows, block_out, source_rows],
        [
            ((1,) + tall, LOW, False), ((1,) + tall, WIDE, False),
            ((1, width, 3 * width), WIDE, False),
            ((1,) + weight_square, WIDE, False), ((1, width, hidden), WIDE, False),
            ((1, hidden, width), WIDE, False), ((half, 3 * width), WIDE, False),
            ((half, width), WIDE, False), ((width, width), WIDE, False),
            ((1, hidden), WIDE, True), ((1, width), WIDE, True), ((1, 2, width), WIDE, True),
            ((1, 2, width), WIDE, True), ((1, half), WIDE, True), ((1, half), WIDE, True),
        ],
        [
            ((sizes[0], width), LOW), ((sizes[1] + sizes[2], width), LOW), (tall, WIDE),
            (tall, LOW), ((sum(sizes), width), WIDE),
        ],
        10**9, count=64,
    )
    return (
        results[0], results[1], results[2], results[3], results[4], results[9], results[5],
        results[10], results[11], results[12], results[6], results[7], results[8],
        results[13].reshape(half), results[14].reshape(half),
    )


def solution(mesh):
    in_specs = (
        P("pipe", "dp", None),
        P("dp"),
        P("dp"),
        P("dp", None),
        P("pipe", None, None),
        P("pipe", None, None),
        P("pipe", None, None),
        P("pipe", None),
        P("pipe", None, None),
        P("pipe", None),
        P("pipe", None, None),
        P("pipe", None, None),
        P("pipe", None),
        P("pipe", None),
        P("pipe", None),
        P("pipe"),
        P("pipe"),
    )
    out_specs = (
        P("pipe", "dp", None),
        P("pipe", "dp", None),
        P("pipe", None, None),
        P("pipe", None, None),
        P("pipe", None, None),
        P("pipe", None),
        P("pipe", None, None),
        P("pipe", None),
        P("pipe", None, None),
        P("pipe", None, None),
        P("pipe", None),
        P("pipe", None),
        P("pipe", None),
        P("pipe"),
        P("pipe"),
    )
    return jax.shard_map(local, mesh=mesh, in_specs=in_specs, out_specs=out_specs, check_vma=False)
```

```python
import functools

import jax
import jax.numpy as jnp
from jax import lax
from jax.experimental import pallas as pl
from jax.experimental.pallas import tpu as pltpu
from jax.sharding import PartitionSpec as P

HEADS = 8
LOW = jnp.bfloat16
WIDE = jnp.float32
HEAD_SIZE = 64
PAIR = 2 * HEAD_SIZE
GELU_SCALE = 0.7978845608
GELU_CUBE = 0.044715
MASKED = -1e30
VMEM_LIMIT = 60 * 2**20


def product(left, right, left_dim=1, right_dim=0):
    return lax.dot_general(
        left, right, (((left_dim,), (right_dim,)), ((), ())), preferred_element_type=WIDE
    )


class Copies:
    def __init__(self, semaphores):
        self.semaphores = semaphores
        self.count = 0

    def start(self, source, target):
        copy = pltpu.make_async_copy(source, target, self.semaphores.at[self.count])
        self.count += 1
        copy.start()
        return copy


def pair_columns(pair):
    return pl.ds(pl.multiple_of(pair * PAIR, PAIR), PAIR)


def lanes(rows):
    return lax.broadcasted_iota(jnp.int32, (rows, PAIR), 1)


def split_three(column):
    high = column.astype(LOW).astype(WIDE)
    rest = column - high
    middle = rest.astype(LOW).astype(WIDE)
    return high, middle, rest - middle


def key_side(keys, head, bias, lane):
    base = HEAD_SIZE * (1 - head)
    own = lane // HEAD_SIZE == head
    extra = jnp.where(lane == base, bias, jnp.where((lane > base) & (lane < base + 4), 1.0, 0.0))
    return jnp.where(own, keys, extra).astype(LOW)


def attend(query_ref, key_ref, value_ref, count, mixed_ref, logsum_ref, tile=512):
    rows = query_ref.shape[0]
    lane = lanes(rows)
    row = lax.broadcasted_iota(jnp.int32, (rows, PAIR), 0)
    bias = jnp.where(row < count, 0.0, MASKED)
    logsum_ref[...] = jnp.zeros_like(logsum_ref)

    def pair_step(pair, carry):
        columns = pair_columns(pair)
        queries = query_ref[:, columns].astype(WIDE) * HEAD_SIZE**-0.5
        keys = key_ref[:, columns].astype(WIDE)
        values = value_ref[:, columns].astype(WIDE)
        sides = []
        for head in range(2):
            base = HEAD_SIZE * (1 - head)
            own = lane // HEAD_SIZE == head
            one = jnp.where(lane == base, 1.0, 0.0)
            sides.append(
                (
                    jnp.where(own, queries, one).astype(LOW),
                    key_side(keys, head, bias, lane),
                    jnp.where(own, values, one).astype(LOW),
                )
            )
        for begin in range(0, rows, tile):
            mixed = []
            logsum = logsum_ref[begin : begin + tile]
            for head in range(2):
                base = HEAD_SIZE * (1 - head)
                query_side, keys_side, value_side = sides[head]
                scores = product(query_side[begin : begin + tile], keys_side, 1, 1)
                top = jnp.max(scores, axis=1, keepdims=True)
                weights = jnp.exp(scores - top).astype(LOW)
                summed = product(weights, value_side)
                total = summed[:, base : base + 1]
                mixed.append(summed * (1.0 / total))
                logsum = jnp.where(
                    lane[:tile] == 2 * pair + head, top + jnp.log(total), logsum
                )
            mixed_ref[begin : begin + tile, columns] = jnp.where(
                lane[:tile] < HEAD_SIZE, mixed[0], mixed[1]
            ).astype(LOW)
            logsum_ref[begin : begin + tile] = logsum
        return carry

    lax.fori_loop(0, HEADS // 2, pair_step, 0, unroll=2)


def attend_back(
    query_ref, key_ref, value_ref, count, mixed_ref, logsum_ref, grad_ref,
    query_grad_ref, key_grad_ref, value_grad_ref, tile=512, after=None,
):
    rows = query_ref.shape[0]
    lane = lanes(rows)
    row = lax.broadcasted_iota(jnp.int32, (rows, PAIR), 0)
    bias = jnp.where(row < count, 0.0, MASKED)

    def pair_step(pair):
        columns = pair_columns(pair)
        queries = query_ref[:, columns].astype(WIDE) * HEAD_SIZE**-0.5
        keys = key_ref[:, columns].astype(WIDE)
        values = value_ref[:, columns].astype(WIDE)
        grads = grad_ref[:, columns].astype(WIDE)
        along = grads * mixed_ref[:, columns].astype(WIDE)
        logsums = logsum_ref[...]
        query_sum = []
        key_parts = []
        value_parts = []
        for head in range(2):
            base = HEAD_SIZE * (1 - head)
            own = lane // HEAD_SIZE == head
            column = jnp.sum(
                jnp.where(lane == 2 * pair + head, logsums, 0.0), axis=1, keepdims=True
            )
            inner = jnp.sum(jnp.where(own, along, 0.0), axis=1, keepdims=True)
            query_side = jnp.where(own, queries, jnp.where(lane == base, 1.0, 0.0))
            grad_side = jnp.where(own, grads, 0.0)
            for place, part in enumerate(split_three(column)):
                query_side = jnp.where(lane == base + 1 + place, -part, query_side)
            for place, part in enumerate(split_three(inner)):
                grad_side = jnp.where(lane == base + 1 + place, -part, grad_side)
            query_side = query_side.astype(LOW)
            grad_side = grad_side.astype(LOW)
            keys_side = key_side(keys, head, bias, lane)
            value_side = key_side(values, head, 0.0, lane)
            query_total = None
            for begin in range(0, rows, tile):
                spot = slice(begin, begin + tile)
                probs = jnp.exp(product(keys_side[spot], query_side, 1, 1))
                slopes = (probs * product(value_side[spot], grad_side, 1, 1)).astype(LOW)
                value_part = product(probs.astype(LOW), grad_side)
                key_part = product(slopes, query_side)
                query_part = product(slopes, keys_side[spot], 0, 0)
                query_total = query_part if query_total is None else query_total + query_part
                key_parts.append(key_part)
                value_parts.append(value_part)
            query_sum.append(query_total)
        query_grad_ref[:, columns] = (
            jnp.where(lane < HEAD_SIZE, query_sum[0], query_sum[1]) * HEAD_SIZE**-0.5
        ).astype(LOW)
        pieces = rows // tile
        for piece in range(pieces):
            spot = slice(piece * tile, (piece + 1) * tile)
            first = lane[:tile] < HEAD_SIZE
            key_grad_ref[spot, columns] = jnp.where(
                first, key_parts[piece], key_parts[pieces + piece]
            ).astype(LOW)
            value_grad_ref[spot, columns] = jnp.where(
                first, value_parts[piece], value_parts[pieces + piece]
            ).astype(LOW)

    def pairs_step(step, carry):
        for place in range(2):
            pair_step(2 * step + place)
        if after is not None:
            after(step)
        return carry

    lax.fori_loop(0, HEADS // 4, pairs_step, 0)


def normed(values):
    shifted = values - jnp.mean(values, axis=1, keepdims=True)
    scale = lax.rsqrt(jnp.mean(shifted * shifted, axis=1, keepdims=True) + 1e-05)
    return shifted * scale, scale


def norm(values, gain, bias):
    return normed(values)[0] * gain + bias


def norm_back(values, gain, grad):
    unit, scale = normed(values)
    inner = grad * gain
    back = scale * (
        inner
        - jnp.mean(inner, axis=1, keepdims=True)
        - unit * jnp.mean(inner * unit, axis=1, keepdims=True)
    )
    return back, column_sum(grad * unit), column_sum(grad)


def column_sum(values):
    return jnp.sum(values, axis=0, keepdims=True)


def row_tiles(rows, tile, body):
    def step(index, carry):
        body(pl.ds(pl.multiple_of(index * tile, tile), tile))
        return carry

    lax.fori_loop(0, rows // tile, step, 0)


def gelu_pair(value):
    square = value * value
    half = 0.5 * jnp.tanh(value * (GELU_SCALE + (GELU_SCALE * GELU_CUBE) * square)) + 0.5
    act = value * half
    slope = half + act * (1.0 - half) * (
        2.0 * GELU_SCALE + (6.0 * GELU_SCALE * GELU_CUBE) * square
    )
    return act, slope


SMALL_ROWS = 16
ROW_TILE = 128
HALF_TILE = 256


def columns_of(index, width):
    return pl.ds(pl.multiple_of(index * width, width), width)


def project(left_ref, right_ref, target_ref, width):
    def step(index, carry):
        columns = columns_of(index, width)
        target_ref[:, columns] = product(left_ref[...], right_ref[:, columns]).astype(LOW)
        return carry

    lax.fori_loop(0, target_ref.shape[1] // width, step, 0)


def wide_row(ref, row):
    return ref[0, row : row + 1, :].astype(WIDE)


def feed_forward(low_ref, wide_ref, in_w, in_b, out2_w, out2_b, act_ref, slope_ref, residual_ref):
    rows, width = low_ref.shape

    for index in range(act_ref.shape[1] // width):
        columns = pl.ds(index * width, width)
        bias = in_b[:, columns].astype(WIDE)
        for begin in range(0, rows, HALF_TILE):
            spot = slice(begin, begin + HALF_TILE)
            act, slope = gelu_pair(product(low_ref[spot], in_w[:, columns]) + bias)
            act_ref[spot, columns] = act.astype(LOW)
            slope_ref[spot, columns] = slope.astype(LOW)
    bias_out = out2_b[...].astype(WIDE)
    for begin in range(0, rows, HALF_TILE):
        spot = slice(begin, begin + HALF_TILE)
        residual_ref[spot] = wide_ref[spot] + product(act_ref[spot], out2_w[...]) + bias_out


def feed_back(residual_grad, grad_low, slope_ref, in_w, out2_w, hidden_grad, bias_rows, out_ref):
    rows, width = grad_low.shape

    for index in range(hidden_grad.shape[1] // width):
        columns = pl.ds(index * width, width)
        total = jnp.zeros((1, width), WIDE)
        for begin in range(0, rows, HALF_TILE):
            spot = slice(begin, begin + HALF_TILE)
            grads = product(grad_low[spot], out2_w[columns, :], 1, 1)
            grads = (grads * slope_ref[spot, columns].astype(WIDE)).astype(LOW)
            hidden_grad[spot, columns] = grads
            total = total + column_sum(grads.astype(WIDE))
        bias_rows[index : index + 1, :] = total
    for begin in range(0, rows, HALF_TILE):
        spot = slice(begin, begin + HALF_TILE)
        out_ref[spot] = residual_grad[spot] + product(hidden_grad[spot], in_w[...], 1, 1)


def feed_back_rolled(
    residual_grad, grad_low, slope_ref, in_w, out2_w, hidden_grad, bias_rows, out_ref
):
    rows, width = grad_low.shape

    def hidden_step(index, carry):
        columns = columns_of(index, width)
        grads = product(grad_low[...], out2_w[columns, :], 1, 1)
        grads = (grads * slope_ref[:, columns].astype(WIDE)).astype(LOW)
        hidden_grad[:, columns] = grads
        bias_rows[pl.ds(index, 1), :] = column_sum(grads.astype(WIDE))
        return carry

    lax.fori_loop(0, hidden_grad.shape[1] // width, hidden_step, 0)

    def out_step(spot):
        out_ref[spot] = residual_grad[spot] + product(hidden_grad[spot], in_w[...], 1, 1)

    row_tiles(rows, HALF_TILE, out_step)


def norm_back_rolled(values_ref, gain, grad_ref, wide_ref, low_ref, gain_row, bias_row):
    rows, width = values_ref.shape
    gain_row[...] = jnp.zeros((1, width), WIDE)
    bias_row[...] = jnp.zeros((1, width), WIDE)

    def step(spot):
        back, gain_part, bias_part = norm_back(values_ref[spot], gain, grad_ref[spot])
        wide_ref[spot] = back
        low_ref[spot] = back.astype(LOW)
        gain_row[...] += gain_part
        bias_row[...] += bias_part

    row_tiles(rows, ROW_TILE, step)


def norm_back_rows(values_ref, gain, grad_ref, wide_ref, low_ref, gain_row, bias_row):
    back, gain_part, bias_part = norm_back(values_ref[...], gain, grad_ref[...])
    wide_ref[...] = back
    low_ref[...] = back.astype(LOW)
    gain_row[...] = gain_part
    bias_row[...] = bias_part


MESH = pl.DeviceIdType.MESH


def ring_place(chip, chips):
    half = chip // 2
    return jnp.where(chip % 2 == 0, half, chips - 1 - half)


def ring_chip(place, chips):
    return jnp.where(place < chips // 2, 2 * place, 2 * (chips - 1 - place) + 1)


def part_count(chunk_rows):
    tiles = chunk_rows // 16
    return 2 if tiles % 4 == 0 else 1


def ring_layout(rows, devices):
    chips = devices // 2
    ways = 2 if rows >= 64 * chips else 1
    return ways, chips, -(-rows // (2 * ways * chips * 16)) * 16


def ring_rows(rows, devices):
    ways, chips, chunk_rows = ring_layout(rows, devices)
    return 2 * ways * chips * chunk_rows


def whenever(flag):
    return pl.when(flag) if not isinstance(flag, bool) else lambda body: body()


class Links:
    def __init__(self, devices):
        self.pipe = lax.axis_index("pipe")
        self.me = lax.axis_index("dp")
        self.chips = devices // 2
        self.levels = devices.bit_length() - 1
        self.core = self.me % 2
        self.place = ring_place(self.me // 2, self.chips)
        self.sides = tuple(
            ring_chip((self.place + step) % self.chips, self.chips) * 2 + self.core
            for step in (1, self.chips - 1)
        )
        self.other = self.paired(1)
        self.across = (1 - self.pipe, self.me)

    def paired(self, bit):
        return self.me + bit - 2 * bit * ((self.me // bit) % 2)

    def greet(self):
        barrier = pltpu.get_barrier_semaphore()
        greeted = list(self.sides) + [self.paired(1 << level) for level in range(self.levels)]
        for friend in greeted:
            pl.semaphore_signal(
                barrier, inc=1, device_id=(self.pipe, friend), device_id_type=MESH
            )
        pl.semaphore_signal(barrier, inc=1, device_id=self.across, device_id_type=MESH)

    def greeted(self):
        pl.semaphore_wait(pltpu.get_barrier_semaphore(), self.levels + 3)

    def copy(self, source, target, send, recv, friend):
        return pltpu.make_async_remote_copy(
            src_ref=source,
            dst_ref=target,
            send_sem=send,
            recv_sem=recv,
            device_id=friend if isinstance(friend, tuple) else (self.pipe, friend),
            device_id_type=MESH,
        )


class Ring:
    def __init__(self, links, layout, total, refs):
        self.links = links
        ways, self.chips, self.chunk_rows = layout
        self.ways = range(ways)
        self.count = part_count(self.chunk_rows)
        self.part_rows = self.chunk_rows // self.count
        self.total = total
        (
            self.mine, self.sibling, self.arrived, self.pair_send, self.pair_recv, self.ring_send,
            self.ring_recv, self.gather_send, self.gather_recv, self.share_send, self.share_recv,
        ) = refs

    def part_at(self, part):
        return pl.ds(pl.multiple_of(part * self.part_rows, 16), self.part_rows)

    def over(self, parts, body):
        low, high = (0, self.count) if parts is None else parts

        def step(part, carry):
            for way in self.ways:
                body(way, part)
            return carry

        lax.fori_loop(low, high, step, 0)

    def chunk_at(self, way, step):
        if way == 0:
            return lax.rem(self.links.place - step + 2 * self.chips, self.chips)
        return lax.rem(self.links.place + step + self.chips, self.chips)

    def start_row(self, core, way, chunk, part):
        begin = 0 if part is None else part * self.part_rows
        return ((core * len(self.ways) + way) * self.chips + chunk) * self.chunk_rows + begin

    def mine_at(self, core, way, chunk, part=None):
        rows = self.chunk_rows if part is None else self.part_rows
        return pl.ds(pl.multiple_of(self.start_row(core, way, chunk, part), 16), rows)

    def total_at(self, way, step, part):
        start = self.start_row(self.links.core, way, self.chunk_at(way, step), part)
        rows = self.part_rows
        if len(self.total.shape) == 2:
            return self.total.at[pl.ds(pl.multiple_of(start, 16), rows)]
        size = self.total.shape[1]
        return self.total.at[
            lax.div(start, size), pl.ds(pl.multiple_of(lax.rem(start, size), 16), rows)
        ]

    def pair_copy(self, way, step, mine=None, sibling=None, send=None, recv=None):
        chunk = self.chunk_at(way, step)
        return self.links.copy(
            (self.mine if mine is None else mine).at[
                self.mine_at(1 - self.links.core, way, chunk)
            ],
            (self.sibling if sibling is None else sibling).at[way, chunk],
            (self.pair_send if send is None else send).at[way, step],
            (self.pair_recv if recv is None else recv).at[way, step],
            self.links.other,
        )

    def ring_copy(self, way, step, part):
        spot = self.part_at(part)
        return self.links.copy(
            self.arrived.at[way, step, spot],
            self.arrived.at[way, step + 1, spot],
            self.ring_send.at[way, step, part],
            self.ring_recv.at[way, step, part],
            self.links.sides[way],
        )

    def gather_copy(self, way, step, part):
        spot = self.total_at(way, step - 1, part)
        return self.links.copy(
            spot,
            spot,
            self.gather_send.at[way, step, part],
            self.gather_recv.at[way, step, part],
            self.links.sides[way],
        )

    def share_copy(self, way, step):
        start = self.start_row(self.links.core, way, self.chunk_at(way, step - 1), None)
        rows = self.chunk_rows
        if len(self.total.shape) == 2:
            spot = self.total.at[pl.ds(pl.multiple_of(start, 16), rows)]
        else:
            size = self.total.shape[1]
            spot = self.total.at[
                lax.div(start, size), pl.ds(pl.multiple_of(lax.rem(start, size), 16), rows)
            ]
        return self.links.copy(
            spot, spot, self.share_send.at[way, step], self.share_recv.at[way, step],
            self.links.other,
        )

    def pairs_start(self):
        def start(step, carry):
            for way in self.ways:
                self.pair_copy(way, step).start()
            return carry

        lax.fori_loop(0, self.chips, start, 0)

    def pair_ready(self, way, step):
        self.pair_copy(way, step).wait()

    def begin(self):
        self.pairs_start()
        for way in self.ways:
            self.pair_ready(way, 0)

        def body(way, part):
            spot = self.part_at(part)
            chunk = self.links.place
            own = self.mine[self.mine_at(self.links.core, way, chunk, part)]
            pair = self.sibling[way, chunk, spot]
            self.arrived[way, 0, spot] = (own.astype(WIDE) + pair.astype(WIDE)).astype(LOW)
            self.ring_copy(way, 0, part).start()

        self.over(None, body)

    def merged(self, way, step, part):
        spot = self.part_at(part)
        chunk = self.chunk_at(way, step + 1)
        self.ring_copy(way, step, part).wait()
        own = self.mine[self.mine_at(self.links.core, way, chunk, part)]
        return (
            self.arrived[way, step + 1, spot].astype(WIDE)
            + own.astype(WIDE)
            + self.sibling[way, chunk, spot].astype(WIDE)
        ).astype(LOW)

    def pairs_ready(self, step):
        for way in self.ways:
            self.pair_ready(way, step)

    def reduce(self, step, parts=None):
        def body(way, part):
            self.arrived[way, step + 1, self.part_at(part)] = self.merged(way, step, part)
            self.ring_copy(way, step + 1, part).start()

        self.over(parts, body)

    def settle(self, parts=None, whole=True):
        def body(way, part):
            self.total_at(way, -1, part)[...] = self.merged(way, self.chips - 2, part)
            self.gather_copy(way, 0, part).start()

        self.over(parts, body)

        @whenever(whole)
        def _():
            for way in self.ways:
                self.share_copy(way, 0).start()

    def gather(self, step, parts=None, whole=True):
        def body(way, part):
            self.gather_copy(way, step, part).wait()
            self.gather_copy(way, step + 1, part).start()

        self.over(parts, body)

        @whenever(whole)
        def _():
            for way in self.ways:
                self.share_copy(way, step + 1).start()
                self.share_copy(way, step).wait()

    def gather_last(self, parts=None, whole=True):
        last = self.chips - 2
        self.over(parts, lambda way, part: self.gather_copy(way, last, part).wait())

        @whenever(whole)
        def _():
            for way in self.ways:
                self.share_copy(way, last + 1).start()
                self.share_copy(way, last).wait()

    def finish(self):
        for way in self.ways:
            self.share_copy(way, self.chips - 1).wait()


class CrossRing(Ring):
    def __init__(self, links, layout, total, refs, foreign_refs):
        super().__init__(links, layout, total, refs)
        self.foreign, self.foreign_sibling = foreign_refs[:2]
        self.foreign_send, self.foreign_recv, self.cross_send, self.cross_recv = foreign_refs[2:]

    def foreign_pair(self, way, step):
        return self.pair_copy(
            way, step, self.foreign, self.foreign_sibling, self.foreign_send, self.foreign_recv
        )

    def cross_copy(self, way, step):
        spot = self.mine_at(self.links.core, way, self.chunk_at(way, step))
        return self.links.copy(
            self.foreign.at[spot],
            self.mine.at[spot],
            self.cross_send.at[way, step],
            self.cross_recv.at[way, step],
            self.links.across,
        )

    def each(self, body):
        def step_all(step, carry):
            for way in self.ways:
                body(way, step)
            return carry

        lax.fori_loop(0, self.chips, step_all, 0)

    def foreign_start(self):
        self.each(lambda way, step: self.foreign_pair(way, step).start())

    def foreign_pass(self):
        def hand_over(way, step):
            chunk = self.chunk_at(way, step)
            spot = self.mine_at(self.links.core, way, chunk)
            self.foreign_pair(way, step).wait()
            self.foreign[spot] = (
                self.foreign[spot].astype(WIDE) + self.foreign_sibling[way, chunk].astype(WIDE)
            ).astype(LOW)
            self.cross_copy(way, step).start()

        self.each(hand_over)

    def pairs_start(self):
        pl.when(self.links.pipe == 1)(super().pairs_start)

        @pl.when(self.links.pipe == 0)
        def _():
            self.sibling[...] = jnp.zeros_like(self.sibling)

    def pair_ready(self, way, step):
        @pl.when(self.links.pipe == 1)
        def _():
            self.pair_copy(way, step).wait()
            self.cross_copy(way, step).wait_send()

        @pl.when(self.links.pipe == 0)
        def _():
            self.cross_copy(way, step).wait_recv()


def ring_scratch(rows, width, devices):
    ways, chips, chunk_rows = ring_layout(rows, devices)
    pieces = part_count(chunk_rows)
    dma = pltpu.SemaphoreType.DMA
    return [
        pltpu.VMEM((2 * ways * chips * chunk_rows, width), LOW),
        pltpu.VMEM((ways, chips, chunk_rows, width), LOW),
        pltpu.VMEM((ways, chips, chunk_rows, width), LOW),
        dma((ways, chips)),
        dma((ways, chips)),
    ] + [dma((ways, chips, pieces)) for _ in range(4)] + [dma((ways, chips))] * 2


def foreign_scratch(rows, width, devices):
    ways, chips, chunk_rows = ring_layout(rows, devices)
    dma = pltpu.SemaphoreType.DMA
    return [
        pltpu.VMEM((2 * ways * chips * chunk_rows, width), LOW),
        pltpu.VMEM((ways, chips, chunk_rows, width), LOW),
    ] + [dma((ways, chips)) for _ in range(4)]


def flat_row(ref):
    return ref[...].astype(WIDE).reshape(1, ref.shape[0])


class Outs:
    def __init__(self, semaphores, table):
        self.semaphores = semaphores
        self.table = table
        self.order = {name: place for place, name in enumerate(table)}

    def copy(self, name, example):
        source, target = self.table[name](example)
        return pltpu.make_async_copy(
            source, target, self.semaphores.at[example, self.order[name]]
        )

    def start(self, name, example):
        self.copy(name, example).start()

    def free(self, name, example):
        @pl.when(example == 1)
        def _():
            self.copy(name, 0).wait()

    def wait(self, names, examples):
        for name in names:
            for example in examples:
                self.copy(name, example).wait()


def main_kernel(
    src_len, tgt_len, in_b, out2_b, gains, biases, cross_gain, cross_bias, inputs, cotangent,
    qkv_w, out_w, in_w, out2_w, cross_qkv, cross_out, slot_w, small_out, block_out, qkv_out,
    logsum_out, mixed_out, residual_out, low_out, act_out, slope_out, second_out, grad_out,
    hidden_out, branch_out, qkv_grad_out, rows_out, query_out, rest_out, memory_out, query_w_out,
    own_out, sent_out, x_s, qkv_w_s, out_w_s, in_w_s, out2_w_s, cross_w_s, cross_out_s, slot_w_s,
    gains_s, qkv_s, logsum_s, mixed_s, residual_s, wide_s, low_s, act_s, slope_s, second_s,
    memory_s, first_s, query_s, pair_s, cross_mixed_s, cross_logsum_s, cross_s, final_s, grad_s,
    earlier_s, slot_s, wide_grad_s, grad_low_s, hidden_s, back_s, rest_s, branch_s, attn_grad_s,
    query_grad_s, pair_grad_s, memory_grad_s, qkv_grad_s, part_s, load_sem, out_sem, memory_send,
    memory_recv, return_send, return_recv, weight_send, weight_recv, near_send, near_recv,
):
    section = lax.axis_index("pipe")
    me = lax.axis_index("dp")
    core = lax.rem(me, 2)
    across, other = (1 - section, me), (section, me + 1 - 2 * core)
    encoder, decoder = section == 0, section == 1
    total_rows, width = x_s.shape
    rows = total_rows // 2
    half = width // 2
    part = half // 2
    barrier = pltpu.get_barrier_semaphore()
    for friend in (across, other):
        pl.semaphore_signal(barrier, inc=1, device_id=friend, device_id_type=MESH)

    copies = Copies(load_sem)
    x_copy = copies.start(inputs.at[0], x_s)
    qkv_w_copy = copies.start(qkv_w.at[0], qkv_w_s)
    out_w_copy = copies.start(out_w.at[0], out_w_s)
    in_w_copy = copies.start(in_w.at[0], in_w_s)
    out2_w_copy = copies.start(out2_w.at[0], out2_w_s)
    decoder_loads = [
        pltpu.make_async_copy(source, target, load_sem.at[copies.count + place])
        for place, (source, target) in enumerate(
            (
                (cotangent, grad_s),
                (cross_qkv, cross_w_s.at[pl.ds(half, half)]),
                (cross_out, cross_out_s.at[pl.ds(half, half)]),
                (slot_w, slot_w_s.at[pl.ds(width, width)]),
            )
        )
    ]

    def remote(source, target, send, recv, friend):
        return pltpu.make_async_remote_copy(
            src_ref=source, dst_ref=target, send_sem=send, recv_sem=recv, device_id=friend,
            device_id_type=MESH,
        )

    def piece(rows_each):
        return pl.ds(pl.multiple_of(core * rows_each, rows_each), rows_each)

    weight_pieces = (
        (cross_qkv, cross_w_s, piece(part)),
        (cross_out, cross_out_s, piece(part)),
        (slot_w, slot_w_s, piece(2 * part)),
    )
    gains_copy = remote(gains_s, gains_s, weight_send.at[3], weight_recv.at[3], across)
    weight_copies = [
        remote(source.at[spot], target.at[spot], weight_send.at[place], weight_recv.at[place], across)
        for place, (source, target, spot) in enumerate(weight_pieces)
    ]
    near_copies = [
        remote(target.at[spot], target.at[spot], near_send.at[place], near_recv.at[place], other)
        for place, (_, target, spot) in enumerate(weight_pieces)
    ]

    def memory_copy(example, tile):
        begin = pl.multiple_of(example * rows + tile * ROW_TILE, ROW_TILE)
        block = memory_s.at[pl.ds(begin, ROW_TILE)]
        return remote(
            block, block, memory_send.at[example, tile], memory_recv.at[example, tile], across
        )

    def return_copy(example, tile):
        spot = pl.ds(pl.multiple_of(tile * HALF_TILE, HALF_TILE), HALF_TILE)
        block = memory_grad_s.at[example, spot]
        return remote(
            block, block, return_send.at[example, tile], return_recv.at[example, tile], across
        )

    def rows_of(example):
        return pl.ds(pl.multiple_of(example * rows, rows), rows)

    outs = Outs(
        out_sem,
        {
            "qkv": lambda e: (qkv_s.at[e], qkv_out.at[e]),
            "logsum": lambda e: (logsum_s.at[e], logsum_out.at[e]),
            "mixed": lambda e: (mixed_s.at[e], mixed_out.at[e]),
            "residual": lambda e: (residual_s.at[e], residual_out.at[e]),
            "low": lambda e: (low_s, low_out.at[e]),
            "act": lambda e: (act_s, act_out.at[e]),
            "slope": lambda e: (slope_s.at[e], slope_out),
            "second": lambda e: (second_s.at[e], second_out),
            "memory": lambda e: (memory_s.at[rows_of(e)], block_out.at[0, rows_of(e)]),
            "slot": lambda e: (slot_s, block_out.at[0, rows_of(e)]),
            "grad": lambda e: (grad_low_s, grad_out.at[e]),
            "hidden": lambda e: (hidden_s, hidden_out.at[e]),
            "rest": lambda e: (rest_s, rest_out.at[e]),
            "query": lambda e: (query_grad_s.at[rows_of(e)], query_out.at[e]),
            "branch": lambda e: (branch_s.at[rows_of(e)], branch_out),
            "qkv_grad": lambda e: (qkv_grad_s, qkv_grad_out),
            "rows": lambda e: (back_s, rows_out.at[0, rows_of(e)]),
            "return": lambda e: (memory_grad_s.at[e], memory_out),
            "query_w": lambda e: (cross_w_s.at[:, pl.ds(0, width)], query_w_out),
        },
    )
    small_out[...] = jnp.zeros_like(small_out)
    gain_first, bias_first = wide_row(gains, 0), wide_row(biases, 0)
    gain_last, bias_last = wide_row(gains, 1), wide_row(biases, 1)
    pl.semaphore_wait(barrier, 2)

    @pl.when(encoder)
    def _():
        row = jnp.concatenate([flat_row(cross_gain), flat_row(cross_bias)], axis=1)
        gains_s[...] = jnp.broadcast_to(row, gains_s.shape).astype(LOW)
        gains_copy.start()
        for copy in weight_copies:
            copy.start()

    @pl.when(decoder)
    def _():
        for copy in decoder_loads:
            copy.start()

    x_copy.wait()
    qkv_w_copy.wait()

    def self_step(example, carry):
        x_rows = x_s.at[rows_of(example)]
        qkv_rows = qkv_s.at[example]
        project(x_rows, qkv_w_s, qkv_rows, width)
        outs.start("qkv", example)
        count = jnp.where(encoder, src_len[example], tgt_len[example])
        attend(
            qkv_s.at[example, :, pl.ds(0, width)],
            qkv_s.at[example, :, pl.ds(width, width)],
            qkv_s.at[example, :, pl.ds(2 * width, width)],
            count,
            mixed_s.at[example],
            logsum_s.at[example],
        )
        outs.start("mixed", example)
        outs.start("logsum", example)

        @pl.when(example == 0)
        def _():
            out_w_copy.wait()

        def residual_step(spot):
            residual_s[example, spot] = x_rows[spot].astype(WIDE) + product(
                mixed_s[example, spot], out_w_s[...]
            )

        row_tiles(rows, HALF_TILE, residual_step)
        outs.start("residual", example)

        @pl.when(example == 0)
        def _():
            in_w_copy.wait()
            out2_w_copy.wait()

        @pl.when(encoder)
        def _():
            outs.free("low", example)

            value = norm(residual_s[example], gain_first, bias_first)
            wide_s[...] = value
            low_s[...] = value.astype(LOW)
            outs.start("low", example)
            outs.free("act", example)
            feed_forward(
                low_s, wide_s, in_w_s, in_b, out2_w_s, out2_b, act_s, slope_s.at[example],
                second_s.at[example],
            )
            outs.start("act", example)

            def memory_step(tile, inner):
                spot = pl.ds(pl.multiple_of(tile * ROW_TILE, ROW_TILE), ROW_TILE)
                row = lax.broadcasted_iota(jnp.int32, (ROW_TILE, width), 0) + tile * ROW_TILE
                value = norm(second_s[example, spot], gain_last, bias_last)
                begin = pl.multiple_of(example * rows + tile * ROW_TILE, ROW_TILE)
                memory_s[pl.ds(begin, ROW_TILE)] = jnp.where(row < count, value, 0.0).astype(LOW)
                memory_copy(example, tile).start()
                return inner

            lax.fori_loop(0, rows // ROW_TILE, memory_step, 0)
            outs.start("memory", example)

            @pl.when(example == 1)
            def _():
                outs.start("slope", 1)
                outs.start("second", 1)

        return carry

    lax.fori_loop(0, 2, self_step, 0)

    @pl.when(encoder)
    def _():
        for tile in range(rows // HALF_TILE):
            return_copy(0, tile).wait_recv()
        row = lax.broadcasted_iota(jnp.int32, (rows, width), 0)
        wide_grad_s[...] = jnp.where(row < src_len[0], memory_grad_s[0].astype(WIDE), 0.0)
        norm_back_rolled(
            second_s.at[0], gain_last, wide_grad_s, wide_s, grad_low_s,
            small_out.at[6:7, :], small_out.at[8:9, :],
        )
        outs.start("grad", 0)
        small_out[4:5, :] = column_sum(grad_low_s[...].astype(WIDE))
        feed_back_rolled(
            wide_s, grad_low_s, slope_s.at[0], in_w_s, out2_w_s, hidden_s, small_out.at[0:4, :],
            wide_grad_s,
        )
        outs.start("hidden", 0)
        norm_back_rolled(
            residual_s.at[0], gain_first, wide_grad_s, rest_s, branch_s.at[pl.ds(0, rows)],
            small_out.at[5:6, :], small_out.at[7:8, :],
        )
        outs.start("branch", 0)
        attn_grad_s[...] = product(branch_s[:rows], out_w_s[...], 1, 1).astype(LOW)
        attend_back(
            qkv_s.at[0, :, pl.ds(0, width)],
            qkv_s.at[0, :, pl.ds(width, width)],
            qkv_s.at[0, :, pl.ds(2 * width, width)],
            src_len[0],
            mixed_s.at[0],
            logsum_s.at[0],
            attn_grad_s,
            qkv_grad_s.at[:, pl.ds(0, width)],
            qkv_grad_s.at[:, pl.ds(width, width)],
            qkv_grad_s.at[:, pl.ds(2 * width, width)],
        )
        outs.start("qkv_grad", 0)

        def rows_step(spot):
            back_s[spot] = rest_s[spot] + product(qkv_grad_s[spot], qkv_w_s[...], 1, 1)

        row_tiles(rows, HALF_TILE, rows_step)
        outs.start("rows", 0)
        gains_copy.wait_send()
        for copy in weight_copies:
            copy.wait_send()

        def sent_step(tile, inner):
            for example in range(2):
                memory_copy(example, tile).wait_send()
            return inner

        lax.fori_loop(0, rows // ROW_TILE, sent_step, 0)
        outs.wait(("low", "act", "slope", "second"), (1,))
        outs.wait(("memory",), (0, 1))
        outs.wait(("grad", "hidden", "branch", "qkv_grad", "rows"), (0,))
        for tile in range(rows // HALF_TILE):
            return_copy(1, tile).wait_recv()
        outs.start("return", 1)
        outs.wait(("return",), (1,))

    @pl.when(decoder)
    def _():
        for copy in decoder_loads:
            copy.wait()
        for example in range(2):
            spot = slice(example * rows, (example + 1) * rows)
            row = lax.broadcasted_iota(jnp.int32, (rows, width), 0)
            slot_grad = jnp.where(
                row < tgt_len[example] - 1, grad_s[spot].astype(WIDE), 0.0
            )
            grad_s[spot] = slot_grad.astype(LOW)
            earlier = jnp.where(row == 0, 0.0, pltpu.roll(slot_grad, 1, 0))
            earlier_s[spot] = earlier.astype(LOW)
        for place in range(3):
            weight_copies[place].wait_recv()
            near_copies[place].start()
        gains_copy.wait_recv()
        for copy in near_copies:
            copy.wait_recv()
        outs.start("query_w", 0)
        came_row = gains_s[0:1, :].astype(WIDE)
        gain_cross = jnp.concatenate([came_row[:, :half], flat_row(cross_gain)], axis=1)
        bias_cross = jnp.concatenate([came_row[:, half:], flat_row(cross_bias)], axis=1)

        def cross_step(example, carry):
            spot_rows = rows_of(example)
            first = first_s.at[spot_rows]
            final = final_s.at[spot_rows]
            slot_grad, earlier = grad_s.at[spot_rows], earlier_s.at[spot_rows]
            mixed, branch = cross_mixed_s.at[spot_rows], branch_s.at[spot_rows]
            query_grad, pair_grad = query_grad_s.at[spot_rows], pair_grad_s.at[spot_rows]
            second = second_s.at[0]
            slope = slope_s.at[0]

            value = norm(residual_s[example], gain_first, bias_first)
            wide_s[...] = value
            first[...] = value.astype(LOW)
            query_s[...] = product(first[...], cross_w_s[:, :width]).astype(LOW)

            def arrive(tile, inner):
                memory_copy(example, tile).wait_recv()
                return inner

            lax.fori_loop(0, rows // ROW_TILE, arrive, 0)
            project(memory_s.at[spot_rows], cross_w_s.at[:, width:], pair_s, width)
            key_ref, value_ref = pair_s.at[:, :width], pair_s.at[:, width:]
            count = src_len[example]
            attend(query_s, key_ref, value_ref, count, mixed, cross_logsum_s)
            outs.free("low", example)

            for begin in range(0, rows, HALF_TILE):
                spot = slice(begin, begin + HALF_TILE)
                value = wide_s[spot] + product(mixed[spot], cross_out_s[...])
                cross_s[spot] = value
                value = norm(value, gain_cross, bias_cross)
                wide_s[spot] = value
                low_s[spot] = value.astype(LOW)
            outs.start("low", example)
            outs.free("act", example)
            feed_forward(
                low_s, wide_s, in_w_s, in_b, out2_w_s, out2_b, act_s, slope, second
            )
            outs.start("act", example)

            final[...] = norm(second[...], gain_last, bias_last).astype(LOW)
            wide_grad_s[...] = product(slot_grad[...], slot_w_s[:width, :], 1, 1) + product(
                earlier[...], slot_w_s[width:, :], 1, 1
            )
            outs.free("grad", example)
            part_s[...] = jnp.zeros_like(part_s)
            norm_back_rows(
                second, gain_last, wide_grad_s, second, grad_low_s,
                part_s.at[6:7, :], part_s.at[8:9, :],
            )
            outs.start("grad", example)
            part_s[4:5, :] = column_sum(grad_low_s[...].astype(WIDE))
            outs.free("hidden", example)
            feed_back(
                second, grad_low_s, slope, in_w_s, out2_w_s, hidden_s, part_s.at[0:4, :], back_s
            )
            outs.start("hidden", example)
            outs.free("rest", example)
            norm_back_rows(
                cross_s, gain_cross, back_s, rest_s, branch, part_s.at[9:10, :],
                part_s.at[10:11, :],
            )
            outs.start("rest", example)
            small_out[...] += part_s[...]
            attn_grad_s[...] = product(branch[...], cross_out_s[...], 1, 1).astype(LOW)
            attend_back(
                query_s, key_ref, value_ref, count, mixed, cross_logsum_s, attn_grad_s,
                query_grad, pair_grad.at[:, pl.ds(0, width)], pair_grad.at[:, pl.ds(width, width)],
            )
            for tile in range(rows // HALF_TILE):
                spot = pl.ds(tile * HALF_TILE, HALF_TILE)
                memory_grad_s[example, spot] = product(
                    pair_grad[spot], cross_w_s[:, width:], 1, 1
                ).astype(LOW)
                return_copy(example, tile).start()
            outs.start("query", example)
            outs.free("slot", example)
            wide_grad_s[...] = product(final[...], slot_w_s[width:, :])
            value = product(final[...], slot_w_s[:width, :]) + pltpu.roll(
                wide_grad_s[...], rows - 1, 0
            )
            row = lax.broadcasted_iota(jnp.int32, (rows, width), 0)
            slot_s[...] = jnp.where(row < tgt_len[example] - 1, value, 0.0).astype(LOW)
            outs.start("slot", example)
            return carry

        lax.fori_loop(0, 2, cross_step, 0)
        outs.wait(("qkv",), (0, 1))

        def keep(place, value):
            block, begin = place // 2, (place % 2) * half
            columns = pl.ds(block * width, width)
            qkv_s[1, pl.ds(begin, half), columns] = value[:half].astype(LOW)
            qkv_s[0, pl.ds(begin, half), columns] = value[half:].astype(LOW)

        last_columns = pl.ds(2 * width, width)
        qkv_s[1, :, last_columns] = product(final_s[...], grad_s[...], 0, 0).astype(LOW)
        qkv_s[0, :, last_columns] = product(final_s[...], earlier_s[...], 0, 0).astype(LOW)
        keep(3, product(cross_mixed_s[...], branch_s[...], 0, 0))
        keep(1, product(memory_s[...], pair_grad_s[:, :width], 0, 0))
        keep(2, product(memory_s[...], pair_grad_s[:, width:], 0, 0))
        keep(0, product(first_s[...], query_grad_s[...], 0, 0))
        kept = []
        for target, slot in ((own_out, 0), (sent_out, 1)):
            for block in range(3):
                kept.append(
                    pltpu.make_async_copy(
                        qkv_s.at[slot, :, pl.ds(block * width, width)],
                        target.at[pl.ds(block * width, width)],
                        load_sem.at[3 * slot + block],
                    )
                )
        for copy in kept:
            copy.start()
        for copy in near_copies:
            copy.wait_send()

        def returned(tile, inner):
            for example in range(2):
                return_copy(example, tile).wait_send()
            return inner

        lax.fori_loop(0, rows // HALF_TILE, returned, 0)
        outs.wait(("low", "act", "grad", "hidden", "rest", "slot"), (1,))
        outs.wait(("query",), (0, 1))
        outs.wait(("query_w",), (0,))
        for copy in kept:
            copy.wait()

    @pl.when(encoder)
    def _():
        outs.wait(("qkv",), (0, 1))

    outs.wait(("mixed", "logsum", "residual"), (0, 1))


def last_kernel(
    devices, src_len, tgt_len, gains, small_in, inputs, qkv_w, out_w, in_w, out2_w, query_w,
    memory_grad, second_in, slope_in, query_grad, rest_in, residual_in, qkv_in, logsum_in, mixed_in,
    low_in, act_in, grad_in, hidden_in, branch_a, qkv_grad_a, own_extra, sent_extra, first_total,
    second_total, cross_total, small_total, rows_out, qkv_w_s, out_w_s, in_w_s, out2_w_s, low_s,
    hidden_s, act_s, grad_s, mixed_s, branch_s, x_s, qkv_grad_s, memory_s, second_s, slope_s,
    back_s, query_w_s, residual_s, qkv_s, logsum_s, rest_s, attn_grad_s, small_s, small_arrived,
    cross_total_s, small_send, small_recv, small_cross_sem, semaphores, *ring_refs,
):
    mixed_a, mixed_b = mixed_in.at[0], mixed_in.at[1]
    low_a, low_b = low_in.at[0], low_in.at[1]
    act_a, act_b = act_in.at[0], act_in.at[1]
    grad_a, grad_b = grad_in.at[0], grad_in.at[1]
    hidden_a, hidden_b = hidden_in.at[0], hidden_in.at[1]
    links = Links(devices)
    links.greet()
    chips, levels = links.chips, links.levels
    section = links.pipe
    rows, width = residual_s.shape
    half = width // 2
    hidden = hidden_s.shape[1]
    hidden_blocks = hidden // width
    extra_rows = own_extra.shape[0]
    sizes = (2 * hidden, 4 * width, extra_rows)
    layouts = [ring_layout(size, devices) for size in sizes]
    early = Ring(links, layouts[0], act_s, ring_refs[:11])
    late = Ring(links, layouts[1], out2_w_s, ring_refs[11:22])
    cross = CrossRing(links, layouts[2], cross_total_s, ring_refs[22:33], ring_refs[33:])
    front, rear = pl.ds(0, rows), pl.ds(rows, rows)
    gain_first, gain_last = wide_row(gains, 0), wide_row(gains, 1)
    small_s[0] = small_in[...]
    partial = small_arrived.at[0]
    partial[...] = jnp.zeros_like(small_in)

    encoder = section == 0
    copies = Copies(semaphores)

    def declared(source, target):
        copy = pltpu.make_async_copy(source, target, semaphores.at[copies.count])
        copies.count += 1
        return copy

    def start(*group):
        for copy in group:
            copy.start()

    def wait(*group):
        for copy in group:
            copy.wait()

    hidden_front = [declared(low_a, low_s.at[front]), declared(low_b, low_s.at[rear]),
                    declared(hidden_a, hidden_s.at[front])]
    act_front = [declared(grad_a, grad_s.at[front])]
    for index in range(hidden_blocks):
        columns = pl.ds(index * width, width)
        act_front.append(declared(act_a.at[:, columns], act_s.at[index, front]))
        act_front.append(declared(act_b.at[:, columns], act_s.at[index, rear]))
    hidden_rear = declared(hidden_b, hidden_s.at[rear])
    grad_rear = declared(grad_b, grad_s.at[rear])
    back_inputs = [declared(memory_grad, memory_s), declared(second_in, second_s),
                   declared(slope_in, slope_s), declared(out2_w.at[0], out2_w_s),
                   declared(in_w.at[0], in_w_s)]
    query_weights = [declared(query_w, query_w_s)]
    out_w_copy = declared(out_w.at[0], out_w_s)
    qkv_w_copy = declared(qkv_w.at[0], qkv_w_s)
    mixed_copies = [declared(mixed_a, mixed_s.at[front]), declared(mixed_b, mixed_s.at[rear])]
    saved = []
    base = copies.count
    for example in range(2):
        copies.count = base
        parts = [
            ref.at[example] for ref in (residual_in, query_grad, rest_in, qkv_in, logsum_in)
        ]
        targets = (residual_s, memory_s, second_s, qkv_s, logsum_s)
        saved.append([declared(source, target) for source, target in zip(parts, targets)])
    encoder_inputs = [declared(branch_a, branch_s.at[front]),
                      declared(qkv_grad_a, qkv_grad_s.at[front])]
    inputs_copy = declared(inputs.at[0], x_s)
    extra_loads = [declared(own_extra, cross.mine.at[pl.ds(0, extra_rows)]),
                   declared(sent_extra, cross.foreign.at[pl.ds(0, extra_rows)])]
    if cross.mine.shape[0] > extra_rows:
        cross.mine[extra_rows:] = jnp.zeros_like(cross.mine[extra_rows:])
        cross.foreign[extra_rows:] = jnp.zeros_like(cross.foreign[extra_rows:])

    def rows_copy(example):
        spot = pl.ds(pl.multiple_of(example * rows, rows), rows)
        return pltpu.make_async_copy(rest_s, rows_out.at[spot], semaphores.at[copies.count])

    @pl.when(encoder)
    def _():
        start(*back_inputs, *hidden_front, *act_front, out_w_copy, qkv_w_copy, *mixed_copies,
              *encoder_inputs, inputs_copy)
        wait(*back_inputs[:2])
        row = lax.broadcasted_iota(jnp.int32, (rows, width), 0)
        rest_s[...] = jnp.where(row < src_len[1], memory_s[...].astype(WIDE), 0.0)
        norm_back_rolled(
            second_s, gain_last, rest_s, second_s, grad_s.at[rear],
            partial.at[6:7, :], partial.at[8:9, :],
        )
        partial[4:5, :] = column_sum(grad_s[rear].astype(WIDE))
        wait(*back_inputs[2:])
        feed_back_rolled(
            second_s, grad_s.at[rear], slope_s, in_w_s, out2_w_s, hidden_s.at[rear],
            partial.at[0:4, :], back_s,
        )
        start(saved[1][0], *saved[1][3:])

    @pl.when(section == 1)
    def _():
        start(*hidden_front, hidden_rear, *act_front, grad_rear, *saved[0], *query_weights,
              out_w_copy, qkv_w_copy, *mixed_copies, *extra_loads, inputs_copy)
        wait(hidden_rear, grad_rear)

    def blocks(target, begin, count, block):
        def step(index, carry):
            target[columns_of(begin + index, width), :] = block(index).astype(LOW)
            return carry

        lax.fori_loop(0, count, step, 0)

    wait(*hidden_front)
    blocks(
        early.mine, 0, hidden_blocks,
        lambda index: product(low_s[...], hidden_s[:, columns_of(index, width)], 0, 0),
    )
    wait(*act_front)
    blocks(
        early.mine, hidden_blocks, hidden_blocks,
        lambda index: product(act_s[index], grad_s[...], 0, 0),
    )
    links.greeted()
    small_cross = links.copy(
        small_s.at[levels], small_arrived.at[1], small_cross_sem.at[0], small_cross_sem.at[1],
        links.across,
    )

    @pl.when(section == 1)
    def _():
        small_s[levels, 0:1, :] = jnp.concatenate(
            [small_s[0, 9:10, :half], small_s[0, 10:11, :half]], axis=1
        )
        small_cross.start()
        wait(*extra_loads)
        cross.foreign_start()

    early.begin()

    @pl.when(section == 1)
    def _():
        cross.foreign_pass()

    cross.begin()
    per_example = 6
    final = 2 * chips - 3
    middle = max(1, early.count // 2)
    begin_at = jnp.where(encoder, 1, 0)
    @pl.when(section == 1)
    def _():
        wait(*query_weights)

    wait(out_w_copy, qkv_w_copy, *mixed_copies)

    def advance(first, count):
        def half_turn(half, carry):
            turn, odd = lax.div(half, 2), lax.rem(half, 2)
            parts = (odd * middle, jnp.where(odd == 1, early.count, middle))

            @pl.when((turn <= chips - 2) & (odd == 0))
            def _():
                early.pairs_ready(turn + 1)

            @pl.when(turn < chips - 2)
            def _():
                early.reduce(turn, parts)

            @pl.when(turn == chips - 2)
            def _():
                early.settle(parts, odd == 1)

            @pl.when((turn > chips - 2) & (turn < final))
            def _():
                early.gather(turn - (chips - 1), parts, odd == 1)

            @pl.when(turn == final)
            def _():
                early.gather_last(parts, odd == 1)

            @pl.when((turn <= chips - 2) & (odd == 1))
            def _():
                cross.pairs_ready(turn + 1)

            @pl.when((turn < chips - 2) & (odd == 1))
            def _():
                cross.reduce(turn)

            @pl.when((turn == chips - 2) & (odd == 1))
            def _():
                cross.settle()

            @pl.when((turn > chips - 2) & (turn < final) & (odd == 1))
            def _():
                cross.gather(turn - (chips - 1))

            @pl.when((turn == final) & (odd == 1))
            def _():
                cross.gather_last()

            return carry

        lax.fori_loop(first, first + count, half_turn, 0)

    def back_step(example, carry):
        spot = pl.ds(pl.multiple_of(example * rows, rows), rows)
        turn = (example - begin_at) * per_example

        @pl.when(section == 1)
        def _():
            wait(*saved[0][:3])

            def first_step(tile):
                back_s[tile] = second_s[tile] + product(memory_s[tile], query_w_s[...], 1, 1)

            row_tiles(rows, HALF_TILE, first_step)

        @pl.when(encoder)
        def _():
            wait(saved[0][0])

        @pl.when((section == 1) & (example == 1))
        def _():
            rows_copy(0).wait()

        low_branch = branch_s.at[spot]
        norm_back_rows(
            residual_s, gain_first, back_s, rest_s, low_branch,
            partial.at[12:13, :], partial.at[13:14, :],
        )
        partial[5:6, :] += partial[12:13, :]
        partial[7:8, :] += partial[13:14, :]
        attn_grad_s[...] = product(low_branch[...], out_w_s[...], 1, 1).astype(LOW)
        wait(*saved[0][3:])
        advance(turn, 2)
        count = jnp.where(encoder, src_len[example], tgt_len[example])
        attend_back(
            qkv_s.at[:, :width],
            qkv_s.at[:, width : 2 * width],
            qkv_s.at[:, 2 * width :],
            count,
            mixed_s.at[spot],
            logsum_s,
            attn_grad_s,
            qkv_grad_s.at[spot, pl.ds(0, width)],
            qkv_grad_s.at[spot, pl.ds(width, width)],
            qkv_grad_s.at[spot, pl.ds(2 * width, width)],
            after=lambda step: advance(turn + 2 + 2 * step, 2),
        )

        @pl.when(example == 0)
        def _():
            start(*saved[1])

        def rows_step(index, inner):
            tile = pl.ds(pl.multiple_of(index * HALF_TILE, HALF_TILE), HALF_TILE)
            begin = pl.multiple_of(example * rows + index * HALF_TILE, HALF_TILE)
            rest_s[tile] += product(qkv_grad_s[pl.ds(begin, HALF_TILE)], qkv_w_s[...], 1, 1)
            return inner

        lax.fori_loop(0, rows // HALF_TILE, rows_step, 0)
        rows_copy(example).start()
        return carry

    lax.fori_loop(begin_at, 2, back_step, 0)
    wait(inputs_copy)

    @pl.when(encoder)
    def _():
        wait(*encoder_inputs)

    blocks(
        late.mine, 0, 3,
        lambda index: product(x_s[...], qkv_grad_s[:, columns_of(index, width)], 0, 0),
    )
    done = (2 - begin_at) * per_example
    advance(done, 2)
    blocks(late.mine, 3, 1, lambda index: product(mixed_s[...], branch_s[...], 0, 0))

    if late.mine.shape[0] > 4 * width:
        late.mine[4 * width :] = jnp.zeros_like(late.mine[4 * width :])
    late.begin()
    advance(done + 2, 2)
    done = done + 4
    ahead = jnp.where(encoder, 2, 1)

    small_s[0] = small_s[0] + partial[...]
    @pl.when(section == 1)
    def _():
        small_s[0, 9:10, :] = jnp.concatenate(
            [small_s[0, 9:10, half:], small_s[0, 10:11, half:]], axis=1
        )
        small_cross.wait_send()

    @pl.when(encoder)
    def _():
        small_cross.wait_recv()
        small_s[0, 9:10, :] = small_arrived[1, 0:1, :]

    def small_copy(level, bit):
        return links.copy(
            small_s.at[level],
            small_arrived.at[level + 2],
            small_send.at[level],
            small_recv.at[level],
            links.paired(bit),
        )

    small_copy(0, 1).start()

    def merge_small(level, bit):
        small_copy(level, bit).wait_recv()
        merged = small_s[level] + small_arrived[level + 2]

        @pl.when(level + 1 < levels)
        def _():
            small_s[level + 1] = merged
            small_copy(level + 1, 2 * bit).start()

        @pl.when(level + 1 == levels)
        def _():
            small_total[...] = merged

    def both_step(step, bit):
        late.pairs_ready(step + 1)
        late.reduce(step)
        advance(done + ahead * step, ahead)

        @pl.when(step < levels)
        def _():
            merge_small(step, bit)

        return 2 * bit

    lax.fori_loop(0, chips - 2, both_step, 1)
    late.pairs_ready(chips - 1)
    late.settle()
    done = done + ahead * (chips - 2)

    def late_step(step, carry):
        late.gather(step)
        advance(done + step, 1)
        return carry

    lax.fori_loop(0, chips - 2, late_step, 0)
    done = done + chips - 2
    advance(done, jnp.maximum(2 * final + 2 - done, 0))
    late.gather_last()
    late.finish()
    cross.finish()
    kept = [
        pltpu.make_async_copy(
            out2_w_s.at[pl.ds(0, second_total.shape[0])], second_total, semaphores.at[0]
        ),
        pltpu.make_async_copy(cross_total_s, cross_total, semaphores.at[1]),
    ]
    for index in range(hidden_blocks):
        kept.append(
            pltpu.make_async_copy(
                act_s.at[index], first_total.at[pl.ds(index * 2 * rows, 2 * rows)],
                semaphores.at[2 + index],
            )
        )
    start(*kept[:2])
    early.finish()
    start(*kept[2:])
    wait(*kept)
    for level in range(levels):
        small_copy(level, 1 << level).wait_send()
    rows_copy(1).wait()


def result_kernel(
    small_total, first_total, second_total, cross_total, rows_in, block_in,
    rows_buffer, block_out, rows_out, qkv_out, out_out,
    in_out, out2_out, cross_qkv_out, cross_out_out, slot_out, in_b_out, out2_b_out, gain_out,
    bias_out, cross_gain_out, cross_bias_out, first_s, second_s, rows_s, block_s,
    wide_s, semaphores,
):
    width = first_s.shape[1]
    half = width // 2
    for index in range(in_b_out.shape[1] // width):
        in_b_out[:, index * width : (index + 1) * width] = small_total[index : index + 1, :]
    out2_b_out[...] = small_total[4:5, :]
    gain_out[0] = small_total[5:7, :]
    bias_out[0] = small_total[7:9, :]
    cross_gain_out[...] = small_total[9:10, :half]
    cross_bias_out[...] = small_total[9:10, half:]
    copies = Copies(semaphores)
    rows = rows_in.shape[0] // 2
    front, rear = pl.ds(0, rows), pl.ds(rows, rows)
    rows_copy = copies.start(rows_in.at[rear], rows_s.at[rear])
    front_sem = semaphores.at[copies.count]
    copies.count += 1
    from_last = pltpu.make_async_copy(rows_in.at[front], rows_s.at[front], front_sem)
    from_main = pltpu.make_async_copy(rows_buffer.at[0, front], rows_s.at[front], front_sem)
    pl.when(lax.axis_index("pipe") == 1)(from_last.start)
    pl.when(lax.axis_index("pipe") == 0)(from_main.start)
    block_copy = copies.start(block_in.at[0], block_s)
    rows = rows_in.shape[0] // 2
    kept = []
    loads = {width: [], half: []}
    second_rows = 4 * width
    for index in range(first_s.shape[0] // width):
        spot = pl.ds(index * width, width)
        loads[width].append(copies.start(first_total.at[spot], first_s.at[spot]))
    for index in range(second_s.shape[0] // half):
        begin = index * half
        if begin < second_rows:
            source = second_total.at[pl.ds(begin, half)]
        else:
            source = cross_total.at[pl.ds(begin - second_rows, half)]
        loads[half].append(copies.start(source, second_s.at[pl.ds(begin, half)]))
    targets = []
    for index in range(first_s.shape[0] // width):
        hidden_blocks = in_out.shape[2] // width
        if index < hidden_blocks:
            target = in_out.at[0, :, pl.ds(index * width, width)]
        else:
            target = out2_out.at[0, pl.ds((index - hidden_blocks) * width, width)]
        targets.append((loads[width][index : index + 1], first_s, index * width, width, target))
    for index in range(4):
        if index < 3:
            target = qkv_out.at[0, :, pl.ds(index * width, width)]
        else:
            target = out_out.at[0]
        targets.append(
            (loads[half][2 * index : 2 * index + 2], second_s, index * width, width, target)
        )
    for index in range(4):
        if index < 3:
            target = cross_qkv_out.at[:, pl.ds(index * width, width)]
        else:
            target = cross_out_out
        targets.append(
            (loads[half][8 + index : 9 + index], second_s, 4 * width + index * half, half, target)
        )
    targets.append((loads[half][12:14], second_s, 6 * width, width, slot_out))
    place = 0
    for waits, stage, begin, size, target in targets:
        for copy in waits:
            copy.wait()
        wide_s[place : place + size] = stage[begin : begin + size].astype(WIDE)
        kept.append(copies.start(wide_s.at[pl.ds(place, size)], target))
        place += size
    block_copy.wait()
    kept.append(copies.start(block_s, block_out.at[0]))
    rows_copy.wait()
    from_last.wait()
    kept.append(copies.start(rows_s, rows_out.at[0]))
    for copy in kept:
        copy.wait()


ANY = pl.BlockSpec(memory_space=pl.ANY)
INNER = pl.BlockSpec(memory_space=pltpu.VMEM)
SCALAR = pl.BlockSpec(memory_space=pltpu.SMEM)


def local_call(
    body, name, scalars, inner, outer, outputs, scratch, flops, aliases=None, count=32,
    semaphores=(), **compiler,
):
    shapes = [jax.ShapeDtypeStruct(shape, kind) for shape, kind, _ in outputs]
    inputs = list(scalars) + list(inner) + list(outer)
    specs = [SCALAR] * len(scalars) + [INNER] * len(inner) + [ANY] * len(outer)
    moved = sum(value.size * value.dtype.itemsize for value in inputs)
    return pl.pallas_call(
        body,
        out_shape=shapes,
        in_specs=specs,
        out_specs=[INNER if kept else ANY for _, _, kept in outputs],
        scratch_shapes=[pltpu.VMEM(shape, kind) for shape, kind in scratch]
        + list(semaphores or [pltpu.SemaphoreType.DMA((count,))]),
        input_output_aliases=aliases or {},
        compiler_params=pltpu.CompilerParams(vmem_limit_bytes=VMEM_LIMIT, **compiler),
        cost_estimate=pl.CostEstimate(flops=flops, bytes_accessed=moved, transcendentals=0),
        name=name,
    )(*inputs)


def local(
    inputs, src_len, tgt_len, cotangent, qkv_w, out_w, in_w, in_b, out2_w, out2_b, norm_gain,
    norm_bias, cross_qkv, cross_out, slot_w, cross_gain, cross_bias,
):
    devices = lax.axis_size("dp")
    blocks = src_len.shape[0]
    total_rows, width = inputs.shape[1:]
    rows = total_rows // blocks
    half = width // 2
    hidden = in_w.shape[2]
    square, wide3, deep = (rows, width), (rows, 3 * width), (rows, hidden)
    weight_square, logsum = (width, width), (rows, PAIR)
    tall, tall3, tall_deep = (total_rows, width), (total_rows, 3 * width), (total_rows, hidden)
    extra_rows = 3 * width
    small_shape = (SMALL_ROWS, width)
    dma = pltpu.SemaphoreType.DMA
    tiles, halves = rows // ROW_TILE, rows // HALF_TILE

    (
        small, block_out, qkv, logsums, mixed, residual, low, act, slope, second, grad, hidden_grad,
        branch, qkv_grad, source_rows, query_grad, rest, memory_grad, query_w, own_extra,
        sent_extra,
    ) = local_call(
        main_kernel, "main_rows", [src_len, tgt_len],
        [
            in_b, out2_b, norm_gain, norm_bias, cross_gain, cross_bias,
        ],
        [inputs, cotangent, qkv_w, out_w, in_w, out2_w, cross_qkv, cross_out, slot_w],
        [
            (small_shape, WIDE, True), ((1,) + tall, LOW, False), ((2,) + wide3, LOW, False),
            ((2,) + logsum, WIDE, False), ((2,) + square, LOW, False), ((2,) + square, WIDE, False),
            ((2,) + square, LOW, False), ((2,) + deep, LOW, False), (deep, LOW, False),
            (square, WIDE, False), ((2,) + square, LOW, False), ((2,) + deep, LOW, False),
            (square, LOW, False), (wide3, LOW, False), ((1,) + tall, WIDE, False),
            ((2,) + square, LOW, False), ((2,) + square, WIDE, False), (square, LOW, False),
            (weight_square, LOW, False), ((extra_rows, width), LOW, False),
            ((extra_rows, width), LOW, False),
        ],
        [
            (tall, LOW), ((width, 3 * width), LOW), (weight_square, LOW), ((width, hidden), LOW),
            ((hidden, width), LOW), ((width, 3 * width), LOW), (weight_square, LOW),
            ((2 * width, width), LOW), (small_shape, LOW), ((2,) + wide3, LOW),
            ((2,) + logsum, WIDE), ((2,) + square, LOW), ((2,) + square, WIDE), (square, WIDE),
            (square, LOW), (deep, LOW), ((2,) + deep, LOW), ((2,) + square, WIDE), (tall, LOW),
            (tall, LOW), (square, LOW), ((rows, 2 * width), LOW), (tall, LOW), (logsum, WIDE),
            (square, WIDE), (tall, LOW), (tall, LOW), (tall, LOW), (square, LOW), (square, WIDE),
            (square, LOW), (deep, LOW), (square, WIDE), (square, WIDE), (tall, LOW), (square, LOW),
            (tall, LOW), ((total_rows, 2 * width), LOW), ((2,) + square, LOW), (wide3, LOW),
            (small_shape, WIDE),
        ],
        70 * 10**9,
        semaphores=[
            dma((16,)), dma((2, 24)), dma((2, tiles)), dma((2, tiles)), dma((2, halves)),
            dma((2, halves)), dma((4,)), dma((4,)), dma((3,)), dma((3,)),
        ],
        collective_id=1, has_side_effects=True,
    )

    sizes = (2 * hidden, 4 * width, extra_rows)
    padded = [ring_rows(size, devices) for size in sizes]
    levels = devices.bit_length() - 1
    rings = [part for size in sizes for part in ring_scratch(size, width, devices)]
    rings += foreign_scratch(extra_rows, width, devices)
    first_total, second_total, cross_total, small_total, last_rows = local_call(
        functools.partial(last_kernel, devices), "last_rows", [src_len, tgt_len],
        [norm_gain, small],
        [
            inputs, qkv_w, out_w, in_w, out2_w, query_w, memory_grad, second, slope, query_grad,
            rest, residual, qkv, logsums, mixed, low, act, grad, hidden_grad, branch, qkv_grad,
            own_extra, sent_extra,
        ],
        [
            ((padded[0], width), LOW, False),
            ((padded[1], width), LOW, False),
            ((padded[2], width), LOW, False),
            (small_shape, WIDE, True),
            (tall, WIDE, False),
        ],
        [
            ((width, 3 * width), LOW), (weight_square, LOW), ((width, hidden), LOW),
            ((hidden, width), LOW), (tall, LOW), (tall_deep, LOW),
            ((hidden // width,) + tall, LOW), (tall, LOW), (tall, LOW), (tall, LOW), (tall, LOW),
            (tall3, LOW), (square, LOW), (square, WIDE), (deep, LOW), (square, WIDE),
            (weight_square, LOW), (square, WIDE), (wide3, LOW), (logsum, WIDE), (square, WIDE),
            (square, LOW), ((levels + 1,) + small_shape, WIDE), ((levels + 2,) + small_shape, WIDE),
            ((padded[2], width), LOW),
        ],
        20 * 10**9,
        semaphores=[dma((levels,)), dma((levels,)), dma((2,)), dma((64,))] + rings,
        collective_id=0, has_side_effects=True,
    )

    results = local_call(
        result_kernel, "results", [], [small_total],
        [first_total, second_total, cross_total, last_rows, block_out, source_rows],
        [
            ((1,) + tall, LOW, False), ((1,) + tall, WIDE, False),
            ((1, width, 3 * width), WIDE, False),
            ((1,) + weight_square, WIDE, False), ((1, width, hidden), WIDE, False),
            ((1, hidden, width), WIDE, False), ((half, 3 * width), WIDE, False),
            ((half, width), WIDE, False), ((width, width), WIDE, False),
            ((1, hidden), WIDE, True), ((1, width), WIDE, True), ((1, 2, width), WIDE, True),
            ((1, 2, width), WIDE, True), ((1, half), WIDE, True), ((1, half), WIDE, True),
        ],
        [
            ((sizes[0], width), LOW), ((sizes[1] + sizes[2], width), LOW), (tall, WIDE),
            (tall, LOW), ((sum(sizes), width), WIDE),
        ],
        10**9, count=64,
    )
    return (
        results[0], results[1], results[2], results[3], results[4], results[9], results[5],
        results[10], results[11], results[12], results[6], results[7], results[8],
        results[13].reshape(half), results[14].reshape(half),
    )


def solution(mesh):
    in_specs = (
        P("pipe", "dp", None),
        P("dp"),
        P("dp"),
        P("dp", None),
        P("pipe", None, None),
        P("pipe", None, None),
        P("pipe", None, None),
        P("pipe", None),
        P("pipe", None, None),
        P("pipe", None),
        P("pipe", None, None),
        P("pipe", None, None),
        P("pipe", None),
        P("pipe", None),
        P("pipe", None),
        P("pipe"),
        P("pipe"),
    )
    out_specs = (
        P("pipe", "dp", None),
        P("pipe", "dp", None),
        P("pipe", None, None),
        P("pipe", None, None),
        P("pipe", None, None),
        P("pipe", None),
        P("pipe", None, None),
        P("pipe", None),
        P("pipe", None, None),
        P("pipe", None, None),
        P("pipe", None),
        P("pipe", None),
        P("pipe", None),
        P("pipe"),
        P("pipe"),
    )
    return jax.shard_map(local, mesh=mesh, in_specs=in_specs, out_specs=out_specs, check_vma=False)
```

```python
import functools

import jax
import jax.numpy as jnp
from jax import lax
from jax.experimental import pallas as pl
from jax.experimental.pallas import tpu as pltpu
from jax.sharding import PartitionSpec as P

HEADS = 8
LOW = jnp.bfloat16
WIDE = jnp.float32
HEAD_SIZE = 64
PAIR = 2 * HEAD_SIZE
GELU_SCALE = 0.7978845608
GELU_CUBE = 0.044715
MASKED = -1e30
VMEM_LIMIT = 60 * 2**20


def product(left, right, left_dim=1, right_dim=0):
    return lax.dot_general(
        left, right, (((left_dim,), (right_dim,)), ((), ())), preferred_element_type=WIDE
    )


class Copies:
    def __init__(self, semaphores):
        self.semaphores = semaphores
        self.count = 0

    def start(self, source, target):
        copy = pltpu.make_async_copy(source, target, self.semaphores.at[self.count])
        self.count += 1
        copy.start()
        return copy


def pair_columns(pair):
    return pl.ds(pl.multiple_of(pair * PAIR, PAIR), PAIR)


def lanes(rows):
    return lax.broadcasted_iota(jnp.int32, (rows, PAIR), 1)


def split_three(column):
    high = column.astype(LOW).astype(WIDE)
    rest = column - high
    middle = rest.astype(LOW).astype(WIDE)
    return high, middle, rest - middle


def key_side(keys, head, bias, lane):
    base = HEAD_SIZE * (1 - head)
    own = lane // HEAD_SIZE == head
    extra = jnp.where(lane == base, bias, jnp.where((lane > base) & (lane < base + 4), 1.0, 0.0))
    return jnp.where(own, keys, extra).astype(LOW)


def attend(query_ref, key_ref, value_ref, count, mixed_ref, logsum_ref, tile=256):
    rows = query_ref.shape[0]
    lane = lanes(rows)
    row = lax.broadcasted_iota(jnp.int32, (rows, PAIR), 0)
    bias = jnp.where(row < count, 0.0, MASKED)
    tile_lane = lanes(tile)
    tiles = range(rows // tile)
    spots = [slice(index * tile, (index + 1) * tile) for index in tiles]
    logsums = [jnp.zeros((tile, PAIR), WIDE) for _ in tiles]
    sides, scores, weights, mixed = {}, {}, {}, {}

    def prepare(index):
        columns = pl.ds(index // 2 * PAIR, PAIR)
        head = index % 2
        own = lane // HEAD_SIZE == head
        one = jnp.where(lane == HEAD_SIZE * (1 - head), 1.0, 0.0)
        queries = query_ref[:, columns].astype(WIDE) * HEAD_SIZE**-0.5
        return (
            jnp.where(own, queries, one).astype(LOW),
            key_side(key_ref[:, columns].astype(WIDE), head, bias, lane),
            jnp.where(own, value_ref[:, columns].astype(WIDE), one).astype(LOW),
        )

    for turn in range(HEADS + 2):
        if turn < HEADS:
            sides[turn] = prepare(turn)
        for place in tiles:
            if turn < HEADS:
                scores[turn, place] = product(sides[turn][0][spots[place]], sides[turn][1], 1, 1)
            index = turn - 1
            if 0 <= index < HEADS:
                block = scores.pop((index, place))
                top = jnp.max(block, axis=1, keepdims=True)
                weights[index, place] = (jnp.exp(block - top).astype(LOW), top)
            index = turn - 2
            if 0 <= index < HEADS:
                block, top = weights.pop((index, place))
                base = HEAD_SIZE * (1 - index % 2)
                summed = product(block, sides[index][2])
                total = summed[:, base : base + 1]
                mixed[index, place] = summed * (1.0 / total)
                logsums[place] = jnp.where(
                    tile_lane == index, top + jnp.log(total), logsums[place]
                )
                if index % 2:
                    mixed_ref[spots[place], pl.ds(index // 2 * PAIR, PAIR)] = jnp.where(
                        tile_lane < HEAD_SIZE, mixed.pop((index - 1, place)),
                        mixed.pop((index, place)),
                    ).astype(LOW)
    for place in tiles:
        logsum_ref[spots[place]] = logsums[place]


def attend_back(
    query_ref, key_ref, value_ref, count, mixed_ref, logsum_ref, grad_ref,
    query_grad_ref, key_grad_ref, value_grad_ref, tile=512, after=None,
):
    rows = query_ref.shape[0]
    lane = lanes(rows)
    row = lax.broadcasted_iota(jnp.int32, (rows, PAIR), 0)
    bias = jnp.where(row < count, 0.0, MASKED)

    def pair_step(pair):
        columns = pair_columns(pair)
        queries = query_ref[:, columns].astype(WIDE) * HEAD_SIZE**-0.5
        keys = key_ref[:, columns].astype(WIDE)
        values = value_ref[:, columns].astype(WIDE)
        grads = grad_ref[:, columns].astype(WIDE)
        along = grads * mixed_ref[:, columns].astype(WIDE)
        logsums = logsum_ref[...]
        query_sum = []
        key_parts = []
        value_parts = []
        for head in range(2):
            base = HEAD_SIZE * (1 - head)
            own = lane // HEAD_SIZE == head
            column = jnp.sum(
                jnp.where(lane == 2 * pair + head, logsums, 0.0), axis=1, keepdims=True
            )
            inner = jnp.sum(jnp.where(own, along, 0.0), axis=1, keepdims=True)
            query_side = jnp.where(own, queries, jnp.where(lane == base, 1.0, 0.0))
            grad_side = jnp.where(own, grads, 0.0)
            for place, part in enumerate(split_three(column)):
                query_side = jnp.where(lane == base + 1 + place, -part, query_side)
            for place, part in enumerate(split_three(inner)):
                grad_side = jnp.where(lane == base + 1 + place, -part, grad_side)
            query_side = query_side.astype(LOW)
            grad_side = grad_side.astype(LOW)
            keys_side = key_side(keys, head, bias, lane)
            value_side = key_side(values, head, 0.0, lane)
            query_total = None
            for begin in range(0, rows, tile):
                spot = slice(begin, begin + tile)
                probs = jnp.exp(product(keys_side[spot], query_side, 1, 1))
                slopes = (probs * product(value_side[spot], grad_side, 1, 1)).astype(LOW)
                value_part = product(probs.astype(LOW), grad_side)
                key_part = product(slopes, query_side)
                query_part = product(slopes, keys_side[spot], 0, 0)
                query_total = query_part if query_total is None else query_total + query_part
                key_parts.append(key_part)
                value_parts.append(value_part)
            query_sum.append(query_total)
        query_grad_ref[:, columns] = (
            jnp.where(lane < HEAD_SIZE, query_sum[0], query_sum[1]) * HEAD_SIZE**-0.5
        ).astype(LOW)
        pieces = rows // tile
        for piece in range(pieces):
            spot = slice(piece * tile, (piece + 1) * tile)
            first = lane[:tile] < HEAD_SIZE
            key_grad_ref[spot, columns] = jnp.where(
                first, key_parts[piece], key_parts[pieces + piece]
            ).astype(LOW)
            value_grad_ref[spot, columns] = jnp.where(
                first, value_parts[piece], value_parts[pieces + piece]
            ).astype(LOW)

    def pairs_step(step, carry):
        for place in range(2):
            pair_step(2 * step + place)
        if after is not None:
            after(step)
        return carry

    lax.fori_loop(0, HEADS // 4, pairs_step, 0)


def normed(values):
    shifted = values - jnp.mean(values, axis=1, keepdims=True)
    scale = lax.rsqrt(jnp.mean(shifted * shifted, axis=1, keepdims=True) + 1e-05)
    return shifted * scale, scale


def norm(values, gain, bias):
    return normed(values)[0] * gain + bias


def norm_back(values, gain, grad):
    unit, scale = normed(values)
    inner = grad * gain
    back = scale * (
        inner
        - jnp.mean(inner, axis=1, keepdims=True)
        - unit * jnp.mean(inner * unit, axis=1, keepdims=True)
    )
    return back, column_sum(grad * unit), column_sum(grad)


def column_sum(values):
    return jnp.sum(values, axis=0, keepdims=True)


def row_tiles(rows, tile, body):
    def step(index, carry):
        body(pl.ds(pl.multiple_of(index * tile, tile), tile))
        return carry

    lax.fori_loop(0, rows // tile, step, 0)


def gelu_pair(value):
    square = value * value
    half = 0.5 * jnp.tanh(value * (GELU_SCALE + (GELU_SCALE * GELU_CUBE) * square)) + 0.5
    act = value * half
    slope = half + act * (1.0 - half) * (
        2.0 * GELU_SCALE + (6.0 * GELU_SCALE * GELU_CUBE) * square
    )
    return act, slope


SMALL_ROWS = 16
ROW_TILE = 128
HALF_TILE = 256


def columns_of(index, width):
    return pl.ds(pl.multiple_of(index * width, width), width)


def project(left_ref, right_ref, target_ref, width):
    def step(index, carry):
        columns = columns_of(index, width)
        target_ref[:, columns] = product(left_ref[...], right_ref[:, columns]).astype(LOW)
        return carry

    lax.fori_loop(0, target_ref.shape[1] // width, step, 0)


def wide_row(ref, row):
    return ref[0, row : row + 1, :].astype(WIDE)


def feed_forward(low_ref, wide_ref, in_w, in_b, out2_w, out2_b, act_ref, slope_ref, residual_ref):
    rows, width = low_ref.shape

    for index in range(act_ref.shape[1] // width):
        columns = pl.ds(index * width, width)
        bias = in_b[:, columns].astype(WIDE)
        for begin in range(0, rows, HALF_TILE):
            spot = slice(begin, begin + HALF_TILE)
            act, slope = gelu_pair(product(low_ref[spot], in_w[:, columns]) + bias)
            act_ref[spot, columns] = act.astype(LOW)
            slope_ref[spot, columns] = slope.astype(LOW)
    bias_out = out2_b[...].astype(WIDE)
    for begin in range(0, rows, HALF_TILE):
        spot = slice(begin, begin + HALF_TILE)
        residual_ref[spot] = wide_ref[spot] + product(act_ref[spot], out2_w[...]) + bias_out


def feed_back(residual_grad, grad_low, slope_ref, in_w, out2_w, hidden_grad, bias_rows, out_ref):
    rows, width = grad_low.shape

    for index in range(hidden_grad.shape[1] // width):
        columns = pl.ds(index * width, width)
        total = jnp.zeros((1, width), WIDE)
        for begin in range(0, rows, HALF_TILE):
            spot = slice(begin, begin + HALF_TILE)
            grads = product(grad_low[spot], out2_w[columns, :], 1, 1)
            grads = (grads * slope_ref[spot, columns].astype(WIDE)).astype(LOW)
            hidden_grad[spot, columns] = grads
            total = total + column_sum(grads.astype(WIDE))
        bias_rows[index : index + 1, :] = total
    for begin in range(0, rows, HALF_TILE):
        spot = slice(begin, begin + HALF_TILE)
        out_ref[spot] = residual_grad[spot] + product(hidden_grad[spot], in_w[...], 1, 1)


def feed_back_rolled(
    residual_grad, grad_low, slope_ref, in_w, out2_w, hidden_grad, bias_rows, out_ref
):
    rows, width = grad_low.shape

    def hidden_step(index, carry):
        columns = columns_of(index, width)
        grads = product(grad_low[...], out2_w[columns, :], 1, 1)
        grads = (grads * slope_ref[:, columns].astype(WIDE)).astype(LOW)
        hidden_grad[:, columns] = grads
        bias_rows[pl.ds(index, 1), :] = column_sum(grads.astype(WIDE))
        return carry

    lax.fori_loop(0, hidden_grad.shape[1] // width, hidden_step, 0)

    def out_step(spot):
        out_ref[spot] = residual_grad[spot] + product(hidden_grad[spot], in_w[...], 1, 1)

    row_tiles(rows, HALF_TILE, out_step)


def norm_back_rolled(values_ref, gain, grad_ref, wide_ref, low_ref, gain_row, bias_row):
    rows, width = values_ref.shape
    gain_row[...] = jnp.zeros((1, width), WIDE)
    bias_row[...] = jnp.zeros((1, width), WIDE)

    def step(spot):
        back, gain_part, bias_part = norm_back(values_ref[spot], gain, grad_ref[spot])
        wide_ref[spot] = back
        low_ref[spot] = back.astype(LOW)
        gain_row[...] += gain_part
        bias_row[...] += bias_part

    row_tiles(rows, ROW_TILE, step)


def norm_back_rows(values_ref, gain, grad_ref, wide_ref, low_ref, gain_row, bias_row):
    back, gain_part, bias_part = norm_back(values_ref[...], gain, grad_ref[...])
    wide_ref[...] = back
    low_ref[...] = back.astype(LOW)
    gain_row[...] = gain_part
    bias_row[...] = bias_part


MESH = pl.DeviceIdType.MESH


def ring_place(chip, chips):
    half = chip // 2
    return jnp.where(chip % 2 == 0, half, chips - 1 - half)


def ring_chip(place, chips):
    return jnp.where(place < chips // 2, 2 * place, 2 * (chips - 1 - place) + 1)


def part_count(chunk_rows):
    tiles = chunk_rows // 16
    return 2 if tiles % 4 == 0 else 1


def ring_layout(rows, devices):
    chips = devices // 2
    ways = 2 if rows >= 64 * chips else 1
    return ways, chips, -(-rows // (2 * ways * chips * 16)) * 16


def ring_rows(rows, devices):
    ways, chips, chunk_rows = ring_layout(rows, devices)
    return 2 * ways * chips * chunk_rows


def whenever(flag):
    return pl.when(flag) if not isinstance(flag, bool) else lambda body: body()


class Links:
    def __init__(self, devices):
        self.pipe = lax.axis_index("pipe")
        self.me = lax.axis_index("dp")
        self.chips = devices // 2
        self.levels = devices.bit_length() - 1
        self.core = self.me % 2
        self.place = ring_place(self.me // 2, self.chips)
        self.sides = tuple(
            ring_chip((self.place + step) % self.chips, self.chips) * 2 + self.core
            for step in (1, self.chips - 1)
        )
        self.other = self.paired(1)
        self.across = (1 - self.pipe, self.me)

    def paired(self, bit):
        return self.me + bit - 2 * bit * ((self.me // bit) % 2)

    def greet(self):
        barrier = pltpu.get_barrier_semaphore()
        greeted = list(self.sides) + [self.paired(1 << level) for level in range(self.levels)]
        for friend in greeted:
            pl.semaphore_signal(
                barrier, inc=1, device_id=(self.pipe, friend), device_id_type=MESH
            )
        pl.semaphore_signal(barrier, inc=1, device_id=self.across, device_id_type=MESH)

    def greeted(self):
        pl.semaphore_wait(pltpu.get_barrier_semaphore(), self.levels + 3)

    def copy(self, source, target, send, recv, friend):
        return pltpu.make_async_remote_copy(
            src_ref=source,
            dst_ref=target,
            send_sem=send,
            recv_sem=recv,
            device_id=friend if isinstance(friend, tuple) else (self.pipe, friend),
            device_id_type=MESH,
        )


class Ring:
    def __init__(self, links, layout, total, refs):
        self.links = links
        ways, self.chips, self.chunk_rows = layout
        self.ways = range(ways)
        self.count = part_count(self.chunk_rows)
        self.part_rows = self.chunk_rows // self.count
        self.total = total
        (
            self.mine, self.sibling, self.arrived, self.pair_send, self.pair_recv, self.ring_send,
            self.ring_recv, self.gather_send, self.gather_recv, self.share_send, self.share_recv,
        ) = refs

    def part_at(self, part):
        return pl.ds(pl.multiple_of(part * self.part_rows, 16), self.part_rows)

    def over(self, parts, body):
        low, high = (0, self.count) if parts is None else parts

        def step(part, carry):
            for way in self.ways:
                body(way, part)
            return carry

        lax.fori_loop(low, high, step, 0)

    def chunk_at(self, way, step):
        if way == 0:
            return lax.rem(self.links.place - step + 2 * self.chips, self.chips)
        return lax.rem(self.links.place + step + self.chips, self.chips)

    def start_row(self, core, way, chunk, part):
        begin = 0 if part is None else part * self.part_rows
        return ((core * len(self.ways) + way) * self.chips + chunk) * self.chunk_rows + begin

    def mine_at(self, core, way, chunk, part=None):
        rows = self.chunk_rows if part is None else self.part_rows
        return pl.ds(pl.multiple_of(self.start_row(core, way, chunk, part), 16), rows)

    def total_at(self, way, step, part):
        start = self.start_row(self.links.core, way, self.chunk_at(way, step), part)
        rows = self.part_rows
        if len(self.total.shape) == 2:
            return self.total.at[pl.ds(pl.multiple_of(start, 16), rows)]
        size = self.total.shape[1]
        return self.total.at[
            lax.div(start, size), pl.ds(pl.multiple_of(lax.rem(start, size), 16), rows)
        ]

    def pair_copy(self, way, step, mine=None, sibling=None, send=None, recv=None):
        chunk = self.chunk_at(way, step)
        return self.links.copy(
            (self.mine if mine is None else mine).at[
                self.mine_at(1 - self.links.core, way, chunk)
            ],
            (self.sibling if sibling is None else sibling).at[way, chunk],
            (self.pair_send if send is None else send).at[way, step],
            (self.pair_recv if recv is None else recv).at[way, step],
            self.links.other,
        )

    def ring_copy(self, way, step, part):
        spot = self.part_at(part)
        return self.links.copy(
            self.arrived.at[way, step, spot],
            self.arrived.at[way, step + 1, spot],
            self.ring_send.at[way, step, part],
            self.ring_recv.at[way, step, part],
            self.links.sides[way],
        )

    def gather_copy(self, way, step, part):
        spot = self.total_at(way, step - 1, part)
        return self.links.copy(
            spot,
            spot,
            self.gather_send.at[way, step, part],
            self.gather_recv.at[way, step, part],
            self.links.sides[way],
        )

    def share_copy(self, way, step):
        start = self.start_row(self.links.core, way, self.chunk_at(way, step - 1), None)
        rows = self.chunk_rows
        if len(self.total.shape) == 2:
            spot = self.total.at[pl.ds(pl.multiple_of(start, 16), rows)]
        else:
            size = self.total.shape[1]
            spot = self.total.at[
                lax.div(start, size), pl.ds(pl.multiple_of(lax.rem(start, size), 16), rows)
            ]
        return self.links.copy(
            spot, spot, self.share_send.at[way, step], self.share_recv.at[way, step],
            self.links.other,
        )

    def pairs_start(self):
        def start(step, carry):
            for way in self.ways:
                self.pair_copy(way, step).start()
            return carry

        lax.fori_loop(0, self.chips, start, 0)

    def pair_ready(self, way, step):
        self.pair_copy(way, step).wait()

    def begin(self):
        self.pairs_start()
        for way in self.ways:
            self.pair_ready(way, 0)

        def body(way, part):
            spot = self.part_at(part)
            chunk = self.links.place
            own = self.mine[self.mine_at(self.links.core, way, chunk, part)]
            pair = self.sibling[way, chunk, spot]
            self.arrived[way, 0, spot] = (own.astype(WIDE) + pair.astype(WIDE)).astype(LOW)
            self.ring_copy(way, 0, part).start()

        self.over(None, body)

    def merged(self, way, step, part):
        spot = self.part_at(part)
        chunk = self.chunk_at(way, step + 1)
        self.ring_copy(way, step, part).wait()
        own = self.mine[self.mine_at(self.links.core, way, chunk, part)]
        return (
            self.arrived[way, step + 1, spot].astype(WIDE)
            + own.astype(WIDE)
            + self.sibling[way, chunk, spot].astype(WIDE)
        ).astype(LOW)

    def pairs_ready(self, step):
        for way in self.ways:
            self.pair_ready(way, step)

    def reduce(self, step, parts=None):
        def body(way, part):
            self.arrived[way, step + 1, self.part_at(part)] = self.merged(way, step, part)
            self.ring_copy(way, step + 1, part).start()

        self.over(parts, body)

    def settle(self, parts=None, whole=True):
        def body(way, part):
            self.total_at(way, -1, part)[...] = self.merged(way, self.chips - 2, part)
            self.gather_copy(way, 0, part).start()

        self.over(parts, body)

        @whenever(whole)
        def _():
            for way in self.ways:
                self.share_copy(way, 0).start()

    def gather(self, step, parts=None, whole=True):
        def body(way, part):
            self.gather_copy(way, step, part).wait()
            self.gather_copy(way, step + 1, part).start()

        self.over(parts, body)

        @whenever(whole)
        def _():
            for way in self.ways:
                self.share_copy(way, step + 1).start()
                self.share_copy(way, step).wait()

    def gather_last(self, parts=None, whole=True):
        last = self.chips - 2
        self.over(parts, lambda way, part: self.gather_copy(way, last, part).wait())

        @whenever(whole)
        def _():
            for way in self.ways:
                self.share_copy(way, last + 1).start()
                self.share_copy(way, last).wait()

    def finish(self):
        for way in self.ways:
            self.share_copy(way, self.chips - 1).wait()


class CrossRing(Ring):
    def __init__(self, links, layout, total, refs, foreign_refs):
        super().__init__(links, layout, total, refs)
        self.foreign, self.foreign_sibling = foreign_refs[:2]
        self.foreign_send, self.foreign_recv, self.cross_send, self.cross_recv = foreign_refs[2:]

    def foreign_pair(self, way, step):
        return self.pair_copy(
            way, step, self.foreign, self.foreign_sibling, self.foreign_send, self.foreign_recv
        )

    def cross_copy(self, way, step):
        spot = self.mine_at(self.links.core, way, self.chunk_at(way, step))
        return self.links.copy(
            self.foreign.at[spot],
            self.mine.at[spot],
            self.cross_send.at[way, step],
            self.cross_recv.at[way, step],
            self.links.across,
        )

    def each(self, body):
        def step_all(step, carry):
            for way in self.ways:
                body(way, step)
            return carry

        lax.fori_loop(0, self.chips, step_all, 0)

    def foreign_start(self):
        self.each(lambda way, step: self.foreign_pair(way, step).start())

    def foreign_pass(self):
        def hand_over(way, step):
            chunk = self.chunk_at(way, step)
            spot = self.mine_at(self.links.core, way, chunk)
            self.foreign_pair(way, step).wait()
            self.foreign[spot] = (
                self.foreign[spot].astype(WIDE) + self.foreign_sibling[way, chunk].astype(WIDE)
            ).astype(LOW)
            self.cross_copy(way, step).start()

        self.each(hand_over)

    def pairs_start(self):
        pl.when(self.links.pipe == 1)(super().pairs_start)

        @pl.when(self.links.pipe == 0)
        def _():
            self.sibling[...] = jnp.zeros_like(self.sibling)

    def pair_ready(self, way, step):
        @pl.when(self.links.pipe == 1)
        def _():
            self.pair_copy(way, step).wait()
            self.cross_copy(way, step).wait_send()

        @pl.when(self.links.pipe == 0)
        def _():
            self.cross_copy(way, step).wait_recv()


def ring_scratch(rows, width, devices):
    ways, chips, chunk_rows = ring_layout(rows, devices)
    pieces = part_count(chunk_rows)
    dma = pltpu.SemaphoreType.DMA
    return [
        pltpu.VMEM((2 * ways * chips * chunk_rows, width), LOW),
        pltpu.VMEM((ways, chips, chunk_rows, width), LOW),
        pltpu.VMEM((ways, chips, chunk_rows, width), LOW),
        dma((ways, chips)),
        dma((ways, chips)),
    ] + [dma((ways, chips, pieces)) for _ in range(4)] + [dma((ways, chips))] * 2


def foreign_scratch(rows, width, devices):
    ways, chips, chunk_rows = ring_layout(rows, devices)
    dma = pltpu.SemaphoreType.DMA
    return [
        pltpu.VMEM((2 * ways * chips * chunk_rows, width), LOW),
        pltpu.VMEM((ways, chips, chunk_rows, width), LOW),
    ] + [dma((ways, chips)) for _ in range(4)]


def flat_row(ref):
    return ref[...].astype(WIDE).reshape(1, ref.shape[0])


class Outs:
    def __init__(self, semaphores, table):
        self.semaphores = semaphores
        self.table = table
        self.order = {name: place for place, name in enumerate(table)}

    def copy(self, name, example):
        source, target = self.table[name](example)
        return pltpu.make_async_copy(
            source, target, self.semaphores.at[example, self.order[name]]
        )

    def start(self, name, example):
        self.copy(name, example).start()

    def free(self, name, example):
        @pl.when(example == 1)
        def _():
            self.copy(name, 0).wait()

    def wait(self, names, examples):
        for name in names:
            for example in examples:
                self.copy(name, example).wait()


def main_kernel(
    src_len, tgt_len, in_b, out2_b, gains, biases, cross_gain, cross_bias, inputs, cotangent,
    qkv_w, out_w, in_w, out2_w, cross_qkv, cross_out, slot_w, small_out, block_out, qkv_out,
    logsum_out, mixed_out, residual_out, low_out, act_out, slope_out, second_out, grad_out,
    hidden_out, branch_out, qkv_grad_out, rows_out, query_out, rest_out, memory_out, query_w_out,
    own_out, sent_out, x_s, qkv_w_s, out_w_s, in_w_s, out2_w_s, cross_w_s, cross_out_s, slot_w_s,
    gains_s, qkv_s, logsum_s, mixed_s, residual_s, wide_s, low_s, act_s, slope_s, second_s,
    left_s, right_s, query_s, pair_s, cross_logsum_s, cross_s, slot_s, wide_grad_s, grad_low_s, hidden_s, back_s, rest_s, attn_grad_s,
    memory_grad_s, qkv_grad_s, part_s, load_sem, out_sem, memory_send,
    memory_recv, return_send, return_recv, weight_send, weight_recv, near_send, near_recv,
):
    section = lax.axis_index("pipe")
    me = lax.axis_index("dp")
    core = lax.rem(me, 2)
    across, other = (1 - section, me), (section, me + 1 - 2 * core)
    encoder, decoder = section == 0, section == 1
    first_s, memory_s, cross_mixed_s, final_s = [left_s.at[place] for place in range(4)]
    query_grad_s, key_grad_s, value_grad_s, branch_s, grad_s, earlier_s = [
        right_s.at[place] for place in range(6)
    ]
    total_rows, width = x_s.shape
    rows = total_rows // 2
    half = width // 2
    part = half // 2
    barrier = pltpu.get_barrier_semaphore()
    for friend in (across, other):
        pl.semaphore_signal(barrier, inc=1, device_id=friend, device_id_type=MESH)

    copies = Copies(load_sem)
    x_copy = copies.start(inputs.at[0], x_s)
    qkv_w_copy = copies.start(qkv_w.at[0], qkv_w_s)
    out_w_copy = copies.start(out_w.at[0], out_w_s)
    in_w_copy = copies.start(in_w.at[0], in_w_s)
    out2_w_copy = copies.start(out2_w.at[0], out2_w_s)
    decoder_loads = [
        pltpu.make_async_copy(source, target, load_sem.at[copies.count + place])
        for place, (source, target) in enumerate(
            (
                (cotangent, grad_s),
                (cross_qkv, cross_w_s.at[pl.ds(half, half)]),
                (cross_out, cross_out_s.at[pl.ds(half, half)]),
                (slot_w, slot_w_s.at[pl.ds(width, width)]),
            )
        )
    ]

    def remote(source, target, send, recv, friend):
        return pltpu.make_async_remote_copy(
            src_ref=source, dst_ref=target, send_sem=send, recv_sem=recv, device_id=friend,
            device_id_type=MESH,
        )

    def piece(rows_each):
        return pl.ds(pl.multiple_of(core * rows_each, rows_each), rows_each)

    weight_pieces = (
        (cross_qkv, cross_w_s, piece(part)),
        (cross_out, cross_out_s, piece(part)),
        (slot_w, slot_w_s, piece(2 * part)),
    )
    gains_copy = remote(gains_s, gains_s, weight_send.at[3], weight_recv.at[3], across)
    weight_copies = [
        remote(source.at[spot], target.at[spot], weight_send.at[place], weight_recv.at[place], across)
        for place, (source, target, spot) in enumerate(weight_pieces)
    ]
    near_copies = [
        remote(target.at[spot], target.at[spot], near_send.at[place], near_recv.at[place], other)
        for place, (_, target, spot) in enumerate(weight_pieces)
    ]

    def memory_copy(example, tile):
        begin = pl.multiple_of(example * rows + tile * ROW_TILE, ROW_TILE)
        block = memory_s.at[pl.ds(begin, ROW_TILE)]
        return remote(
            block, block, memory_send.at[example, tile], memory_recv.at[example, tile], across
        )

    def return_copy(example, tile):
        spot = pl.ds(pl.multiple_of(tile * HALF_TILE, HALF_TILE), HALF_TILE)
        block = memory_grad_s.at[example, spot]
        return remote(
            block, block, return_send.at[example, tile], return_recv.at[example, tile], across
        )

    def rows_of(example):
        return pl.ds(pl.multiple_of(example * rows, rows), rows)

    outs = Outs(
        out_sem,
        {
            "qkv": lambda e: (qkv_s.at[e], qkv_out.at[e]),
            "logsum": lambda e: (logsum_s.at[e], logsum_out.at[e]),
            "mixed": lambda e: (mixed_s.at[e], mixed_out.at[e]),
            "residual": lambda e: (residual_s.at[e], residual_out.at[e]),
            "low": lambda e: (low_s, low_out.at[e]),
            "act": lambda e: (act_s, act_out.at[e]),
            "slope": lambda e: (slope_s.at[e], slope_out),
            "second": lambda e: (second_s.at[e], second_out),
            "memory": lambda e: (memory_s.at[rows_of(e)], block_out.at[0, rows_of(e)]),
            "slot": lambda e: (slot_s, block_out.at[0, rows_of(e)]),
            "grad": lambda e: (grad_low_s, grad_out.at[e]),
            "hidden": lambda e: (hidden_s, hidden_out.at[e]),
            "rest": lambda e: (rest_s, rest_out.at[e]),
            "query": lambda e: (query_grad_s.at[rows_of(e)], query_out.at[e]),
            "branch": lambda e: (branch_s.at[rows_of(e)], branch_out),
            "qkv_grad": lambda e: (qkv_grad_s, qkv_grad_out),
            "rows": lambda e: (back_s, rows_out.at[0, rows_of(e)]),
            "return": lambda e: (memory_grad_s.at[e], memory_out),
            "query_w": lambda e: (cross_w_s.at[:, pl.ds(0, width)], query_w_out),
        },
    )
    small_out[...] = jnp.zeros_like(small_out)
    gain_first, bias_first = wide_row(gains, 0), wide_row(biases, 0)
    gain_last, bias_last = wide_row(gains, 1), wide_row(biases, 1)
    pl.semaphore_wait(barrier, 2)

    @pl.when(encoder)
    def _():
        row = jnp.concatenate([flat_row(cross_gain), flat_row(cross_bias)], axis=1)
        gains_s[...] = jnp.broadcast_to(row, gains_s.shape).astype(LOW)
        gains_copy.start()
        for copy in weight_copies[:2]:
            copy.start()

    @pl.when(decoder)
    def _():
        for copy in decoder_loads:
            copy.start()

    x_copy.wait()
    qkv_w_copy.wait()

    def self_step(example, carry):
        x_rows = x_s.at[rows_of(example)]
        qkv_rows = qkv_s.at[example]
        project(x_rows, qkv_w_s, qkv_rows, width)
        outs.start("qkv", example)
        count = jnp.where(encoder, src_len[example], tgt_len[example])
        attend(
            qkv_s.at[example, :, pl.ds(0, width)],
            qkv_s.at[example, :, pl.ds(width, width)],
            qkv_s.at[example, :, pl.ds(2 * width, width)],
            count,
            mixed_s.at[example],
            logsum_s.at[example],
        )
        outs.start("mixed", example)
        outs.start("logsum", example)

        @pl.when(example == 0)
        def _():
            out_w_copy.wait()

        def residual_step(spot):
            residual_s[example, spot] = x_rows[spot].astype(WIDE) + product(
                mixed_s[example, spot], out_w_s[...]
            )

        row_tiles(rows, HALF_TILE, residual_step)
        outs.start("residual", example)

        @pl.when(example == 0)
        def _():
            in_w_copy.wait()
            out2_w_copy.wait()

        @pl.when(encoder)
        def _():
            outs.free("low", example)

            value = norm(residual_s[example], gain_first, bias_first)
            wide_s[...] = value
            low_s[...] = value.astype(LOW)
            outs.start("low", example)
            outs.free("act", example)
            feed_forward(
                low_s, wide_s, in_w_s, in_b, out2_w_s, out2_b, act_s, slope_s.at[example],
                second_s.at[example],
            )
            outs.start("act", example)

            def memory_step(tile, inner):
                spot = pl.ds(pl.multiple_of(tile * ROW_TILE, ROW_TILE), ROW_TILE)
                row = lax.broadcasted_iota(jnp.int32, (ROW_TILE, width), 0) + tile * ROW_TILE
                value = norm(second_s[example, spot], gain_last, bias_last)
                begin = pl.multiple_of(example * rows + tile * ROW_TILE, ROW_TILE)
                memory_s[pl.ds(begin, ROW_TILE)] = jnp.where(row < count, value, 0.0).astype(LOW)
                memory_copy(example, tile).start()
                return inner

            lax.fori_loop(0, rows // ROW_TILE, memory_step, 0)
            outs.start("memory", example)
            pl.when(example == 0)(weight_copies[2].start)

            @pl.when(example == 1)
            def _():
                outs.start("slope", 1)
                outs.start("second", 1)

        return carry

    lax.fori_loop(0, 2, self_step, 0)

    @pl.when(encoder)
    def _():
        for tile in range(rows // HALF_TILE):
            return_copy(0, tile).wait_recv()
        row = lax.broadcasted_iota(jnp.int32, (rows, width), 0)
        wide_grad_s[...] = jnp.where(row < src_len[0], memory_grad_s[0].astype(WIDE), 0.0)
        norm_back_rolled(
            second_s.at[0], gain_last, wide_grad_s, wide_s, grad_low_s,
            small_out.at[6:7, :], small_out.at[8:9, :],
        )
        outs.start("grad", 0)
        small_out[4:5, :] = column_sum(grad_low_s[...].astype(WIDE))
        feed_back_rolled(
            wide_s, grad_low_s, slope_s.at[0], in_w_s, out2_w_s, hidden_s, small_out.at[0:4, :],
            wide_grad_s,
        )
        outs.start("hidden", 0)
        norm_back_rolled(
            residual_s.at[0], gain_first, wide_grad_s, rest_s, branch_s.at[pl.ds(0, rows)],
            small_out.at[5:6, :], small_out.at[7:8, :],
        )
        outs.start("branch", 0)
        attn_grad_s[...] = product(branch_s[:rows], out_w_s[...], 1, 1).astype(LOW)
        attend_back(
            qkv_s.at[0, :, pl.ds(0, width)],
            qkv_s.at[0, :, pl.ds(width, width)],
            qkv_s.at[0, :, pl.ds(2 * width, width)],
            src_len[0],
            mixed_s.at[0],
            logsum_s.at[0],
            attn_grad_s,
            qkv_grad_s.at[:, pl.ds(0, width)],
            qkv_grad_s.at[:, pl.ds(width, width)],
            qkv_grad_s.at[:, pl.ds(2 * width, width)],
        )
        outs.start("qkv_grad", 0)

        def rows_step(spot):
            back_s[spot] = rest_s[spot] + product(qkv_grad_s[spot], qkv_w_s[...], 1, 1)

        row_tiles(rows, HALF_TILE, rows_step)
        outs.start("rows", 0)
        gains_copy.wait_send()
        for copy in weight_copies:
            copy.wait_send()

        def sent_step(tile, inner):
            for example in range(2):
                memory_copy(example, tile).wait_send()
            return inner

        lax.fori_loop(0, rows // ROW_TILE, sent_step, 0)
        outs.wait(("low", "act", "slope", "second"), (1,))
        outs.wait(("memory",), (0, 1))
        outs.wait(("grad", "hidden", "branch", "qkv_grad", "rows"), (0,))
        for tile in range(rows // HALF_TILE):
            return_copy(1, tile).wait_recv()
        outs.start("return", 1)
        outs.wait(("return",), (1,))

    @pl.when(decoder)
    def _():
        for copy in decoder_loads:
            copy.wait()
        for example in range(2):
            spot = slice(example * rows, (example + 1) * rows)
            row = lax.broadcasted_iota(jnp.int32, (rows, width), 0)
            slot_grad = jnp.where(
                row < tgt_len[example] - 1, grad_s[spot].astype(WIDE), 0.0
            )
            grad_s[spot] = slot_grad.astype(LOW)
            earlier = jnp.where(row == 0, 0.0, pltpu.roll(slot_grad, 1, 0))
            earlier_s[spot] = earlier.astype(LOW)
        for place in range(2):
            weight_copies[place].wait_recv()
            near_copies[place].start()
        gains_copy.wait_recv()
        for copy in near_copies[:2]:
            copy.wait_recv()
        outs.start("query_w", 0)
        came_row = gains_s[0:1, :].astype(WIDE)
        gain_cross = jnp.concatenate([came_row[:, :half], flat_row(cross_gain)], axis=1)
        bias_cross = jnp.concatenate([came_row[:, half:], flat_row(cross_bias)], axis=1)

        def cross_step(example, carry):
            spot_rows = rows_of(example)
            first = first_s.at[spot_rows]
            final = final_s.at[spot_rows]
            slot_grad, earlier = grad_s.at[spot_rows], earlier_s.at[spot_rows]
            mixed, branch = cross_mixed_s.at[spot_rows], branch_s.at[spot_rows]
            query_grad = query_grad_s.at[spot_rows]
            key_grad, value_grad = key_grad_s.at[spot_rows], value_grad_s.at[spot_rows]
            second = second_s.at[0]
            slope = slope_s.at[0]

            value = norm(residual_s[example], gain_first, bias_first)
            wide_s[...] = value
            first[...] = value.astype(LOW)
            query_s[...] = product(first[...], cross_w_s[:, :width]).astype(LOW)

            def arrive(tile, inner):
                memory_copy(example, tile).wait_recv()
                return inner

            lax.fori_loop(0, rows // ROW_TILE, arrive, 0)
            project(memory_s.at[spot_rows], cross_w_s.at[:, width:], pair_s, width)
            key_ref, value_ref = pair_s.at[:, :width], pair_s.at[:, width:]
            count = src_len[example]
            attend(query_s, key_ref, value_ref, count, mixed, cross_logsum_s)
            outs.free("low", example)

            for begin in range(0, rows, HALF_TILE):
                spot = slice(begin, begin + HALF_TILE)
                value = wide_s[spot] + product(mixed[spot], cross_out_s[...])
                cross_s[spot] = value
                value = norm(value, gain_cross, bias_cross)
                wide_s[spot] = value
                low_s[spot] = value.astype(LOW)
            outs.start("low", example)

            @pl.when(example == 0)
            def _():
                weight_copies[2].wait_recv()
                near_copies[2].start()

            outs.free("act", example)
            feed_forward(
                low_s, wide_s, in_w_s, in_b, out2_w_s, out2_b, act_s, slope, second
            )
            outs.start("act", example)

            final[...] = norm(second[...], gain_last, bias_last).astype(LOW)
            pl.when(example == 0)(near_copies[2].wait_recv)
            wide_grad_s[...] = product(slot_grad[...], slot_w_s[:width, :], 1, 1) + product(
                earlier[...], slot_w_s[width:, :], 1, 1
            )
            outs.free("grad", example)
            part_s[...] = jnp.zeros_like(part_s)
            norm_back_rows(
                second, gain_last, wide_grad_s, second, grad_low_s,
                part_s.at[6:7, :], part_s.at[8:9, :],
            )
            outs.start("grad", example)
            part_s[4:5, :] = column_sum(grad_low_s[...].astype(WIDE))
            outs.free("hidden", example)
            feed_back(
                second, grad_low_s, slope, in_w_s, out2_w_s, hidden_s, part_s.at[0:4, :], back_s
            )
            outs.start("hidden", example)
            outs.free("rest", example)
            norm_back_rows(
                cross_s, gain_cross, back_s, rest_s, branch, part_s.at[9:10, :],
                part_s.at[10:11, :],
            )
            outs.start("rest", example)
            small_out[...] += part_s[...]
            attn_grad_s[...] = product(branch[...], cross_out_s[...], 1, 1).astype(LOW)
            attend_back(
                query_s, key_ref, value_ref, count, mixed, cross_logsum_s, attn_grad_s,
                query_grad, key_grad, value_grad,
            )
            for tile in range(rows // HALF_TILE):
                spot = pl.ds(tile * HALF_TILE, HALF_TILE)
                memory_grad_s[example, spot] = (
                    product(key_grad[spot], cross_w_s[:, width : 2 * width], 1, 1)
                    + product(value_grad[spot], cross_w_s[:, 2 * width :], 1, 1)
                ).astype(LOW)
                return_copy(example, tile).start()
            outs.start("query", example)
            outs.free("slot", example)
            wide_grad_s[...] = product(final[...], slot_w_s[width:, :])
            value = product(final[...], slot_w_s[:width, :]) + pltpu.roll(
                wide_grad_s[...], rows - 1, 0
            )
            row = lax.broadcasted_iota(jnp.int32, (rows, width), 0)
            slot_s[...] = jnp.where(row < tgt_len[example] - 1, value, 0.0).astype(LOW)
            outs.start("slot", example)
            return carry

        lax.fori_loop(0, 2, cross_step, 0)
        outs.wait(("qkv",), (0, 1))

        def weight_step(place, carry):
            value = product(
                left_s[lax.div(2 * place + 1, 3)], right_s[place], 0, 0
            ).astype(LOW)
            block = lax.div(place, 2)
            columns = columns_of(block, width)
            begin = pl.multiple_of((place - 2 * block) * half, half)

            @pl.when(place < 4)
            def _():
                qkv_s[1, pl.ds(begin, half), columns] = value[:half]
                qkv_s[0, pl.ds(begin, half), columns] = value[half:]

            @pl.when(place >= 4)
            def _():
                qkv_s[5 - place, :, columns] = value

            return carry

        lax.fori_loop(0, 6, weight_step, 0)
        kept = []
        for target, slot in ((own_out, 0), (sent_out, 1)):
            for block in range(3):
                kept.append(
                    pltpu.make_async_copy(
                        qkv_s.at[slot, :, pl.ds(block * width, width)],
                        target.at[pl.ds(block * width, width)],
                        load_sem.at[3 * slot + block],
                    )
                )
        for copy in kept:
            copy.start()
        for copy in near_copies:
            copy.wait_send()

        def returned(tile, inner):
            for example in range(2):
                return_copy(example, tile).wait_send()
            return inner

        lax.fori_loop(0, rows // HALF_TILE, returned, 0)
        outs.wait(("low", "act", "grad", "hidden", "rest", "slot"), (1,))
        outs.wait(("query",), (0, 1))
        outs.wait(("query_w",), (0,))
        for copy in kept:
            copy.wait()

    @pl.when(encoder)
    def _():
        outs.wait(("qkv",), (0, 1))

    outs.wait(("mixed", "logsum", "residual"), (0, 1))


def last_kernel(
    devices, src_len, tgt_len, gains, small_in, inputs, qkv_w, out_w, in_w, out2_w, query_w,
    memory_grad, second_in, slope_in, query_grad, rest_in, residual_in, qkv_in, logsum_in, mixed_in,
    low_in, act_in, grad_in, hidden_in, branch_a, qkv_grad_a, own_extra, sent_extra, first_total,
    second_total, cross_total, small_total, rows_out, qkv_w_s, out_w_s, in_w_s, out2_w_s, low_s,
    hidden_s, act_s, grad_s, mixed_s, branch_s, x_s, qkv_grad_s, memory_s, second_s, slope_s,
    back_s, query_w_s, residual_s, qkv_s, logsum_s, rest_s, attn_grad_s, small_s, small_arrived,
    cross_total_s, small_send, small_recv, small_cross_sem, semaphores, *ring_refs,
):
    mixed_a, mixed_b = mixed_in.at[0], mixed_in.at[1]
    low_a, low_b = low_in.at[0], low_in.at[1]
    act_a, act_b = act_in.at[0], act_in.at[1]
    grad_a, grad_b = grad_in.at[0], grad_in.at[1]
    hidden_a, hidden_b = hidden_in.at[0], hidden_in.at[1]
    links = Links(devices)
    links.greet()
    chips, levels = links.chips, links.levels
    section = links.pipe
    rows, width = residual_s.shape
    half = width // 2
    hidden = hidden_s.shape[1]
    hidden_blocks = hidden // width
    extra_rows = own_extra.shape[0]
    sizes = (2 * hidden, 4 * width, extra_rows)
    layouts = [ring_layout(size, devices) for size in sizes]
    early = Ring(links, layouts[0], act_s, ring_refs[:11])
    late = Ring(links, layouts[1], out2_w_s, ring_refs[11:22])
    cross = CrossRing(links, layouts[2], cross_total_s, ring_refs[22:33], ring_refs[33:])
    front, rear = pl.ds(0, rows), pl.ds(rows, rows)
    gain_first, gain_last = wide_row(gains, 0), wide_row(gains, 1)
    small_s[0] = small_in[...]
    partial = small_arrived.at[0]
    partial[...] = jnp.zeros_like(small_in)

    encoder = section == 0
    copies = Copies(semaphores)

    def declared(source, target):
        copy = pltpu.make_async_copy(source, target, semaphores.at[copies.count])
        copies.count += 1
        return copy

    def start(*group):
        for copy in group:
            copy.start()

    def wait(*group):
        for copy in group:
            copy.wait()

    hidden_front = [declared(low_a, low_s.at[front]), declared(low_b, low_s.at[rear]),
                    declared(hidden_a, hidden_s.at[front])]
    act_front = [declared(grad_a, grad_s.at[front])]
    for index in range(hidden_blocks):
        columns = pl.ds(index * width, width)
        act_front.append(declared(act_a.at[:, columns], act_s.at[index, front]))
        act_front.append(declared(act_b.at[:, columns], act_s.at[index, rear]))
    hidden_rear = declared(hidden_b, hidden_s.at[rear])
    grad_rear = declared(grad_b, grad_s.at[rear])
    back_inputs = [declared(memory_grad, memory_s), declared(second_in, second_s),
                   declared(slope_in, slope_s), declared(out2_w.at[0], out2_w_s),
                   declared(in_w.at[0], in_w_s)]
    query_weights = [declared(query_w, query_w_s)]
    out_w_copy = declared(out_w.at[0], out_w_s)
    qkv_w_copy = declared(qkv_w.at[0], qkv_w_s)
    mixed_copies = [declared(mixed_a, mixed_s.at[front]), declared(mixed_b, mixed_s.at[rear])]
    saved = []
    base = copies.count
    for example in range(2):
        copies.count = base
        parts = [
            ref.at[example] for ref in (residual_in, query_grad, rest_in, qkv_in, logsum_in)
        ]
        targets = (residual_s, memory_s, second_s, qkv_s, logsum_s)
        saved.append([declared(source, target) for source, target in zip(parts, targets)])
    encoder_inputs = [declared(branch_a, branch_s.at[front]),
                      declared(qkv_grad_a, qkv_grad_s.at[front])]
    inputs_copy = declared(inputs.at[0], x_s)
    extra_loads = [declared(own_extra, cross.mine.at[pl.ds(0, extra_rows)]),
                   declared(sent_extra, cross.foreign.at[pl.ds(0, extra_rows)])]
    if cross.mine.shape[0] > extra_rows:
        cross.mine[extra_rows:] = jnp.zeros_like(cross.mine[extra_rows:])
        cross.foreign[extra_rows:] = jnp.zeros_like(cross.foreign[extra_rows:])

    def rows_copy(example):
        spot = pl.ds(pl.multiple_of(example * rows, rows), rows)
        return pltpu.make_async_copy(rest_s, rows_out.at[spot], semaphores.at[copies.count])

    @pl.when(encoder)
    def _():
        start(*back_inputs, *hidden_front, *act_front, out_w_copy, qkv_w_copy, *mixed_copies,
              *encoder_inputs, inputs_copy)
        wait(*back_inputs[:2])
        row = lax.broadcasted_iota(jnp.int32, (rows, width), 0)
        rest_s[...] = jnp.where(row < src_len[1], memory_s[...].astype(WIDE), 0.0)
        norm_back_rolled(
            second_s, gain_last, rest_s, second_s, grad_s.at[rear],
            partial.at[6:7, :], partial.at[8:9, :],
        )
        partial[4:5, :] = column_sum(grad_s[rear].astype(WIDE))
        wait(*back_inputs[2:])
        feed_back_rolled(
            second_s, grad_s.at[rear], slope_s, in_w_s, out2_w_s, hidden_s.at[rear],
            partial.at[0:4, :], back_s,
        )
        start(saved[1][0], *saved[1][3:])

    @pl.when(section == 1)
    def _():
        start(*hidden_front, hidden_rear, *act_front, grad_rear, *saved[0], *query_weights,
              out_w_copy, qkv_w_copy, *mixed_copies, *extra_loads, inputs_copy)
        wait(hidden_rear, grad_rear)

    def blocks(target, begin, count, block):
        def step(index, carry):
            target[columns_of(begin + index, width), :] = block(index).astype(LOW)
            return carry

        lax.fori_loop(0, count, step, 0)

    wait(*hidden_front)
    blocks(
        early.mine, 0, hidden_blocks,
        lambda index: product(low_s[...], hidden_s[:, columns_of(index, width)], 0, 0),
    )
    wait(*act_front)
    blocks(
        early.mine, hidden_blocks, hidden_blocks,
        lambda index: product(act_s[index], grad_s[...], 0, 0),
    )
    links.greeted()
    small_cross = links.copy(
        small_s.at[levels], small_arrived.at[1], small_cross_sem.at[0], small_cross_sem.at[1],
        links.across,
    )

    @pl.when(section == 1)
    def _():
        small_s[levels, 0:1, :] = jnp.concatenate(
            [small_s[0, 9:10, :half], small_s[0, 10:11, :half]], axis=1
        )
        small_cross.start()
        wait(*extra_loads)
        cross.foreign_start()

    early.begin()

    @pl.when(section == 1)
    def _():
        cross.foreign_pass()

    cross.begin()
    per_example = 6
    final = 2 * chips - 3
    middle = max(1, early.count // 2)
    begin_at = jnp.where(encoder, 1, 0)
    @pl.when(section == 1)
    def _():
        wait(*query_weights)

    wait(out_w_copy, qkv_w_copy, *mixed_copies)

    def advance(first, count):
        def half_turn(half, carry):
            turn, odd = lax.div(half, 2), lax.rem(half, 2)
            parts = (odd * middle, jnp.where(odd == 1, early.count, middle))

            @pl.when((turn <= chips - 2) & (odd == 0))
            def _():
                early.pairs_ready(turn + 1)

            @pl.when(turn < chips - 2)
            def _():
                early.reduce(turn, parts)

            @pl.when(turn == chips - 2)
            def _():
                early.settle(parts, odd == 1)

            @pl.when((turn > chips - 2) & (turn < final))
            def _():
                early.gather(turn - (chips - 1), parts, odd == 1)

            @pl.when(turn == final)
            def _():
                early.gather_last(parts, odd == 1)

            @pl.when((turn <= chips - 2) & (odd == 1))
            def _():
                cross.pairs_ready(turn + 1)

            @pl.when((turn < chips - 2) & (odd == 1))
            def _():
                cross.reduce(turn)

            @pl.when((turn == chips - 2) & (odd == 1))
            def _():
                cross.settle()

            @pl.when((turn > chips - 2) & (turn < final) & (odd == 1))
            def _():
                cross.gather(turn - (chips - 1))

            @pl.when((turn == final) & (odd == 1))
            def _():
                cross.gather_last()

            return carry

        lax.fori_loop(first, first + count, half_turn, 0)

    def back_step(example, carry):
        spot = pl.ds(pl.multiple_of(example * rows, rows), rows)
        turn = (example - begin_at) * per_example

        @pl.when(section == 1)
        def _():
            wait(*saved[0][:3])

            def first_step(tile):
                back_s[tile] = second_s[tile] + product(memory_s[tile], query_w_s[...], 1, 1)

            row_tiles(rows, HALF_TILE, first_step)

        @pl.when(encoder)
        def _():
            wait(saved[0][0])

        @pl.when((section == 1) & (example == 1))
        def _():
            rows_copy(0).wait()

        low_branch = branch_s.at[spot]
        norm_back_rows(
            residual_s, gain_first, back_s, rest_s, low_branch,
            partial.at[12:13, :], partial.at[13:14, :],
        )
        partial[5:6, :] += partial[12:13, :]
        partial[7:8, :] += partial[13:14, :]
        attn_grad_s[...] = product(low_branch[...], out_w_s[...], 1, 1).astype(LOW)
        wait(*saved[0][3:])
        advance(turn, 2)
        count = jnp.where(encoder, src_len[example], tgt_len[example])
        attend_back(
            qkv_s.at[:, :width],
            qkv_s.at[:, width : 2 * width],
            qkv_s.at[:, 2 * width :],
            count,
            mixed_s.at[spot],
            logsum_s,
            attn_grad_s,
            qkv_grad_s.at[spot, pl.ds(0, width)],
            qkv_grad_s.at[spot, pl.ds(width, width)],
            qkv_grad_s.at[spot, pl.ds(2 * width, width)],
            after=lambda step: advance(turn + 2 + 2 * step, 2),
        )

        @pl.when(example == 0)
        def _():
            start(*saved[1])

        def rows_step(index, inner):
            tile = pl.ds(pl.multiple_of(index * HALF_TILE, HALF_TILE), HALF_TILE)
            begin = pl.multiple_of(example * rows + index * HALF_TILE, HALF_TILE)
            rest_s[tile] += product(qkv_grad_s[pl.ds(begin, HALF_TILE)], qkv_w_s[...], 1, 1)
            return inner

        lax.fori_loop(0, rows // HALF_TILE, rows_step, 0)
        rows_copy(example).start()
        return carry

    lax.fori_loop(begin_at, 2, back_step, 0)
    wait(inputs_copy)

    @pl.when(encoder)
    def _():
        wait(*encoder_inputs)

    blocks(
        late.mine, 0, 3,
        lambda index: product(x_s[...], qkv_grad_s[:, columns_of(index, width)], 0, 0),
    )
    done = (2 - begin_at) * per_example
    advance(done, 2)
    blocks(late.mine, 3, 1, lambda index: product(mixed_s[...], branch_s[...], 0, 0))

    if late.mine.shape[0] > 4 * width:
        late.mine[4 * width :] = jnp.zeros_like(late.mine[4 * width :])
    late.begin()
    advance(done + 2, 2)
    done = done + 4
    ahead = jnp.where(encoder, 2, 1)

    small_s[0] = small_s[0] + partial[...]
    @pl.when(section == 1)
    def _():
        small_s[0, 9:10, :] = jnp.concatenate(
            [small_s[0, 9:10, half:], small_s[0, 10:11, half:]], axis=1
        )
        small_cross.wait_send()

    @pl.when(encoder)
    def _():
        small_cross.wait_recv()
        small_s[0, 9:10, :] = small_arrived[1, 0:1, :]

    def small_copy(level, bit):
        return links.copy(
            small_s.at[level],
            small_arrived.at[level + 2],
            small_send.at[level],
            small_recv.at[level],
            links.paired(bit),
        )

    small_copy(0, 1).start()

    def merge_small(level, bit):
        small_copy(level, bit).wait_recv()
        merged = small_s[level] + small_arrived[level + 2]

        @pl.when(level + 1 < levels)
        def _():
            small_s[level + 1] = merged
            small_copy(level + 1, 2 * bit).start()

        @pl.when(level + 1 == levels)
        def _():
            small_total[...] = merged

    def both_step(step, bit):
        late.pairs_ready(step + 1)
        late.reduce(step)
        advance(done + ahead * step, ahead)

        @pl.when(step < levels)
        def _():
            merge_small(step, bit)

        return 2 * bit

    lax.fori_loop(0, chips - 2, both_step, 1)
    late.pairs_ready(chips - 1)
    late.settle()
    done = done + ahead * (chips - 2)

    def late_step(step, carry):
        late.gather(step)
        advance(done + step, 1)
        return carry

    lax.fori_loop(0, chips - 2, late_step, 0)
    done = done + chips - 2
    advance(done, jnp.maximum(2 * final + 2 - done, 0))
    late.gather_last()
    late.finish()
    cross.finish()
    kept = [
        pltpu.make_async_copy(
            out2_w_s.at[pl.ds(0, second_total.shape[0])], second_total, semaphores.at[0]
        ),
        pltpu.make_async_copy(cross_total_s, cross_total, semaphores.at[1]),
    ]
    for index in range(hidden_blocks):
        kept.append(
            pltpu.make_async_copy(
                act_s.at[index], first_total.at[pl.ds(index * 2 * rows, 2 * rows)],
                semaphores.at[2 + index],
            )
        )
    start(*kept[:2])
    early.finish()
    start(*kept[2:])
    wait(*kept)
    for level in range(levels):
        small_copy(level, 1 << level).wait_send()
    rows_copy(1).wait()


def result_kernel(
    small_total, first_total, second_total, cross_total, rows_in, block_in,
    rows_buffer, block_out, rows_out, qkv_out, out_out,
    in_out, out2_out, cross_qkv_out, cross_out_out, slot_out, in_b_out, out2_b_out, gain_out,
    bias_out, cross_gain_out, cross_bias_out, first_s, second_s, rows_s, block_s,
    wide_s, semaphores,
):
    width = first_s.shape[1]
    half = width // 2
    for index in range(in_b_out.shape[1] // width):
        in_b_out[:, index * width : (index + 1) * width] = small_total[index : index + 1, :]
    out2_b_out[...] = small_total[4:5, :]
    gain_out[0] = small_total[5:7, :]
    bias_out[0] = small_total[7:9, :]
    cross_gain_out[...] = small_total[9:10, :half]
    cross_bias_out[...] = small_total[9:10, half:]
    copies = Copies(semaphores)
    rows = rows_in.shape[0] // 2
    front, rear = pl.ds(0, rows), pl.ds(rows, rows)
    rows_copy = copies.start(rows_in.at[rear], rows_s.at[rear])
    front_sem = semaphores.at[copies.count]
    copies.count += 1
    from_last = pltpu.make_async_copy(rows_in.at[front], rows_s.at[front], front_sem)
    from_main = pltpu.make_async_copy(rows_buffer.at[0, front], rows_s.at[front], front_sem)
    pl.when(lax.axis_index("pipe") == 1)(from_last.start)
    pl.when(lax.axis_index("pipe") == 0)(from_main.start)
    block_copy = copies.start(block_in.at[0], block_s)
    rows = rows_in.shape[0] // 2
    kept = []
    loads = {width: [], half: []}
    second_rows = 4 * width
    for index in range(first_s.shape[0] // width):
        spot = pl.ds(index * width, width)
        loads[width].append(copies.start(first_total.at[spot], first_s.at[spot]))
    for index in range(second_s.shape[0] // half):
        begin = index * half
        if begin < second_rows:
            source = second_total.at[pl.ds(begin, half)]
        else:
            source = cross_total.at[pl.ds(begin - second_rows, half)]
        loads[half].append(copies.start(source, second_s.at[pl.ds(begin, half)]))
    targets = []
    for index in range(first_s.shape[0] // width):
        hidden_blocks = in_out.shape[2] // width
        if index < hidden_blocks:
            target = in_out.at[0, :, pl.ds(index * width, width)]
        else:
            target = out2_out.at[0, pl.ds((index - hidden_blocks) * width, width)]
        targets.append((loads[width][index : index + 1], first_s, index * width, width, target))
    for index in range(4):
        if index < 3:
            target = qkv_out.at[0, :, pl.ds(index * width, width)]
        else:
            target = out_out.at[0]
        targets.append(
            (loads[half][2 * index : 2 * index + 2], second_s, index * width, width, target)
        )
    for index in range(4):
        if index < 3:
            target = cross_qkv_out.at[:, pl.ds(index * width, width)]
        else:
            target = cross_out_out
        targets.append(
            (loads[half][8 + index : 9 + index], second_s, 4 * width + index * half, half, target)
        )
    targets.append((loads[half][12:14], second_s, 6 * width, width, slot_out))
    place = 0
    for waits, stage, begin, size, target in targets:
        for copy in waits:
            copy.wait()
        wide_s[place : place + size] = stage[begin : begin + size].astype(WIDE)
        kept.append(copies.start(wide_s.at[pl.ds(place, size)], target))
        place += size
    block_copy.wait()
    kept.append(copies.start(block_s, block_out.at[0]))
    rows_copy.wait()
    from_last.wait()
    kept.append(copies.start(rows_s, rows_out.at[0]))
    for copy in kept:
        copy.wait()


ANY = pl.BlockSpec(memory_space=pl.ANY)
INNER = pl.BlockSpec(memory_space=pltpu.VMEM)
SCALAR = pl.BlockSpec(memory_space=pltpu.SMEM)


def local_call(
    body, name, scalars, inner, outer, outputs, scratch, flops, aliases=None, count=32,
    semaphores=(), **compiler,
):
    shapes = [jax.ShapeDtypeStruct(shape, kind) for shape, kind, _ in outputs]
    inputs = list(scalars) + list(inner) + list(outer)
    specs = [SCALAR] * len(scalars) + [INNER] * len(inner) + [ANY] * len(outer)
    moved = sum(value.size * value.dtype.itemsize for value in inputs)
    return pl.pallas_call(
        body,
        out_shape=shapes,
        in_specs=specs,
        out_specs=[INNER if kept else ANY for _, _, kept in outputs],
        scratch_shapes=[pltpu.VMEM(shape, kind) for shape, kind in scratch]
        + list(semaphores or [pltpu.SemaphoreType.DMA((count,))]),
        input_output_aliases=aliases or {},
        compiler_params=pltpu.CompilerParams(vmem_limit_bytes=VMEM_LIMIT, **compiler),
        cost_estimate=pl.CostEstimate(flops=flops, bytes_accessed=moved, transcendentals=0),
        name=name,
    )(*inputs)


def local(
    inputs, src_len, tgt_len, cotangent, qkv_w, out_w, in_w, in_b, out2_w, out2_b, norm_gain,
    norm_bias, cross_qkv, cross_out, slot_w, cross_gain, cross_bias,
):
    devices = lax.axis_size("dp")
    blocks = src_len.shape[0]
    total_rows, width = inputs.shape[1:]
    rows = total_rows // blocks
    half = width // 2
    hidden = in_w.shape[2]
    square, wide3, deep = (rows, width), (rows, 3 * width), (rows, hidden)
    weight_square, logsum = (width, width), (rows, PAIR)
    tall, tall3, tall_deep = (total_rows, width), (total_rows, 3 * width), (total_rows, hidden)
    extra_rows = 3 * width
    small_shape = (SMALL_ROWS, width)
    dma = pltpu.SemaphoreType.DMA
    tiles, halves = rows // ROW_TILE, rows // HALF_TILE

    (
        small, block_out, qkv, logsums, mixed, residual, low, act, slope, second, grad, hidden_grad,
        branch, qkv_grad, source_rows, query_grad, rest, memory_grad, query_w, own_extra,
        sent_extra,
    ) = local_call(
        main_kernel, "main_rows", [src_len, tgt_len],
        [
            in_b, out2_b, norm_gain, norm_bias, cross_gain, cross_bias,
        ],
        [inputs, cotangent, qkv_w, out_w, in_w, out2_w, cross_qkv, cross_out, slot_w],
        [
            (small_shape, WIDE, True), ((1,) + tall, LOW, False), ((2,) + wide3, LOW, False),
            ((2,) + logsum, WIDE, False), ((2,) + square, LOW, False), ((2,) + square, WIDE, False),
            ((2,) + square, LOW, False), ((2,) + deep, LOW, False), (deep, LOW, False),
            (square, WIDE, False), ((2,) + square, LOW, False), ((2,) + deep, LOW, False),
            (square, LOW, False), (wide3, LOW, False), ((1,) + tall, WIDE, False),
            ((2,) + square, LOW, False), ((2,) + square, WIDE, False), (square, LOW, False),
            (weight_square, LOW, False), ((extra_rows, width), LOW, False),
            ((extra_rows, width), LOW, False),
        ],
        [
            (tall, LOW), ((width, 3 * width), LOW), (weight_square, LOW), ((width, hidden), LOW),
            ((hidden, width), LOW), ((width, 3 * width), LOW), (weight_square, LOW),
            ((2 * width, width), LOW), (small_shape, LOW), ((2,) + wide3, LOW),
            ((2,) + logsum, WIDE), ((2,) + square, LOW), ((2,) + square, WIDE), (square, WIDE),
            (square, LOW), (deep, LOW), ((2,) + deep, LOW), ((2,) + square, WIDE),
            ((4,) + tall, LOW), ((6,) + tall, LOW), (square, LOW), ((rows, 2 * width), LOW),
            (logsum, WIDE), (square, WIDE), (square, LOW), (square, WIDE), (square, LOW),
            (deep, LOW), (square, WIDE), (square, WIDE), (square, LOW), ((2,) + square, LOW),
            (wide3, LOW), (small_shape, WIDE),
        ],
        70 * 10**9,
        semaphores=[
            dma((16,)), dma((2, 24)), dma((2, tiles)), dma((2, tiles)), dma((2, halves)),
            dma((2, halves)), dma((4,)), dma((4,)), dma((3,)), dma((3,)),
        ],
        collective_id=1, has_side_effects=True,
    )

    sizes = (2 * hidden, 4 * width, extra_rows)
    padded = [ring_rows(size, devices) for size in sizes]
    levels = devices.bit_length() - 1
    rings = [part for size in sizes for part in ring_scratch(size, width, devices)]
    rings += foreign_scratch(extra_rows, width, devices)
    first_total, second_total, cross_total, small_total, last_rows = local_call(
        functools.partial(last_kernel, devices), "last_rows", [src_len, tgt_len],
        [norm_gain, small],
        [
            inputs, qkv_w, out_w, in_w, out2_w, query_w, memory_grad, second, slope, query_grad,
            rest, residual, qkv, logsums, mixed, low, act, grad, hidden_grad, branch, qkv_grad,
            own_extra, sent_extra,
        ],
        [
            ((padded[0], width), LOW, False),
            ((padded[1], width), LOW, False),
            ((padded[2], width), LOW, False),
            (small_shape, WIDE, True),
            (tall, WIDE, False),
        ],
        [
            ((width, 3 * width), LOW), (weight_square, LOW), ((width, hidden), LOW),
            ((hidden, width), LOW), (tall, LOW), (tall_deep, LOW),
            ((hidden // width,) + tall, LOW), (tall, LOW), (tall, LOW), (tall, LOW), (tall, LOW),
            (tall3, LOW), (square, LOW), (square, WIDE), (deep, LOW), (square, WIDE),
            (weight_square, LOW), (square, WIDE), (wide3, LOW), (logsum, WIDE), (square, WIDE),
            (square, LOW), ((levels + 1,) + small_shape, WIDE), ((levels + 2,) + small_shape, WIDE),
            ((padded[2], width), LOW),
        ],
        20 * 10**9,
        semaphores=[dma((levels,)), dma((levels,)), dma((2,)), dma((64,))] + rings,
        collective_id=0, has_side_effects=True,
    )

    results = local_call(
        result_kernel, "results", [], [small_total],
        [first_total, second_total, cross_total, last_rows, block_out, source_rows],
        [
            ((1,) + tall, LOW, False), ((1,) + tall, WIDE, False),
            ((1, width, 3 * width), WIDE, False),
            ((1,) + weight_square, WIDE, False), ((1, width, hidden), WIDE, False),
            ((1, hidden, width), WIDE, False), ((half, 3 * width), WIDE, False),
            ((half, width), WIDE, False), ((width, width), WIDE, False),
            ((1, hidden), WIDE, True), ((1, width), WIDE, True), ((1, 2, width), WIDE, True),
            ((1, 2, width), WIDE, True), ((1, half), WIDE, True), ((1, half), WIDE, True),
        ],
        [
            ((sizes[0], width), LOW), ((sizes[1] + sizes[2], width), LOW), (tall, WIDE),
            (tall, LOW), ((sum(sizes), width), WIDE),
        ],
        10**9, count=64,
    )
    return (
        results[0], results[1], results[2], results[3], results[4], results[9], results[5],
        results[10], results[11], results[12], results[6], results[7], results[8],
        results[13].reshape(half), results[14].reshape(half),
    )


def solution(mesh):
    in_specs = (
        P("pipe", "dp", None),
        P("dp"),
        P("dp"),
        P("dp", None),
        P("pipe", None, None),
        P("pipe", None, None),
        P("pipe", None, None),
        P("pipe", None),
        P("pipe", None, None),
        P("pipe", None),
        P("pipe", None, None),
        P("pipe", None, None),
        P("pipe", None),
        P("pipe", None),
        P("pipe", None),
        P("pipe"),
        P("pipe"),
    )
    out_specs = (
        P("pipe", "dp", None),
        P("pipe", "dp", None),
        P("pipe", None, None),
        P("pipe", None, None),
        P("pipe", None, None),
        P("pipe", None),
        P("pipe", None, None),
        P("pipe", None),
        P("pipe", None, None),
        P("pipe", None, None),
        P("pipe", None),
        P("pipe", None),
        P("pipe", None),
        P("pipe"),
        P("pipe"),
    )
    return jax.shard_map(local, mesh=mesh, in_specs=in_specs, out_specs=out_specs, check_vma=False)
```

```python
import functools

import jax
import jax.numpy as jnp
from jax import lax
from jax.experimental import pallas as pl
from jax.experimental.pallas import tpu as pltpu
from jax.sharding import PartitionSpec as P

HEADS = 8
LOW = jnp.bfloat16
WIDE = jnp.float32
HEAD_SIZE = 64
PAIR = 2 * HEAD_SIZE
GELU_SCALE = 0.7978845608
GELU_CUBE = 0.044715
MASKED = -1e30
VMEM_LIMIT = 60 * 2**20


def product(left, right, left_dim=1, right_dim=0):
    return lax.dot_general(
        left, right, (((left_dim,), (right_dim,)), ((), ())), preferred_element_type=WIDE
    )


class Copies:
    def __init__(self, semaphores):
        self.semaphores = semaphores
        self.count = 0

    def start(self, source, target):
        copy = pltpu.make_async_copy(source, target, self.semaphores.at[self.count])
        self.count += 1
        copy.start()
        return copy


def pair_columns(pair):
    return pl.ds(pl.multiple_of(pair * PAIR, PAIR), PAIR)


def lanes(rows):
    return lax.broadcasted_iota(jnp.int32, (rows, PAIR), 1)


def split_three(column):
    high = column.astype(LOW).astype(WIDE)
    rest = column - high
    middle = rest.astype(LOW).astype(WIDE)
    return high, middle, rest - middle


def key_side(keys, head, bias, lane):
    base = HEAD_SIZE * (1 - head)
    own = lane // HEAD_SIZE == head
    extra = jnp.where(lane == base, bias, jnp.where((lane > base) & (lane < base + 4), 1.0, 0.0))
    return jnp.where(own, keys, extra).astype(LOW)


def attend(query_ref, key_ref, value_ref, count, mixed_ref, logsum_ref, tile=256):
    rows = query_ref.shape[0]
    lane = lanes(rows)
    row = lax.broadcasted_iota(jnp.int32, (rows, PAIR), 0)
    bias = jnp.where(row < count, 0.0, MASKED)
    tile_lane = lanes(tile)
    tiles = range(rows // tile)
    spots = [slice(index * tile, (index + 1) * tile) for index in tiles]
    logsums = [jnp.zeros((tile, PAIR), WIDE) for _ in tiles]
    sides, scores, weights, mixed = {}, {}, {}, {}

    def prepare(index):
        columns = pl.ds(index // 2 * PAIR, PAIR)
        head = index % 2
        own = lane // HEAD_SIZE == head
        one = jnp.where(lane == HEAD_SIZE * (1 - head), 1.0, 0.0)
        queries = query_ref[:, columns].astype(WIDE) * HEAD_SIZE**-0.5
        return (
            jnp.where(own, queries, one).astype(LOW),
            key_side(key_ref[:, columns].astype(WIDE), head, bias, lane),
            jnp.where(own, value_ref[:, columns].astype(WIDE), one).astype(LOW),
        )

    for turn in range(HEADS + 2):
        if turn < HEADS:
            sides[turn] = prepare(turn)
        for place in tiles:
            if turn < HEADS:
                scores[turn, place] = product(sides[turn][0][spots[place]], sides[turn][1], 1, 1)
            index = turn - 1
            if 0 <= index < HEADS:
                block = scores.pop((index, place))
                top = jnp.max(block, axis=1, keepdims=True)
                weights[index, place] = (jnp.exp(block - top).astype(LOW), top)
            index = turn - 2
            if 0 <= index < HEADS:
                block, top = weights.pop((index, place))
                base = HEAD_SIZE * (1 - index % 2)
                summed = product(block, sides[index][2])
                total = summed[:, base : base + 1]
                mixed[index, place] = summed * (1.0 / total)
                logsums[place] = jnp.where(
                    tile_lane == index, top + jnp.log(total), logsums[place]
                )
                if index % 2:
                    mixed_ref[spots[place], pl.ds(index // 2 * PAIR, PAIR)] = jnp.where(
                        tile_lane < HEAD_SIZE, mixed.pop((index - 1, place)),
                        mixed.pop((index, place)),
                    ).astype(LOW)
    for place in tiles:
        logsum_ref[spots[place]] = logsums[place]


def attend_back(
    query_ref, key_ref, value_ref, count, mixed_ref, logsum_ref, grad_ref,
    query_grad_ref, key_grad_ref, value_grad_ref, tile=512, after=None,
):
    rows = query_ref.shape[0]
    lane = lanes(rows)
    row = lax.broadcasted_iota(jnp.int32, (rows, PAIR), 0)
    bias = jnp.where(row < count, 0.0, MASKED)

    def pair_step(pair):
        columns = pair_columns(pair)
        queries = query_ref[:, columns].astype(WIDE) * HEAD_SIZE**-0.5
        keys = key_ref[:, columns].astype(WIDE)
        values = value_ref[:, columns].astype(WIDE)
        grads = grad_ref[:, columns].astype(WIDE)
        along = grads * mixed_ref[:, columns].astype(WIDE)
        logsums = logsum_ref[...]
        query_sum = []
        key_parts = []
        value_parts = []
        for head in range(2):
            base = HEAD_SIZE * (1 - head)
            own = lane // HEAD_SIZE == head
            column = jnp.sum(
                jnp.where(lane == 2 * pair + head, logsums, 0.0), axis=1, keepdims=True
            )
            inner = jnp.sum(jnp.where(own, along, 0.0), axis=1, keepdims=True)
            query_side = jnp.where(own, queries, jnp.where(lane == base, 1.0, 0.0))
            grad_side = jnp.where(own, grads, 0.0)
            for place, part in enumerate(split_three(column)):
                query_side = jnp.where(lane == base + 1 + place, -part, query_side)
            for place, part in enumerate(split_three(inner)):
                grad_side = jnp.where(lane == base + 1 + place, -part, grad_side)
            query_side = query_side.astype(LOW)
            grad_side = grad_side.astype(LOW)
            keys_side = key_side(keys, head, bias, lane)
            value_side = key_side(values, head, 0.0, lane)
            query_total = None
            for begin in range(0, rows, tile):
                spot = slice(begin, begin + tile)
                probs = jnp.exp(product(keys_side[spot], query_side, 1, 1))
                slopes = (probs * product(value_side[spot], grad_side, 1, 1)).astype(LOW)
                value_part = product(probs.astype(LOW), grad_side)
                key_part = product(slopes, query_side)
                query_part = product(slopes, keys_side[spot], 0, 0)
                query_total = query_part if query_total is None else query_total + query_part
                key_parts.append(key_part)
                value_parts.append(value_part)
            query_sum.append(query_total)
        query_grad_ref[:, columns] = (
            jnp.where(lane < HEAD_SIZE, query_sum[0], query_sum[1]) * HEAD_SIZE**-0.5
        ).astype(LOW)
        pieces = rows // tile
        for piece in range(pieces):
            spot = slice(piece * tile, (piece + 1) * tile)
            first = lane[:tile] < HEAD_SIZE
            key_grad_ref[spot, columns] = jnp.where(
                first, key_parts[piece], key_parts[pieces + piece]
            ).astype(LOW)
            value_grad_ref[spot, columns] = jnp.where(
                first, value_parts[piece], value_parts[pieces + piece]
            ).astype(LOW)

    def pairs_step(step, carry):
        for place in range(2):
            pair_step(2 * step + place)
        if after is not None:
            after(step)
        return carry

    lax.fori_loop(0, HEADS // 4, pairs_step, 0)


def normed(values):
    shifted = values - jnp.mean(values, axis=1, keepdims=True)
    scale = lax.rsqrt(jnp.mean(shifted * shifted, axis=1, keepdims=True) + 1e-05)
    return shifted * scale, scale


def norm(values, gain, bias):
    return normed(values)[0] * gain + bias


def norm_back(values, gain, grad):
    unit, scale = normed(values)
    inner = grad * gain
    back = scale * (
        inner
        - jnp.mean(inner, axis=1, keepdims=True)
        - unit * jnp.mean(inner * unit, axis=1, keepdims=True)
    )
    return back, column_sum(grad * unit), column_sum(grad)


def column_sum(values):
    return jnp.sum(values, axis=0, keepdims=True)


def row_tiles(rows, tile, body):
    def step(index, carry):
        body(pl.ds(pl.multiple_of(index * tile, tile), tile))
        return carry

    lax.fori_loop(0, rows // tile, step, 0)


def gelu_pair(value):
    square = value * value
    half = 0.5 * jnp.tanh(value * (GELU_SCALE + (GELU_SCALE * GELU_CUBE) * square)) + 0.5
    act = value * half
    slope = half + act * (1.0 - half) * (
        2.0 * GELU_SCALE + (6.0 * GELU_SCALE * GELU_CUBE) * square
    )
    return act, slope


SMALL_ROWS = 16
ROW_TILE = 128
HALF_TILE = 256


def columns_of(index, width):
    return pl.ds(pl.multiple_of(index * width, width), width)


def project(left_ref, right_ref, target_ref, width):
    def step(index, carry):
        columns = columns_of(index, width)
        target_ref[:, columns] = product(left_ref[...], right_ref[:, columns]).astype(LOW)
        return carry

    lax.fori_loop(0, target_ref.shape[1] // width, step, 0)


def wide_row(ref, row):
    return ref[0, row : row + 1, :].astype(WIDE)


def feed_forward(low_ref, wide_ref, in_w, in_b, out2_w, out2_b, act_ref, slope_ref, residual_ref):
    rows, width = low_ref.shape

    for index in range(act_ref.shape[1] // width):
        columns = pl.ds(index * width, width)
        bias = in_b[:, columns].astype(WIDE)
        for begin in range(0, rows, HALF_TILE):
            spot = slice(begin, begin + HALF_TILE)
            act, slope = gelu_pair(product(low_ref[spot], in_w[:, columns]) + bias)
            act_ref[spot, columns] = act.astype(LOW)
            slope_ref[spot, columns] = slope.astype(LOW)
    bias_out = out2_b[...].astype(WIDE)
    for begin in range(0, rows, HALF_TILE):
        spot = slice(begin, begin + HALF_TILE)
        residual_ref[spot] = wide_ref[spot] + product(act_ref[spot], out2_w[...]) + bias_out


def feed_back(residual_grad, grad_low, slope_ref, in_w, out2_w, hidden_grad, bias_rows, out_ref):
    rows, width = grad_low.shape

    for index in range(hidden_grad.shape[1] // width):
        columns = pl.ds(index * width, width)
        total = jnp.zeros((1, width), WIDE)
        for begin in range(0, rows, HALF_TILE):
            spot = slice(begin, begin + HALF_TILE)
            grads = product(grad_low[spot], out2_w[columns, :], 1, 1)
            grads = (grads * slope_ref[spot, columns].astype(WIDE)).astype(LOW)
            hidden_grad[spot, columns] = grads
            total = total + column_sum(grads.astype(WIDE))
        bias_rows[index : index + 1, :] = total
    for begin in range(0, rows, HALF_TILE):
        spot = slice(begin, begin + HALF_TILE)
        out_ref[spot] = residual_grad[spot] + product(hidden_grad[spot], in_w[...], 1, 1)


def feed_back_rolled(
    residual_grad, grad_low, slope_ref, in_w, out2_w, hidden_grad, bias_rows, out_ref
):
    rows, width = grad_low.shape

    def hidden_step(index, carry):
        columns = columns_of(index, width)
        grads = product(grad_low[...], out2_w[columns, :], 1, 1)
        grads = (grads * slope_ref[:, columns].astype(WIDE)).astype(LOW)
        hidden_grad[:, columns] = grads
        bias_rows[pl.ds(index, 1), :] = column_sum(grads.astype(WIDE))
        return carry

    lax.fori_loop(0, hidden_grad.shape[1] // width, hidden_step, 0)

    def out_step(spot):
        out_ref[spot] = residual_grad[spot] + product(hidden_grad[spot], in_w[...], 1, 1)

    row_tiles(rows, HALF_TILE, out_step)


def norm_back_rolled(values_ref, gain, grad_ref, wide_ref, low_ref, gain_row, bias_row):
    rows, width = values_ref.shape
    gain_row[...] = jnp.zeros((1, width), WIDE)
    bias_row[...] = jnp.zeros((1, width), WIDE)

    def step(spot):
        back, gain_part, bias_part = norm_back(values_ref[spot], gain, grad_ref[spot])
        wide_ref[spot] = back
        low_ref[spot] = back.astype(LOW)
        gain_row[...] += gain_part
        bias_row[...] += bias_part

    row_tiles(rows, ROW_TILE, step)


def norm_back_rows(values_ref, gain, grad_ref, wide_ref, low_ref, gain_row, bias_row):
    back, gain_part, bias_part = norm_back(values_ref[...], gain, grad_ref[...])
    wide_ref[...] = back
    low_ref[...] = back.astype(LOW)
    gain_row[...] = gain_part
    bias_row[...] = bias_part


MESH = pl.DeviceIdType.MESH


def ring_place(chip, chips):
    half = chip // 2
    return jnp.where(chip % 2 == 0, half, chips - 1 - half)


def ring_chip(place, chips):
    return jnp.where(place < chips // 2, 2 * place, 2 * (chips - 1 - place) + 1)


def part_count(chunk_rows):
    tiles = chunk_rows // 16
    return 2 if tiles % 4 == 0 else 1


def ring_layout(rows, devices):
    chips = devices // 2
    ways = 2 if rows >= 64 * chips else 1
    return ways, chips, -(-rows // (2 * ways * chips * 16)) * 16


def ring_rows(rows, devices):
    ways, chips, chunk_rows = ring_layout(rows, devices)
    return 2 * ways * chips * chunk_rows


def whenever(flag):
    return pl.when(flag) if not isinstance(flag, bool) else lambda body: body()


class Links:
    def __init__(self, devices):
        self.pipe = lax.axis_index("pipe")
        self.me = lax.axis_index("dp")
        self.chips = devices // 2
        self.levels = devices.bit_length() - 1
        self.core = self.me % 2
        self.place = ring_place(self.me // 2, self.chips)
        self.sides = tuple(
            ring_chip((self.place + step) % self.chips, self.chips) * 2 + self.core
            for step in (1, self.chips - 1)
        )
        self.other = self.paired(1)
        self.across = (1 - self.pipe, self.me)

    def paired(self, bit):
        return self.me + bit - 2 * bit * ((self.me // bit) % 2)

    def greet(self):
        barrier = pltpu.get_barrier_semaphore()
        greeted = list(self.sides) + [self.paired(1 << level) for level in range(self.levels)]
        for friend in greeted:
            pl.semaphore_signal(
                barrier, inc=1, device_id=(self.pipe, friend), device_id_type=MESH
            )
        pl.semaphore_signal(barrier, inc=1, device_id=self.across, device_id_type=MESH)

    def greeted(self):
        pl.semaphore_wait(pltpu.get_barrier_semaphore(), self.levels + 3)

    def copy(self, source, target, send, recv, friend):
        return pltpu.make_async_remote_copy(
            src_ref=source,
            dst_ref=target,
            send_sem=send,
            recv_sem=recv,
            device_id=friend if isinstance(friend, tuple) else (self.pipe, friend),
            device_id_type=MESH,
        )


class Ring:
    def __init__(self, links, layout, total, refs):
        self.links = links
        ways, self.chips, self.chunk_rows = layout
        self.ways = range(ways)
        self.count = part_count(self.chunk_rows)
        self.part_rows = self.chunk_rows // self.count
        self.total = total
        (
            self.mine, self.sibling, self.arrived, self.pair_send, self.pair_recv, self.ring_send,
            self.ring_recv, self.gather_send, self.gather_recv, self.share_send, self.share_recv,
        ) = refs

    def part_at(self, part):
        return pl.ds(pl.multiple_of(part * self.part_rows, 16), self.part_rows)

    def over(self, parts, body):
        low, high = (0, self.count) if parts is None else parts

        def step(part, carry):
            for way in self.ways:
                body(way, part)
            return carry

        lax.fori_loop(low, high, step, 0)

    def chunk_at(self, way, step):
        if way == 0:
            return lax.rem(self.links.place - step + 2 * self.chips, self.chips)
        return lax.rem(self.links.place + step + self.chips, self.chips)

    def start_row(self, core, way, chunk, part):
        begin = 0 if part is None else part * self.part_rows
        return ((core * len(self.ways) + way) * self.chips + chunk) * self.chunk_rows + begin

    def mine_at(self, core, way, chunk, part=None):
        rows = self.chunk_rows if part is None else self.part_rows
        return pl.ds(pl.multiple_of(self.start_row(core, way, chunk, part), 16), rows)

    def total_at(self, way, step, part):
        start = self.start_row(self.links.core, way, self.chunk_at(way, step), part)
        rows = self.part_rows
        if len(self.total.shape) == 2:
            return self.total.at[pl.ds(pl.multiple_of(start, 16), rows)]
        size = self.total.shape[1]
        return self.total.at[
            lax.div(start, size), pl.ds(pl.multiple_of(lax.rem(start, size), 16), rows)
        ]

    def pair_copy(self, way, step, mine=None, sibling=None, send=None, recv=None):
        chunk = self.chunk_at(way, step)
        return self.links.copy(
            (self.mine if mine is None else mine).at[
                self.mine_at(1 - self.links.core, way, chunk)
            ],
            (self.sibling if sibling is None else sibling).at[way, chunk],
            (self.pair_send if send is None else send).at[way, step],
            (self.pair_recv if recv is None else recv).at[way, step],
            self.links.other,
        )

    def ring_copy(self, way, step, part):
        spot = self.part_at(part)
        return self.links.copy(
            self.arrived.at[way, step, spot],
            self.arrived.at[way, step + 1, spot],
            self.ring_send.at[way, step, part],
            self.ring_recv.at[way, step, part],
            self.links.sides[way],
        )

    def gather_copy(self, way, step, part):
        spot = self.total_at(way, step - 1, part)
        return self.links.copy(
            spot,
            spot,
            self.gather_send.at[way, step, part],
            self.gather_recv.at[way, step, part],
            self.links.sides[way],
        )

    def share_copy(self, way, step):
        start = self.start_row(self.links.core, way, self.chunk_at(way, step - 1), None)
        rows = self.chunk_rows
        if len(self.total.shape) == 2:
            spot = self.total.at[pl.ds(pl.multiple_of(start, 16), rows)]
        else:
            size = self.total.shape[1]
            spot = self.total.at[
                lax.div(start, size), pl.ds(pl.multiple_of(lax.rem(start, size), 16), rows)
            ]
        return self.links.copy(
            spot, spot, self.share_send.at[way, step], self.share_recv.at[way, step],
            self.links.other,
        )

    def pairs_start(self):
        def start(step, carry):
            for way in self.ways:
                self.pair_copy(way, step).start()
            return carry

        lax.fori_loop(0, self.chips, start, 0)

    def pair_ready(self, way, step):
        self.pair_copy(way, step).wait()

    def begin(self):
        self.pairs_start()
        for way in self.ways:
            self.pair_ready(way, 0)

        def body(way, part):
            spot = self.part_at(part)
            chunk = self.links.place
            own = self.mine[self.mine_at(self.links.core, way, chunk, part)]
            pair = self.sibling[way, chunk, spot]
            self.arrived[way, 0, spot] = (own.astype(WIDE) + pair.astype(WIDE)).astype(LOW)
            self.ring_copy(way, 0, part).start()

        self.over(None, body)

    def merged(self, way, step, part):
        spot = self.part_at(part)
        chunk = self.chunk_at(way, step + 1)
        self.ring_copy(way, step, part).wait()
        own = self.mine[self.mine_at(self.links.core, way, chunk, part)]
        return (
            self.arrived[way, step + 1, spot].astype(WIDE)
            + own.astype(WIDE)
            + self.sibling[way, chunk, spot].astype(WIDE)
        ).astype(LOW)

    def pairs_ready(self, step):
        for way in self.ways:
            self.pair_ready(way, step)

    def reduce(self, step, parts=None):
        def body(way, part):
            self.arrived[way, step + 1, self.part_at(part)] = self.merged(way, step, part)
            self.ring_copy(way, step + 1, part).start()

        self.over(parts, body)

    def settle(self, parts=None, whole=True):
        def body(way, part):
            self.total_at(way, -1, part)[...] = self.merged(way, self.chips - 2, part)
            self.gather_copy(way, 0, part).start()

        self.over(parts, body)

        @whenever(whole)
        def _():
            for way in self.ways:
                self.share_copy(way, 0).start()

    def gather(self, step, parts=None, whole=True):
        def body(way, part):
            self.gather_copy(way, step, part).wait()
            self.gather_copy(way, step + 1, part).start()

        self.over(parts, body)

        @whenever(whole)
        def _():
            for way in self.ways:
                self.share_copy(way, step + 1).start()
                self.share_copy(way, step).wait()

    def gather_last(self, parts=None, whole=True):
        last = self.chips - 2
        self.over(parts, lambda way, part: self.gather_copy(way, last, part).wait())

        @whenever(whole)
        def _():
            for way in self.ways:
                self.share_copy(way, last + 1).start()
                self.share_copy(way, last).wait()

    def finish(self):
        for way in self.ways:
            self.share_copy(way, self.chips - 1).wait()


class CrossRing(Ring):
    def __init__(self, links, layout, total, refs, foreign_refs):
        super().__init__(links, layout, total, refs)
        self.foreign, self.foreign_sibling = foreign_refs[:2]
        self.foreign_send, self.foreign_recv, self.cross_send, self.cross_recv = foreign_refs[2:]

    def foreign_pair(self, way, step):
        return self.pair_copy(
            way, step, self.foreign, self.foreign_sibling, self.foreign_send, self.foreign_recv
        )

    def cross_copy(self, way, step):
        spot = self.mine_at(self.links.core, way, self.chunk_at(way, step))
        return self.links.copy(
            self.foreign.at[spot],
            self.mine.at[spot],
            self.cross_send.at[way, step],
            self.cross_recv.at[way, step],
            self.links.across,
        )

    def each(self, body):
        def step_all(step, carry):
            for way in self.ways:
                body(way, step)
            return carry

        lax.fori_loop(0, self.chips, step_all, 0)

    def foreign_start(self):
        self.each(lambda way, step: self.foreign_pair(way, step).start())

    def foreign_pass(self):
        def hand_over(way, step):
            chunk = self.chunk_at(way, step)
            spot = self.mine_at(self.links.core, way, chunk)
            self.foreign_pair(way, step).wait()
            self.foreign[spot] = (
                self.foreign[spot].astype(WIDE) + self.foreign_sibling[way, chunk].astype(WIDE)
            ).astype(LOW)
            self.cross_copy(way, step).start()

        self.each(hand_over)

    def pairs_start(self):
        pl.when(self.links.pipe == 1)(super().pairs_start)

        @pl.when(self.links.pipe == 0)
        def _():
            self.sibling[...] = jnp.zeros_like(self.sibling)

    def pair_ready(self, way, step):
        @pl.when(self.links.pipe == 1)
        def _():
            self.pair_copy(way, step).wait()
            self.cross_copy(way, step).wait_send()

        @pl.when(self.links.pipe == 0)
        def _():
            self.cross_copy(way, step).wait_recv()


def ring_scratch(rows, width, devices):
    ways, chips, chunk_rows = ring_layout(rows, devices)
    pieces = part_count(chunk_rows)
    dma = pltpu.SemaphoreType.DMA
    return [
        pltpu.VMEM((2 * ways * chips * chunk_rows, width), LOW),
        pltpu.VMEM((ways, chips, chunk_rows, width), LOW),
        pltpu.VMEM((ways, chips, chunk_rows, width), LOW),
        dma((ways, chips)),
        dma((ways, chips)),
    ] + [dma((ways, chips, pieces)) for _ in range(4)] + [dma((ways, chips))] * 2


def foreign_scratch(rows, width, devices):
    ways, chips, chunk_rows = ring_layout(rows, devices)
    dma = pltpu.SemaphoreType.DMA
    return [
        pltpu.VMEM((2 * ways * chips * chunk_rows, width), LOW),
        pltpu.VMEM((ways, chips, chunk_rows, width), LOW),
    ] + [dma((ways, chips)) for _ in range(4)]


def flat_row(ref):
    return ref[...].astype(WIDE).reshape(1, ref.shape[0])


class Outs:
    def __init__(self, semaphores, table):
        self.semaphores = semaphores
        self.table = table
        self.order = {name: place for place, name in enumerate(table)}

    def copy(self, name, example):
        source, target = self.table[name](example)
        return pltpu.make_async_copy(
            source, target, self.semaphores.at[example, self.order[name]]
        )

    def start(self, name, example):
        self.copy(name, example).start()

    def free(self, name, example):
        @pl.when(example == 1)
        def _():
            self.copy(name, 0).wait()

    def wait(self, names, examples):
        for name in names:
            for example in examples:
                self.copy(name, example).wait()


def main_kernel(
    src_len, tgt_len, in_b, out2_b, gains, biases, cross_gain, cross_bias, inputs, cotangent,
    qkv_w, out_w, in_w, out2_w, cross_qkv, cross_out, slot_w, small_out, block_out, qkv_out,
    logsum_out, mixed_out, residual_out, low_out, act_out, slope_out, second_out, grad_out,
    hidden_out, branch_out, qkv_grad_out, rows_out, query_out, rest_out, memory_out, query_w_out,
    own_out, sent_out, x_s, qkv_w_s, out_w_s, in_w_s, out2_w_s, cross_w_s, cross_out_s, slot_w_s,
    gains_s, qkv_s, logsum_s, mixed_s, residual_s, wide_s, low_s, act_s, slope_s, second_s,
    left_s, right_s, query_s, pair_s, cross_logsum_s, cross_s, slot_s, wide_grad_s, grad_low_s, hidden_s, back_s, rest_s, attn_grad_s,
    memory_grad_s, qkv_grad_s, part_s, load_sem, out_sem, memory_send,
    memory_recv, return_send, return_recv, weight_send, weight_recv, near_send, near_recv,
):
    section = lax.axis_index("pipe")
    me = lax.axis_index("dp")
    core = lax.rem(me, 2)
    across, other = (1 - section, me), (section, me + 1 - 2 * core)
    encoder, decoder = section == 0, section == 1
    first_s, memory_s, cross_mixed_s, final_s = [left_s.at[place] for place in range(4)]
    query_grad_s, key_grad_s, value_grad_s, branch_s, grad_s, earlier_s = [
        right_s.at[place] for place in range(6)
    ]
    total_rows, width = x_s.shape
    rows = total_rows // 2
    half = width // 2
    part = half // 2
    barrier = pltpu.get_barrier_semaphore()
    for friend in (across, other):
        pl.semaphore_signal(barrier, inc=1, device_id=friend, device_id_type=MESH)

    copies = Copies(load_sem)
    x_copy = copies.start(inputs.at[0], x_s)
    qkv_w_copy = copies.start(qkv_w.at[0], qkv_w_s)
    out_w_copy = copies.start(out_w.at[0], out_w_s)
    in_w_copy = copies.start(in_w.at[0], in_w_s)
    out2_w_copy = copies.start(out2_w.at[0], out2_w_s)
    decoder_loads = [
        pltpu.make_async_copy(source, target, load_sem.at[copies.count + place])
        for place, (source, target) in enumerate(
            (
                (cotangent, grad_s),
                (cross_qkv, cross_w_s.at[pl.ds(half, half)]),
                (cross_out, cross_out_s.at[pl.ds(half, half)]),
                (slot_w, slot_w_s.at[pl.ds(width, width)]),
            )
        )
    ]

    def remote(source, target, send, recv, friend):
        return pltpu.make_async_remote_copy(
            src_ref=source, dst_ref=target, send_sem=send, recv_sem=recv, device_id=friend,
            device_id_type=MESH,
        )

    def piece(rows_each):
        return pl.ds(pl.multiple_of(core * rows_each, rows_each), rows_each)

    weight_pieces = (
        (cross_qkv, cross_w_s, piece(part)),
        (cross_out, cross_out_s, piece(part)),
        (slot_w, slot_w_s, piece(2 * part)),
    )
    gains_copy = remote(gains_s, gains_s, weight_send.at[3], weight_recv.at[3], across)
    weight_copies = [
        remote(source.at[spot], target.at[spot], weight_send.at[place], weight_recv.at[place], across)
        for place, (source, target, spot) in enumerate(weight_pieces)
    ]
    near_copies = [
        remote(target.at[spot], target.at[spot], near_send.at[place], near_recv.at[place], other)
        for place, (_, target, spot) in enumerate(weight_pieces)
    ]

    def memory_copy(example, tile):
        begin = pl.multiple_of(example * rows + tile * ROW_TILE, ROW_TILE)
        block = memory_s.at[pl.ds(begin, ROW_TILE)]
        return remote(
            block, block, memory_send.at[example, tile], memory_recv.at[example, tile], across
        )

    def return_copy(example, tile):
        spot = pl.ds(pl.multiple_of(tile * HALF_TILE, HALF_TILE), HALF_TILE)
        block = memory_grad_s.at[example, spot]
        return remote(
            block, block, return_send.at[example, tile], return_recv.at[example, tile], across
        )

    def rows_of(example):
        return pl.ds(pl.multiple_of(example * rows, rows), rows)

    outs = Outs(
        out_sem,
        {
            "qkv": lambda e: (qkv_s.at[e], qkv_out.at[e]),
            "logsum": lambda e: (logsum_s.at[e], logsum_out.at[e]),
            "mixed": lambda e: (mixed_s.at[e], mixed_out.at[e]),
            "residual": lambda e: (residual_s.at[e], residual_out.at[e]),
            "low": lambda e: (low_s, low_out.at[e]),
            "act": lambda e: (act_s, act_out.at[e]),
            "slope": lambda e: (slope_s.at[e], slope_out),
            "second": lambda e: (second_s.at[e], second_out),
            "memory": lambda e: (memory_s.at[rows_of(e)], block_out.at[0, rows_of(e)]),
            "slot": lambda e: (slot_s, block_out.at[0, rows_of(e)]),
            "grad": lambda e: (grad_low_s, grad_out.at[e]),
            "hidden": lambda e: (hidden_s, hidden_out.at[e]),
            "rest": lambda e: (rest_s, rest_out.at[e]),
            "query": lambda e: (query_grad_s.at[rows_of(e)], query_out.at[e]),
            "branch": lambda e: (branch_s.at[rows_of(e)], branch_out),
            "qkv_grad": lambda e: (qkv_grad_s, qkv_grad_out),
            "rows": lambda e: (back_s, rows_out.at[0, rows_of(e)]),
            "return": lambda e: (memory_grad_s.at[e], memory_out),
            "query_w": lambda e: (cross_w_s.at[:, pl.ds(0, width)], query_w_out),
        },
    )
    small_out[...] = jnp.zeros_like(small_out)
    gain_first, bias_first = wide_row(gains, 0), wide_row(biases, 0)
    gain_last, bias_last = wide_row(gains, 1), wide_row(biases, 1)
    @pl.when(decoder)
    def _():
        for copy in decoder_loads:
            copy.start()

    x_copy.wait()
    qkv_w_copy.wait()

    def self_step(example, carry):
        x_rows = x_s.at[rows_of(example)]
        qkv_rows = qkv_s.at[example]
        project(x_rows, qkv_w_s, qkv_rows, width)
        outs.start("qkv", example)

        @pl.when(example == 0)
        def _():
            pl.semaphore_wait(barrier, 2)

        @pl.when((example == 0) & encoder)
        def _():
            row = jnp.concatenate([flat_row(cross_gain), flat_row(cross_bias)], axis=1)
            gains_s[...] = jnp.broadcast_to(row, gains_s.shape).astype(LOW)
            gains_copy.start()
            for copy in weight_copies[:2]:
                copy.start()

        count = jnp.where(encoder, src_len[example], tgt_len[example])
        attend(
            qkv_s.at[example, :, pl.ds(0, width)],
            qkv_s.at[example, :, pl.ds(width, width)],
            qkv_s.at[example, :, pl.ds(2 * width, width)],
            count,
            mixed_s.at[example],
            logsum_s.at[example],
        )
        outs.start("mixed", example)
        outs.start("logsum", example)

        @pl.when(example == 0)
        def _():
            out_w_copy.wait()

        def residual_step(spot):
            residual_s[example, spot] = x_rows[spot].astype(WIDE) + product(
                mixed_s[example, spot], out_w_s[...]
            )

        row_tiles(rows, HALF_TILE, residual_step)
        outs.start("residual", example)

        @pl.when(example == 0)
        def _():
            in_w_copy.wait()
            out2_w_copy.wait()

        @pl.when(encoder)
        def _():
            outs.free("low", example)

            value = norm(residual_s[example], gain_first, bias_first)
            wide_s[...] = value
            low_s[...] = value.astype(LOW)
            outs.start("low", example)
            outs.free("act", example)
            feed_forward(
                low_s, wide_s, in_w_s, in_b, out2_w_s, out2_b, act_s, slope_s.at[example],
                second_s.at[example],
            )
            outs.start("act", example)

            def memory_step(tile, inner):
                spot = pl.ds(pl.multiple_of(tile * ROW_TILE, ROW_TILE), ROW_TILE)
                row = lax.broadcasted_iota(jnp.int32, (ROW_TILE, width), 0) + tile * ROW_TILE
                value = norm(second_s[example, spot], gain_last, bias_last)
                begin = pl.multiple_of(example * rows + tile * ROW_TILE, ROW_TILE)
                memory_s[pl.ds(begin, ROW_TILE)] = jnp.where(row < count, value, 0.0).astype(LOW)
                memory_copy(example, tile).start()
                return inner

            lax.fori_loop(0, rows // ROW_TILE, memory_step, 0)
            outs.start("memory", example)
            pl.when(example == 0)(weight_copies[2].start)

            @pl.when(example == 1)
            def _():
                outs.start("slope", 1)
                outs.start("second", 1)

        return carry

    lax.fori_loop(0, 2, self_step, 0)

    @pl.when(encoder)
    def _():
        for tile in range(rows // HALF_TILE):
            return_copy(0, tile).wait_recv()
        row = lax.broadcasted_iota(jnp.int32, (rows, width), 0)
        wide_grad_s[...] = jnp.where(row < src_len[0], memory_grad_s[0].astype(WIDE), 0.0)
        norm_back_rolled(
            second_s.at[0], gain_last, wide_grad_s, wide_s, grad_low_s,
            small_out.at[6:7, :], small_out.at[8:9, :],
        )
        outs.start("grad", 0)
        small_out[4:5, :] = column_sum(grad_low_s[...].astype(WIDE))
        feed_back_rolled(
            wide_s, grad_low_s, slope_s.at[0], in_w_s, out2_w_s, hidden_s, small_out.at[0:4, :],
            wide_grad_s,
        )
        outs.start("hidden", 0)
        norm_back_rolled(
            residual_s.at[0], gain_first, wide_grad_s, rest_s, branch_s.at[pl.ds(0, rows)],
            small_out.at[5:6, :], small_out.at[7:8, :],
        )
        outs.start("branch", 0)
        attn_grad_s[...] = product(branch_s[:rows], out_w_s[...], 1, 1).astype(LOW)
        attend_back(
            qkv_s.at[0, :, pl.ds(0, width)],
            qkv_s.at[0, :, pl.ds(width, width)],
            qkv_s.at[0, :, pl.ds(2 * width, width)],
            src_len[0],
            mixed_s.at[0],
            logsum_s.at[0],
            attn_grad_s,
            qkv_grad_s.at[:, pl.ds(0, width)],
            qkv_grad_s.at[:, pl.ds(width, width)],
            qkv_grad_s.at[:, pl.ds(2 * width, width)],
        )
        outs.start("qkv_grad", 0)

        def rows_step(spot):
            back_s[spot] = rest_s[spot] + product(qkv_grad_s[spot], qkv_w_s[...], 1, 1)

        row_tiles(rows, HALF_TILE, rows_step)
        outs.start("rows", 0)
        gains_copy.wait_send()
        for copy in weight_copies:
            copy.wait_send()

        def sent_step(tile, inner):
            for example in range(2):
                memory_copy(example, tile).wait_send()
            return inner

        lax.fori_loop(0, rows // ROW_TILE, sent_step, 0)
        outs.wait(("low", "act", "slope", "second"), (1,))
        outs.wait(("memory",), (0, 1))
        outs.wait(("grad", "hidden", "branch", "qkv_grad", "rows"), (0,))
        for tile in range(rows // HALF_TILE):
            return_copy(1, tile).wait_recv()
        outs.start("return", 1)
        outs.wait(("return",), (1,))

    @pl.when(decoder)
    def _():
        for copy in decoder_loads:
            copy.wait()
        for example in range(2):
            spot = slice(example * rows, (example + 1) * rows)
            row = lax.broadcasted_iota(jnp.int32, (rows, width), 0)
            slot_grad = jnp.where(
                row < tgt_len[example] - 1, grad_s[spot].astype(WIDE), 0.0
            )
            grad_s[spot] = slot_grad.astype(LOW)
            earlier = jnp.where(row == 0, 0.0, pltpu.roll(slot_grad, 1, 0))
            earlier_s[spot] = earlier.astype(LOW)
        for place in range(2):
            weight_copies[place].wait_recv()
            near_copies[place].start()
        gains_copy.wait_recv()
        for copy in near_copies[:2]:
            copy.wait_recv()
        outs.start("query_w", 0)
        came_row = gains_s[0:1, :].astype(WIDE)
        gain_cross = jnp.concatenate([came_row[:, :half], flat_row(cross_gain)], axis=1)
        bias_cross = jnp.concatenate([came_row[:, half:], flat_row(cross_bias)], axis=1)

        def cross_step(example, carry):
            spot_rows = rows_of(example)
            first = first_s.at[spot_rows]
            final = final_s.at[spot_rows]
            slot_grad, earlier = grad_s.at[spot_rows], earlier_s.at[spot_rows]
            mixed, branch = cross_mixed_s.at[spot_rows], branch_s.at[spot_rows]
            query_grad = query_grad_s.at[spot_rows]
            key_grad, value_grad = key_grad_s.at[spot_rows], value_grad_s.at[spot_rows]
            second = second_s.at[0]
            slope = slope_s.at[0]

            value = norm(residual_s[example], gain_first, bias_first)
            wide_s[...] = value
            first[...] = value.astype(LOW)
            query_s[...] = product(first[...], cross_w_s[:, :width]).astype(LOW)

            def arrive(tile, inner):
                memory_copy(example, tile).wait_recv()
                return inner

            lax.fori_loop(0, rows // ROW_TILE, arrive, 0)
            project(memory_s.at[spot_rows], cross_w_s.at[:, width:], pair_s, width)
            key_ref, value_ref = pair_s.at[:, :width], pair_s.at[:, width:]
            count = src_len[example]
            attend(query_s, key_ref, value_ref, count, mixed, cross_logsum_s)
            outs.free("low", example)

            for begin in range(0, rows, HALF_TILE):
                spot = slice(begin, begin + HALF_TILE)
                value = wide_s[spot] + product(mixed[spot], cross_out_s[...])
                cross_s[spot] = value
                value = norm(value, gain_cross, bias_cross)
                wide_s[spot] = value
                low_s[spot] = value.astype(LOW)
            outs.start("low", example)

            @pl.when(example == 0)
            def _():
                weight_copies[2].wait_recv()
                near_copies[2].start()

            outs.free("act", example)
            feed_forward(
                low_s, wide_s, in_w_s, in_b, out2_w_s, out2_b, act_s, slope, second
            )
            outs.start("act", example)

            pl.when(example == 0)(near_copies[2].wait_recv)
            wide_grad_s[...] = product(slot_grad[...], slot_w_s[:width, :], 1, 1) + product(
                earlier[...], slot_w_s[width:, :], 1, 1
            )
            outs.free("grad", example)
            part_s[...] = jnp.zeros_like(part_s)
            norm_back_rows(
                second, gain_last, wide_grad_s, second_s.at[1], grad_low_s,
                part_s.at[6:7, :], part_s.at[8:9, :],
            )
            outs.start("grad", example)
            outs.free("hidden", example)
            feed_back(
                second_s.at[1], grad_low_s, slope, in_w_s, out2_w_s, hidden_s,
                part_s.at[0:4, :], back_s,
            )
            outs.start("hidden", example)
            outs.free("rest", example)
            norm_back_rows(
                cross_s, gain_cross, back_s, rest_s, branch, part_s.at[9:10, :],
                part_s.at[10:11, :],
            )
            outs.start("rest", example)
            attn_grad_s[...] = product(branch[...], cross_out_s[...], 1, 1).astype(LOW)
            attend_back(
                query_s, key_ref, value_ref, count, mixed, cross_logsum_s, attn_grad_s,
                query_grad, key_grad, value_grad,
            )
            for tile in range(rows // HALF_TILE):
                spot = pl.ds(tile * HALF_TILE, HALF_TILE)
                memory_grad_s[example, spot] = (
                    product(key_grad[spot], cross_w_s[:, width : 2 * width], 1, 1)
                    + product(value_grad[spot], cross_w_s[:, 2 * width :], 1, 1)
                ).astype(LOW)
                return_copy(example, tile).start()
            outs.start("query", example)
            part_s[4:5, :] = column_sum(grad_low_s[...].astype(WIDE))
            small_out[...] += part_s[...]
            final[...] = norm(second[...], gain_last, bias_last).astype(LOW)
            outs.free("slot", example)
            wide_grad_s[...] = product(final[...], slot_w_s[width:, :])
            value = product(final[...], slot_w_s[:width, :]) + pltpu.roll(
                wide_grad_s[...], rows - 1, 0
            )
            row = lax.broadcasted_iota(jnp.int32, (rows, width), 0)
            slot_s[...] = jnp.where(row < tgt_len[example] - 1, value, 0.0).astype(LOW)
            outs.start("slot", example)
            return carry

        lax.fori_loop(0, 2, cross_step, 0)
        outs.wait(("qkv",), (0, 1))

        def weight_step(place, carry):
            value = product(
                left_s[lax.div(2 * place + 1, 3)], right_s[place], 0, 0
            ).astype(LOW)
            block = lax.div(place, 2)
            columns = columns_of(block, width)
            begin = pl.multiple_of((place - 2 * block) * half, half)

            @pl.when(place < 4)
            def _():
                qkv_s[1, pl.ds(begin, half), columns] = value[:half]
                qkv_s[0, pl.ds(begin, half), columns] = value[half:]

            @pl.when(place >= 4)
            def _():
                qkv_s[5 - place, :, columns] = value

            return carry

        lax.fori_loop(0, 6, weight_step, 0)
        kept = []
        for target, slot in ((own_out, 0), (sent_out, 1)):
            for block in range(3):
                kept.append(
                    pltpu.make_async_copy(
                        qkv_s.at[slot, :, pl.ds(block * width, width)],
                        target.at[pl.ds(block * width, width)],
                        load_sem.at[3 * slot + block],
                    )
                )
        for copy in kept:
            copy.start()
        for copy in near_copies:
            copy.wait_send()

        def returned(tile, inner):
            for example in range(2):
                return_copy(example, tile).wait_send()
            return inner

        lax.fori_loop(0, rows // HALF_TILE, returned, 0)
        outs.wait(("low", "act", "grad", "hidden", "rest", "slot"), (1,))
        outs.wait(("query",), (0, 1))
        outs.wait(("query_w",), (0,))
        for copy in kept:
            copy.wait()

    @pl.when(encoder)
    def _():
        outs.wait(("qkv",), (0, 1))

    outs.wait(("mixed", "logsum", "residual"), (0, 1))


def last_kernel(
    devices, src_len, tgt_len, gains, small_in, inputs, qkv_w, out_w, in_w, out2_w, query_w,
    memory_grad, second_in, slope_in, query_grad, rest_in, residual_in, qkv_in, logsum_in, mixed_in,
    low_in, act_in, grad_in, hidden_in, branch_a, qkv_grad_a, own_extra, sent_extra, first_total,
    second_total, cross_total, small_total, rows_out, qkv_w_s, out_w_s, in_w_s, out2_w_s, low_s,
    hidden_s, act_s, grad_s, mixed_s, branch_s, x_s, qkv_grad_s, memory_s, second_s, slope_s,
    back_s, query_w_s, residual_s, qkv_s, logsum_s, rest_s, attn_grad_s, small_s, small_arrived,
    cross_total_s, small_send, small_recv, small_cross_sem, semaphores, *ring_refs,
):
    mixed_a, mixed_b = mixed_in.at[0], mixed_in.at[1]
    low_a, low_b = low_in.at[0], low_in.at[1]
    act_a, act_b = act_in.at[0], act_in.at[1]
    grad_a, grad_b = grad_in.at[0], grad_in.at[1]
    hidden_a, hidden_b = hidden_in.at[0], hidden_in.at[1]
    links = Links(devices)
    links.greet()
    chips, levels = links.chips, links.levels
    section = links.pipe
    rows, width = residual_s.shape
    half = width // 2
    hidden = hidden_s.shape[1]
    hidden_blocks = hidden // width
    extra_rows = own_extra.shape[0]
    sizes = (2 * hidden, 4 * width, extra_rows)
    layouts = [ring_layout(size, devices) for size in sizes]
    early = Ring(links, layouts[0], act_s, ring_refs[:11])
    late = Ring(links, layouts[1], out2_w_s, ring_refs[11:22])
    cross = CrossRing(links, layouts[2], cross_total_s, ring_refs[22:33], ring_refs[33:])
    front, rear = pl.ds(0, rows), pl.ds(rows, rows)
    gain_first, gain_last = wide_row(gains, 0), wide_row(gains, 1)
    small_s[0] = small_in[...]
    partial = small_arrived.at[0]
    partial[...] = jnp.zeros_like(small_in)

    encoder = section == 0
    copies = Copies(semaphores)

    def declared(source, target):
        copy = pltpu.make_async_copy(source, target, semaphores.at[copies.count])
        copies.count += 1
        return copy

    def start(*group):
        for copy in group:
            copy.start()

    def wait(*group):
        for copy in group:
            copy.wait()

    hidden_front = [declared(low_a, low_s.at[front]), declared(low_b, low_s.at[rear]),
                    declared(hidden_a, hidden_s.at[front])]
    act_front = [declared(grad_a, grad_s.at[front])]
    for index in range(hidden_blocks):
        columns = pl.ds(index * width, width)
        act_front.append(declared(act_a.at[:, columns], act_s.at[index, front]))
        act_front.append(declared(act_b.at[:, columns], act_s.at[index, rear]))
    hidden_rear = declared(hidden_b, hidden_s.at[rear])
    grad_rear = declared(grad_b, grad_s.at[rear])
    back_inputs = [declared(memory_grad, memory_s), declared(second_in, second_s),
                   declared(slope_in, slope_s), declared(out2_w.at[0], out2_w_s),
                   declared(in_w.at[0], in_w_s)]
    query_weights = [declared(query_w, query_w_s)]
    out_w_copy = declared(out_w.at[0], out_w_s)
    qkv_w_copy = declared(qkv_w.at[0], qkv_w_s)
    mixed_copies = [declared(mixed_a, mixed_s.at[front]), declared(mixed_b, mixed_s.at[rear])]
    saved = []
    base = copies.count
    for example in range(2):
        copies.count = base
        parts = [
            ref.at[example] for ref in (residual_in, query_grad, rest_in, qkv_in, logsum_in)
        ]
        targets = (residual_s, memory_s, second_s, qkv_s, logsum_s)
        saved.append([declared(source, target) for source, target in zip(parts, targets)])
    encoder_inputs = [declared(branch_a, branch_s.at[front]),
                      declared(qkv_grad_a, qkv_grad_s.at[front])]
    inputs_copy = declared(inputs.at[0], x_s)
    extra_loads = [declared(own_extra, cross.mine.at[pl.ds(0, extra_rows)]),
                   declared(sent_extra, cross.foreign.at[pl.ds(0, extra_rows)])]
    if cross.mine.shape[0] > extra_rows:
        cross.mine[extra_rows:] = jnp.zeros_like(cross.mine[extra_rows:])
        cross.foreign[extra_rows:] = jnp.zeros_like(cross.foreign[extra_rows:])

    def rows_copy(example):
        spot = pl.ds(pl.multiple_of(example * rows, rows), rows)
        return pltpu.make_async_copy(rest_s, rows_out.at[spot], semaphores.at[copies.count])

    @pl.when(encoder)
    def _():
        start(*back_inputs, *hidden_front, *act_front, out_w_copy, qkv_w_copy, *mixed_copies,
              *encoder_inputs, inputs_copy)
        wait(*back_inputs[:2])
        row = lax.broadcasted_iota(jnp.int32, (rows, width), 0)
        rest_s[...] = jnp.where(row < src_len[1], memory_s[...].astype(WIDE), 0.0)
        norm_back_rolled(
            second_s, gain_last, rest_s, second_s, grad_s.at[rear],
            partial.at[6:7, :], partial.at[8:9, :],
        )
        partial[4:5, :] = column_sum(grad_s[rear].astype(WIDE))
        wait(*back_inputs[2:])
        feed_back_rolled(
            second_s, grad_s.at[rear], slope_s, in_w_s, out2_w_s, hidden_s.at[rear],
            partial.at[0:4, :], back_s,
        )
        start(saved[1][0], *saved[1][3:])

    @pl.when(section == 1)
    def _():
        start(*hidden_front, hidden_rear, *act_front, grad_rear, *saved[0], *query_weights,
              out_w_copy, qkv_w_copy, *mixed_copies, *extra_loads, inputs_copy)
        wait(hidden_rear, grad_rear)

    def blocks(target, begin, count, block):
        def step(index, carry):
            target[columns_of(begin + index, width), :] = block(index).astype(LOW)
            return carry

        lax.fori_loop(0, count, step, 0)

    wait(*hidden_front)
    blocks(
        early.mine, 0, hidden_blocks,
        lambda index: product(low_s[...], hidden_s[:, columns_of(index, width)], 0, 0),
    )
    wait(*act_front)
    blocks(
        early.mine, hidden_blocks, hidden_blocks,
        lambda index: product(act_s[index], grad_s[...], 0, 0),
    )
    links.greeted()
    small_cross = links.copy(
        small_s.at[levels], small_arrived.at[1], small_cross_sem.at[0], small_cross_sem.at[1],
        links.across,
    )

    @pl.when(section == 1)
    def _():
        small_s[levels, 0:1, :] = jnp.concatenate(
            [small_s[0, 9:10, :half], small_s[0, 10:11, :half]], axis=1
        )
        small_cross.start()
        wait(*extra_loads)
        cross.foreign_start()

    early.begin()

    @pl.when(section == 1)
    def _():
        cross.foreign_pass()

    cross.begin()
    per_example = 6
    final = 2 * chips - 3
    middle = max(1, early.count // 2)
    begin_at = jnp.where(encoder, 1, 0)
    @pl.when(section == 1)
    def _():
        wait(*query_weights)

    wait(out_w_copy, qkv_w_copy, *mixed_copies)

    def advance(first, count):
        def half_turn(half, carry):
            turn, odd = lax.div(half, 2), lax.rem(half, 2)
            parts = (odd * middle, jnp.where(odd == 1, early.count, middle))

            @pl.when((turn <= chips - 2) & (odd == 0))
            def _():
                early.pairs_ready(turn + 1)

            @pl.when(turn < chips - 2)
            def _():
                early.reduce(turn, parts)

            @pl.when(turn == chips - 2)
            def _():
                early.settle(parts, odd == 1)

            @pl.when((turn > chips - 2) & (turn < final))
            def _():
                early.gather(turn - (chips - 1), parts, odd == 1)

            @pl.when(turn == final)
            def _():
                early.gather_last(parts, odd == 1)

            @pl.when((turn <= chips - 2) & (odd == 1))
            def _():
                cross.pairs_ready(turn + 1)

            @pl.when((turn < chips - 2) & (odd == 1))
            def _():
                cross.reduce(turn)

            @pl.when((turn == chips - 2) & (odd == 1))
            def _():
                cross.settle()

            @pl.when((turn > chips - 2) & (turn < final) & (odd == 1))
            def _():
                cross.gather(turn - (chips - 1))

            @pl.when((turn == final) & (odd == 1))
            def _():
                cross.gather_last()

            return carry

        lax.fori_loop(first, first + count, half_turn, 0)

    def back_step(example, carry):
        spot = pl.ds(pl.multiple_of(example * rows, rows), rows)
        turn = (example - begin_at) * per_example

        @pl.when(section == 1)
        def _():
            wait(*saved[0][:3])

            def first_step(tile):
                back_s[tile] = second_s[tile] + product(memory_s[tile], query_w_s[...], 1, 1)

            row_tiles(rows, HALF_TILE, first_step)

        @pl.when(encoder)
        def _():
            wait(saved[0][0])

        @pl.when((section == 1) & (example == 1))
        def _():
            rows_copy(0).wait()

        low_branch = branch_s.at[spot]
        norm_back_rows(
            residual_s, gain_first, back_s, rest_s, low_branch,
            partial.at[12:13, :], partial.at[13:14, :],
        )
        partial[5:6, :] += partial[12:13, :]
        partial[7:8, :] += partial[13:14, :]
        attn_grad_s[...] = product(low_branch[...], out_w_s[...], 1, 1).astype(LOW)
        wait(*saved[0][3:])
        advance(turn, 2)
        count = jnp.where(encoder, src_len[example], tgt_len[example])
        attend_back(
            qkv_s.at[:, :width],
            qkv_s.at[:, width : 2 * width],
            qkv_s.at[:, 2 * width :],
            count,
            mixed_s.at[spot],
            logsum_s,
            attn_grad_s,
            qkv_grad_s.at[spot, pl.ds(0, width)],
            qkv_grad_s.at[spot, pl.ds(width, width)],
            qkv_grad_s.at[spot, pl.ds(2 * width, width)],
            after=lambda step: advance(turn + 2 + 2 * step, 2),
        )

        @pl.when(example == 0)
        def _():
            start(*saved[1])

        def rows_step(index, inner):
            tile = pl.ds(pl.multiple_of(index * HALF_TILE, HALF_TILE), HALF_TILE)
            begin = pl.multiple_of(example * rows + index * HALF_TILE, HALF_TILE)
            rest_s[tile] += product(qkv_grad_s[pl.ds(begin, HALF_TILE)], qkv_w_s[...], 1, 1)
            return inner

        lax.fori_loop(0, rows // HALF_TILE, rows_step, 0)
        rows_copy(example).start()
        return carry

    lax.fori_loop(begin_at, 2, back_step, 0)
    wait(inputs_copy)

    @pl.when(encoder)
    def _():
        wait(*encoder_inputs)

    blocks(
        late.mine, 0, 3,
        lambda index: product(x_s[...], qkv_grad_s[:, columns_of(index, width)], 0, 0),
    )
    done = (2 - begin_at) * per_example
    advance(done, 2)
    blocks(late.mine, 3, 1, lambda index: product(mixed_s[...], branch_s[...], 0, 0))

    if late.mine.shape[0] > 4 * width:
        late.mine[4 * width :] = jnp.zeros_like(late.mine[4 * width :])
    late.begin()
    advance(done + 2, 2)
    done = done + 4
    ahead = jnp.where(encoder, 2, 1)

    small_s[0] = small_s[0] + partial[...]
    @pl.when(section == 1)
    def _():
        small_s[0, 9:10, :] = jnp.concatenate(
            [small_s[0, 9:10, half:], small_s[0, 10:11, half:]], axis=1
        )
        small_cross.wait_send()

    @pl.when(encoder)
    def _():
        small_cross.wait_recv()
        small_s[0, 9:10, :] = small_arrived[1, 0:1, :]

    def small_copy(level, bit):
        return links.copy(
            small_s.at[level],
            small_arrived.at[level + 2],
            small_send.at[level],
            small_recv.at[level],
            links.paired(bit),
        )

    small_copy(0, 1).start()

    def merge_small(level, bit):
        small_copy(level, bit).wait_recv()
        merged = small_s[level] + small_arrived[level + 2]

        @pl.when(level + 1 < levels)
        def _():
            small_s[level + 1] = merged
            small_copy(level + 1, 2 * bit).start()

        @pl.when(level + 1 == levels)
        def _():
            small_total[...] = merged

    def both_step(step, bit):
        late.pairs_ready(step + 1)
        late.reduce(step)
        advance(done + ahead * step, ahead)

        @pl.when(step < levels)
        def _():
            merge_small(step, bit)

        return 2 * bit

    lax.fori_loop(0, chips - 2, both_step, 1)
    late.pairs_ready(chips - 1)
    late.settle()
    done = done + ahead * (chips - 2)

    def late_step(step, carry):
        late.gather(step)
        advance(done + step, 1)
        return carry

    lax.fori_loop(0, chips - 2, late_step, 0)
    done = done + chips - 2
    advance(done, jnp.maximum(2 * final + 2 - done, 0))
    late.gather_last()
    late.finish()
    cross.finish()
    kept = [
        pltpu.make_async_copy(
            out2_w_s.at[pl.ds(0, second_total.shape[0])], second_total, semaphores.at[0]
        ),
        pltpu.make_async_copy(cross_total_s, cross_total, semaphores.at[1]),
    ]
    for index in range(hidden_blocks):
        kept.append(
            pltpu.make_async_copy(
                act_s.at[index], first_total.at[pl.ds(index * 2 * rows, 2 * rows)],
                semaphores.at[2 + index],
            )
        )
    start(*kept[:2])
    early.finish()
    start(*kept[2:])
    wait(*kept)
    for level in range(levels):
        small_copy(level, 1 << level).wait_send()
    rows_copy(1).wait()


def result_kernel(
    small_total, first_total, second_total, cross_total, rows_in, block_in,
    rows_buffer, block_out, rows_out, qkv_out, out_out,
    in_out, out2_out, cross_qkv_out, cross_out_out, slot_out, in_b_out, out2_b_out, gain_out,
    bias_out, cross_gain_out, cross_bias_out, first_s, second_s, rows_s, block_s,
    wide_s, semaphores,
):
    width = first_s.shape[1]
    half = width // 2
    for index in range(in_b_out.shape[1] // width):
        in_b_out[:, index * width : (index + 1) * width] = small_total[index : index + 1, :]
    out2_b_out[...] = small_total[4:5, :]
    gain_out[0] = small_total[5:7, :]
    bias_out[0] = small_total[7:9, :]
    cross_gain_out[...] = small_total[9:10, :half]
    cross_bias_out[...] = small_total[9:10, half:]
    copies = Copies(semaphores)
    rows = rows_in.shape[0] // 2
    front, rear = pl.ds(0, rows), pl.ds(rows, rows)
    rows_copy = copies.start(rows_in.at[rear], rows_s.at[rear])
    front_sem = semaphores.at[copies.count]
    copies.count += 1
    from_last = pltpu.make_async_copy(rows_in.at[front], rows_s.at[front], front_sem)
    from_main = pltpu.make_async_copy(rows_buffer.at[0, front], rows_s.at[front], front_sem)
    pl.when(lax.axis_index("pipe") == 1)(from_last.start)
    pl.when(lax.axis_index("pipe") == 0)(from_main.start)
    block_copy = copies.start(block_in.at[0], block_s)
    rows = rows_in.shape[0] // 2
    kept = []
    loads = {width: [], half: []}
    second_rows = 4 * width
    for index in range(first_s.shape[0] // width):
        spot = pl.ds(index * width, width)
        loads[width].append(copies.start(first_total.at[spot], first_s.at[spot]))
    for index in range(second_s.shape[0] // half):
        begin = index * half
        if begin < second_rows:
            source = second_total.at[pl.ds(begin, half)]
        else:
            source = cross_total.at[pl.ds(begin - second_rows, half)]
        loads[half].append(copies.start(source, second_s.at[pl.ds(begin, half)]))
    targets = []
    for index in range(first_s.shape[0] // width):
        hidden_blocks = in_out.shape[2] // width
        if index < hidden_blocks:
            target = in_out.at[0, :, pl.ds(index * width, width)]
        else:
            target = out2_out.at[0, pl.ds((index - hidden_blocks) * width, width)]
        targets.append((loads[width][index : index + 1], first_s, index * width, width, target))
    for index in range(4):
        if index < 3:
            target = qkv_out.at[0, :, pl.ds(index * width, width)]
        else:
            target = out_out.at[0]
        targets.append(
            (loads[half][2 * index : 2 * index + 2], second_s, index * width, width, target)
        )
    for index in range(4):
        if index < 3:
            target = cross_qkv_out.at[:, pl.ds(index * width, width)]
        else:
            target = cross_out_out
        targets.append(
            (loads[half][8 + index : 9 + index], second_s, 4 * width + index * half, half, target)
        )
    targets.append((loads[half][12:14], second_s, 6 * width, width, slot_out))
    block_copy.wait()
    kept.append(copies.start(block_s, block_out.at[0]))
    rows_copy.wait()
    from_last.wait()
    kept.append(copies.start(rows_s, rows_out.at[0]))
    place = 0
    for waits, stage, begin, size, target in targets:
        for copy in waits:
            copy.wait()
        wide_s[place : place + size] = stage[begin : begin + size].astype(WIDE)
        kept.append(copies.start(wide_s.at[pl.ds(place, size)], target))
        place += size
    for copy in kept:
        copy.wait()


ANY = pl.BlockSpec(memory_space=pl.ANY)
INNER = pl.BlockSpec(memory_space=pltpu.VMEM)
SCALAR = pl.BlockSpec(memory_space=pltpu.SMEM)


def local_call(
    body, name, scalars, inner, outer, outputs, scratch, flops, aliases=None, count=32,
    semaphores=(), **compiler,
):
    shapes = [jax.ShapeDtypeStruct(shape, kind) for shape, kind, _ in outputs]
    inputs = list(scalars) + list(inner) + list(outer)
    specs = [SCALAR] * len(scalars) + [INNER] * len(inner) + [ANY] * len(outer)
    moved = sum(value.size * value.dtype.itemsize for value in inputs)
    return pl.pallas_call(
        body,
        out_shape=shapes,
        in_specs=specs,
        out_specs=[INNER if kept else ANY for _, _, kept in outputs],
        scratch_shapes=[pltpu.VMEM(shape, kind) for shape, kind in scratch]
        + list(semaphores or [pltpu.SemaphoreType.DMA((count,))]),
        input_output_aliases=aliases or {},
        compiler_params=pltpu.CompilerParams(vmem_limit_bytes=VMEM_LIMIT, **compiler),
        cost_estimate=pl.CostEstimate(flops=flops, bytes_accessed=moved, transcendentals=0),
        name=name,
    )(*inputs)


def local(
    inputs, src_len, tgt_len, cotangent, qkv_w, out_w, in_w, in_b, out2_w, out2_b, norm_gain,
    norm_bias, cross_qkv, cross_out, slot_w, cross_gain, cross_bias,
):
    devices = lax.axis_size("dp")
    blocks = src_len.shape[0]
    total_rows, width = inputs.shape[1:]
    rows = total_rows // blocks
    half = width // 2
    hidden = in_w.shape[2]
    square, wide3, deep = (rows, width), (rows, 3 * width), (rows, hidden)
    weight_square, logsum = (width, width), (rows, PAIR)
    tall, tall3, tall_deep = (total_rows, width), (total_rows, 3 * width), (total_rows, hidden)
    extra_rows = 3 * width
    small_shape = (SMALL_ROWS, width)
    dma = pltpu.SemaphoreType.DMA
    tiles, halves = rows // ROW_TILE, rows // HALF_TILE

    (
        small, block_out, qkv, logsums, mixed, residual, low, act, slope, second, grad, hidden_grad,
        branch, qkv_grad, source_rows, query_grad, rest, memory_grad, query_w, own_extra,
        sent_extra,
    ) = local_call(
        main_kernel, "main_rows", [src_len, tgt_len],
        [
            in_b, out2_b, norm_gain, norm_bias, cross_gain, cross_bias,
        ],
        [inputs, cotangent, qkv_w, out_w, in_w, out2_w, cross_qkv, cross_out, slot_w],
        [
            (small_shape, WIDE, True), ((1,) + tall, LOW, False), ((2,) + wide3, LOW, False),
            ((2,) + logsum, WIDE, False), ((2,) + square, LOW, False), ((2,) + square, WIDE, False),
            ((2,) + square, LOW, False), ((2,) + deep, LOW, False), (deep, LOW, False),
            (square, WIDE, False), ((2,) + square, LOW, False), ((2,) + deep, LOW, False),
            (square, LOW, False), (wide3, LOW, False), ((1,) + tall, WIDE, False),
            ((2,) + square, LOW, False), ((2,) + square, WIDE, False), (square, LOW, False),
            (weight_square, LOW, False), ((extra_rows, width), LOW, False),
            ((extra_rows, width), LOW, False),
        ],
        [
            (tall, LOW), ((width, 3 * width), LOW), (weight_square, LOW), ((width, hidden), LOW),
            ((hidden, width), LOW), ((width, 3 * width), LOW), (weight_square, LOW),
            ((2 * width, width), LOW), (small_shape, LOW), ((2,) + wide3, LOW),
            ((2,) + logsum, WIDE), ((2,) + square, LOW), ((2,) + square, WIDE), (square, WIDE),
            (square, LOW), (deep, LOW), ((2,) + deep, LOW), ((2,) + square, WIDE),
            ((4,) + tall, LOW), ((6,) + tall, LOW), (square, LOW), ((rows, 2 * width), LOW),
            (logsum, WIDE), (square, WIDE), (square, LOW), (square, WIDE), (square, LOW),
            (deep, LOW), (square, WIDE), (square, WIDE), (square, LOW), ((2,) + square, LOW),
            (wide3, LOW), (small_shape, WIDE),
        ],
        70 * 10**9,
        semaphores=[
            dma((16,)), dma((2, 24)), dma((2, tiles)), dma((2, tiles)), dma((2, halves)),
            dma((2, halves)), dma((4,)), dma((4,)), dma((3,)), dma((3,)),
        ],
        collective_id=1, has_side_effects=True,
    )

    sizes = (2 * hidden, 4 * width, extra_rows)
    padded = [ring_rows(size, devices) for size in sizes]
    levels = devices.bit_length() - 1
    rings = [part for size in sizes for part in ring_scratch(size, width, devices)]
    rings += foreign_scratch(extra_rows, width, devices)
    first_total, second_total, cross_total, small_total, last_rows = local_call(
        functools.partial(last_kernel, devices), "last_rows", [src_len, tgt_len],
        [norm_gain, small],
        [
            inputs, qkv_w, out_w, in_w, out2_w, query_w, memory_grad, second, slope, query_grad,
            rest, residual, qkv, logsums, mixed, low, act, grad, hidden_grad, branch, qkv_grad,
            own_extra, sent_extra,
        ],
        [
            ((padded[0], width), LOW, False),
            ((padded[1], width), LOW, False),
            ((padded[2], width), LOW, False),
            (small_shape, WIDE, True),
            (tall, WIDE, False),
        ],
        [
            ((width, 3 * width), LOW), (weight_square, LOW), ((width, hidden), LOW),
            ((hidden, width), LOW), (tall, LOW), (tall_deep, LOW),
            ((hidden // width,) + tall, LOW), (tall, LOW), (tall, LOW), (tall, LOW), (tall, LOW),
            (tall3, LOW), (square, LOW), (square, WIDE), (deep, LOW), (square, WIDE),
            (weight_square, LOW), (square, WIDE), (wide3, LOW), (logsum, WIDE), (square, WIDE),
            (square, LOW), ((levels + 1,) + small_shape, WIDE), ((levels + 2,) + small_shape, WIDE),
            ((padded[2], width), LOW),
        ],
        20 * 10**9,
        semaphores=[dma((levels,)), dma((levels,)), dma((2,)), dma((64,))] + rings,
        collective_id=0, has_side_effects=True,
    )

    results = local_call(
        result_kernel, "results", [], [small_total],
        [first_total, second_total, cross_total, last_rows, block_out, source_rows],
        [
            ((1,) + tall, LOW, False), ((1,) + tall, WIDE, False),
            ((1, width, 3 * width), WIDE, False),
            ((1,) + weight_square, WIDE, False), ((1, width, hidden), WIDE, False),
            ((1, hidden, width), WIDE, False), ((half, 3 * width), WIDE, False),
            ((half, width), WIDE, False), ((width, width), WIDE, False),
            ((1, hidden), WIDE, True), ((1, width), WIDE, True), ((1, 2, width), WIDE, True),
            ((1, 2, width), WIDE, True), ((1, half), WIDE, True), ((1, half), WIDE, True),
        ],
        [
            ((sizes[0], width), LOW), ((sizes[1] + sizes[2], width), LOW), (tall, WIDE),
            (tall, LOW), ((sum(sizes), width), WIDE),
        ],
        10**9, count=64,
    )
    return (
        results[0], results[1], results[2], results[3], results[4], results[9], results[5],
        results[10], results[11], results[12], results[6], results[7], results[8],
        results[13].reshape(half), results[14].reshape(half),
    )


def solution(mesh):
    in_specs = (
        P("pipe", "dp", None),
        P("dp"),
        P("dp"),
        P("dp", None),
        P("pipe", None, None),
        P("pipe", None, None),
        P("pipe", None, None),
        P("pipe", None),
        P("pipe", None, None),
        P("pipe", None),
        P("pipe", None, None),
        P("pipe", None, None),
        P("pipe", None),
        P("pipe", None),
        P("pipe", None),
        P("pipe"),
        P("pipe"),
    )
    out_specs = (
        P("pipe", "dp", None),
        P("pipe", "dp", None),
        P("pipe", None, None),
        P("pipe", None, None),
        P("pipe", None, None),
        P("pipe", None),
        P("pipe", None, None),
        P("pipe", None),
        P("pipe", None, None),
        P("pipe", None, None),
        P("pipe", None),
        P("pipe", None),
        P("pipe", None),
        P("pipe"),
        P("pipe"),
    )
    return jax.shard_map(local, mesh=mesh, in_specs=in_specs, out_specs=out_specs, check_vma=False)
```
